128 devices in a mesh: grp: 2 (over x_hi), seq: 8 (over y, core), tp: 8 (over x_lo, z).
Axes of the slice: x: 4 (x_hi: 2, x_lo: 2; x = x_hi * 2 + x_lo), y: 4, z: 4, core: 2. Of those that a mesh axis runs over, the one named last changes fastest.
Arguments:
- tokens: bfloat16 [2, 8, 256, 4096], P('grp', 'seq', 'tp'), may hold values from -6 to 6
- text_gaps: int32 [8, 5], P('seq'), may hold values from 1 to 128, 256 in all within a row
- image_runs: int32 [8, 4], P('seq'), may hold values from 1 to 64, 128 in all within a row
- gains: bfloat16 [2, 4096], P('grp'), may hold values from 0.099609375 to 1.8984375
- w_qkv: bfloat16 [2, 4096, 3, 4096], P('grp', None, None, 'tp')
- w_out: bfloat16 [2, 4096, 4096], P('grp', None, 'tp'), may hold values from -0.09375 to 0.09375
- cotangent: bfloat16 [2, 8, 256, 4096], P('grp', 'seq', 'tp'), may hold values from -1.5 to 1.5
Outputs:
- layer_out: bfloat16 [2, 8, 256, 4096], P('grp', 'seq', 'tp')
- tokens_grad: bfloat16 [2, 8, 256, 4096], P('grp', 'seq', 'tp')
- gain_grad: float32 [2, 4096], P('grp')
- qkv_weight_grad: float32 [2, 4096, 3, 4096], P('grp', 'seq', None, 'tp')
- out_weight_grad: float32 [2, 4096, 4096], P('grp', 'seq', 'tp')
The draws below stay inside these ranges and needn't reach their ends.
Inputs may be any that keep to these rules, and one draw needn't show every extreme that they name: `text_gaps`: the text runs of a sequence add up to 256; some run has exactly 128 tokens. `image_runs`: the image runs of a sequence add up to 128; some run has exactly 64 tokens.
All inputs are finite; a program needn't handle non-finite values.
Results may differ from the reference program's by a relative error of at most 0.034.
The reference program's roundings to bfloat16 on the way (of `normed`, `qkv`, `attn_b`, `mixed`, `grad_rows`, `grad_mixed`, `score_grad` and `qkv_grad`) count: a program that leaves them out, or rounds other values in their place, can miss the bound.
Values may be sent and summed in bfloat16 or wider, within the bound.
No kernel may reach another device: no remote copies, remote signals or barrier semaphores. Data moves between devices by JAX's collectives and lax.ppermute only.
A program may use at most 128 MiB of HBM per device.

```python
import math
import jax
import jax.numpy as jnp
import numpy as np
from jax import lax

D = 4096
NH = 32
HS = 128
LT = 256
LI = 128
NSPAN = 4
SEQS = 8
N_TP = 8


def draw_w_qkv(key, part):
    key = jax.random.fold_in(key, 11)
    base_key = jax.random.fold_in(key, 0)
    entries = jax.random.normal(base_key, (2, D, 3, NH * HS), jnp.float32) * D ** (-0.5)
    return entries.astype(jnp.bfloat16)


def with_spikes(values, rng, source, target, parts, factor):
    owner, partner = [(jnp.arange(values.shape[dim]) // (values.shape[dim] // parts)).reshape([-1 if axis == dim else 1 for axis in range(values.ndim)]) for dim in (source, target)]
    chosen = jax.random.permutation(rng, parts)[partner]
    strong = (owner == chosen) | (owner == (partner + parts // 2) % parts)
    return jnp.where(strong, factor * values, values)


def level_of(key, dims, shards, low, top_value):
    def one(position, shards_of):
        steps = jax.random.uniform(jax.random.fold_in(jax.random.fold_in(key, 6), position), (shards_of,), jnp.float32, low / len(shards), top_value / len(shards))
        return jnp.repeat(jnp.exp(steps), dims[position] // shards_of).reshape((-1,) + (1,) * (len(dims) - position - 1))

    gain = one(*shards[0])
    for cut in shards[1:]:
        gain = gain * one(*cut)
    return gain


def length_profile(amount, total, most, lean):
    loads = [(1 << 20) // math.isqrt(rank ** lean) + 1 for rank in range(2, amount + 1)]
    spare, given = total - most - (amount - 1), [1] * (amount - 1)
    while spare > 0:
        movable = [i for i in range(amount - 1) if given[i] < most]
        pool, budget = sum([loads[i] for i in movable]), spare
        for i in movable:
            addition = min(most - given[i], max(1, budget * loads[i] // pool), spare)
            given[i] = given[i] + addition
            spare = spare - addition
    return np.array([most] + given)


def ragged(key, count, total, most, skew):
    if count == 2:
        one = jax.random.randint(key, (), max(1, total - most), min(most, total - 1) + 1)
        return jnp.stack([one, total - one])
    tallies = jnp.asarray(length_profile(count, total, most, skew), jnp.int32)
    twos = (count - 1) // 2
    giver, sink = tallies[1:1 + 2 * twos:2], tallies[2:2 + 2 * twos:2]
    margin = jnp.minimum(giver - 1, most - sink)
    passed = jax.random.randint(jax.random.fold_in(key, 1), (twos,), 0, 1 << 20) % (margin + 1)
    tallies = tallies.at[1:1 + 2 * twos:2].set(giver - passed).at[2:2 + 2 * twos:2].set(sink + passed)
    return tallies[jax.random.permutation(jax.random.fold_in(key, 2), count)]


def bell_draw(key, shape, width, bound, cuts=(), kind=jnp.bfloat16):
    values = jax.random.normal(key, shape, jnp.float32) * width
    if len(cuts) > 0:
        values = level_of(key, shape, cuts, -0.22, 0.18) * values
    return jnp.clip(values, min=-bound, max=bound).astype(kind)


def gaussian_with(rng, dims, deviation, limit, pieces, heavy, held_as=jnp.bfloat16):
    drawn = deviation * jax.random.normal(rng, dims, jnp.float32)
    if pieces:
        drawn = drawn * level_of(rng, dims, pieces, -0.22, 0.18)
    return jnp.clip(with_spikes(drawn, jax.random.fold_in(rng, 3), *heavy), -limit, limit).astype(held_as)


def setup_inputs(seed: int = 0) -> dict:
    key_of = jax.random.split(jax.random.key(seed), 8)
    return {
        "tokens": bell_draw(key_of[0], (2, SEQS, LT, D), 1.0, 6.0, ((0, 2), (1, 8), (2, 8))),
        "text_gaps": jax.vmap(lambda own: ragged(own, NSPAN + 1, LT, LT // 2, 2))(jax.random.split(key_of[1], SEQS)).reshape((SEQS, NSPAN + 1)).astype(jnp.int32),
        "image_runs": jax.vmap(lambda own: ragged(own, NSPAN, LI, LI // 2, 2))(jax.random.split(key_of[2], SEQS)).reshape((SEQS, NSPAN)).astype(jnp.int32),
        "gains": jnp.clip(1.0 + 0.18 * jax.random.normal(key_of[3], (2, D), jnp.float32), 0.099609375, 1.8984375).astype(jnp.bfloat16),
        "w_qkv": draw_w_qkv(jax.random.fold_in(key_of[7], 71), 0),
        "w_out": bell_draw(key_of[5], (2, D, NH * HS), (NH * HS) ** -0.5, 0.09375, ((0, 2), (2, 8))),
        "cotangent": gaussian_with(key_of[6], (2, SEQS, LT, D), 0.25, 1.5, ((0, 2), (1, 8), (2, 8)), (1, 3, 8, 2.0)),
    }


far_place = 1073741824

def place_tokens(text_gaps, image_runs, slot_count, image_count):
    text_ends = jnp.cumsum(text_gaps).astype(jnp.int32)
    image_ends = jnp.cumsum(image_runs).astype(jnp.int32)
    run_count = image_runs.shape[0]
    slot_ids = jnp.arange(slot_count, dtype=jnp.int32)
    run_ids = jnp.arange(run_count + 1, dtype=jnp.int32)
    image_before = jnp.concatenate([jnp.zeros((1,), jnp.int32), image_ends]).astype(jnp.int32)
    text_run = lax.optimization_barrier(jnp.sum((slot_ids[:, None] >= text_ends[None, :]).astype(jnp.int32), axis=1)).astype(jnp.int32)
    text_shift = lax.optimization_barrier(jnp.sum(jnp.where(run_ids[None, :] == text_run[:, None], image_before[None, :], 0), axis=1)).astype(jnp.int32)
    image_run = lax.optimization_barrier(jnp.sum((slot_ids[:, None] >= image_ends[None, :]).astype(jnp.int32), axis=1)).astype(jnp.int32)
    image_shift = lax.optimization_barrier(jnp.sum(jnp.where(run_ids[None, :] == image_run[:, None], text_ends[None, :], 0), axis=1)).astype(jnp.int32)
    text_place = (slot_ids + text_shift).astype(jnp.int32)
    image_place = jnp.where(slot_ids < image_count, slot_ids + image_shift, far_place).astype(jnp.int32)
    return (text_place, image_place)

def attend_rows(queries, query_place, all_keys, key_place, scale):
    scores = jnp.einsum('qhd,khd->hqk', queries.astype(jnp.float32), all_keys.astype(jnp.float32)) * scale
    allowed = key_place[None, :] <= query_place[:, None]
    scores = jnp.where(allowed[None], scores, -1e+30)
    row_max = lax.optimization_barrier(jnp.max(scores, axis=2, keepdims=True))
    weights = jnp.exp(scores - row_max)
    row_sum = lax.optimization_barrier(jnp.sum(weights, axis=2, keepdims=True))
    return weights / row_sum

def rounded(values):
    return lax.optimization_barrier(values.astype(jnp.bfloat16)).astype(jnp.float32)

def reference(tokens, text_gaps, image_runs, gains, w_qkv, w_out, cotangent):
    f32 = jnp.float32
    bf16 = jnp.bfloat16
    scale = HS ** (-0.5)
    head_cols = NH * HS // N_TP
    gain_rows = gains.astype(f32)
    qkv_weight_grad = jnp.zeros((2, D, 3 * NH * HS), f32)
    out_weight_grad = jnp.zeros((2, D, NH * HS), f32)
    gain_grad = jnp.zeros((2, D), f32)
    out_lists = [[], []]
    grad_lists = [[], []]
    for seq_index in range(SEQS):
        text_place, image_place = place_tokens(text_gaps[seq_index], image_runs[seq_index], LT, LI)
        places = [text_place, image_place]
        saved_state = []
        for group_index in range(2):
            x_float = tokens[group_index, seq_index].astype(f32)
            inv_rms = lax.rsqrt(lax.optimization_barrier(jnp.mean(x_float * x_float, axis=1, keepdims=True)) + 1e-05)
            normed = (x_float * inv_rms * gain_rows[group_index]).astype(bf16)
            qkv = jnp.dot(normed, w_qkv[group_index].reshape(D, 3 * NH * HS), preferred_element_type=f32)
            qkv = qkv.astype(bf16).reshape(LT, 3, NH, HS)
            saved_state.append((x_float, inv_rms, normed, qkv))
        attn_saved = []
        for group_index in range(2):
            other_group = 1 - group_index
            x_float, inv_rms, normed, qkv = saved_state[group_index]
            other_qkv = saved_state[other_group][3]
            all_keys = jnp.concatenate([qkv[:, 1], other_qkv[:, 1]], axis=0)
            all_values = jnp.concatenate([qkv[:, 2], other_qkv[:, 2]], axis=0)
            key_place = jnp.concatenate([places[group_index], places[other_group]], axis=0)
            attn = attend_rows(qkv[:, 0], places[group_index], all_keys, key_place, scale)
            attn_b = attn.astype(bf16)
            mixed = jnp.einsum('hqk,khd->qhd', attn_b.astype(f32), all_values.astype(f32)).astype(bf16)
            mixed_flat = mixed.reshape(LT, NH * HS)
            valid = (places[group_index] < far_place).astype(f32)[:, None]
            proj = jnp.zeros((LT, D), f32)
            for part in range(N_TP):
                cols = slice(part * head_cols, (part + 1) * head_cols)
                term = jnp.dot(mixed_flat[:, cols], w_out[group_index][:, cols].T, preferred_element_type=f32)
                proj = proj + rounded(term)
            out_lists[group_index].append(((x_float + proj) * valid).astype(bf16))
            grad_rows = cotangent[group_index, seq_index] * valid.astype(bf16)
            grad_mixed = jnp.dot(grad_rows, w_out[group_index], preferred_element_type=f32).astype(bf16)
            grad_mixed = grad_mixed.reshape(LT, NH, HS)
            value_grad = jnp.einsum('hqk,qhd->khd', attn_b.astype(f32), grad_mixed.astype(f32))
            weight_grad = jnp.einsum('qhd,khd->hqk', grad_mixed.astype(f32), all_values.astype(f32))
            row_dot = jnp.einsum('qhd,qhd->hq', grad_mixed.astype(f32), mixed.astype(f32))[:, :, None]
            score_grad = (attn * (weight_grad - row_dot)).astype(bf16)
            query_grad = jnp.einsum('hqk,khd->qhd', score_grad.astype(f32), all_keys.astype(f32)) * scale
            key_grad = jnp.einsum('hqk,qhd->khd', score_grad.astype(f32), qkv[:, 0].astype(f32)) * scale
            attn_saved.append((grad_rows, mixed_flat, query_grad, key_grad, value_grad))
        for group_index in range(2):
            other_group = 1 - group_index
            x_float, inv_rms, normed, qkv = saved_state[group_index]
            grad_rows, mixed_flat, query_grad, key_grad, value_grad = attn_saved[group_index]
            other_key = attn_saved[other_group][3]
            other_value = attn_saved[other_group][4]
            own_key = key_grad[:LT] + other_key[LT:]
            own_value = value_grad[:LT] + other_value[LT:]
            qkv_grad = jnp.stack([query_grad, own_key, own_value], axis=1).astype(bf16).reshape(LT, 3, NH * HS)
            normed_grad = jnp.zeros((LT, D), f32)
            for part in range(N_TP):
                cols = slice(part * head_cols, (part + 1) * head_cols)
                left = qkv_grad[:, :, cols].reshape(LT, 3 * head_cols)
                right = w_qkv[group_index][:, :, cols].reshape(D, 3 * head_cols)
                normed_grad = normed_grad + rounded(jnp.dot(left, right.T, preferred_element_type=f32))
            gain_row = gain_rows[group_index]
            gain_grad = gain_grad.at[group_index].add(lax.optimization_barrier(jnp.sum(normed_grad * x_float * inv_rms, axis=0)))
            scaled = gain_row * normed_grad
            x_grad = grad_rows.astype(f32) + inv_rms * scaled - x_float * (inv_rms * inv_rms * inv_rms) * lax.optimization_barrier(jnp.mean(scaled * x_float, axis=1, keepdims=True))
            grad_lists[group_index].append(x_grad.astype(bf16))
            flat_grad = qkv_grad.reshape(LT, 3 * NH * HS)
            qkv_term = lax.dot_general(normed, flat_grad, (((0,), (0,)), ((), ())), preferred_element_type=f32)
            out_term = lax.dot_general(grad_rows, mixed_flat, (((0,), (0,)), ((), ())), preferred_element_type=f32)
            qkv_weight_grad = qkv_weight_grad.at[group_index].add(rounded(qkv_term))
            out_weight_grad = out_weight_grad.at[group_index].add(rounded(out_term))
    layer_out = jnp.stack([jnp.stack(out_lists[0]), jnp.stack(out_lists[1])])
    tokens_grad = jnp.stack([jnp.stack(grad_lists[0]), jnp.stack(grad_lists[1])])
    return (layer_out, tokens_grad, gain_grad, qkv_weight_grad.reshape(2, D, 3, NH * HS), out_weight_grad)
```

```python
import jax
import jax.numpy as jnp
from jax import lax
from jax.sharding import PartitionSpec as P

HS = 128
LI = 128


far_place = 1073741824
f32 = jnp.float32
bf16 = jnp.bfloat16


def z_shift(k):
    return [(i, (i // 4) * 4 + (i + k) % 4) for i in range(8)]


X_SWAP = [(i, i ^ 4) for i in range(8)]


def y_shift(k):
    return [(i, (i + 2 * k) % 8) for i in range(8)]


CORE_SWAP = [(i, i ^ 1) for i in range(8)]
STEPS = (1, 3, 2)


def place_tokens(text_gaps, image_runs, slot_count, image_count):
    text_ends = jnp.cumsum(text_gaps)
    image_ends = jnp.cumsum(image_runs)
    run_count = image_runs.shape[0]
    slot_ids = jnp.arange(slot_count, dtype=jnp.int32)
    run_ids = jnp.arange(run_count + 1, dtype=jnp.int32)
    image_before = jnp.concatenate([jnp.zeros((1,), jnp.int32), image_ends])
    text_run = jnp.sum((slot_ids[:, None] >= text_ends[None, :]).astype(jnp.int32), axis=1)
    text_shift = jnp.sum(
        jnp.where(run_ids[None, :] == text_run[:, None], image_before[None, :], 0), axis=1
    )
    image_run = jnp.sum((slot_ids[:, None] >= image_ends[None, :]).astype(jnp.int32), axis=1)
    image_shift = jnp.sum(
        jnp.where(run_ids[None, :] == image_run[:, None], text_ends[None, :], 0), axis=1
    )
    text_place = slot_ids + text_shift
    image_place = jnp.where(slot_ids < image_count, slot_ids + image_shift, far_place)
    return (text_place, image_place)


def block_at(blocks, index):
    return lax.dynamic_index_in_dim(blocks, index, 0, keepdims=False)


def gather_blocks(rows, x_index, z_index):
    half = rows.shape[1] // 2
    left, right = rows[:, :half], rows[:, half:]
    right_pair = jnp.stack([right, lax.ppermute(right, "tp", X_SWAP)])
    left_four = [left] + [lax.ppermute(left, "tp", z_shift(k)) for k in STEPS]
    right_four = [right_pair] + [lax.ppermute(right_pair, "tp", z_shift(k)) for k in STEPS]
    left_other = lax.ppermute(jnp.stack(left_four), "tp", X_SWAP)
    found = []
    for slot, k in enumerate((0,) + STEPS):
        z_from = (z_index + 4 - k) % 4
        own, other = x_index * 4 + z_from, (1 - x_index) * 4 + z_from
        found.append((own, 0, left_four[slot]))
        found.append((other, 0, left_other[slot]))
        found.append((own, 1, right_four[slot][0]))
        found.append((other, 1, right_four[slot][1]))
    return found


def scatter_left(part, x_index, z_index):
    blocks = part.reshape((2, 4) + part.shape[1:])

    def column(z):
        return lax.dynamic_index_in_dim(blocks, z, 1, keepdims=False)

    total = column(z_index).astype(f32)
    for k in STEPS:
        total = total + lax.ppermute(column((z_index + k) % 4), "tp", z_shift(k)).astype(f32)
    sent = block_at(total, 1 - x_index).astype(bf16)
    return block_at(total, x_index) + lax.ppermute(sent, "tp", X_SWAP).astype(f32)


def scatter_right(part, x_index, z_index):
    blocks = part.reshape((2, 4) + part.shape[1:])
    came = lax.ppermute(block_at(blocks, 1 - x_index), "tp", X_SWAP)
    pair = block_at(blocks, x_index).astype(f32) + came.astype(f32)
    pair_b = pair.astype(bf16)
    total = block_at(pair, z_index)
    for k in STEPS:
        sent = block_at(pair_b, (z_index + k) % 4)
        total = total + lax.ppermute(sent, "tp", z_shift(k)).astype(f32)
    return total


def attend_rows(queries, query_place, all_keys, key_place, scale):
    scores = (
        jnp.einsum("qhd,khd->hqk", queries, all_keys, preferred_element_type=jnp.float32) * scale
    )
    allowed = key_place[None, :] <= query_place[:, None]
    scores = jnp.where(allowed[None], scores, -1e30)
    row_max = jnp.max(scores, axis=2, keepdims=True)
    weights = jnp.exp(scores - row_max)
    row_sum = jnp.sum(weights, axis=2, keepdims=True)
    return weights / row_sum


def dot_rows(left, right):
    return lax.dot_general(left, right, (((1,), (1,)), ((), ())), preferred_element_type=f32)


def dot_tokens(left, right):
    return lax.dot_general(left, right, (((0,), (0,)), ((), ())), preferred_element_type=f32)


def per_device(tokens, text_gaps, image_runs, gains, w_qkv, w_out, cotangent):
    scale = HS ** (-0.5)
    group_index = lax.axis_index("grp")
    tp_index = lax.axis_index("tp")
    seq_index = lax.axis_index("seq")
    x_index, z_index = tp_index // 4, tp_index % 4
    y_index, core = seq_index // 2, seq_index % 2
    x_rows = tokens[0, 0]
    row_count, width = x_rows.shape
    w_parts = jnp.transpose(w_qkv[0], (1, 0, 2))
    head_cols = w_parts.shape[2]
    head_count = head_cols // HS
    out_w = w_out[0]
    gain_row = gains[0].astype(f32)
    slot_count = row_count * 8
    text_place, image_place = place_tokens(text_gaps[0], image_runs[0], slot_count, LI)
    own_place = jnp.where(group_index == 0, text_place, image_place)
    other_place = jnp.where(group_index == 0, image_place, text_place)
    key_place = jnp.concatenate([own_place, other_place], axis=0)
    valid_all = (own_place < far_place).astype(f32)
    valid_rows = lax.dynamic_slice_in_dim(valid_all, tp_index * row_count, row_count, 0)[:, None]

    grad_rows = cotangent[0, 0] * valid_rows.astype(bf16)
    grad_full = lax.all_gather(grad_rows, "tp", axis=0, tiled=True)
    x_float = x_rows.astype(f32)
    inv_rms = lax.rsqrt(jnp.mean(x_float * x_float, axis=1, keepdims=True) + 1e-05)
    normed = (x_float * inv_rms * gain_row).astype(bf16)
    half = width // 2
    normed_full = jnp.zeros((slot_count, width), bf16)
    for index, side, block in gather_blocks(normed, x_index, z_index):
        normed_full = lax.dynamic_update_slice(
            normed_full, block, (index * row_count, side * half)
        )

    pair_rows = width // 4
    chunks = [lax.dynamic_slice_in_dim(normed_full, y_index * pair_rows, pair_rows, 1)]
    for k in STEPS:
        sent = lax.dynamic_slice_in_dim(normed_full, (y_index + k) % 4 * pair_rows, pair_rows, 1)
        chunks.append(lax.ppermute(sent, "seq", y_shift(k)))

    def project(part):
        return jnp.dot(normed_full, w_parts[part], preferred_element_type=f32).astype(bf16)

    own_kv = jnp.stack([project(1), project(2)])
    other_kv = lax.ppermute(own_kv, "grp", [(0, 1), (1, 0)])
    own_q = project(0).reshape(slot_count, head_count, HS)
    all_kv = jnp.concatenate([own_kv, other_kv], axis=1)
    all_keys = all_kv[0].reshape(2 * slot_count, head_count, HS)
    all_values = all_kv[1].reshape(2 * slot_count, head_count, HS)
    attn = attend_rows(own_q, own_place, all_keys, key_place, scale)
    attn_b = attn.astype(bf16)
    mixed = jnp.einsum("hqk,khd->qhd", attn_b, all_values, preferred_element_type=f32).astype(bf16)
    mixed_flat = mixed.reshape(slot_count, head_cols)
    proj_rows = lax.psum_scatter(
        dot_rows(mixed_flat, out_w).astype(bf16), "tp", scatter_dimension=0, tiled=True
    ).astype(f32)
    layer_out = ((x_float + proj_rows) * valid_rows).astype(bf16)
    grad_mixed = jnp.dot(grad_full, out_w, preferred_element_type=f32).astype(bf16)
    out_share = lax.psum_scatter(
        dot_tokens(grad_full, mixed_flat).astype(bf16), "seq", scatter_dimension=0, tiled=True
    ).astype(f32)

    grad_heads = grad_mixed.reshape(slot_count, head_count, HS)
    value_grad = jnp.einsum("hqk,qhd->khd", attn_b, grad_heads, preferred_element_type=f32)
    weight_grad = jnp.einsum("qhd,khd->hqk", grad_heads, all_values, preferred_element_type=f32)
    row_dot = jnp.einsum("qhd,qhd->hq", grad_heads, mixed, preferred_element_type=f32)[:, :, None]
    score_grad = (attn * (weight_grad - row_dot)).astype(bf16)
    query_grad = jnp.einsum("hqk,khd->qhd", score_grad, all_keys, preferred_element_type=f32) * scale
    key_grad = jnp.einsum("hqk,qhd->khd", score_grad, own_q, preferred_element_type=f32) * scale
    kv_grad = jnp.stack([key_grad, value_grad]).reshape(2, 2 * slot_count, head_cols)
    back = lax.ppermute(kv_grad[:, slot_count:].astype(bf16), "grp", [(0, 1), (1, 0)])
    own_kv_grad = (kv_grad[:, :slot_count] + back.astype(f32)).astype(bf16)
    own_q_grad = query_grad.astype(bf16).reshape(slot_count, head_cols)

    def normed_part(rows):
        part = dot_rows(own_q_grad, w_parts[0][rows])
        part = part + dot_rows(own_kv_grad[0], w_parts[1][rows])
        part = part + dot_rows(own_kv_grad[1], w_parts[2][rows])
        return part.astype(bf16)

    halves = [normed_part(slice(0, half)), normed_part(slice(half, width))]
    inv_gain = 1.0 / gain_row
    gain_term = jnp.concatenate(
        [
            jnp.sum(part.astype(f32) * normed_full[:, cols].astype(f32), axis=0)
            for part, cols in zip(halves, (slice(0, half), slice(half, width)))
        ]
    )
    gain_grad = gain_term * inv_gain
    for axis, flip in (("tp", 1), ("tp", 2), ("tp", 4), ("seq", 1), ("seq", 2), ("seq", 4)):
        gain_grad = gain_grad + lax.ppermute(gain_grad, axis, [(i, i ^ flip) for i in range(8)])
    part_shape = (8, row_count, half)
    normed_grad = jnp.concatenate(
        [
            scatter_left(halves[0].reshape(part_shape), x_index, z_index),
            scatter_right(halves[1].reshape(part_shape), x_index, z_index),
        ],
        axis=1,
    )
    scaled = gain_row * normed_grad
    x_grad = (
        grad_rows.astype(f32)
        + inv_rms * scaled
        - x_float
        * (inv_rms * inv_rms * inv_rms)
        * jnp.mean(scaled * x_float, axis=1, keepdims=True)
    )
    tokens_grad = x_grad.astype(bf16)

    q_grads = [own_q_grad] + [lax.ppermute(own_q_grad, "seq", y_shift(k)) for k in STEPS]
    kv_grads = [own_kv_grad] + [lax.ppermute(own_kv_grad, "seq", y_shift(k)) for k in STEPS]
    share = []
    for part in range(3):
        right = [q_grads[i] if part == 0 else kv_grads[i][part - 1] for i in range(4)]
        share.append(dot_tokens(jnp.concatenate(chunks, axis=0), jnp.concatenate(right, axis=0)))
    share = jnp.stack(share).reshape(3, 2, pair_rows // 2, head_cols)
    mine = lax.dynamic_index_in_dim(share, core, 1, keepdims=False)
    sent = lax.dynamic_index_in_dim(share, 1 - core, 1, keepdims=False).astype(bf16)
    qkv_share = mine + lax.ppermute(sent, "seq", CORE_SWAP).astype(f32)
    return (
        layer_out.reshape(1, 1, row_count, width),
        tokens_grad.reshape(1, 1, row_count, width),
        gain_grad.reshape(1, width),
        jnp.transpose(qkv_share, (1, 0, 2))[None],
        out_share[None],
    )


def solution(mesh):
    in_specs = (
        P("grp", "seq", "tp", None),
        P("seq", None),
        P("seq", None),
        P("grp", None),
        P("grp", None, None, "tp"),
        P("grp", None, "tp"),
        P("grp", "seq", "tp", None),
    )
    out_specs = (
        P("grp", "seq", "tp", None),
        P("grp", "seq", "tp", None),
        P("grp", None),
        P("grp", "seq", None, "tp"),
        P("grp", "seq", "tp"),
    )
    return jax.shard_map(
        per_device, mesh=mesh, in_specs=in_specs, out_specs=out_specs, check_vma=False
    )
```

```python
import functools

import jax
import jax.numpy as jnp
from jax import lax
from jax.experimental import pallas as pl
from jax.experimental.pallas import tpu as pltpu
from jax.sharding import PartitionSpec as P

HS = 128
LI = 128
HEADS = 4
SLOTS = 256
ROWS = 32
WIDTH = 4096
HALF = 2048
COLS = 512
FAR = 1073741824
f32 = jnp.float32
bf16 = jnp.bfloat16
VMEM_LIMIT = 40 * 1024 * 1024

STEPS = (0, 1, 3, 2)


def z_shift(k):
    return [(i, (i // 4) * 4 + (i + k) % 4) for i in range(8)]


X_SWAP = [(i, i ^ 4) for i in range(8)]


def y_shift(k):
    return [(i, (i + 2 * k) % 8) for i in range(8)]


CORE_SWAP = [(i, i ^ 1) for i in range(8)]
GRP_SWAP = [(0, 1), (1, 0)]


def sds(shape, dtype):
    return jax.ShapeDtypeStruct(shape, dtype)


def call(kernel, out_shape, flops=0, nbytes=0, **kwargs):
    return pl.pallas_call(
        kernel,
        out_shape=out_shape,
        compiler_params=pltpu.CompilerParams(vmem_limit_bytes=VMEM_LIMIT),
        cost_estimate=pl.CostEstimate(flops=flops, bytes_accessed=nbytes, transcendentals=0),
        **kwargs,
    )


def whole(shape):
    return pl.BlockSpec(shape, lambda *_: (0,) * len(shape))


SMEM = pl.BlockSpec(memory_space=pltpu.SMEM)


def dot(left, right):
    return jnp.dot(left, right, preferred_element_type=f32)


def dot_rows(left, right):
    return lax.dot_general(left, right, (((1,), (1,)), ((), ())), preferred_element_type=f32)


def dot_tokens(left, right):
    return lax.dot_general(left, right, (((0,), (0,)), ((), ())), preferred_element_type=f32)


def norm_kernel(valid, x, gain, cot, n_left, n_right, c_left, c_right, inv):
    x_float = x[...].astype(f32)
    scale = lax.rsqrt(jnp.mean(x_float * x_float, axis=1, keepdims=True) + 1e-05)
    normed = (x_float * scale * gain[...].astype(f32)).astype(bf16)
    n_left[...] = normed[:, :HALF]
    n_right[...] = normed[:, HALF:]
    grad = (cot[...].astype(f32) * valid[0]).astype(bf16)
    c_left[...] = grad[:, :HALF]
    c_right[...] = grad[:, HALF:]
    inv[...] = jnp.broadcast_to(scale, (ROWS, 128))


def norm_rows(valid, x, gain, cot):
    part = sds((ROWS, HALF), bf16)
    return call(
        norm_kernel,
        [part, part, part, part, sds((ROWS, 128), f32)],
        nbytes=4 * ROWS * WIDTH * 2,
        in_specs=[SMEM] + [pl.BlockSpec(memory_space=pltpu.VMEM)] * 3,
        name="norm_rows",
    )(valid, x, gain, cot)


def gather_blocks(left, right):
    right_pair = jnp.stack([right, lax.ppermute(right, "tp", X_SWAP)])
    left_four = [left] + [lax.ppermute(left, "tp", z_shift(k)) for k in STEPS[1:]]
    right_four = [right_pair] + [lax.ppermute(right_pair, "tp", z_shift(k)) for k in STEPS[1:]]
    left_own = jnp.stack(left_four)
    left_other = lax.ppermute(left_own, "tp", X_SWAP)
    return [left_own, left_other] + right_four


def place_pieces(pieces, whole_ref):
    left_own, left_other = pieces[:2]
    for slot in range(4):
        rows = pl.ds(slot * ROWS, ROWS)
        other = pl.ds((4 + slot) * ROWS, ROWS)
        whole_ref[rows, :HALF] = left_own[slot]
        whole_ref[other, :HALF] = left_other[slot]
        whole_ref[rows, HALF:] = pieces[2 + slot][0]
        whole_ref[other, HALF:] = pieces[2 + slot][1]


PIECE_SHAPES = [(4, ROWS, HALF)] * 2 + [(2, ROWS, HALF)] * 4


def scatter_left(own, sends):
    total = own.astype(f32)
    for k, sent in zip(STEPS[1:], sends):
        total = total + lax.ppermute(sent, "tp", z_shift(-k)).astype(f32)
    return total[0] + lax.ppermute(total[1].astype(bf16), "tp", X_SWAP).astype(f32)


def scatter_right(own, sent):
    four = own.astype(f32) + lax.ppermute(sent, "tp", X_SWAP).astype(f32)
    total = four[0]
    for slot in range(1, 4):
        came = lax.ppermute(four[slot].astype(bf16), "tp", z_shift(-STEPS[slot]))
        total = total + came.astype(f32)
    return total


def gather_dot_kernel(*refs):
    pieces, weight, full, out = refs[:6], refs[6], refs[7], refs[8]
    first = functools.reduce(
        jnp.logical_and, [pl.program_id(i) == 0 for i in range(2)]
    )

    @pl.when(first)
    def _():
        place_pieces(pieces, full)

    out[0] = dot(full[...], weight[0]).astype(bf16)


def gather_dot(pieces, weights, parts):
    count = len(parts)
    block = 256
    low = parts[0]
    return call(
        gather_dot_kernel,
        [sds((SLOTS, WIDTH), bf16), sds((count, SLOTS, COLS), bf16)],
        flops=2 * count * SLOTS * WIDTH * COLS,
        nbytes=count * WIDTH * COLS * 2 + 2 * SLOTS * WIDTH * 2,
        grid=(count, COLS // block),
        in_specs=[whole(s) for s in PIECE_SHAPES]
        + [pl.BlockSpec((1, WIDTH, block), lambda p, j: (p + low, 0, j))],
        out_specs=[
            whole((SLOTS, WIDTH)),
            pl.BlockSpec((1, SLOTS, block), lambda p, j: (p, 0, j)),
        ],
        name="gather_dot",
    )(*pieces, weights)


def one_dot_kernel(full, weight, out):
    out[...] = dot(full[...], weight[0]).astype(bf16)


def one_dot(full, weights, part):
    block = 256
    return call(
        one_dot_kernel,
        sds((SLOTS, COLS), bf16),
        flops=2 * SLOTS * WIDTH * COLS,
        nbytes=WIDTH * COLS * 2 + SLOTS * WIDTH * 2,
        grid=(COLS // block,),
        in_specs=[
            whole((SLOTS, WIDTH)),
            pl.BlockSpec((1, WIDTH, block), lambda j: (part, 0, j)),
        ],
        out_specs=pl.BlockSpec((SLOTS, block), lambda j: (0, j)),
        name="one_dot",
    )(full, weights)


def back_kernel(count, left_half, with_gain, *refs):
    lefts, weight = refs[:count], refs[count]
    refs = refs[count + 1:]
    total = dot_rows(lefts[0][...], weight[0])
    for part in range(1, count):
        total = total + dot_rows(lefts[part][...], weight[part])
    rounded = total.astype(bf16)
    if with_gain:
        normed, refs = refs[0], refs[1:]
        refs[-1][...] = jnp.sum(
            rounded.astype(f32) * normed[...].astype(f32), axis=0, keepdims=True
        )
    for xbit in range(2):
        for slot in range(4):
            start = (xbit * 4 + slot) * ROWS
            block = rounded[start:start + ROWS]
            if left_half:
                refs[slot][xbit] = block
            else:
                refs[xbit][slot] = block


def back_dot(lefts, weights, left_half, normed=None):
    count = len(lefts)
    block = 512
    first = 0 if left_half else HALF // block
    with_gain = normed is not None
    operands = list(lefts) + [weights]
    in_specs = [whole((SLOTS, COLS))] * count + [
        pl.BlockSpec((count, block, COLS), lambda j: (0, j + first, 0))
    ]
    if with_gain:
        operands.append(normed)
        in_specs.append(pl.BlockSpec((SLOTS, block), lambda j: (0, j + first)))
    lead, outs = (2, 4) if left_half else (4, 2)
    out_shape = [sds((lead, ROWS, HALF), bf16)] * outs
    out_specs = [pl.BlockSpec((lead, ROWS, block), lambda j: (0, 0, j))] * outs
    if with_gain:
        out_shape = out_shape + [sds((1, HALF), f32)]
        out_specs = out_specs + [pl.BlockSpec((1, block), lambda j: (0, j))]
    return call(
        functools.partial(back_kernel, count, left_half, with_gain),
        out_shape,
        flops=2 * count * SLOTS * HALF * COLS,
        nbytes=count * HALF * COLS * 2 + 2 * SLOTS * HALF * 2,
        grid=(HALF // block,),
        in_specs=in_specs,
        out_specs=out_specs,
        name="back_dot",
    )(*operands)


def slot_of(row, x_index, z_index):
    block = row // ROWS
    xbit = block // 4
    slot = block - xbit * 4
    back = jnp.where(slot == 2, 3, jnp.where(slot == 3, 2, slot))
    x_from = jnp.where(xbit == 0, x_index, 1 - x_index)
    z_from = z_index - back
    z_from = jnp.where(z_from < 0, z_from + 4, z_from)
    return (x_from * 4 + z_from) * ROWS + (row - block * ROWS)


def places(meta, rows, is_text):
    slot = slot_of(rows, meta[10], meta[11])
    text = slot
    end = jnp.int32(0)
    for run in range(4):
        end = end + meta[run]
        text = text + jnp.where(slot >= end, meta[5 + run], 0)
    image = slot + meta[0]
    end = jnp.int32(0)
    for run in range(3):
        end = end + meta[5 + run]
        image = image + jnp.where(slot >= end, meta[run + 1], 0)
    image = jnp.where(slot < LI, image, FAR)
    return jnp.where(is_text, text, image)


def admitted(meta):
    group = meta[9]
    query = places(meta, lax.broadcasted_iota(jnp.int32, (SLOTS, 1), 0), group == 0)
    key_row = lax.broadcasted_iota(jnp.int32, (1, SLOTS), 1)
    own = places(meta, key_row, group == 0)
    other = places(meta, key_row, group != 0)
    return own <= query, other <= query


def head_attn(query, own_key, other_key, own_ok, other_ok):
    scale = HS ** (-0.5)
    own = jnp.where(own_ok, dot_rows(query, own_key) * scale, -1e30)
    other = jnp.where(other_ok, dot_rows(query, other_key) * scale, -1e30)
    row_max = jnp.maximum(
        jnp.max(own, axis=1, keepdims=True), jnp.max(other, axis=1, keepdims=True)
    )
    own = jnp.exp(own - row_max)
    other = jnp.exp(other - row_max)
    row_sum = jnp.sum(own, axis=1, keepdims=True) + jnp.sum(other, axis=1, keepdims=True)
    share = 1.0 / row_sum
    return own * share, other * share


def forward_kernel(meta, query, own_kv, other_kv, mixed):
    own_ok, other_ok = admitted(meta)
    for head in range(HEADS):
        cols = slice(head * HS, (head + 1) * HS)
        own, other = head_attn(
            query[:, cols], own_kv[0, :, cols], other_kv[0, :, cols], own_ok, other_ok
        )
        total = dot(own.astype(bf16), own_kv[1, :, cols])
        total = total + dot(other.astype(bf16), other_kv[1, :, cols])
        mixed[:, cols] = total.astype(bf16)


def backward_kernel(meta, query, own_kv, other_kv, mixed, grad, q_grad, own_grad, other_grad):
    scale = HS ** (-0.5)
    own_ok, other_ok = admitted(meta)
    for head in range(HEADS):
        cols = slice(head * HS, (head + 1) * HS)
        q, g = query[:, cols], grad[:, cols]
        row_dot = jnp.sum(g.astype(f32) * mixed[:, cols].astype(f32), axis=1, keepdims=True)
        attns = head_attn(q, own_kv[0, :, cols], other_kv[0, :, cols], own_ok, other_ok)
        dq = None
        for attn, kv, kv_grad in zip(attns, (own_kv, other_kv), (own_grad, other_grad)):
            value_grad = dot_tokens(attn.astype(bf16), g)
            weight_grad = dot_rows(g, kv[1, :, cols])
            score_grad = (attn * (weight_grad - row_dot)).astype(bf16)
            part = dot(score_grad, kv[0, :, cols])
            dq = part if dq is None else dq + part
            key_grad = dot_tokens(score_grad, q) * scale
            kv_grad[0, :, cols] = key_grad.astype(kv_grad.dtype)
            kv_grad[1, :, cols] = value_grad.astype(kv_grad.dtype)
        q_grad[:, cols] = (dq * scale).astype(bf16)


ATTN_FLOPS = 2 * HEADS * SLOTS * 2 * SLOTS * HS
VMEM = pl.BlockSpec(memory_space=pltpu.VMEM)


def attend_forward(meta, query, own_kv, other_kv):
    return call(
        forward_kernel,
        sds((SLOTS, COLS), bf16),
        flops=4 * ATTN_FLOPS,
        nbytes=6 * SLOTS * COLS * 2,
        in_specs=[SMEM] + [VMEM] * 3,
        out_specs=VMEM,
        name="attend_forward",
    )(meta, query, own_kv, other_kv)


def attend_backward(meta, query, own_kv, other_kv, mixed, grad):
    kv = (2, SLOTS, COLS)
    return call(
        backward_kernel,
        [sds((SLOTS, COLS), bf16), sds(kv, f32), sds(kv, bf16)],
        flops=8 * ATTN_FLOPS,
        nbytes=12 * SLOTS * COLS * 2,
        in_specs=[SMEM] + [VMEM] * 5,
        out_specs=[VMEM] * 3,
        name="attend_backward",
    )(meta, query, own_kv, other_kv, mixed, grad)


def out_kernel(order, grad, mixed, sent, kept):
    share = dot_tokens(grad[...], mixed[...]).astype(bf16)

    @pl.when(pl.program_id(0) < 4)
    def _():
        sent[0] = share

    @pl.when(pl.program_id(0) >= 4)
    def _():
        kept[0] = share


def out_weight_parts(order, grad_full, mixed):
    return call(
        out_kernel,
        [sds((4, COLS, COLS), bf16)] * 2,
        flops=2 * SLOTS * WIDTH * COLS,
        nbytes=SLOTS * WIDTH * 2 + WIDTH * COLS * 2,
        grid_spec=pltpu.PrefetchScalarGridSpec(
            num_scalar_prefetch=1,
            grid=(8,),
            in_specs=[
                pl.BlockSpec((SLOTS, COLS), lambda i, order: (0, order[i])),
                pl.BlockSpec((SLOTS, COLS), lambda i, order: (0, 0)),
            ],
            out_specs=[
                pl.BlockSpec((1, COLS, COLS), lambda i, order: (jnp.minimum(i, 3), 0, 0)),
                pl.BlockSpec((1, COLS, COLS), lambda i, order: (jnp.maximum(i - 4, 0), 0, 0)),
            ],
        ),
        name="out_weight_parts",
    )(order, grad_full, mixed)


def share_kernel(core, *refs):
    chunks, grads, sent, mine = refs[:4], refs[4:8], refs[8], refs[9]
    total = dot_tokens(chunks[0][...], grads[0][0])
    for chunk, grad in zip(chunks[1:], grads[1:]):
        total = total + dot_tokens(chunk[...], grad[0])

    @pl.when(pl.program_id(0) == 0)
    def _():
        sent[0] = total.astype(bf16)

    @pl.when(pl.program_id(0) == 1)
    def _():
        mine[0] = total


def qkv_weight_parts(core, chunks, grads):
    count = grads[0].shape[0]
    return call(
        share_kernel,
        [sds((count, COLS, COLS), bf16), sds((count, COLS, COLS), f32)],
        flops=2 * count * 4 * SLOTS * 2 * COLS * COLS,
        nbytes=8 * SLOTS * COLS * 2 * (count + 1) + count * COLS * COLS * 6,
        grid_spec=pltpu.PrefetchScalarGridSpec(
            num_scalar_prefetch=1,
            grid=(2, count),
            in_specs=[
                pl.BlockSpec((SLOTS, COLS), lambda i, p, core: (0, jnp.abs(core[0] - 1 + i)))
            ]
            * 4
            + [pl.BlockSpec((1, SLOTS, COLS), lambda i, p, core: (p, 0, 0))] * 4,
            out_specs=[
                pl.BlockSpec(
                    (1, COLS, COLS),
                    lambda i, p, core: (jnp.where(i == 0, p, count - 1), 0, 0),
                ),
                pl.BlockSpec(
                    (1, COLS, COLS), lambda i, p, core: (jnp.where(i == 0, 0, p), 0, 0)
                ),
            ],
        ),
        name="qkv_weight_parts",
    )(core, *chunks, *grads)


def per_device(tokens, text_gaps, image_runs, gains, w_qkv, w_out, cotangent):
    group = lax.axis_index("grp")
    tp_index = lax.axis_index("tp")
    seq_index = lax.axis_index("seq")
    x_index, z_index = tp_index // 4, tp_index % 4
    y_index, core = seq_index // 2, seq_index % 2
    x_rows = tokens[0, 0]
    w_parts = jnp.transpose(w_qkv[0], (1, 0, 2))
    gain_row = gains.astype(f32)
    valid = jnp.where((group == 0) | (tp_index * ROWS < LI), 1.0, 0.0).astype(f32)
    meta = jnp.concatenate(
        [text_gaps[0], image_runs[0], jnp.stack([group, x_index, z_index]).astype(jnp.int32)]
    )

    n_left, n_right, c_left, c_right, inv = norm_rows(
        valid.reshape(1), x_rows, gains, cotangent[0, 0]
    )
    inv_rms = inv[:, :1]
    pieces = gather_blocks(n_left, n_right)
    grad_pieces = gather_blocks(c_left, c_right)
    normed_full, own_kv = gather_dot(pieces, w_parts, (1, 2))
    other_kv = lax.ppermute(own_kv, "grp", GRP_SWAP)
    query = one_dot(normed_full, w_parts, 0)

    chunks = []
    for k in STEPS:
        sent = lax.dynamic_slice_in_dim(normed_full, (y_index + k) % 4 * 1024, 1024, 1)
        chunks.append(lax.ppermute(sent, "seq", y_shift(k)) if k else sent)

    mixed = attend_forward(meta, query, own_kv, other_kv)
    grad_full, grad_mixed = gather_dot(grad_pieces, w_out, (0,))

    def summed(lefts, weights, normed=None):
        left = back_dot(lefts, weights, True, normed)
        right = back_dot(lefts, weights, False, normed)
        total_left = scatter_left(left[0], left[1:4])
        total_right = scatter_right(right[0], right[1])
        return jnp.concatenate([total_left, total_right], axis=1), left[4:], right[2:]

    x_float = x_rows.astype(f32)
    proj_rows, _, _ = summed([mixed], w_out)
    layer_out = ((x_float + proj_rows) * valid).astype(bf16)

    q_grad, own_part, other_part = attend_backward(
        meta, query, own_kv, other_kv, mixed, grad_mixed[0]
    )
    back = lax.ppermute(other_part, "grp", GRP_SWAP)
    q_grads = [q_grad] + [lax.ppermute(q_grad, "seq", y_shift(k)) for k in STEPS[1:]]
    kv_grad = (own_part + back.astype(f32)).astype(bf16)
    kv_grads = [kv_grad] + [lax.ppermute(kv_grad, "seq", y_shift(k)) for k in STEPS[1:]]

    back_y = jnp.stack([(y_index - k) % 4 for k in STEPS]) * 2
    order = jnp.concatenate([back_y + 1 - core, back_y + core]).astype(jnp.int32)
    out_sent, out_kept = out_weight_parts(order, grad_full, mixed)
    out_came = lax.ppermute(out_sent, "seq", CORE_SWAP)
    out_share = out_kept[0].astype(f32) + out_came[0].astype(f32)
    for slot in range(1, 4):
        term = (out_kept[slot].astype(f32) + out_came[slot].astype(f32)).astype(bf16)
        out_share = out_share + lax.ppermute(term, "seq", y_shift(-STEPS[slot])).astype(f32)

    normed_grad, gain_left, gain_right = summed(
        [q_grad, kv_grad[0], kv_grad[1]], w_parts, normed_full
    )
    gain_grad = jnp.concatenate([gain_left[0], gain_right[0]], axis=1) / gain_row
    for axis, flip in (("tp", 1), ("tp", 2), ("tp", 4), ("seq", 1), ("seq", 2), ("seq", 4)):
        gain_grad = gain_grad + lax.ppermute(gain_grad, axis, [(i, i ^ flip) for i in range(8)])
    scaled = gain_row * normed_grad
    x_grad = (
        cotangent[0, 0].astype(f32) * valid
        + inv_rms * scaled
        - x_float
        * (inv_rms * inv_rms * inv_rms)
        * jnp.mean(scaled * x_float, axis=1, keepdims=True)
    )
    tokens_grad = x_grad.astype(bf16)

    core_ref = core.reshape(1).astype(jnp.int32)
    q_sent, q_mine = qkv_weight_parts(core_ref, chunks, [g[None] for g in q_grads])
    q_share = q_mine + lax.ppermute(q_sent, "seq", CORE_SWAP).astype(f32)
    kv_sent, kv_mine = qkv_weight_parts(core_ref, chunks, kv_grads)
    kv_share = kv_mine + lax.ppermute(kv_sent, "seq", CORE_SWAP).astype(f32)
    qkv_share = jnp.concatenate([q_share, kv_share], axis=0)
    return (
        layer_out[None, None],
        tokens_grad[None, None],
        gain_grad,
        jnp.transpose(qkv_share, (1, 0, 2))[None],
        out_share[None],
    )


def solution(mesh):
    in_specs = (
        P("grp", "seq", "tp", None),
        P("seq", None),
        P("seq", None),
        P("grp", None),
        P("grp", None, None, "tp"),
        P("grp", None, "tp"),
        P("grp", "seq", "tp", None),
    )
    out_specs = (
        P("grp", "seq", "tp", None),
        P("grp", "seq", "tp", None),
        P("grp", None),
        P("grp", "seq", None, "tp"),
        P("grp", "seq", "tp"),
    )
    return jax.shard_map(
        per_device, mesh=mesh, in_specs=in_specs, out_specs=out_specs, check_vma=False
    )
```

```python
import functools

import jax
import jax.numpy as jnp
from jax import lax
from jax.experimental import pallas as pl
from jax.experimental.pallas import tpu as pltpu
from jax.sharding import PartitionSpec as P

HS = 128
LI = 128
HEADS = 4
SLOTS = 256
ROWS = 32
WIDTH = 4096
HALF = 2048
COLS = 512
FAR = 1073741824
f32 = jnp.float32
bf16 = jnp.bfloat16
VMEM_LIMIT = 40 * 1024 * 1024

STEPS = (0, 1, 3, 2)


def z_shift(k):
    return [(i, (i // 4) * 4 + (i + k) % 4) for i in range(8)]


X_SWAP = [(i, i ^ 4) for i in range(8)]


def y_shift(k):
    return [(i, (i + 2 * k) % 8) for i in range(8)]


CORE_SWAP = [(i, i ^ 1) for i in range(8)]
GRP_SWAP = [(0, 1), (1, 0)]


def sds(shape, dtype):
    return jax.ShapeDtypeStruct(shape, dtype)


def call(kernel, out_shape, flops=0, nbytes=0, **kwargs):
    return pl.pallas_call(
        kernel,
        out_shape=out_shape,
        compiler_params=pltpu.CompilerParams(vmem_limit_bytes=VMEM_LIMIT),
        cost_estimate=pl.CostEstimate(flops=flops, bytes_accessed=nbytes, transcendentals=0),
        **kwargs,
    )


def whole(shape):
    return pl.BlockSpec(shape, lambda *_: (0,) * len(shape))


SMEM = pl.BlockSpec(memory_space=pltpu.SMEM)
VMEM = pl.BlockSpec(memory_space=pltpu.VMEM)
ANY = pl.BlockSpec(memory_space=pl.ANY)


def dot(left, right):
    return jnp.dot(left, right, preferred_element_type=f32)


def dot_rows(left, right):
    return lax.dot_general(left, right, (((1,), (1,)), ((), ())), preferred_element_type=f32)


def dot_tokens(left, right):
    return lax.dot_general(left, right, (((0,), (0,)), ((), ())), preferred_element_type=f32)


def norm_kernel(valid, x, gain, cot, n_left, n_right, grad, inv):
    x_float = x[...].astype(f32)
    scale = lax.rsqrt(jnp.mean(x_float * x_float, axis=1, keepdims=True) + 1e-05)
    normed = (x_float * scale * gain[...].astype(f32)).astype(bf16)
    n_left[...] = normed[:, :HALF]
    n_right[...] = normed[:, HALF:]
    grad[...] = (cot[...].astype(f32) * valid[0]).astype(bf16)
    inv[...] = jnp.broadcast_to(scale, (ROWS, 128))


def norm_rows(valid, x, gain, cot):
    part = sds((ROWS, HALF), bf16)
    return call(
        norm_kernel,
        [part, part, sds((ROWS, WIDTH), bf16), sds((ROWS, 128), f32)],
        nbytes=4 * ROWS * WIDTH * 2,
        in_specs=[SMEM] + [VMEM] * 3,
        name="norm_rows",
    )(valid, x, gain, cot)


def gather_blocks(left, right):
    right_pair = jnp.stack([right, lax.ppermute(right, "tp", X_SWAP)])
    left_four = [left] + [lax.ppermute(left, "tp", z_shift(k)) for k in STEPS[1:]]
    right_four = [right_pair] + [lax.ppermute(right_pair, "tp", z_shift(k)) for k in STEPS[1:]]
    left_own = jnp.stack(left_four)
    left_other = lax.ppermute(left_own, "tp", X_SWAP)
    return [left_own, left_other] + right_four


def place_pieces(pieces, whole_ref):
    left_own, left_other = pieces[:2]
    for slot in range(4):
        rows = pl.ds(slot * ROWS, ROWS)
        other = pl.ds((4 + slot) * ROWS, ROWS)
        whole_ref[rows, :HALF] = left_own[slot]
        whole_ref[other, :HALF] = left_other[slot]
        whole_ref[rows, HALF:] = pieces[2 + slot][0]
        whole_ref[other, HALF:] = pieces[2 + slot][1]


PIECE_SHAPES = [(4, ROWS, HALF)] * 2 + [(2, ROWS, HALF)] * 4


def sum_z_kernel(own, c1, c2, c3, *refs):
    kept, sent = refs[-2:]
    total = own[...].astype(f32)
    for came in (c1, c2, c3):
        total = total + came[...].astype(f32)
    kept[...] = total[0]
    sent[...] = total[1].astype(bf16)


def sum_z(own, came, after=()):
    shape = own.shape[1:]
    return call(
        sum_z_kernel,
        [sds(shape, f32), sds(shape, bf16)],
        nbytes=11 * shape[0] * shape[1] * 2,
        in_specs=[VMEM] * 4 + [ANY] * len(after),
        out_specs=[VMEM] * 2,
        name="sum_z",
    )(own, *came, *after)


def sum_left_kernel(own, c1, c2, c3, *refs):
    kept, sent, gain = refs[-3:]
    for part in range(2):
        total = own[part].astype(f32)
        for came in (c1, c2, c3):
            total = total + came[part].astype(f32)
        kept[pl.ds(part * 16, 16)] = total
        total = own[2 + part].astype(f32)
        for came in (c1, c2, c3):
            total = total + came[2 + part].astype(f32)
        sent[part] = total.astype(bf16)
    left, right = gain_from(own[4])
    for came in (c1, c2, c3):
        more_left, more_right = gain_from(came[4])
        left, right = left + more_left, right + more_right
    sent[2] = gain_rows_of(left, right)
    gain[0:1] = left
    gain[1:2] = right


def sum_left(own, came, after=()):
    return call(
        sum_left_kernel,
        [sds((ROWS, HALF), f32), sds((3, 16, HALF), bf16), sds((2, HALF), f32)],
        nbytes=11 * ROWS * HALF * 2,
        in_specs=[VMEM] * 4 + [ANY] * len(after),
        out_specs=[VMEM] * 3,
        name="sum_left",
    )(own, *came, *after)


def sum_gain_kernel(own, came, gain, out):
    left, right = gain_from(came[2])
    out[:, :HALF] = (own[0:1] + left) / gain[:, :HALF].astype(f32)
    out[:, HALF:] = (own[1:2] + right) / gain[:, HALF:].astype(f32)


def sum_gain(own, came, gain):
    return call(
        sum_gain_kernel,
        sds((1, WIDTH), f32),
        nbytes=10 * WIDTH * 2,
        in_specs=[VMEM] * 3,
        out_specs=VMEM,
        name="sum_gain",
    )(own, came, gain)


def sum_x_kernel(own, came, *refs):
    kept, sends = refs[-4], refs[-3:]
    kept[...] = own[0].astype(f32) + came[0].astype(f32)
    for slot, sent in enumerate(sends, 1):
        sent[...] = (own[slot].astype(f32) + came[slot].astype(f32)).astype(bf16)


def sum_x(own, came, after=()):
    shape = own.shape[1:]
    return call(
        sum_x_kernel,
        [sds(shape, f32)] + [sds(shape, bf16)] * 3,
        nbytes=13 * shape[0] * shape[1] * 2,
        in_specs=[VMEM] * 2 + [ANY] * len(after),
        out_specs=[VMEM] * 4,
        name="sum_x",
    )(own, came, *after)


def sum_keys_kernel(own, came, *refs):
    refs[-1][...] = (own[...] + came[...].astype(f32)).astype(bf16)


def sum_keys(own, came, after=()):
    return call(
        sum_keys_kernel,
        sds(came.shape, bf16),
        nbytes=8 * came.size,
        in_specs=[VMEM] * 2 + [ANY] * len(after),
        out_specs=VMEM,
        name="sum_keys",
    )(own, came, *after)


def rows_kernel(x, grad, gain, inv, l_kept, l_came, r_kept, r1, r2, r3, *refs):
    out = refs[-1]
    left = l_kept[...] + l_came[0:2].reshape(ROWS, HALF).astype(f32)
    right = r_kept[...]
    for came in (r1, r2, r3):
        right = right + came[...].astype(f32)
    scale = inv[:, :1]
    halves = []
    dots = jnp.zeros((ROWS, 1), f32)
    for part, cols in ((left, slice(0, HALF)), (right, slice(HALF, WIDTH))):
        scaled = gain[:, cols].astype(f32) * part
        rows = x[:, cols].astype(f32)
        dots = dots + jnp.sum(scaled * rows, axis=1, keepdims=True)
        halves.append((scaled, rows, cols))
    mean = dots * (1.0 / WIDTH)
    for scaled, rows, cols in halves:
        total = grad[:, cols].astype(f32) + scale * scaled - rows * (scale * scale * scale) * mean
        out[:, cols] = total.astype(bf16)


def token_rows(x, grad, gain, inv, left, right, after=()):
    return call(
        rows_kernel,
        sds((ROWS, WIDTH), bf16),
        nbytes=6 * ROWS * WIDTH * 2,
        in_specs=[VMEM] * 10 + [ANY] * len(after),
        out_specs=VMEM,
        name="token_rows",
    )(x, grad, gain, inv, *left, *right, *after)


def first_step():
    return jnp.logical_and(pl.program_id(0) == 0, pl.program_id(1) == 0)


def key_value_kernel(*refs):
    pieces, weight, grad, grad_other = refs[:6], refs[6], refs[7], refs[8]
    full, out, pair = refs[9:]

    @pl.when(first_step())
    def _():
        place_pieces(pieces, full)
        pair[0] = grad[...]
        pair[1] = grad_other[...]

    out[0] = dot(full[...], weight[0]).astype(bf16)


def key_value(pieces, weights, grad, grad_other):
    block = 256
    return call(
        key_value_kernel,
        [
            sds((SLOTS, WIDTH), bf16),
            sds((2, SLOTS, COLS), bf16),
            sds((2, ROWS, WIDTH), bf16),
        ],
        flops=4 * SLOTS * WIDTH * COLS,
        nbytes=2 * WIDTH * COLS * 2 + 2 * SLOTS * WIDTH * 2,
        grid=(2, COLS // block),
        in_specs=[whole(s) for s in PIECE_SHAPES]
        + [pl.BlockSpec((1, WIDTH, block), lambda p, j: (p + 1, 0, j))]
        + [whole((ROWS, WIDTH))] * 2,
        out_specs=[
            whole((SLOTS, WIDTH)),
            pl.BlockSpec((1, SLOTS, block), lambda p, j: (p, 0, j)),
            whole((2, ROWS, WIDTH)),
        ],
        name="key_value",
    )(*pieces, weights, grad, grad_other)


def grad_mixed_kernel(p0, p1, p2, p3, weight, *refs):
    full, out = refs[-2:]

    @pl.when(pl.program_id(0) == 0)
    def _():
        for slot, pair in enumerate((p0, p1, p2, p3)):
            full[pl.ds(slot * ROWS, ROWS)] = pair[0]
            full[pl.ds((4 + slot) * ROWS, ROWS)] = pair[1]

    out[...] = dot(full[...], weight[0]).astype(bf16)


def grad_mixed_of(pairs, weights, after):
    block = 256
    return call(
        grad_mixed_kernel,
        [sds((SLOTS, WIDTH), bf16), sds((SLOTS, COLS), bf16)],
        flops=2 * SLOTS * WIDTH * COLS,
        nbytes=WIDTH * COLS * 2 + 2 * SLOTS * WIDTH * 2,
        grid=(COLS // block,),
        in_specs=[whole((2, ROWS, WIDTH))] * 4
        + [pl.BlockSpec((1, WIDTH, block), lambda j: (0, 0, j))]
        + [ANY] * len(after),
        out_specs=[whole((SLOTS, WIDTH)), pl.BlockSpec((SLOTS, block), lambda j: (0, j))],
        name="grad_mixed",
    )(*pairs, weights, *after)


def one_dot_kernel(full, weight, out):
    out[...] = dot(full[...], weight[0]).astype(bf16)


def one_dot(full, weights, part):
    block = 256
    return call(
        one_dot_kernel,
        sds((SLOTS, COLS), bf16),
        flops=2 * SLOTS * WIDTH * COLS,
        nbytes=WIDTH * COLS * 2 + SLOTS * WIDTH * 2,
        grid=(COLS // block,),
        in_specs=[
            whole((SLOTS, WIDTH)),
            pl.BlockSpec((1, WIDTH, block), lambda j: (part, 0, j)),
        ],
        out_specs=pl.BlockSpec((SLOTS, block), lambda j: (0, j)),
        name="one_dot",
    )(full, weights)


def gain_rows_of(left, right):
    row = lax.broadcasted_iota(jnp.int32, (16, left.shape[1]), 0)
    rows = jnp.zeros((16, left.shape[1]), f32)
    for first, part in ((0, left), (2, right)):
        high = part.astype(bf16).astype(f32)
        rows = jnp.where(row == first, high, rows)
        rows = jnp.where(row == first + 1, part - high, rows)
    return rows.astype(bf16)


def gain_from(rows):
    rows = rows.astype(f32)
    return rows[0:1] + rows[1:2], rows[2:3] + rows[3:4]


def back_total(lefts, weight, normed):
    total = dot_rows(lefts[0][...], weight[0])
    for part in range(1, 3):
        total = total + dot_rows(lefts[part][...], weight[part])
    rounded = total.astype(bf16)
    gain = jnp.sum(rounded.astype(f32) * normed[...].astype(f32), axis=0, keepdims=True)
    return rounded, gain


def back_right_kernel(l0, l1, l2, weight, normed, *refs):
    own, sent, gain = refs[-3:]
    rounded, gain[...] = back_total((l0, l1, l2), weight, normed)
    for xbit, out in enumerate((own, sent)):
        for slot in range(4):
            start = (xbit * 4 + slot) * ROWS
            out[slot] = rounded[start:start + ROWS]


def back_left_kernel(l0, l1, l2, weight, normed, gain_right, *refs):
    rounded, gain = back_total((l0, l1, l2), weight, normed)
    gains = gain_rows_of(gain, gain_right[...])
    for slot, out in enumerate(refs[-4:]):
        for xbit in range(2):
            start = (xbit * 4 + slot) * ROWS
            out[2 * xbit] = rounded[start:start + 16]
            out[2 * xbit + 1] = rounded[start + 16:start + ROWS]
        out[4] = gains


def back_dot(kernel, first, lefts, weights, normed, extra, out_shape, after, name):
    block = 512
    return call(
        kernel,
        out_shape,
        flops=2 * 3 * SLOTS * HALF * COLS,
        nbytes=3 * HALF * COLS * 2 + 2 * SLOTS * HALF * 2,
        grid=(HALF // block,),
        in_specs=[whole((SLOTS, COLS))] * 3
        + [
            pl.BlockSpec((3, block, COLS), lambda j: (0, j + first, 0)),
            pl.BlockSpec((SLOTS, block), lambda j: (0, j + first)),
        ]
        + [pl.BlockSpec((1, block), lambda j: (0, j))] * len(extra)
        + [ANY] * len(after),
        out_specs=[
            pl.BlockSpec(v.shape[:-1] + (block,), lambda j, n=len(v.shape): (0,) * (n - 1) + (j,))
            for v in out_shape
        ],
        name=name,
    )(*lefts, weights, normed, *extra, *after)


def back_right(lefts, weights, normed, after=()):
    out = [sds((4, ROWS, HALF), bf16)] * 2 + [sds((1, HALF), f32)]
    return back_dot(
        back_right_kernel, HALF // 512, lefts, weights, normed, [], out, after, "back_right"
    )


def back_left(lefts, weights, normed, gain_right, after=()):
    out = [sds((5, 16, HALF), bf16)] * 4
    return back_dot(
        back_left_kernel, 0, lefts, weights, normed, [gain_right], out, after, "back_left"
    )


def proj_kernel(left, weight, *refs):
    rounded = dot_rows(left[...], weight[0]).astype(bf16)
    for slot in range(4):
        for xbit in range(2):
            start = (xbit * 4 + slot) * ROWS
            refs[slot][xbit] = rounded[start:start + ROWS]


def proj_parts(mixed, weights):
    block = 512
    return call(
        proj_kernel,
        [sds((2, ROWS, WIDTH), bf16)] * 4,
        flops=2 * SLOTS * WIDTH * COLS,
        nbytes=WIDTH * COLS * 2 + SLOTS * WIDTH * 2,
        grid=(WIDTH // block,),
        in_specs=[whole((SLOTS, COLS)), pl.BlockSpec((1, block, COLS), lambda j: (0, j, 0))],
        out_specs=[pl.BlockSpec((2, ROWS, block), lambda j: (0, 0, j))] * 4,
        name="proj_parts",
    )(mixed, weights)


def slot_of(row, x_index, z_index):
    block = row // ROWS
    xbit = block // 4
    slot = block - xbit * 4
    back = jnp.where(slot == 2, 3, jnp.where(slot == 3, 2, slot))
    x_from = jnp.where(xbit == 0, x_index, 1 - x_index)
    z_from = z_index - back
    z_from = jnp.where(z_from < 0, z_from + 4, z_from)
    return (x_from * 4 + z_from) * ROWS + (row - block * ROWS)


def places(meta, rows, is_text):
    slot = slot_of(rows, meta[10], meta[11])
    text = slot
    end = jnp.int32(0)
    for run in range(4):
        end = end + meta[run]
        text = text + jnp.where(slot >= end, meta[5 + run], 0)
    image = slot + meta[0]
    end = jnp.int32(0)
    for run in range(3):
        end = end + meta[5 + run]
        image = image + jnp.where(slot >= end, meta[run + 1], 0)
    image = jnp.where(slot < LI, image, FAR)
    return jnp.where(is_text, text, image)


def admitted(meta):
    group = meta[9]
    query = places(meta, lax.broadcasted_iota(jnp.int32, (SLOTS, 1), 0), group == 0)
    key_row = lax.broadcasted_iota(jnp.int32, (1, SLOTS), 1)
    own = places(meta, key_row, group == 0)
    other = places(meta, key_row, group != 0)
    return own <= query, other <= query


def head_attn(query, own_key, other_key, own_ok, other_ok):
    scale = HS ** (-0.5)
    own = jnp.where(own_ok, dot_rows(query, own_key) * scale, -1e30)
    other = jnp.where(other_ok, dot_rows(query, other_key) * scale, -1e30)
    row_max = jnp.maximum(
        jnp.max(own, axis=1, keepdims=True), jnp.max(other, axis=1, keepdims=True)
    )
    own = jnp.exp(own - row_max)
    other = jnp.exp(other - row_max)
    row_sum = jnp.sum(own, axis=1, keepdims=True) + jnp.sum(other, axis=1, keepdims=True)
    share = 1.0 / row_sum
    return own * share, other * share


def forward_kernel(meta, query, own_kv, other_kv, mixed):
    own_ok, other_ok = admitted(meta)
    for head in range(HEADS):
        cols = slice(head * HS, (head + 1) * HS)
        own, other = head_attn(
            query[:, cols], own_kv[0, :, cols], other_kv[0, :, cols], own_ok, other_ok
        )
        total = dot(own.astype(bf16), own_kv[1, :, cols])
        total = total + dot(other.astype(bf16), other_kv[1, :, cols])
        mixed[:, cols] = total.astype(bf16)


def backward_kernel(meta, query, own_kv, other_kv, mixed, grad, *refs):
    pair, own_grad, other_grad = refs[-3:]
    pair[0] = mixed[...]
    scale = HS ** (-0.5)
    own_ok, other_ok = admitted(meta)
    for head in range(HEADS):
        cols = slice(head * HS, (head + 1) * HS)
        q, g = query[:, cols], grad[:, cols]
        row_dot = jnp.sum(g.astype(f32) * mixed[:, cols].astype(f32), axis=1, keepdims=True)
        attns = head_attn(q, own_kv[0, :, cols], other_kv[0, :, cols], own_ok, other_ok)
        dq = None
        for attn, kv, kv_grad in zip(attns, (own_kv, other_kv), (own_grad, other_grad)):
            value_grad = dot_tokens(attn.astype(bf16), g)
            weight_grad = dot_rows(g, kv[1, :, cols])
            score_grad = (attn * (weight_grad - row_dot)).astype(bf16)
            part = dot(score_grad, kv[0, :, cols])
            dq = part if dq is None else dq + part
            key_grad = dot_tokens(score_grad, q) * scale
            kv_grad[0, :, cols] = key_grad.astype(kv_grad.dtype)
            kv_grad[1, :, cols] = value_grad.astype(kv_grad.dtype)
        pair[1, :, cols] = (dq * scale).astype(bf16)


ATTN_FLOPS = 2 * HEADS * SLOTS * 2 * SLOTS * HS


def attend_forward(meta, query, own_kv, other_kv):
    return call(
        forward_kernel,
        sds((SLOTS, COLS), bf16),
        flops=4 * ATTN_FLOPS,
        nbytes=6 * SLOTS * COLS * 2,
        in_specs=[SMEM] + [VMEM] * 3,
        out_specs=VMEM,
        name="attend_forward",
    )(meta, query, own_kv, other_kv)


def attend_backward(meta, query, own_kv, other_kv, mixed, grad, after):
    kv = (2, SLOTS, COLS)
    return call(
        backward_kernel,
        [sds(kv, bf16), sds(kv, f32), sds(kv, bf16)],
        flops=8 * ATTN_FLOPS,
        nbytes=12 * SLOTS * COLS * 2,
        in_specs=[SMEM] + [VMEM] * 5 + [ANY] * len(after),
        out_specs=[VMEM] * 3,
        name="attend_backward",
    )(meta, query, own_kv, other_kv, mixed, grad, *after)


def share_kernel(count, *refs):
    refs = refs[1:]
    grads = refs[3 * count:3 * count + 4]
    sent, mine = refs[-2:]

    def share(part, own, came, other):
        total = dot_tokens(own[...], grads[0][part])
        for k in range(3):
            total = total + dot_tokens(came[k], grads[k + 1][part, :SLOTS // 2])
            total = total + dot_tokens(other[k], grads[k + 1][part, SLOTS // 2:])

        @pl.when(pl.program_id(0) == 0)
        def _():
            sent[part] = total.astype(bf16)

        @pl.when(pl.program_id(0) == 1)
        def _():
            mine[part] = total

    for part in range(2):
        first = 3 * (part if count == 2 else 0)
        share(part, *refs[first:first + 3])


def weight_shares(core, chunks, grads, after=()):
    count = len(chunks)
    flat = [ref for triple in chunks for ref in triple]

    def column(i, core):
        return jnp.abs(core[0] - 1 + i)

    triple = [
        pl.BlockSpec((SLOTS, COLS), lambda i, core: (0, column(i, core))),
        pl.BlockSpec((3, SLOTS // 2, COLS), lambda i, core: (0, 0, column(i, core))),
        pl.BlockSpec((3, SLOTS // 2, COLS), lambda i, core: (0, 0, column(i, core))),
    ]
    return call(
        functools.partial(share_kernel, count),
        [sds((2, COLS, COLS), bf16), sds((2, COLS, COLS), f32)],
        flops=4 * 4 * SLOTS * 2 * COLS * COLS,
        nbytes=8 * SLOTS * COLS * 2 * (count + 2) + 2 * COLS * COLS * 6,
        grid_spec=pltpu.PrefetchScalarGridSpec(
            num_scalar_prefetch=1,
            grid=(2,),
            in_specs=triple * count + [whole((2, SLOTS, COLS))] * 4 + [ANY] * len(after),
            out_specs=[whole((2, COLS, COLS))] * 2,
        ),
        name="weight_shares",
    )(core, *flat, *grads, *after)


def chunks_over_y(full, y_index):
    sent = [
        lax.dynamic_slice(full, (0, (y_index + k) % 4 * 1024), (SLOTS // 2, 1024))
        for k in STEPS[1:]
    ]
    came = jnp.stack([lax.ppermute(v, "seq", y_shift(k)) for v, k in zip(sent, STEPS[1:])])
    other = lax.ppermute(came, "tp", X_SWAP)
    own = lax.dynamic_slice_in_dim(full, y_index * 1024, 1024, 1)
    return own, came, other


def per_device(tokens, text_gaps, image_runs, gains, w_qkv, w_out, cotangent):
    group = lax.axis_index("grp")
    tp_index = lax.axis_index("tp")
    seq_index = lax.axis_index("seq")
    x_index, z_index = tp_index // 4, tp_index % 4
    y_index, core = seq_index // 2, seq_index % 2
    x_rows = tokens[0, 0]
    w_parts = jnp.transpose(w_qkv[0], (1, 0, 2))
    valid = jnp.where((group == 0) | (tp_index * ROWS < LI), 1.0, 0.0).astype(f32)
    meta = jnp.concatenate(
        [text_gaps[0], image_runs[0], jnp.stack([group, x_index, z_index]).astype(jnp.int32)]
    )

    n_left, n_right, grad_rows, inv = norm_rows(valid.reshape(1), x_rows, gains, cotangent[0, 0])
    pieces = gather_blocks(n_left, n_right)
    grad_other = lax.ppermute(grad_rows, "tp", X_SWAP)
    normed_full, own_kv, grad_pair = key_value(pieces, w_parts, grad_rows, grad_other)
    other_kv = lax.ppermute(own_kv, "grp", GRP_SWAP)
    grad_pairs = [grad_pair] + [lax.ppermute(grad_pair, "tp", z_shift(k)) for k in STEPS[1:]]
    query = one_dot(normed_full, w_parts, 0)
    normed_chunks = chunks_over_y(normed_full, y_index)

    mixed = attend_forward(meta, query, own_kv, other_kv)
    proj = proj_parts(mixed, w_out)
    grad_full, grad_mixed = grad_mixed_of(grad_pairs, w_out, [proj[0]])
    grad_chunks = chunks_over_y(grad_full, y_index)
    pair, own_part, other_part = attend_backward(
        meta, query, own_kv, other_kv, mixed, grad_mixed, [normed_chunks[2]]
    )
    back = lax.ppermute(other_part, "grp", GRP_SWAP)

    proj_came = [lax.ppermute(proj[i], "tp", z_shift(-STEPS[i])) for i in range(1, 4)]
    pairs = [pair] + [lax.ppermute(pair, "seq", y_shift(k)) for k in STEPS[1:]]
    kv_grad = sum_keys(own_part, back, [grad_chunks[1]])
    kv_grads = [kv_grad] + [lax.ppermute(kv_grad, "seq", y_shift(k)) for k in STEPS[1:]]

    lefts = [pair[1], kv_grad[0], kv_grad[1]]
    right = back_right(lefts, w_parts, normed_full)
    proj_kept, proj_sent = sum_z(proj[0], proj_came)
    right_x = lax.ppermute(right[1], "tp", X_SWAP)
    left = back_left(lefts, w_parts, normed_full, right[2], [proj_sent])
    left_came = [lax.ppermute(left[i], "tp", z_shift(-STEPS[i])) for i in range(1, 4)]
    proj_x = lax.ppermute(proj_sent, "tp", X_SWAP)
    right_kept, *right_sends = sum_x(right[0], right_x, pairs[1:3] + [proj_x])
    right_came = [
        lax.ppermute(sent, "tp", z_shift(-k)) for sent, k in zip(right_sends, STEPS[1:])
    ]
    left_kept, left_sent, gain_kept = sum_left(left[0], left_came, pairs[3:])
    left_x = lax.ppermute(left_sent, "tp", X_SWAP)
    layer_out = ((x_rows.astype(f32) + proj_kept + proj_x.astype(f32)) * valid).astype(bf16)

    core_ref = core.reshape(1).astype(jnp.int32)
    pair_sent, pair_mine = weight_shares(
        core_ref, [grad_chunks, normed_chunks], pairs, kv_grads[1:3]
    )
    tokens_grad = token_rows(
        x_rows, grad_rows, gains, inv, (left_kept, left_x), (right_kept, *right_came), kv_grads[3:]
    )
    kv_sent, kv_mine = weight_shares(core_ref, [normed_chunks], kv_grads)
    gain_grad = sum_gain(gain_kept, left_x, gains)
    for flip in (2, 4, 1):
        gain_grad = gain_grad + lax.ppermute(gain_grad, "seq", [(i, i ^ flip) for i in range(8)])
    pair_share = pair_mine + lax.ppermute(pair_sent, "seq", CORE_SWAP).astype(f32)
    kv_share = kv_mine + lax.ppermute(kv_sent, "seq", CORE_SWAP).astype(f32)
    out_share = pair_share[0]
    qkv_share = jnp.concatenate([pair_share[1:], kv_share], axis=0)
    return (
        layer_out[None, None],
        tokens_grad[None, None],
        gain_grad,
        jnp.transpose(qkv_share, (1, 0, 2))[None],
        out_share[None],
    )


def solution(mesh):
    in_specs = (
        P("grp", "seq", "tp", None),
        P("seq", None),
        P("seq", None),
        P("grp", None),
        P("grp", None, None, "tp"),
        P("grp", None, "tp"),
        P("grp", "seq", "tp", None),
    )
    out_specs = (
        P("grp", "seq", "tp", None),
        P("grp", "seq", "tp", None),
        P("grp", None),
        P("grp", "seq", None, "tp"),
        P("grp", "seq", "tp"),
    )
    return jax.shard_map(
        per_device, mesh=mesh, in_specs=in_specs, out_specs=out_specs, check_vma=False
    )
```

```python
import functools

import jax
import jax.numpy as jnp
from jax import lax
from jax.experimental import pallas as pl
from jax.experimental.pallas import tpu as pltpu
from jax.sharding import PartitionSpec as P

HS = 128
LI = 128
HEADS = 4
SLOTS = 256
ROWS = 32
WIDTH = 4096
HALF = 2048
COLS = 512
FAR = 1073741824
f32 = jnp.float32
bf16 = jnp.bfloat16
MIB = 1024 * 1024

STEPS = (0, 1, 3, 2)


def z_shift(k):
    return [(i, (i // 4) * 4 + (i + k) % 4) for i in range(8)]


X_SWAP = [(i, i ^ 4) for i in range(8)]


def y_shift(k):
    return [(i, (i + 2 * k) % 8) for i in range(8)]


CORE_SWAP = [(i, i ^ 1) for i in range(8)]
GRP_SWAP = [(0, 1), (1, 0)]


def sds(shape, dtype):
    return jax.ShapeDtypeStruct(shape, dtype)


def call(kernel, out_shape, vmem, flops=0, nbytes=0, **kwargs):
    return pl.pallas_call(
        kernel,
        out_shape=out_shape,
        compiler_params=pltpu.CompilerParams(vmem_limit_bytes=vmem * MIB),
        cost_estimate=pl.CostEstimate(flops=flops, bytes_accessed=nbytes, transcendentals=0),
        **kwargs,
    )


def whole(shape):
    return pl.BlockSpec(shape, lambda *_: (0,) * len(shape))


SMEM = pl.BlockSpec(memory_space=pltpu.SMEM)
VMEM = pl.BlockSpec(memory_space=pltpu.VMEM)
ANY = pl.BlockSpec(memory_space=pl.ANY)


def dot(left, right):
    return jnp.dot(left, right, preferred_element_type=f32)


def dot_rows(left, right):
    return lax.dot_general(left, right, (((1,), (1,)), ((), ())), preferred_element_type=f32)


def dot_tokens(left, right):
    return lax.dot_general(left, right, (((0,), (0,)), ((), ())), preferred_element_type=f32)


def norm_kernel(valid, x, gain, cot, n_left, n_right, grad, inv):
    x_float = x[...].astype(f32)
    scale = lax.rsqrt(jnp.mean(x_float * x_float, axis=1, keepdims=True) + 1e-05)
    normed = (x_float * scale * gain[...].astype(f32)).astype(bf16)
    n_left[...] = normed[:, :HALF]
    n_right[...] = normed[:, HALF:]
    grad[...] = (cot[...].astype(f32) * valid[0]).astype(bf16)
    inv[...] = jnp.broadcast_to(scale, (ROWS, 128))


def norm_rows(valid, x, gain, cot):
    part = sds((ROWS, HALF), bf16)
    return call(
        norm_kernel,
        [part, part, sds((ROWS, WIDTH), bf16), sds((ROWS, 128), f32)],
        vmem=4,
        nbytes=4 * ROWS * WIDTH * 2,
        in_specs=[SMEM] + [VMEM] * 3,
        name="norm_rows",
    )(valid, x, gain, cot)


def gather_blocks(left, right):
    right_pair = jnp.stack([right, lax.ppermute(right, "tp", X_SWAP)])
    left_four = [left] + [lax.ppermute(left, "tp", z_shift(k)) for k in STEPS[1:]]
    right_four = [right_pair] + [lax.ppermute(right_pair, "tp", z_shift(k)) for k in STEPS[1:]]
    left_own = jnp.stack(left_four)
    left_other = lax.ppermute(left_own, "tp", X_SWAP)
    return [left_own, left_other] + right_four


def place_pieces(pieces, whole_ref):
    left_own, left_other = pieces[:2]
    for slot in range(4):
        rows = pl.ds(slot * ROWS, ROWS)
        other = pl.ds((4 + slot) * ROWS, ROWS)
        whole_ref[rows, :HALF] = left_own[slot]
        whole_ref[other, :HALF] = left_other[slot]
        whole_ref[rows, HALF:] = pieces[2 + slot][0]
        whole_ref[other, HALF:] = pieces[2 + slot][1]


PIECE_SHAPES = [(4, ROWS, HALF)] * 2 + [(2, ROWS, HALF)] * 4


def sum_left_kernel(own, c1, c2, c3, *refs):
    kept, sent, gain = refs[-3:]
    for part in range(2):
        total = own[part].astype(f32)
        for came in (c1, c2, c3):
            total = total + came[part].astype(f32)
        kept[pl.ds(part * 16, 16)] = total
        total = own[2 + part].astype(f32)
        for came in (c1, c2, c3):
            total = total + came[2 + part].astype(f32)
        sent[part] = total.astype(bf16)
    left, right = gain_from(own[4])
    for came in (c1, c2, c3):
        more_left, more_right = gain_from(came[4])
        left, right = left + more_left, right + more_right
    sent[2] = gain_rows_of(left, right)
    gain[0:1] = left
    gain[1:2] = right


def sum_left(own, came, after=()):
    return call(
        sum_left_kernel,
        [sds((ROWS, HALF), f32), sds((3, 16, HALF), bf16), sds((2, HALF), f32)],
        vmem=4,
        nbytes=11 * ROWS * HALF * 2,
        in_specs=[VMEM] * 4 + [ANY] * len(after),
        out_specs=[VMEM] * 3,
        name="sum_left",
    )(own, *came, *after)


def sum_gain_kernel(own, came, gain, out):
    left, right = gain_from(came[2])
    out[:, :HALF] = (own[0:1] + left) / gain[:, :HALF].astype(f32)
    out[:, HALF:] = (own[1:2] + right) / gain[:, HALF:].astype(f32)


def sum_gain(own, came, gain):
    return call(
        sum_gain_kernel,
        sds((1, WIDTH), f32),
        vmem=2,
        nbytes=10 * WIDTH * 2,
        in_specs=[VMEM] * 3,
        out_specs=VMEM,
        name="sum_gain",
    )(own, came, gain)


def sum_x_kernel(own, came, *refs):
    kept, sends = refs[-4], refs[-3:]
    kept[...] = own[0].astype(f32) + came[0].astype(f32)
    for slot, sent in enumerate(sends, 1):
        sent[...] = (own[slot].astype(f32) + came[slot].astype(f32)).astype(bf16)


def sum_x(own, came, after=()):
    shape = own.shape[1:]
    return call(
        sum_x_kernel,
        [sds(shape, f32)] + [sds(shape, bf16)] * 3,
        vmem=4,
        nbytes=13 * shape[0] * shape[1] * 2,
        in_specs=[VMEM] * 2 + [ANY] * len(after),
        out_specs=[VMEM] * 4,
        name="sum_x",
    )(own, came, *after)


def sum_keys_kernel(own, came, *refs):
    refs[-1][...] = (own[...] + came[...].astype(f32)).astype(bf16)


def sum_keys(own, came, after=()):
    return call(
        sum_keys_kernel,
        sds(came.shape, bf16),
        vmem=6,
        nbytes=8 * came.size,
        in_specs=[VMEM] * 2 + [ANY] * len(after),
        out_specs=VMEM,
        name="sum_keys",
    )(own, came, *after)


def rows_kernel(x, grad, gain, inv, l_kept, l_came, r_kept, r1, r2, r3, *refs):
    out = refs[-1]
    left = l_kept[...] + l_came[0:2].reshape(ROWS, HALF).astype(f32)
    right = r_kept[...]
    for came in (r1, r2, r3):
        right = right + came[...].astype(f32)
    scale = inv[:, :1]
    halves = []
    dots = jnp.zeros((ROWS, 1), f32)
    for part, cols in ((left, slice(0, HALF)), (right, slice(HALF, WIDTH))):
        scaled = gain[:, cols].astype(f32) * part
        rows = x[:, cols].astype(f32)
        dots = dots + jnp.sum(scaled * rows, axis=1, keepdims=True)
        halves.append((scaled, rows, cols))
    mean = dots * (1.0 / WIDTH)
    for scaled, rows, cols in halves:
        total = grad[:, cols].astype(f32) + scale * scaled - rows * (scale * scale * scale) * mean
        out[:, cols] = total.astype(bf16)


def token_rows(x, grad, gain, inv, left, right, after=()):
    return call(
        rows_kernel,
        sds((ROWS, WIDTH), bf16),
        vmem=4,
        nbytes=6 * ROWS * WIDTH * 2,
        in_specs=[VMEM] * 10 + [ANY] * len(after),
        out_specs=VMEM,
        name="token_rows",
    )(x, grad, gain, inv, *left, *right, *after)


def first_step():
    return jnp.logical_and(pl.program_id(0) == 0, pl.program_id(1) == 0)


def key_value_kernel(*refs):
    pieces, weight, full, out = refs[:6], refs[6], refs[7], refs[8]

    @pl.when(first_step())
    def _():
        place_pieces(pieces, full)

    out[0] = dot(full[...], weight[0]).astype(bf16)


def key_value(pieces, weights):
    block = 256
    return call(
        key_value_kernel,
        [sds((SLOTS, WIDTH), bf16), sds((2, SLOTS, COLS), bf16)],
        vmem=18,
        flops=4 * SLOTS * WIDTH * COLS,
        nbytes=2 * WIDTH * COLS * 2 + 2 * SLOTS * WIDTH * 2,
        grid=(2, COLS // block),
        in_specs=[whole(s) for s in PIECE_SHAPES]
        + [pl.BlockSpec((1, WIDTH, block), lambda p, j: (p + 1, 0, j))],
        out_specs=[
            whole((SLOTS, WIDTH)),
            pl.BlockSpec((1, SLOTS, block), lambda p, j: (p, 0, j)),
        ],
        name="key_value",
    )(*pieces, weights)


def grad_mixed_kernel(order, came, weight, full, out):
    @pl.when(pl.program_id(0) == 0)
    def _():
        for block in range(8):
            start = pl.multiple_of(order[block] * ROWS, ROWS)
            full[pl.ds(block * ROWS, ROWS)] = came[pl.ds(start, ROWS)]

    out[...] = dot(full[...], weight[0]).astype(bf16)


def grad_mixed_of(order, came, weights):
    block = 256
    return call(
        grad_mixed_kernel,
        [sds((SLOTS, WIDTH), bf16), sds((SLOTS, COLS), bf16)],
        vmem=16,
        flops=2 * SLOTS * WIDTH * COLS,
        nbytes=WIDTH * COLS * 2 + 2 * SLOTS * WIDTH * 2,
        grid=(COLS // block,),
        in_specs=[
            SMEM,
            whole((SLOTS, WIDTH)),
            pl.BlockSpec((1, WIDTH, block), lambda j: (0, 0, j)),
        ],
        out_specs=[whole((SLOTS, WIDTH)), pl.BlockSpec((SLOTS, block), lambda j: (0, j))],
        name="grad_mixed",
    )(order, came, weights)


def one_dot_kernel(full, weight, out):
    out[...] = dot(full[...], weight[0]).astype(bf16)


def one_dot(full, weights, part):
    block = 256
    return call(
        one_dot_kernel,
        sds((SLOTS, COLS), bf16),
        vmem=12,
        flops=2 * SLOTS * WIDTH * COLS,
        nbytes=WIDTH * COLS * 2 + SLOTS * WIDTH * 2,
        grid=(COLS // block,),
        in_specs=[
            whole((SLOTS, WIDTH)),
            pl.BlockSpec((1, WIDTH, block), lambda j: (part, 0, j)),
        ],
        out_specs=pl.BlockSpec((SLOTS, block), lambda j: (0, j)),
        name="one_dot",
    )(full, weights)


def gain_rows_of(left, right):
    row = lax.broadcasted_iota(jnp.int32, (16, left.shape[1]), 0)
    rows = jnp.zeros((16, left.shape[1]), f32)
    for first, part in ((0, left), (2, right)):
        high = part.astype(bf16).astype(f32)
        rows = jnp.where(row == first, high, rows)
        rows = jnp.where(row == first + 1, part - high, rows)
    return rows.astype(bf16)


def gain_from(rows):
    rows = rows.astype(f32)
    return rows[0:1] + rows[1:2], rows[2:3] + rows[3:4]


def back_total(pair, kv_grad, weight, normed):
    total = dot_rows(pair[1], weight[0])
    for part in range(2):
        total = total + dot_rows(kv_grad[part], weight[1 + part])
    rounded = total.astype(bf16)
    gain = jnp.sum(rounded.astype(f32) * normed[...].astype(f32), axis=0, keepdims=True)
    return rounded, gain


def back_right_kernel(pair, kv_grad, weight, normed, *refs):
    own, sent, gain = refs[-3:]
    rounded, gain[...] = back_total(pair, kv_grad, weight, normed)
    for xbit, out in enumerate((own, sent)):
        for slot in range(4):
            start = (xbit * 4 + slot) * ROWS
            out[slot] = rounded[start:start + ROWS]


def back_left_kernel(pair, kv_grad, weight, normed, gain_right, *refs):
    rounded, gain = back_total(pair, kv_grad, weight, normed)
    gains = gain_rows_of(gain, gain_right[...])
    for slot, out in enumerate(refs[-4:]):
        for xbit in range(2):
            start = (xbit * 4 + slot) * ROWS
            out[2 * xbit] = rounded[start:start + 16]
            out[2 * xbit + 1] = rounded[start + 16:start + ROWS]
        out[4] = gains


def back_dot(kernel, first, lefts, weights, normed, extra, out_shape, after, name):
    block = 512
    return call(
        kernel,
        out_shape,
        vmem=12,
        flops=2 * 3 * SLOTS * HALF * COLS,
        nbytes=3 * HALF * COLS * 2 + 2 * SLOTS * HALF * 2,
        grid=(HALF // block,),
        in_specs=[whole((2, SLOTS, COLS))] * 2
        + [
            pl.BlockSpec((3, block, COLS), lambda j: (0, j + first, 0)),
            pl.BlockSpec((SLOTS, block), lambda j: (0, j + first)),
        ]
        + [pl.BlockSpec((1, block), lambda j: (0, j))] * len(extra)
        + [ANY] * len(after),
        out_specs=[
            pl.BlockSpec(v.shape[:-1] + (block,), lambda j, n=len(v.shape): (0,) * (n - 1) + (j,))
            for v in out_shape
        ],
        name=name,
    )(*lefts, weights, normed, *extra, *after)


def back_right(lefts, weights, normed, after=()):
    out = [sds((4, ROWS, HALF), bf16)] * 2 + [sds((1, HALF), f32)]
    return back_dot(
        back_right_kernel, HALF // 512, lefts, weights, normed, [], out, after, "back_right"
    )


def back_left(lefts, weights, normed, gain_right, after=()):
    out = [sds((5, 16, HALF), bf16)] * 4
    return back_dot(
        back_left_kernel, 0, lefts, weights, normed, [gain_right], out, after, "back_left"
    )


def proj_kernel(order, left, weight, out):
    rounded = dot_rows(left[...], weight[0]).astype(bf16)
    for block in range(8):
        start = pl.multiple_of(order[block] * ROWS, ROWS)
        out[pl.ds(start, ROWS)] = rounded[block * ROWS:(block + 1) * ROWS]


def proj_parts(order, mixed, weights):
    block = 512
    return call(
        proj_kernel,
        sds((SLOTS, WIDTH), bf16),
        vmem=6,
        flops=2 * SLOTS * WIDTH * COLS,
        nbytes=WIDTH * COLS * 2 + SLOTS * WIDTH * 2,
        grid=(WIDTH // block,),
        in_specs=[
            SMEM,
            whole((SLOTS, COLS)),
            pl.BlockSpec((1, block, COLS), lambda j: (0, j, 0)),
        ],
        out_specs=pl.BlockSpec((SLOTS, block), lambda j: (0, j)),
        name="proj_parts",
    )(order, mixed, weights)


def slot_of(row, x_index, z_index):
    block = row // ROWS
    xbit = block // 4
    slot = block - xbit * 4
    back = jnp.where(slot == 2, 3, jnp.where(slot == 3, 2, slot))
    x_from = jnp.where(xbit == 0, x_index, 1 - x_index)
    z_from = z_index - back
    z_from = jnp.where(z_from < 0, z_from + 4, z_from)
    return (x_from * 4 + z_from) * ROWS + (row - block * ROWS)


def places(meta, rows, is_text):
    slot = slot_of(rows, meta[10], meta[11])
    text = slot
    end = jnp.int32(0)
    for run in range(4):
        end = end + meta[run]
        text = text + jnp.where(slot >= end, meta[5 + run], 0)
    image = slot + meta[0]
    end = jnp.int32(0)
    for run in range(3):
        end = end + meta[5 + run]
        image = image + jnp.where(slot >= end, meta[run + 1], 0)
    image = jnp.where(slot < LI, image, FAR)
    return jnp.where(is_text, text, image)


def admitted(meta):
    group = meta[9]
    query = places(meta, lax.broadcasted_iota(jnp.int32, (SLOTS, 1), 0), group == 0)
    key_row = lax.broadcasted_iota(jnp.int32, (1, SLOTS), 1)
    own = places(meta, key_row, group == 0)
    other = places(meta, key_row, group != 0)
    return own <= query, other <= query


def head_attn(query, own_key, other_key, own_ok, other_ok):
    scale = HS ** (-0.5)
    own = jnp.where(own_ok, dot_rows(query, own_key) * scale, -1e30)
    other = jnp.where(other_ok, dot_rows(query, other_key) * scale, -1e30)
    row_max = jnp.maximum(
        jnp.max(own, axis=1, keepdims=True), jnp.max(other, axis=1, keepdims=True)
    )
    own = jnp.exp(own - row_max)
    other = jnp.exp(other - row_max)
    row_sum = jnp.sum(own, axis=1, keepdims=True) + jnp.sum(other, axis=1, keepdims=True)
    share = 1.0 / row_sum
    return own * share, other * share


def forward_kernel(meta, query, own_kv, other_kv, mixed):
    own_ok, other_ok = admitted(meta)
    for head in range(HEADS):
        cols = slice(head * HS, (head + 1) * HS)
        own, other = head_attn(
            query[:, cols], own_kv[0, :, cols], other_kv[0, :, cols], own_ok, other_ok
        )
        total = dot(own.astype(bf16), own_kv[1, :, cols])
        total = total + dot(other.astype(bf16), other_kv[1, :, cols])
        mixed[:, cols] = total.astype(bf16)


def backward_kernel(meta, query, own_kv, other_kv, mixed, grad, *refs):
    pair, own_grad, other_grad = refs[-3:]
    pair[0] = mixed[...]
    scale = HS ** (-0.5)
    own_ok, other_ok = admitted(meta)
    for head in range(HEADS):
        cols = slice(head * HS, (head + 1) * HS)
        q, g = query[:, cols], grad[:, cols]
        row_dot = jnp.sum(g.astype(f32) * mixed[:, cols].astype(f32), axis=1, keepdims=True)
        attns = head_attn(q, own_kv[0, :, cols], other_kv[0, :, cols], own_ok, other_ok)
        dq = None
        for attn, kv, kv_grad in zip(attns, (own_kv, other_kv), (own_grad, other_grad)):
            value_grad = dot_tokens(attn.astype(bf16), g)
            weight_grad = dot_rows(g, kv[1, :, cols])
            score_grad = (attn * (weight_grad - row_dot)).astype(bf16)
            part = dot(score_grad, kv[0, :, cols])
            dq = part if dq is None else dq + part
            key_grad = dot_tokens(score_grad, q) * scale
            kv_grad[0, :, cols] = key_grad.astype(kv_grad.dtype)
            kv_grad[1, :, cols] = value_grad.astype(kv_grad.dtype)
        pair[1, :, cols] = (dq * scale).astype(bf16)


ATTN_FLOPS = 2 * HEADS * SLOTS * 2 * SLOTS * HS


def attend_forward(meta, query, own_kv, other_kv):
    return call(
        forward_kernel,
        sds((SLOTS, COLS), bf16),
        vmem=10,
        flops=4 * ATTN_FLOPS,
        nbytes=6 * SLOTS * COLS * 2,
        in_specs=[SMEM] + [VMEM] * 3,
        out_specs=VMEM,
        name="attend_forward",
    )(meta, query, own_kv, other_kv)


def attend_backward(meta, query, own_kv, other_kv, mixed, grad, after):
    kv = (2, SLOTS, COLS)
    return call(
        backward_kernel,
        [sds(kv, bf16), sds(kv, f32), sds(kv, bf16)],
        vmem=14,
        flops=8 * ATTN_FLOPS,
        nbytes=12 * SLOTS * COLS * 2,
        in_specs=[SMEM] + [VMEM] * 5 + [ANY] * len(after),
        out_specs=[VMEM] * 3,
        name="attend_backward",
    )(meta, query, own_kv, other_kv, mixed, grad, *after)


def share_kernel(arrays, column, *refs):
    count = len(arrays)
    chunks, grads = refs[:3 * count], refs[3 * count:3 * count + 4]
    sent, mine, lefts, rights = refs[-4:]

    @pl.when(pl.program_id(0) == 0)
    def _():
        for k, grad in enumerate(grads):
            rights[:, pl.ds(k * SLOTS, SLOTS)] = grad[...]

    for i in range(count):
        own, came, other = chunks[3 * i:3 * i + 3]
        lefts[i, :SLOTS] = own[...]
        for k in range(3):
            start = (k + 1) * SLOTS
            lefts[i, start:start + SLOTS // 2] = came[k, 0]
            lefts[i, start + SLOTS // 2:start + SLOTS] = other[k, 0]
    for part in range(2):
        total = dot_tokens(lefts[part % count], rights[part])

        @pl.when(pl.program_id(0) == 0)
        def _():
            sent[part] = total.astype(bf16)

        @pl.when(pl.program_id(0) == 1)
        def _():
            mine[part] = total


def weight_shares(column, fulls, came, other, grads, arrays, after=()):
    half = SLOTS // 2
    chunks, specs = [], []
    for array in arrays:
        chunks += [fulls[array], came, other]
        specs += [pl.BlockSpec((SLOTS, COLS), lambda i, column: (0, column[i]))]
        specs += [
            pl.BlockSpec(
                (3, 1, half, COLS), lambda i, column, array=array: (0, array, 0, column[2 + i])
            )
        ] * 2
    return call(
        functools.partial(share_kernel, arrays),
        [sds((2, COLS, COLS), bf16), sds((2, COLS, COLS), f32)],
        vmem=24,
        flops=4 * 4 * SLOTS * 2 * COLS * COLS,
        nbytes=8 * SLOTS * COLS * 2 * 4 + 2 * COLS * COLS * 6,
        grid_spec=pltpu.PrefetchScalarGridSpec(
            num_scalar_prefetch=1,
            grid=(2,),
            in_specs=specs + [whole((2, SLOTS, COLS))] * 4 + [ANY] * len(after),
            out_specs=[whole((2, COLS, COLS))] * 2,
            scratch_shapes=[
                pltpu.VMEM((len(arrays), 4 * SLOTS, COLS), bf16),
                pltpu.VMEM((2, 4 * SLOTS, COLS), bf16),
            ],
        ),
        name="weight_shares",
    )(column, *chunks, *grads, *after)


def chunks_over_y(fulls, y_index):
    came = []
    for k in STEPS[1:]:
        start = (y_index + k) % 4 * 1024
        sent = jnp.stack([lax.dynamic_slice(v, (0, start), (SLOTS // 2, 1024)) for v in fulls])
        came.append(lax.ppermute(sent, "seq", y_shift(k)))
    came = jnp.stack(came)
    return came, lax.ppermute(came, "tp", X_SWAP)


def per_device(tokens, text_gaps, image_runs, gains, w_qkv, w_out, cotangent):
    group = lax.axis_index("grp")
    tp_index = lax.axis_index("tp")
    seq_index = lax.axis_index("seq")
    x_index, z_index = tp_index // 4, tp_index % 4
    y_index, core = seq_index // 2, seq_index % 2
    x_rows = tokens[0, 0]
    w_parts = jnp.transpose(w_qkv[0], (1, 0, 2))
    valid = jnp.where((group == 0) | (tp_index * ROWS < LI), 1.0, 0.0).astype(f32)
    meta = jnp.concatenate(
        [text_gaps[0], image_runs[0], jnp.stack([group, x_index, z_index]).astype(jnp.int32)]
    )

    order = jnp.stack(
        [
            jnp.where(xbit == 0, x_index, 1 - x_index) * 4 + (z_index + 4 - k) % 4
            for xbit in range(2)
            for k in STEPS
        ]
    ).astype(jnp.int32)

    n_left, n_right, grad_rows, inv = norm_rows(valid.reshape(1), x_rows, gains, cotangent[0, 0])
    grad_came = lax.all_gather(grad_rows, "tp", axis=0, tiled=True)
    pieces = gather_blocks(n_left, n_right)
    normed_full, own_kv = key_value(pieces, w_parts)
    other_kv = lax.ppermute(own_kv, "grp", GRP_SWAP)
    query = one_dot(normed_full, w_parts, 0)
    grad_full, grad_mixed = grad_mixed_of(order, grad_came, w_out)
    fulls = (normed_full, grad_full)
    chunk_came, chunk_other = chunks_over_y(fulls, y_index)

    mixed = attend_forward(meta, query, own_kv, other_kv)
    pair, own_part, other_part = attend_backward(
        meta, query, own_kv, other_kv, mixed, grad_mixed, []
    )
    proj_rows = lax.psum_scatter(
        proj_parts(order, mixed, w_out), "tp", scatter_dimension=0, tiled=True
    )
    back = lax.ppermute(other_part, "grp", GRP_SWAP)

    pairs = [pair] + [lax.ppermute(pair, "seq", y_shift(k)) for k in STEPS[1:]]
    kv_grad = sum_keys(own_part, back, [chunk_came])
    kv_grads = [kv_grad] + [lax.ppermute(kv_grad, "seq", y_shift(k)) for k in STEPS[1:]]

    lefts = [pair, kv_grad]
    right = back_right(lefts, w_parts, normed_full)
    right_x = lax.ppermute(right[1], "tp", X_SWAP)
    left = back_left(lefts, w_parts, normed_full, right[2])
    left_came = [lax.ppermute(left[i], "tp", z_shift(-STEPS[i])) for i in range(1, 4)]
    right_kept, *right_sends = sum_x(right[0], right_x, pairs[1:3])
    right_came = [
        lax.ppermute(sent, "tp", z_shift(-k)) for sent, k in zip(right_sends, STEPS[1:])
    ]
    left_kept, left_sent, gain_kept = sum_left(left[0], left_came, pairs[3:])
    left_x = lax.ppermute(left_sent, "tp", X_SWAP)
    layer_out = ((x_rows.astype(f32) + proj_rows.astype(f32)) * valid).astype(bf16)

    columns = jnp.stack(
        [y_index * 2 + 1 - core, y_index * 2 + core, 1 - core, core]
    ).astype(jnp.int32)
    chunks = (columns, fulls, chunk_came, chunk_other)
    pair_sent, pair_mine = weight_shares(*chunks, pairs, (1, 0), kv_grads[1:3])
    tokens_grad = token_rows(
        x_rows, grad_rows, gains, inv, (left_kept, left_x), (right_kept, *right_came), kv_grads[3:]
    )
    kv_sent, kv_mine = weight_shares(*chunks, kv_grads, (0,))
    gain_grad = sum_gain(gain_kept, left_x, gains)
    for flip in (2, 4, 1):
        gain_grad = gain_grad + lax.ppermute(gain_grad, "seq", [(i, i ^ flip) for i in range(8)])
    pair_share = pair_mine + lax.ppermute(pair_sent, "seq", CORE_SWAP).astype(f32)
    kv_share = kv_mine + lax.ppermute(kv_sent, "seq", CORE_SWAP).astype(f32)
    out_share = pair_share[0]
    qkv_share = jnp.concatenate([pair_share[1:], kv_share], axis=0)
    return (
        layer_out[None, None],
        tokens_grad[None, None],
        gain_grad,
        jnp.transpose(qkv_share, (1, 0, 2))[None],
        out_share[None],
    )


def solution(mesh):
    in_specs = (
        P("grp", "seq", "tp", None),
        P("seq", None),
        P("seq", None),
        P("grp", None),
        P("grp", None, None, "tp"),
        P("grp", None, "tp"),
        P("grp", "seq", "tp", None),
    )
    out_specs = (
        P("grp", "seq", "tp", None),
        P("grp", "seq", "tp", None),
        P("grp", None),
        P("grp", "seq", None, "tp"),
        P("grp", "seq", "tp"),
    )
    return jax.shard_map(
        per_device, mesh=mesh, in_specs=in_specs, out_specs=out_specs, check_vma=False
    )
```

```python
import functools

import jax
import jax.numpy as jnp
from jax import lax
from jax.experimental import pallas as pl
from jax.experimental.pallas import tpu as pltpu
from jax.sharding import PartitionSpec as P

HS = 128
LI = 128
HEADS = 4
SLOTS = 256
ROWS = 32
WIDTH = 4096
HALF = 2048
COLS = 512
FAR = 1073741824
f32 = jnp.float32
bf16 = jnp.bfloat16
MIB = 1024 * 1024

STEPS = (0, 1, 3, 2)


def z_shift(k):
    return [(i, (i // 4) * 4 + (i + k) % 4) for i in range(8)]


X_SWAP = [(i, i ^ 4) for i in range(8)]


def y_shift(k):
    return [(i, (i + 2 * k) % 8) for i in range(8)]


CORE_SWAP = [(i, i ^ 1) for i in range(8)]
GRP_SWAP = [(0, 1), (1, 0)]


def sds(shape, dtype):
    return jax.ShapeDtypeStruct(shape, dtype)


def call(kernel, out_shape, vmem, flops=0, nbytes=0, **kwargs):
    return pl.pallas_call(
        kernel,
        out_shape=out_shape,
        compiler_params=pltpu.CompilerParams(vmem_limit_bytes=vmem * MIB),
        cost_estimate=pl.CostEstimate(flops=flops, bytes_accessed=nbytes, transcendentals=0),
        **kwargs,
    )


def whole(shape):
    return pl.BlockSpec(shape, lambda *_: (0,) * len(shape))


SMEM = pl.BlockSpec(memory_space=pltpu.SMEM)
VMEM = pl.BlockSpec(memory_space=pltpu.VMEM)
ANY = pl.BlockSpec(memory_space=pl.ANY)


def dot(left, right):
    return jnp.dot(left, right, preferred_element_type=f32)


def dot_rows(left, right):
    return lax.dot_general(left, right, (((1,), (1,)), ((), ())), preferred_element_type=f32)


def dot_tokens(left, right):
    return lax.dot_general(left, right, (((0,), (0,)), ((), ())), preferred_element_type=f32)


def hold_kernel(*refs):
    count = (len(refs) - 1) // 2
    sems = refs[-1]
    copies = [
        pltpu.make_async_copy(refs[i], refs[count + i], sems.at[i]) for i in range(count)
    ]
    for copy in copies:
        copy.start()
    for copy in copies:
        copy.wait()


def hold(*arrays):
    count = len(arrays)
    return call(
        hold_kernel,
        [sds(v.shape, v.dtype) for v in arrays],
        vmem=1,
        nbytes=2 * sum(v.size * 2 for v in arrays),
        in_specs=[ANY] * count,
        out_specs=[ANY] * count,
        scratch_shapes=[pltpu.SemaphoreType.DMA((count,))],
        name="hold",
    )(*arrays)


def norm_kernel(valid, x, gain, cot, n_left, n_right, grad, inv):
    x_float = x[...].astype(f32)
    scale = lax.rsqrt(jnp.mean(x_float * x_float, axis=1, keepdims=True) + 1e-05)
    normed = (x_float * scale * gain[...].astype(f32)).astype(bf16)
    n_left[...] = normed[:, :HALF]
    n_right[...] = normed[:, HALF:]
    grad[...] = (cot[...].astype(f32) * valid[0]).astype(bf16)
    inv[...] = jnp.broadcast_to(scale, (ROWS, 128))


def norm_rows(valid, x, gain, cot):
    part = sds((ROWS, HALF), bf16)
    return call(
        norm_kernel,
        [part, part, sds((ROWS, WIDTH), bf16), sds((ROWS, 128), f32)],
        vmem=4,
        nbytes=4 * ROWS * WIDTH * 2,
        in_specs=[SMEM] + [VMEM] * 3,
        name="norm_rows",
    )(valid, x, gain, cot)


def gather_blocks(left, right):
    right_pair = jnp.stack([right, lax.ppermute(right, "tp", X_SWAP)])
    left_four = [left] + [lax.ppermute(left, "tp", z_shift(k)) for k in STEPS[1:]]
    right_four = [right_pair] + [lax.ppermute(right_pair, "tp", z_shift(k)) for k in STEPS[1:]]
    left_own = jnp.stack(left_four)
    left_other = lax.ppermute(left_own, "tp", X_SWAP)
    return [left_own, left_other] + right_four


def place_pieces(pieces, whole_ref):
    left_own, left_other = pieces[:2]
    for slot in range(4):
        rows = pl.ds(slot * ROWS, ROWS)
        other = pl.ds((4 + slot) * ROWS, ROWS)
        whole_ref[rows, :HALF] = left_own[slot]
        whole_ref[other, :HALF] = left_other[slot]
        whole_ref[rows, HALF:] = pieces[2 + slot][0]
        whole_ref[other, HALF:] = pieces[2 + slot][1]


PIECE_SHAPES = [(4, ROWS, HALF)] * 2 + [(2, ROWS, HALF)] * 4


def sum_left_kernel(own, c1, c2, c3, *refs):
    kept, sent, gain = refs[-3:]
    for part in range(2):
        total = own[part].astype(f32)
        for came in (c1, c2, c3):
            total = total + came[part].astype(f32)
        kept[pl.ds(part * 16, 16)] = total
        total = own[2 + part].astype(f32)
        for came in (c1, c2, c3):
            total = total + came[2 + part].astype(f32)
        sent[part] = total.astype(bf16)
    left, right = gain_from(own[4])
    for came in (c1, c2, c3):
        more_left, more_right = gain_from(came[4])
        left, right = left + more_left, right + more_right
    sent[2] = gain_rows_of(left, right)
    gain[0:1] = left
    gain[1:2] = right


def sum_left(own, came, after=()):
    return call(
        sum_left_kernel,
        [sds((ROWS, HALF), f32), sds((3, 16, HALF), bf16), sds((2, HALF), f32)],
        vmem=4,
        nbytes=11 * ROWS * HALF * 2,
        in_specs=[VMEM] * 4 + [ANY] * len(after),
        out_specs=[VMEM] * 3,
        name="sum_left",
    )(own, *came, *after)


def sum_gain_kernel(own, came, gain, out):
    left, right = gain_from(came[2])
    out[:, :HALF] = (own[0:1] + left) / gain[:, :HALF].astype(f32)
    out[:, HALF:] = (own[1:2] + right) / gain[:, HALF:].astype(f32)


def sum_gain(own, came, gain):
    return call(
        sum_gain_kernel,
        sds((1, WIDTH), f32),
        vmem=2,
        nbytes=10 * WIDTH * 2,
        in_specs=[VMEM] * 3,
        out_specs=VMEM,
        name="sum_gain",
    )(own, came, gain)


def sum_x_kernel(own, came, *refs):
    kept, sends = refs[-4], refs[-3:]
    kept[...] = own[0].astype(f32) + came[0].astype(f32)
    for slot, sent in enumerate(sends, 1):
        sent[...] = (own[slot].astype(f32) + came[slot].astype(f32)).astype(bf16)


def sum_x(own, came, after=()):
    shape = own.shape[1:]
    return call(
        sum_x_kernel,
        [sds(shape, f32)] + [sds(shape, bf16)] * 3,
        vmem=12,
        nbytes=13 * shape[0] * shape[1] * 2,
        in_specs=[VMEM] * 2 + [ANY] * len(after),
        out_specs=[VMEM] * 4,
        name="sum_x",
    )(own, came, *after)


def sum_keys_kernel(own, came, *refs):
    refs[-1][...] = (own[...] + came[...].astype(f32)).astype(bf16)


def sum_keys(own, came, after=()):
    return call(
        sum_keys_kernel,
        sds(came.shape, bf16),
        vmem=6,
        nbytes=8 * came.size,
        in_specs=[VMEM] * 2 + [ANY] * len(after),
        out_specs=VMEM,
        name="sum_keys",
    )(own, came, *after)


def rows_kernel(x, grad, gain, inv, l_kept, l_came, r_kept, r1, r2, r3, *refs):
    out = refs[-1]
    left = l_kept[...] + l_came[0:2].reshape(ROWS, HALF).astype(f32)
    right = r_kept[...]
    for came in (r1, r2, r3):
        right = right + came[...].astype(f32)
    scale = inv[:, :1]
    halves = []
    dots = jnp.zeros((ROWS, 1), f32)
    for part, cols in ((left, slice(0, HALF)), (right, slice(HALF, WIDTH))):
        scaled = gain[:, cols].astype(f32) * part
        rows = x[:, cols].astype(f32)
        dots = dots + jnp.sum(scaled * rows, axis=1, keepdims=True)
        halves.append((scaled, rows, cols))
    mean = dots * (1.0 / WIDTH)
    for scaled, rows, cols in halves:
        total = grad[:, cols].astype(f32) + scale * scaled - rows * (scale * scale * scale) * mean
        out[:, cols] = total.astype(bf16)


def token_rows(x, grad, gain, inv, left, right, after=()):
    return call(
        rows_kernel,
        sds((ROWS, WIDTH), bf16),
        vmem=4,
        nbytes=6 * ROWS * WIDTH * 2,
        in_specs=[VMEM] * 10 + [ANY] * len(after),
        out_specs=VMEM,
        name="token_rows",
    )(x, grad, gain, inv, *left, *right, *after)


def first_step():
    return jnp.logical_and(pl.program_id(0) == 0, pl.program_id(1) == 0)


def key_value_kernel(*refs):
    pieces, weight, full, out = refs[:6], refs[6], refs[7], refs[8]

    @pl.when(first_step())
    def _():
        place_pieces(pieces, full)

    out[0] = dot(full[...], weight[0]).astype(bf16)


def key_value(pieces, weights):
    block = 256
    return call(
        key_value_kernel,
        [sds((SLOTS, WIDTH), bf16), sds((2, SLOTS, COLS), bf16)],
        vmem=18,
        flops=4 * SLOTS * WIDTH * COLS,
        nbytes=2 * WIDTH * COLS * 2 + 2 * SLOTS * WIDTH * 2,
        grid=(2, COLS // block),
        in_specs=[whole(s) for s in PIECE_SHAPES]
        + [pl.BlockSpec((1, WIDTH, block), lambda p, j: (p + 1, 0, j))],
        out_specs=[
            whole((SLOTS, WIDTH)),
            pl.BlockSpec((1, SLOTS, block), lambda p, j: (p, 0, j)),
        ],
        name="key_value",
    )(*pieces, weights)


def grad_mixed_kernel(p0, p1, p2, p3, weight, full, out):
    @pl.when(pl.program_id(0) == 0)
    def _():
        for slot, pair in enumerate((p0, p1, p2, p3)):
            full[pl.ds(slot * ROWS, ROWS)] = pair[0]
            full[pl.ds((4 + slot) * ROWS, ROWS)] = pair[1]

    out[...] = dot(full[...], weight[0]).astype(bf16)


def grad_mixed_of(pairs, weights):
    block = 512
    return call(
        grad_mixed_kernel,
        [sds((SLOTS, WIDTH), bf16), sds((SLOTS, COLS), bf16)],
        vmem=18,
        flops=2 * SLOTS * WIDTH * COLS,
        nbytes=WIDTH * COLS * 2 + 2 * SLOTS * WIDTH * 2,
        grid=(COLS // block,),
        in_specs=[whole((2, ROWS, WIDTH))] * 4
        + [pl.BlockSpec((1, WIDTH, block), lambda j: (0, 0, j))],
        out_specs=[whole((SLOTS, WIDTH)), pl.BlockSpec((SLOTS, block), lambda j: (0, j))],
        name="grad_mixed",
    )(*pairs, weights)


def one_dot_kernel(full, weight, out):
    out[...] = dot(full[...], weight[0]).astype(bf16)


def one_dot(full, weights, part):
    block = 512
    return call(
        one_dot_kernel,
        sds((SLOTS, COLS), bf16),
        vmem=18,
        flops=2 * SLOTS * WIDTH * COLS,
        nbytes=WIDTH * COLS * 2 + SLOTS * WIDTH * 2,
        grid=(COLS // block,),
        in_specs=[
            whole((SLOTS, WIDTH)),
            pl.BlockSpec((1, WIDTH, block), lambda j: (part, 0, j)),
        ],
        out_specs=pl.BlockSpec((SLOTS, block), lambda j: (0, j)),
        name="one_dot",
    )(full, weights)


def gain_rows_of(left, right):
    row = lax.broadcasted_iota(jnp.int32, (16, left.shape[1]), 0)
    rows = jnp.zeros((16, left.shape[1]), f32)
    for first, part in ((0, left), (2, right)):
        high = part.astype(bf16).astype(f32)
        rows = jnp.where(row == first, high, rows)
        rows = jnp.where(row == first + 1, part - high, rows)
    return rows.astype(bf16)


def gain_from(rows):
    rows = rows.astype(f32)
    return rows[0:1] + rows[1:2], rows[2:3] + rows[3:4]


def back_total(pair, kv_grad, weight, normed):
    total = dot_rows(pair[...], weight[0][0])
    for part in range(2):
        total = total + dot_rows(kv_grad[part], weight[1 + part][0])
    rounded = total.astype(bf16)
    gain = jnp.sum(rounded.astype(f32) * normed[...].astype(f32), axis=0, keepdims=True)
    return rounded, gain


def back_right_kernel(pair, kv_grad, w0, w1, w2, normed, *refs):
    own, sent, gain = refs[-3:]
    rounded, gain[...] = back_total(pair, kv_grad, (w0, w1, w2), normed)
    for xbit, out in enumerate((own, sent)):
        for slot in range(4):
            start = (xbit * 4 + slot) * ROWS
            out[slot] = rounded[start:start + ROWS]


def back_left_kernel(pair, kv_grad, w0, w1, w2, normed, gain_right, *refs):
    rounded, gain = back_total(pair, kv_grad, (w0, w1, w2), normed)
    gains = gain_rows_of(gain, gain_right[...])
    for slot, out in enumerate(refs[-4:]):
        for xbit in range(2):
            start = (xbit * 4 + slot) * ROWS
            out[2 * xbit] = rounded[start:start + 16]
            out[2 * xbit + 1] = rounded[start + 16:start + ROWS]
        out[4] = gains


def back_dot(kernel, first, lefts, weights, normed, extra, out_shape, after, name):
    block = 512
    return call(
        kernel,
        out_shape,
        vmem=12,
        flops=2 * 3 * SLOTS * HALF * COLS,
        nbytes=3 * HALF * COLS * 2 + 2 * SLOTS * HALF * 2,
        grid=(HALF // block,),
        in_specs=[whole((SLOTS, COLS)), whole((2, SLOTS, COLS))]
        + [
            pl.BlockSpec((1, block, COLS), lambda j, part=part: (part, j + first, 0))
            for part in range(3)
        ]
        + [pl.BlockSpec((SLOTS, block), lambda j: (0, j + first))]
        + [pl.BlockSpec((1, block), lambda j: (0, j))] * len(extra)
        + [ANY] * len(after),
        out_specs=[
            pl.BlockSpec(v.shape[:-1] + (block,), lambda j, n=len(v.shape): (0,) * (n - 1) + (j,))
            for v in out_shape
        ],
        name=name,
    )(*lefts, weights, weights, weights, normed, *extra, *after)


def back_right(lefts, weights, normed, after=()):
    out = [sds((4, ROWS, HALF), bf16)] * 2 + [sds((1, HALF), f32)]
    return back_dot(
        back_right_kernel, HALF // 512, lefts, weights, normed, [], out, after, "back_right"
    )


def back_left(lefts, weights, normed, gain_right, after=()):
    out = [sds((5, 16, HALF), bf16)] * 4
    return back_dot(
        back_left_kernel, 0, lefts, weights, normed, [gain_right], out, after, "back_left"
    )


def proj_kernel(left, weight, own, sent):
    rounded = dot_rows(left[...], weight[0]).astype(bf16)
    for xbit, out in enumerate((own, sent)):
        for slot in range(4):
            start = (xbit * 4 + slot) * ROWS
            out[slot] = rounded[start:start + ROWS]


def proj_parts(mixed, weights):
    block = 512
    return call(
        proj_kernel,
        [sds((4, ROWS, WIDTH), bf16)] * 2,
        vmem=6,
        flops=2 * SLOTS * WIDTH * COLS,
        nbytes=WIDTH * COLS * 2 + SLOTS * WIDTH * 2,
        grid=(WIDTH // block,),
        in_specs=[whole((SLOTS, COLS)), pl.BlockSpec((1, block, COLS), lambda j: (0, j, 0))],
        out_specs=[pl.BlockSpec((4, ROWS, block), lambda j: (0, 0, j))] * 2,
        name="proj_parts",
    )(mixed, weights)


def slot_of(row, x_index, z_index):
    block = row // ROWS
    xbit = block // 4
    slot = block - xbit * 4
    back = jnp.where(slot == 2, 3, jnp.where(slot == 3, 2, slot))
    x_from = jnp.where(xbit == 0, x_index, 1 - x_index)
    z_from = z_index - back
    z_from = jnp.where(z_from < 0, z_from + 4, z_from)
    return (x_from * 4 + z_from) * ROWS + (row - block * ROWS)


def places(meta, rows, is_text):
    slot = slot_of(rows, meta[10], meta[11])
    text = slot
    end = jnp.int32(0)
    for run in range(4):
        end = end + meta[run]
        text = text + jnp.where(slot >= end, meta[5 + run], 0)
    image = slot + meta[0]
    end = jnp.int32(0)
    for run in range(3):
        end = end + meta[5 + run]
        image = image + jnp.where(slot >= end, meta[run + 1], 0)
    image = jnp.where(slot < LI, image, FAR)
    return jnp.where(is_text, text, image)


def admitted(meta):
    group = meta[9]
    query = places(meta, lax.broadcasted_iota(jnp.int32, (SLOTS, 1), 0), group == 0)
    key_row = lax.broadcasted_iota(jnp.int32, (1, SLOTS), 1)
    own = places(meta, key_row, group == 0)
    other = places(meta, key_row, group != 0)
    return own <= query, other <= query


def head_attn(query, own_key, other_key, own_ok, other_ok):
    scale = HS ** (-0.5)
    own = jnp.where(own_ok, dot_rows(query, own_key) * scale, -1e30)
    other = jnp.where(other_ok, dot_rows(query, other_key) * scale, -1e30)
    row_max = jnp.maximum(
        jnp.max(own, axis=1, keepdims=True), jnp.max(other, axis=1, keepdims=True)
    )
    own = jnp.exp(own - row_max)
    other = jnp.exp(other - row_max)
    row_sum = jnp.sum(own, axis=1, keepdims=True) + jnp.sum(other, axis=1, keepdims=True)
    share = 1.0 / row_sum
    return own * share, other * share


def forward_kernel(meta, query, own_kv, other_kv, *refs):
    mixed = refs[-1]
    own_ok, other_ok = admitted(meta)
    for head in range(HEADS):
        cols = slice(head * HS, (head + 1) * HS)
        own, other = head_attn(
            query[:, cols], own_kv[0, :, cols], other_kv[0, :, cols], own_ok, other_ok
        )
        total = dot(own.astype(bf16), own_kv[1, :, cols])
        total = total + dot(other.astype(bf16), other_kv[1, :, cols])
        mixed[:, cols] = total.astype(bf16)


def backward_kernel(meta, query, own_kv, other_kv, mixed, grad, *refs):
    q_grad, own_grad, other_grad = refs[-3:]
    scale = HS ** (-0.5)
    own_ok, other_ok = admitted(meta)
    for head in range(HEADS):
        cols = slice(head * HS, (head + 1) * HS)
        q, g = query[:, cols], grad[:, cols]
        row_dot = jnp.sum(g.astype(f32) * mixed[:, cols].astype(f32), axis=1, keepdims=True)
        attns = head_attn(q, own_kv[0, :, cols], other_kv[0, :, cols], own_ok, other_ok)
        dq = None
        for attn, kv, kv_grad in zip(attns, (own_kv, other_kv), (own_grad, other_grad)):
            value_grad = dot_tokens(attn.astype(bf16), g)
            weight_grad = dot_rows(g, kv[1, :, cols])
            score_grad = (attn * (weight_grad - row_dot)).astype(bf16)
            part = dot(score_grad, kv[0, :, cols])
            dq = part if dq is None else dq + part
            key_grad = dot_tokens(score_grad, q) * scale
            kv_grad[0, :, cols] = key_grad.astype(kv_grad.dtype)
            kv_grad[1, :, cols] = value_grad.astype(kv_grad.dtype)
        q_grad[:, cols] = (dq * scale).astype(bf16)


ATTN_FLOPS = 2 * HEADS * SLOTS * 2 * SLOTS * HS


def attend_forward(meta, query, own_kv, other_kv, after):
    return call(
        forward_kernel,
        sds((SLOTS, COLS), bf16),
        vmem=10,
        flops=4 * ATTN_FLOPS,
        nbytes=6 * SLOTS * COLS * 2,
        in_specs=[SMEM] + [VMEM] * 3 + [ANY] * len(after),
        out_specs=VMEM,
        name="attend_forward",
    )(meta, query, own_kv, other_kv, *after)


def attend_backward(meta, query, own_kv, other_kv, mixed, grad, after):
    kv = (2, SLOTS, COLS)
    return call(
        backward_kernel,
        [sds((SLOTS, COLS), bf16), sds(kv, f32), sds(kv, bf16)],
        vmem=14,
        flops=8 * ATTN_FLOPS,
        nbytes=12 * SLOTS * COLS * 2,
        in_specs=[SMEM] + [VMEM] * 5 + [ANY] * len(after),
        out_specs=[VMEM] * 3,
        name="attend_backward",
    )(meta, query, own_kv, other_kv, mixed, grad, *after)


def out_kernel(order, grad, mixed, own, sent):
    share = dot_tokens(grad[...], mixed[...]).astype(bf16)

    @pl.when(pl.program_id(0) < 4)
    def _():
        sent[0] = share

    @pl.when(pl.program_id(0) >= 4)
    def _():
        own[0] = share


def out_weight_parts(order, grad_full, mixed):
    return call(
        out_kernel,
        [sds((4, COLS, COLS), bf16)] * 2,
        vmem=6,
        flops=2 * SLOTS * WIDTH * COLS,
        nbytes=SLOTS * WIDTH * 2 + WIDTH * COLS * 2,
        grid_spec=pltpu.PrefetchScalarGridSpec(
            num_scalar_prefetch=1,
            grid=(8,),
            in_specs=[
                pl.BlockSpec((SLOTS, COLS), lambda i, order: (0, order[i])),
                pl.BlockSpec((SLOTS, COLS), lambda i, order: (0, 0)),
            ],
            out_specs=[
                pl.BlockSpec((1, COLS, COLS), lambda i, order: (jnp.maximum(i - 4, 0), 0, 0)),
                pl.BlockSpec((1, COLS, COLS), lambda i, order: (jnp.minimum(i, 3), 0, 0)),
            ],
        ),
        name="out_weight_parts",
    )(order, grad_full, mixed)


def share_kernel(columns, own, came, other, *refs):
    q_grads, kv_grads = refs[:4], refs[4:8]
    out, lefts = refs[-2:]
    half = SLOTS // 2
    part = pl.program_id(0)

    @pl.when(part == 0)
    def _():
        lefts[0] = own[...]
        for k in range(3):
            lefts[k + 1, :half] = came[k]
            lefts[k + 1, half:] = other[k]

    def share(grads):
        total = dot_tokens(lefts[0], grads[0])
        for k in range(1, 4):
            total = total + dot_tokens(lefts[k], grads[k])
        out[0] = total.astype(out.dtype)

    @pl.when(part == 0)
    def _():
        share([grad[...] for grad in q_grads])

    @pl.when(part > 0)
    def _():
        share([grad[0] for grad in kv_grads])


def weight_shares(columns, which, full, came, other, q_grads, kv_grads, dtype, after=()):
    half = SLOTS // 2
    return call(
        share_kernel,
        sds((3, COLS, COLS), dtype),
        vmem=16,
        flops=3 * 4 * 2 * SLOTS * COLS * COLS,
        nbytes=16 * SLOTS * COLS * 2 + 3 * COLS * COLS * 4,
        grid_spec=pltpu.PrefetchScalarGridSpec(
            num_scalar_prefetch=1,
            grid=(3,),
            in_specs=[
                pl.BlockSpec((SLOTS, COLS), lambda p, columns: (0, columns[which])),
                pl.BlockSpec((3, half, COLS), lambda p, columns: (0, 0, columns[2 + which])),
                pl.BlockSpec((3, half, COLS), lambda p, columns: (0, 0, columns[2 + which])),
            ]
            + [whole((SLOTS, COLS))] * 4
            + [
                pl.BlockSpec(
                    (1, SLOTS, COLS), lambda p, columns: (jnp.maximum(p - 1, 0), 0, 0)
                )
            ]
            * 4
            + [ANY] * len(after),
            out_specs=pl.BlockSpec((1, COLS, COLS), lambda p, columns: (p, 0, 0)),
            scratch_shapes=[pltpu.VMEM((4, SLOTS, COLS), bf16)],
        ),
        name="weight_shares",
    )(columns, full, came, other, *q_grads, *kv_grads, *after)


def chunks_over_y(full, y_index):
    came = []
    for k in STEPS[1:]:
        start = (y_index + k) % 4 * 1024
        sent = lax.dynamic_slice(full, (0, start), (SLOTS // 2, 1024))
        came.append(lax.ppermute(sent, "seq", y_shift(k)))
    came = jnp.stack(came)
    return came, lax.ppermute(came, "tp", X_SWAP)


def per_device(tokens, text_gaps, image_runs, gains, w_qkv, w_out, cotangent):
    group = lax.axis_index("grp")
    tp_index = lax.axis_index("tp")
    seq_index = lax.axis_index("seq")
    x_index, z_index = tp_index // 4, tp_index % 4
    y_index, core = seq_index // 2, seq_index % 2
    x_rows = tokens[0, 0]
    w_parts = jnp.transpose(w_qkv[0], (1, 0, 2))
    valid = jnp.where((group == 0) | (tp_index * ROWS < LI), 1.0, 0.0).astype(f32)
    meta = jnp.concatenate(
        [text_gaps[0], image_runs[0], jnp.stack([group, x_index, z_index]).astype(jnp.int32)]
    )

    back_y = jnp.stack([(y_index - k) % 4 for k in STEPS]) * 2
    out_order = jnp.concatenate([back_y + 1 - core, back_y + core]).astype(jnp.int32)
    columns = jnp.stack(
        [y_index * 2 + 1 - core, y_index * 2 + core, 1 - core, core]
    ).astype(jnp.int32)

    n_left, n_right, grad_rows, inv = norm_rows(valid.reshape(1), x_rows, gains, cotangent[0, 0])
    w_parts, w_out = hold(w_parts, w_out)
    pieces = gather_blocks(n_left, n_right)
    grad_other = lax.ppermute(grad_rows, "tp", X_SWAP)
    grad_pair = jnp.stack([grad_rows, grad_other])
    grad_pairs = [grad_pair] + [lax.ppermute(grad_pair, "tp", z_shift(k)) for k in STEPS[1:]]
    normed_full, own_kv = key_value(pieces, w_parts)
    other_kv = lax.ppermute(own_kv, "grp", GRP_SWAP)
    query = one_dot(normed_full, w_parts, 0)
    grad_full, grad_mixed = grad_mixed_of(grad_pairs, w_out)
    chunk_came, chunk_other = chunks_over_y(normed_full, y_index)

    mixed = attend_forward(meta, query, own_kv, other_kv, [grad_mixed])
    proj = proj_parts(mixed, w_out)
    proj_x = lax.ppermute(proj[1], "tp", X_SWAP)
    q_grad, own_part, other_part = attend_backward(
        meta, query, own_kv, other_kv, mixed, grad_mixed, [proj[0]]
    )
    back = lax.ppermute(other_part, "grp", GRP_SWAP)
    q_grads = [q_grad] + [lax.ppermute(q_grad, "seq", y_shift(k)) for k in STEPS[1:]]
    out_own, out_sent = out_weight_parts(out_order, grad_full, mixed)
    out_came = lax.ppermute(out_sent, "seq", CORE_SWAP)
    kv_grad = sum_keys(own_part, back, [chunk_came, out_own] + q_grads[1:3])
    kv_grads = [kv_grad] + [lax.ppermute(kv_grad, "seq", y_shift(k)) for k in STEPS[1:]]

    lefts = [q_grad, kv_grad]
    right = back_right(lefts, w_parts, normed_full, [chunk_other])
    right_x = lax.ppermute(right[1], "tp", X_SWAP)
    left = back_left(lefts, w_parts, normed_full, right[2], q_grads[3:] + kv_grads[1:3] + [proj_x, out_came])
    left_came = [lax.ppermute(left[i], "tp", z_shift(-STEPS[i])) for i in range(1, 4)]
    out_kept, *out_sends = sum_x(out_own, out_came, left_came[:1])
    out_terms = [lax.ppermute(v, "seq", y_shift(-k)) for v, k in zip(out_sends, STEPS[1:])]
    left_kept, left_sent, gain_kept = sum_left(
        left[0], left_came, [kv_grads[3], right_x, out_sends[0]]
    )
    left_x = lax.ppermute(left_sent, "tp", X_SWAP)
    shares = (normed_full, chunk_came, chunk_other, q_grads, kv_grads)
    qkv_sent = weight_shares(columns, 0, *shares, bf16)
    right_kept, *right_sends = sum_x(
        right[0], right_x, [left_x, qkv_sent] + out_terms[:2]
    )
    right_came = [lax.ppermute(v, "tp", z_shift(-k)) for v, k in zip(right_sends, STEPS[1:])]
    proj_kept, *proj_sends = sum_x(proj[0], proj_x, [right_sends[0]])
    proj_came = [lax.ppermute(v, "tp", z_shift(-k)) for v, k in zip(proj_sends, STEPS[1:])]
    gain_sum = sum_gain(gain_kept, left_x, gains)
    gain_sum = gain_sum + lax.ppermute(gain_sum, "seq", CORE_SWAP)
    gain_grad = gain_sum
    for k in STEPS[1:]:
        gain_grad = gain_grad + lax.ppermute(gain_sum, "seq", y_shift(k))
    tokens_grad = token_rows(
        x_rows, grad_rows, gains, inv, (left_kept, left_x), (right_kept, *right_came)
    )

    qkv_mine = weight_shares(columns, 1, *shares, f32, [qkv_sent] + out_terms[2:])
    qkv_share = qkv_mine + lax.ppermute(qkv_sent, "seq", CORE_SWAP).astype(f32)
    proj_rows = proj_kept
    for came in proj_came:
        proj_rows = proj_rows + came.astype(f32)
    layer_out = ((x_rows.astype(f32) + proj_rows) * valid).astype(bf16)
    out_share = out_kept
    for came in out_terms:
        out_share = out_share + came.astype(f32)
    return (
        layer_out[None, None],
        tokens_grad[None, None],
        gain_grad,
        jnp.transpose(qkv_share, (1, 0, 2))[None],
        out_share[None],
    )


def solution(mesh):
    in_specs = (
        P("grp", "seq", "tp", None),
        P("seq", None),
        P("seq", None),
        P("grp", None),
        P("grp", None, None, "tp"),
        P("grp", None, "tp"),
        P("grp", "seq", "tp", None),
    )
    out_specs = (
        P("grp", "seq", "tp", None),
        P("grp", "seq", "tp", None),
        P("grp", None),
        P("grp", "seq", None, "tp"),
        P("grp", "seq", "tp"),
    )
    return jax.shard_map(
        per_device, mesh=mesh, in_specs=in_specs, out_specs=out_specs, check_vma=False
    )
```

```python
import functools

import jax
import jax.numpy as jnp
from jax import lax
from jax.experimental import pallas as pl
from jax.experimental.pallas import tpu as pltpu
from jax.sharding import PartitionSpec as P

HS = 128
LI = 128
HEADS = 4
SLOTS = 256
ROWS = 32
WIDTH = 4096
HALF = 2048
COLS = 512
FAR = 1073741824
f32 = jnp.float32
bf16 = jnp.bfloat16
MIB = 1024 * 1024

STEPS = (0, 1, 3, 2)


def z_shift(k):
    return [(i, (i // 4) * 4 + (i + k) % 4) for i in range(8)]


X_SWAP = [(i, i ^ 4) for i in range(8)]


def y_shift(k):
    return [(i, (i + 2 * k) % 8) for i in range(8)]


CORE_SWAP = [(i, i ^ 1) for i in range(8)]
GRP_SWAP = [(0, 1), (1, 0)]


def sds(shape, dtype):
    return jax.ShapeDtypeStruct(shape, dtype)


def call(kernel, out_shape, vmem, flops=0, nbytes=0, **kwargs):
    return pl.pallas_call(
        kernel,
        out_shape=out_shape,
        compiler_params=pltpu.CompilerParams(vmem_limit_bytes=vmem * MIB),
        cost_estimate=pl.CostEstimate(flops=flops, bytes_accessed=nbytes, transcendentals=0),
        **kwargs,
    )


def whole(shape):
    return pl.BlockSpec(shape, lambda *_: (0,) * len(shape))


SMEM = pl.BlockSpec(memory_space=pltpu.SMEM)
VMEM = pl.BlockSpec(memory_space=pltpu.VMEM)
ANY = pl.BlockSpec(memory_space=pl.ANY)
HBM = pl.BlockSpec(memory_space=pltpu.HBM)


def dot(left, right):
    return jnp.dot(left, right, preferred_element_type=f32)


def dot_rows(left, right):
    return lax.dot_general(left, right, (((1,), (1,)), ((), ())), preferred_element_type=f32)


def dot_tokens(left, right):
    return lax.dot_general(left, right, (((0,), (0,)), ((), ())), preferred_element_type=f32)


def load(sources, targets, sems):
    copies = [
        pltpu.make_async_copy(source, target, sems.at[i])
        for i, (source, target) in enumerate(zip(sources, targets))
    ]
    for copy in copies:
        copy.start()
    return copies


KCUT = 1024
KCUTS = WIDTH // KCUT


def dot_loaded(full, buffer, copies):
    total = None
    for i, copy in enumerate(copies):
        copy.wait()
        cut = slice(i * KCUT, (i + 1) * KCUT)
        part = dot(full[:, cut], buffer[cut])
        total = part if total is None else total + part
    return total


def k_cuts(ref):
    return [ref.at[pl.ds(i * KCUT, KCUT)] for i in range(KCUTS)]


def norm_kernel(valid, x, gain, cot, n_left, n_right, grad, inv):
    x_float = x[...].astype(f32)
    scale = lax.rsqrt(jnp.mean(x_float * x_float, axis=1, keepdims=True) + 1e-05)
    normed = (x_float * scale * gain[...].astype(f32)).astype(bf16)
    n_left[...] = normed[:, :HALF]
    n_right[...] = normed[:, HALF:]
    grad[...] = (cot[...].astype(f32) * valid[0]).astype(bf16)
    inv[...] = jnp.broadcast_to(scale, (ROWS, 128))


def norm_rows(valid, x, gain, cot):
    part = sds((ROWS, HALF), bf16)
    return call(
        norm_kernel,
        [part, part, sds((ROWS, WIDTH), bf16), sds((ROWS, 128), f32)],
        vmem=4,
        nbytes=4 * ROWS * WIDTH * 2,
        in_specs=[SMEM] + [VMEM] * 3,
        name="norm_rows",
    )(valid, x, gain, cot)


def gather_blocks(left, right):
    right_pair = jnp.stack([right, lax.ppermute(right, "tp", X_SWAP)])
    left_four = [left] + [lax.ppermute(left, "tp", z_shift(k)) for k in STEPS[1:]]
    right_four = [right_pair] + [lax.ppermute(right_pair, "tp", z_shift(k)) for k in STEPS[1:]]
    left_own = jnp.stack(left_four)
    left_other = lax.ppermute(left_own, "tp", X_SWAP)
    return [left_own, left_other] + right_four


def place_pieces(pieces, whole_ref):
    left_own, left_other = pieces[:2]
    for slot in range(4):
        rows = pl.ds(slot * ROWS, ROWS)
        other = pl.ds((4 + slot) * ROWS, ROWS)
        whole_ref[rows, :HALF] = left_own[slot]
        whole_ref[other, :HALF] = left_other[slot]
        whole_ref[rows, HALF:] = pieces[2 + slot][0]
        whole_ref[other, HALF:] = pieces[2 + slot][1]


PIECE_SHAPES = [(4, ROWS, HALF)] * 2 + [(2, ROWS, HALF)] * 4


def sum_z_kernel(own, c1, c2, c3, *refs):
    kept, sent = refs[-2:]
    total = own[...].astype(f32)
    for came in (c1, c2, c3):
        total = total + came[...].astype(f32)
    kept[...] = total[0]
    sent[...] = total[1].astype(bf16)


def sum_z(own, came, after=()):
    shape = own.shape[1:]
    return call(
        sum_z_kernel,
        [sds(shape, f32), sds(shape, bf16)],
        vmem=6,
        nbytes=11 * shape[0] * shape[1] * 2,
        in_specs=[VMEM] * 4 + [ANY] * len(after),
        out_specs=[VMEM] * 2,
        name="sum_z",
    )(own, *came, *after)


def sum_left_kernel(own, c1, c2, c3, *refs):
    kept, sent, gain = refs[-3:]
    for part in range(2):
        total = own[part].astype(f32)
        for came in (c1, c2, c3):
            total = total + came[part].astype(f32)
        kept[pl.ds(part * 16, 16)] = total
        total = own[2 + part].astype(f32)
        for came in (c1, c2, c3):
            total = total + came[2 + part].astype(f32)
        sent[part] = total.astype(bf16)
    left, right = gain_from(own[4])
    for came in (c1, c2, c3):
        more_left, more_right = gain_from(came[4])
        left, right = left + more_left, right + more_right
    sent[2] = gain_rows_of(left, right)
    gain[0:1] = left
    gain[1:2] = right


def sum_left(own, came, after=()):
    return call(
        sum_left_kernel,
        [sds((ROWS, HALF), f32), sds((3, 16, HALF), bf16), sds((2, HALF), f32)],
        vmem=4,
        nbytes=11 * ROWS * HALF * 2,
        in_specs=[VMEM] * 4 + [ANY] * len(after),
        out_specs=[VMEM] * 3,
        name="sum_left",
    )(own, *came, *after)


def sum_gain_kernel(own, came, gain, out):
    left, right = gain_from(came[2])
    out[:, :HALF] = (own[0:1] + left) / gain[:, :HALF].astype(f32)
    out[:, HALF:] = (own[1:2] + right) / gain[:, HALF:].astype(f32)


def sum_gain(own, came, gain):
    return call(
        sum_gain_kernel,
        sds((1, WIDTH), f32),
        vmem=2,
        nbytes=10 * WIDTH * 2,
        in_specs=[VMEM] * 3,
        out_specs=VMEM,
        name="sum_gain",
    )(own, came, gain)


def sum_x_kernel(own, came, *refs):
    kept, sends = refs[-4], refs[-3:]
    kept[...] = own[0].astype(f32) + came[0].astype(f32)
    for slot, sent in enumerate(sends, 1):
        sent[...] = (own[slot].astype(f32) + came[slot].astype(f32)).astype(bf16)


def sum_x(own, came, after=()):
    shape = own.shape[1:]
    return call(
        sum_x_kernel,
        [sds(shape, f32)] + [sds(shape, bf16)] * 3,
        vmem=12,
        nbytes=13 * shape[0] * shape[1] * 2,
        in_specs=[VMEM] * 2 + [ANY] * len(after),
        out_specs=[VMEM] * 4,
        name="sum_x",
    )(own, came, *after)


def sum_rest_kernel(kept, c1, c2, c3, *refs):
    total = kept[...]
    for came in (c1, c2, c3):
        total = total + came[...].astype(f32)
    refs[-1][...] = total


def sum_rest(kept, came, after=()):
    return call(
        sum_rest_kernel,
        sds(kept.shape, f32),
        vmem=6,
        nbytes=14 * kept.size,
        in_specs=[VMEM] * 4 + [ANY] * len(after),
        out_specs=VMEM,
        name="sum_rest",
    )(kept, *came, *after)


def sum_keys_kernel(q_grad, own, came, *refs):
    out = refs[-1]
    out[0] = q_grad[...]
    out[1:] = (own[...] + came[...].astype(f32)).astype(bf16)


def sum_keys(q_grad, own, came, after=()):
    return call(
        sum_keys_kernel,
        sds((3, SLOTS, COLS), bf16),
        vmem=8,
        nbytes=10 * came.size,
        in_specs=[VMEM] * 3 + [ANY] * len(after),
        out_specs=VMEM,
        name="sum_keys",
    )(q_grad, own, came, *after)


def rows_kernel(x, grad, gain, inv, l_kept, l_came, r_kept, r1, r2, r3, *refs):
    out = refs[-1]
    left = l_kept[...] + l_came[0:2].reshape(ROWS, HALF).astype(f32)
    right = r_kept[...]
    for came in (r1, r2, r3):
        right = right + came[...].astype(f32)
    scale = inv[:, :1]
    halves = []
    dots = jnp.zeros((ROWS, 1), f32)
    for part, cols in ((left, slice(0, HALF)), (right, slice(HALF, WIDTH))):
        scaled = gain[:, cols].astype(f32) * part
        rows = x[:, cols].astype(f32)
        dots = dots + jnp.sum(scaled * rows, axis=1, keepdims=True)
        halves.append((scaled, rows, cols))
    mean = dots * (1.0 / WIDTH)
    for scaled, rows, cols in halves:
        total = grad[:, cols].astype(f32) + scale * scaled - rows * (scale * scale * scale) * mean
        out[:, cols] = total.astype(bf16)


def token_rows(x, grad, gain, inv, left, right, after=()):
    return call(
        rows_kernel,
        sds((ROWS, WIDTH), bf16),
        vmem=4,
        nbytes=6 * ROWS * WIDTH * 2,
        in_specs=[VMEM] * 10 + [ANY] * len(after),
        out_specs=VMEM,
        name="token_rows",
    )(x, grad, gain, inv, *left, *right, *after)


def key_value_kernel(*refs):
    pieces, weight = refs[:6], refs[6]
    full, out, buffer, sems = refs[-4:]
    copies = [
        load(k_cuts(weight.at[part + 1]), k_cuts(buffer.at[part]), sems.at[part])
        for part in range(2)
    ]
    place_pieces(pieces, full)
    for part in range(2):
        out[part] = dot_loaded(full, buffer.at[part], copies[part]).astype(bf16)


def key_value(pieces, weights, after):
    return call(
        key_value_kernel,
        [sds((SLOTS, WIDTH), bf16), sds((2, SLOTS, COLS), bf16)],
        vmem=20,
        flops=4 * SLOTS * WIDTH * COLS,
        nbytes=2 * WIDTH * COLS * 2 + 2 * SLOTS * WIDTH * 2,
        in_specs=[VMEM] * 6 + [HBM] + [ANY] * len(after),
        out_specs=[VMEM] * 2,
        scratch_shapes=[
            pltpu.VMEM((2, WIDTH, COLS), bf16),
            pltpu.SemaphoreType.DMA((2, KCUTS)),
        ],
        name="key_value",
    )(*pieces, weights, *after)


def query_kernel(full, weight, *refs):
    out, buffer, sems = refs[-3:]
    copies = load(k_cuts(weight.at[0]), k_cuts(buffer), sems)
    out[...] = dot_loaded(full, buffer, copies).astype(bf16)


DOT_SCRATCH = [pltpu.VMEM((WIDTH, COLS), bf16), pltpu.SemaphoreType.DMA((KCUTS,))]


def query_of(full, weights, after):
    return call(
        query_kernel,
        sds((SLOTS, COLS), bf16),
        vmem=12,
        flops=2 * SLOTS * WIDTH * COLS,
        nbytes=WIDTH * COLS * 2 + SLOTS * WIDTH * 2,
        in_specs=[VMEM, HBM] + [ANY] * len(after),
        out_specs=VMEM,
        scratch_shapes=DOT_SCRATCH,
        name="query",
    )(full, weights, *after)


def grad_mixed_kernel(p0, p1, p2, p3, weight, *refs):
    full, out, buffer, sems = refs[-4:]
    copies = load(k_cuts(weight.at[0]), k_cuts(buffer), sems)
    for slot, pair in enumerate((p0, p1, p2, p3)):
        full[pl.ds(slot * ROWS, ROWS)] = pair[0]
        full[pl.ds((4 + slot) * ROWS, ROWS)] = pair[1]
    out[...] = dot_loaded(full, buffer, copies).astype(bf16)


def grad_mixed_of(pairs, weights, after):
    return call(
        grad_mixed_kernel,
        [sds((SLOTS, WIDTH), bf16), sds((SLOTS, COLS), bf16)],
        vmem=16,
        flops=2 * SLOTS * WIDTH * COLS,
        nbytes=WIDTH * COLS * 2 + 2 * SLOTS * WIDTH * 2,
        in_specs=[VMEM] * 4 + [HBM] + [ANY] * len(after),
        out_specs=[VMEM] * 2,
        scratch_shapes=DOT_SCRATCH,
        name="grad_mixed",
    )(*pairs, weights, *after)


def gain_rows_of(left, right):
    row = lax.broadcasted_iota(jnp.int32, (16, left.shape[1]), 0)
    rows = jnp.zeros((16, left.shape[1]), f32)
    for first, part in ((0, left), (2, right)):
        high = part.astype(bf16).astype(f32)
        rows = jnp.where(row == first, high, rows)
        rows = jnp.where(row == first + 1, part - high, rows)
    return rows.astype(bf16)


def gain_from(rows):
    rows = rows.astype(f32)
    return rows[0:1] + rows[1:2], rows[2:3] + rows[3:4]


FCUT = 512
FCUTS = HALF // FCUT


def back_products(grads, weight, first, normed, buffer, sems):
    copies = [
        load(
            [weight.at[part, pl.ds(first + cut * FCUT, FCUT)] for part in range(3)],
            [buffer.at[part, pl.ds(cut * FCUT, FCUT)] for part in range(3)],
            sems.at[cut],
        )
        for cut in range(FCUTS)
    ]
    for cut in range(FCUTS):
        for copy in copies[cut]:
            copy.wait()
        rows = slice(cut * FCUT, (cut + 1) * FCUT)
        total = dot_rows(grads[0], buffer[0, rows])
        for part in range(1, 3):
            total = total + dot_rows(grads[part], buffer[part, rows])
        rounded = total.astype(bf16)
        terms = normed[:, first + cut * FCUT:first + (cut + 1) * FCUT].astype(f32)
        gain = jnp.sum(rounded.astype(f32) * terms, axis=0, keepdims=True)
        yield rows, rounded, gain


def back_right_kernel(waits, grads, weight, normed, *refs):
    own, sent, gain, buffer, sems = refs[waits:]
    for cols, rounded, terms in back_products(
        grads, weight, HALF, normed, buffer, sems
    ):
        gain[:, cols] = terms
        for xbit, out in enumerate((own, sent)):
            for slot in range(4):
                start = (xbit * 4 + slot) * ROWS
                out[slot, :, cols] = rounded[start:start + ROWS]


def back_left_kernel(waits, grads, weight, normed, gain_right, *refs):
    outs, buffer, sems = refs[waits:waits + 4], refs[-2], refs[-1]
    for cols, rounded, terms in back_products(
        grads, weight, 0, normed, buffer, sems
    ):
        gains = gain_rows_of(terms, gain_right[:, cols])
        for slot, out in enumerate(outs):
            for xbit in range(2):
                start = (xbit * 4 + slot) * ROWS
                out[2 * xbit, :, cols] = rounded[start:start + 16]
                out[2 * xbit + 1, :, cols] = rounded[start + 16:start + ROWS]
            out[4, :, cols] = gains


def back_dot(kernel, grads, weights, normed, extra, out_shape, after, name):
    return call(
        functools.partial(kernel, len(after)),
        out_shape,
        vmem=20,
        flops=2 * 3 * SLOTS * HALF * COLS,
        nbytes=3 * HALF * COLS * 2 + 2 * SLOTS * HALF * 2,
        in_specs=[VMEM, HBM, VMEM] + [VMEM] * len(extra) + [ANY] * len(after),
        out_specs=[VMEM] * len(out_shape),
        scratch_shapes=[
            pltpu.VMEM((3, HALF, COLS), bf16),
            pltpu.SemaphoreType.DMA((FCUTS, 3)),
        ],
        name=name,
    )(grads, weights, normed, *extra, *after)


def back_right(grads, weights, normed, after=()):
    out = [sds((4, ROWS, HALF), bf16)] * 2 + [sds((1, HALF), f32)]
    return back_dot(back_right_kernel, grads, weights, normed, [], out, after, "back_right")


def back_left(grads, weights, normed, gain_right, after=()):
    out = [sds((5, 16, HALF), bf16)] * 4
    return back_dot(back_left_kernel, grads, weights, normed, [gain_right], out, after, "back_left")


def proj_kernel(left, weight, *refs):
    outs, buffer, sems = refs[:4], refs[4], refs[5]
    copies = load(k_cuts(weight.at[0]), k_cuts(buffer), sems)
    for cut, copy in enumerate(copies):
        copy.wait()
        cols = slice(cut * KCUT, (cut + 1) * KCUT)
        rounded = dot_rows(left[...], buffer[cols]).astype(bf16)
        for slot in range(4):
            for xbit in range(2):
                start = (xbit * 4 + slot) * ROWS
                outs[slot][xbit, :, cols] = rounded[start:start + ROWS]


def proj_parts(mixed, weights):
    return call(
        proj_kernel,
        [sds((2, ROWS, WIDTH), bf16)] * 4,
        vmem=14,
        flops=2 * SLOTS * WIDTH * COLS,
        nbytes=WIDTH * COLS * 2 + SLOTS * WIDTH * 2,
        in_specs=[VMEM, HBM],
        out_specs=[VMEM] * 4,
        scratch_shapes=DOT_SCRATCH,
        name="proj_parts",
    )(mixed, weights)


def slot_of(row, x_index, z_index):
    block = row // ROWS
    xbit = block // 4
    slot = block - xbit * 4
    back = jnp.where(slot == 2, 3, jnp.where(slot == 3, 2, slot))
    x_from = jnp.where(xbit == 0, x_index, 1 - x_index)
    z_from = z_index - back
    z_from = jnp.where(z_from < 0, z_from + 4, z_from)
    return (x_from * 4 + z_from) * ROWS + (row - block * ROWS)


def places(meta, rows, is_text):
    slot = slot_of(rows, meta[10], meta[11])
    text = slot
    end = jnp.int32(0)
    for run in range(4):
        end = end + meta[run]
        text = text + jnp.where(slot >= end, meta[5 + run], 0)
    image = slot + meta[0]
    end = jnp.int32(0)
    for run in range(3):
        end = end + meta[5 + run]
        image = image + jnp.where(slot >= end, meta[run + 1], 0)
    image = jnp.where(slot < LI, image, FAR)
    return jnp.where(is_text, text, image)


def admitted(meta):
    group = meta[9]
    query = places(meta, lax.broadcasted_iota(jnp.int32, (SLOTS, 1), 0), group == 0)
    key_row = lax.broadcasted_iota(jnp.int32, (1, SLOTS), 1)
    own = places(meta, key_row, group == 0)
    other = places(meta, key_row, group != 0)
    return own <= query, other <= query


def head_attn(query, own_key, other_key, own_ok, other_ok):
    scale = HS ** (-0.5)
    own = jnp.where(own_ok, dot_rows(query, own_key) * scale, -1e30)
    other = jnp.where(other_ok, dot_rows(query, other_key) * scale, -1e30)
    row_max = jnp.maximum(
        jnp.max(own, axis=1, keepdims=True), jnp.max(other, axis=1, keepdims=True)
    )
    own = jnp.exp(own - row_max)
    other = jnp.exp(other - row_max)
    row_sum = jnp.sum(own, axis=1, keepdims=True) + jnp.sum(other, axis=1, keepdims=True)
    share = 1.0 / row_sum
    return own * share, other * share


def forward_kernel(meta, query, own_kv, other_kv, *refs):
    mixed = refs[-1]
    own_ok, other_ok = admitted(meta)
    for head in range(HEADS):
        cols = slice(head * HS, (head + 1) * HS)
        own, other = head_attn(
            query[:, cols], own_kv[0, :, cols], other_kv[0, :, cols], own_ok, other_ok
        )
        total = dot(own.astype(bf16), own_kv[1, :, cols])
        total = total + dot(other.astype(bf16), other_kv[1, :, cols])
        mixed[:, cols] = total.astype(bf16)


def backward_kernel(meta, query, own_kv, other_kv, mixed, grad, *refs):
    q_grad, own_grad, other_grad = refs[-3:]
    scale = HS ** (-0.5)
    own_ok, other_ok = admitted(meta)
    for head in range(HEADS):
        cols = slice(head * HS, (head + 1) * HS)
        q, g = query[:, cols], grad[:, cols]
        row_dot = jnp.sum(g.astype(f32) * mixed[:, cols].astype(f32), axis=1, keepdims=True)
        attns = head_attn(q, own_kv[0, :, cols], other_kv[0, :, cols], own_ok, other_ok)
        dq = None
        for attn, kv, kv_grad in zip(attns, (own_kv, other_kv), (own_grad, other_grad)):
            value_grad = dot_tokens(attn.astype(bf16), g)
            weight_grad = dot_rows(g, kv[1, :, cols])
            score_grad = (attn * (weight_grad - row_dot)).astype(bf16)
            part = dot(score_grad, kv[0, :, cols])
            dq = part if dq is None else dq + part
            key_grad = dot_tokens(score_grad, q) * scale
            kv_grad[0, :, cols] = key_grad.astype(kv_grad.dtype)
            kv_grad[1, :, cols] = value_grad.astype(kv_grad.dtype)
        q_grad[:, cols] = (dq * scale).astype(bf16)


ATTN_FLOPS = 2 * HEADS * SLOTS * 2 * SLOTS * HS


def attend_forward(meta, query, own_kv, other_kv, after):
    return call(
        forward_kernel,
        sds((SLOTS, COLS), bf16),
        vmem=10,
        flops=4 * ATTN_FLOPS,
        nbytes=6 * SLOTS * COLS * 2,
        in_specs=[SMEM] + [VMEM] * 3 + [ANY] * len(after),
        out_specs=VMEM,
        name="attend_forward",
    )(meta, query, own_kv, other_kv, *after)


def attend_backward(meta, query, own_kv, other_kv, mixed, grad, after):
    kv = (2, SLOTS, COLS)
    return call(
        backward_kernel,
        [sds((SLOTS, COLS), bf16), sds(kv, f32), sds(kv, bf16)],
        vmem=14,
        flops=8 * ATTN_FLOPS,
        nbytes=12 * SLOTS * COLS * 2,
        in_specs=[SMEM] + [VMEM] * 5 + [ANY] * len(after),
        out_specs=[VMEM] * 3,
        name="attend_backward",
    )(meta, query, own_kv, other_kv, mixed, grad, *after)


def out_kernel(order, grad, mixed, *refs):
    own, sent = refs[-2:]
    for i in range(8):
        start = pl.multiple_of(order[i] * COLS, COLS)
        share = dot_tokens(grad[:, pl.ds(start, COLS)], mixed[...]).astype(bf16)
        if i < 4:
            sent[i] = share
        else:
            own[i - 4] = share


def out_weight_parts(order, grad_full, mixed):
    return call(
        out_kernel,
        [sds((4, COLS, COLS), bf16)] * 2,
        vmem=12,
        flops=2 * SLOTS * WIDTH * COLS,
        nbytes=SLOTS * WIDTH * 2 + WIDTH * COLS * 2,
        in_specs=[SMEM, VMEM, VMEM],
        out_specs=[VMEM] * 2,
        name="out_weight_parts",
    )(order, grad_full, mixed)


def share_kernel(which, columns, full, c1, c2, c3, g0, g1, g2, g3, g4, *refs):
    out, lefts = refs[-2:]
    start = pl.multiple_of(columns[which] * COLS, COLS)
    lefts[0] = full[:, pl.ds(start, COLS)].T
    start = pl.multiple_of(columns[2 + which] * COLS, COLS)
    for k, came in enumerate((c1, c2, c3), 1):
        lefts[k] = came[:, pl.ds(start, COLS)].T
    for part in range(3):
        total = dot(lefts[0], g0[part])
        for k, grad in enumerate((g1, g2), 1):
            total = total + dot(lefts[k], grad[part])
        total = total + dot(lefts[3, :, :SLOTS // 2], g3[part])
        total = total + dot(lefts[3, :, SLOTS // 2:], g4[part])
        out[part] = total.astype(out.dtype)


def weight_shares(columns, which, full, came, grads, dtype, after=()):
    return call(
        functools.partial(share_kernel, which),
        sds((3, COLS, COLS), dtype),
        vmem=20,
        flops=3 * 4 * 2 * SLOTS * COLS * COLS,
        nbytes=16 * SLOTS * COLS * 2 + 3 * COLS * COLS * 4,
        in_specs=[SMEM] + [VMEM] * 9 + [ANY] * len(after),
        out_specs=VMEM,
        scratch_shapes=[pltpu.VMEM((4, COLS, SLOTS), bf16)],
        name="weight_shares",
    )(columns, full, *came, *grads, *after)


def chunks_over_y(full, y_index):
    came = []
    for k in STEPS[1:]:
        sent = lax.dynamic_slice_in_dim(full, (y_index + k) % 4 * 1024, 1024, 1)
        came.append(lax.ppermute(sent, "seq", y_shift(k)))
    return came


def per_device(tokens, text_gaps, image_runs, gains, w_qkv, w_out, cotangent):
    group = lax.axis_index("grp")
    tp_index = lax.axis_index("tp")
    seq_index = lax.axis_index("seq")
    x_index, z_index = tp_index // 4, tp_index % 4
    y_index, core = seq_index // 2, seq_index % 2
    x_rows = tokens[0, 0]
    w_parts = jnp.transpose(w_qkv[0], (1, 0, 2))
    valid = jnp.where((group == 0) | (tp_index * ROWS < LI), 1.0, 0.0).astype(f32)
    meta = jnp.concatenate(
        [text_gaps[0], image_runs[0], jnp.stack([group, x_index, z_index]).astype(jnp.int32)]
    )

    back_y = jnp.stack([(y_index - k) % 4 for k in STEPS]) * 2
    out_order = jnp.concatenate([back_y + 1 - core, back_y + core]).astype(jnp.int32)
    columns = jnp.stack(
        [y_index * 2 + 1 - core, y_index * 2 + core, 1 - core, core]
    ).astype(jnp.int32)

    n_left, n_right, grad_rows, inv = norm_rows(valid.reshape(1), x_rows, gains, cotangent[0, 0])
    pieces = gather_blocks(n_left, n_right)
    grad_other = lax.ppermute(grad_rows, "tp", X_SWAP)
    grad_pair = jnp.stack([grad_rows, grad_other])
    grad_pairs = [grad_pair] + [lax.ppermute(grad_pair, "tp", z_shift(k)) for k in STEPS[1:]]
    normed_full, own_kv = key_value(pieces, w_parts, [grad_pair])
    other_kv = lax.ppermute(own_kv, "grp", GRP_SWAP)
    query = query_of(normed_full, w_parts, grad_pairs[1:3])
    chunks = chunks_over_y(normed_full, y_index)

    mixed = attend_forward(meta, query, own_kv, other_kv, [])
    proj = proj_parts(mixed, w_out)
    proj_came = [lax.ppermute(proj[i], "tp", z_shift(-STEPS[i])) for i in range(1, 4)]
    grad_full, grad_mixed = grad_mixed_of(grad_pairs, w_out, [proj[0]] + chunks[:2])
    q_grad, own_part, other_part = attend_backward(
        meta, query, own_kv, other_kv, mixed, grad_mixed, []
    )
    back = lax.ppermute(other_part, "grp", GRP_SWAP)
    out_own, out_sent = out_weight_parts(out_order, grad_full, mixed)
    out_came = lax.ppermute(out_sent, "seq", CORE_SWAP)
    out_kept, *out_sends = sum_x(out_own, out_came)
    out_terms = [lax.ppermute(v, "seq", y_shift(-k)) for v, k in zip(out_sends, STEPS[1:])]
    own_grads = sum_keys(q_grad, own_part, back, [out_own] + proj_came[:2])
    half = SLOTS // 2
    back_grads = lax.ppermute(own_grads, "seq", y_shift(1))
    next_grads = lax.ppermute(own_grads, "seq", y_shift(3))
    far_grads = [
        lax.ppermute(back_grads[:, :half], "seq", y_shift(1)),
        lax.ppermute(next_grads[:, half:], "seq", y_shift(3)),
    ]
    grads = [own_grads, back_grads, next_grads] + far_grads

    right = back_right(own_grads, w_parts, normed_full, chunks[2:])
    right_x = lax.ppermute(right[1], "tp", X_SWAP)
    left = back_left(own_grads, w_parts, normed_full, right[2], [out_sends[0]])
    left_came = [lax.ppermute(left[i], "tp", z_shift(-STEPS[i])) for i in range(1, 4)]
    left_kept, left_sent, gain_kept = sum_left(left[0], left_came, [right_x])
    left_x = lax.ppermute(left_sent, "tp", X_SWAP)
    gain_sum = sum_gain(gain_kept, left_x, gains)
    gain_sum = gain_sum + lax.ppermute(gain_sum, "seq", CORE_SWAP)
    gain_grad = gain_sum
    for k in STEPS[1:]:
        gain_grad = gain_grad + lax.ppermute(gain_sum, "seq", y_shift(k))
    shares = (normed_full, chunks, grads)
    qkv_sent = weight_shares(columns, 0, *shares, bf16)
    right_kept, *right_sends = sum_x(right[0], right_x, [left_x, qkv_sent])
    proj_kept, proj_sent = sum_z(proj[0], proj_came, [left_sent])
    right_came = [lax.ppermute(v, "tp", z_shift(-k)) for v, k in zip(right_sends, STEPS[1:])]
    tokens_grad = token_rows(
        x_rows, grad_rows, gains, inv, (left_kept, left_x), (right_kept, *right_came)
    )

    qkv_mine = weight_shares(columns, 1, *shares, f32, [qkv_sent, right_came[0]] + out_terms[:2])
    qkv_share = qkv_mine + lax.ppermute(qkv_sent, "seq", CORE_SWAP).astype(f32)
    proj_rows = proj_kept + lax.ppermute(proj_sent, "tp", X_SWAP).astype(f32)
    layer_out = ((x_rows.astype(f32) + proj_rows) * valid).astype(bf16)
    out_share = sum_rest(out_kept, out_terms, right_came[:2])
    return (
        layer_out[None, None],
        tokens_grad[None, None],
        gain_grad,
        jnp.transpose(qkv_share, (1, 0, 2))[None],
        out_share[None],
    )


def solution(mesh):
    in_specs = (
        P("grp", "seq", "tp", None),
        P("seq", None),
        P("seq", None),
        P("grp", None),
        P("grp", None, None, "tp"),
        P("grp", None, "tp"),
        P("grp", "seq", "tp", None),
    )
    out_specs = (
        P("grp", "seq", "tp", None),
        P("grp", "seq", "tp", None),
        P("grp", None),
        P("grp", "seq", None, "tp"),
        P("grp", "seq", "tp"),
    )
    return jax.shard_map(
        per_device, mesh=mesh, in_specs=in_specs, out_specs=out_specs, check_vma=False
    )
```

```python
import functools

import jax
import jax.numpy as jnp
from jax import lax
from jax.experimental import pallas as pl
from jax.experimental.pallas import tpu as pltpu
from jax.sharding import PartitionSpec as P

HS = 128
LI = 128
HEADS = 4
SLOTS = 256
ROWS = 32
WIDTH = 4096
HALF = 2048
COLS = 512
FAR = 1073741824
f32 = jnp.float32
bf16 = jnp.bfloat16
MIB = 1024 * 1024

STEPS = (0, 1, 3, 2)


def z_shift(k):
    return [(i, (i // 4) * 4 + (i + k) % 4) for i in range(8)]


X_SWAP = [(i, i ^ 4) for i in range(8)]


def y_shift(k):
    return [(i, (i + 2 * k) % 8) for i in range(8)]


CORE_SWAP = [(i, i ^ 1) for i in range(8)]
GRP_SWAP = [(0, 1), (1, 0)]


def sds(shape, dtype):
    return jax.ShapeDtypeStruct(shape, dtype)


def call(kernel, out_shape, vmem, flops=0, nbytes=0, **kwargs):
    return pl.pallas_call(
        kernel,
        out_shape=out_shape,
        compiler_params=pltpu.CompilerParams(vmem_limit_bytes=vmem * MIB),
        cost_estimate=pl.CostEstimate(flops=flops, bytes_accessed=nbytes, transcendentals=0),
        **kwargs,
    )


def whole(shape):
    return pl.BlockSpec(shape, lambda *_: (0,) * len(shape))


SMEM = pl.BlockSpec(memory_space=pltpu.SMEM)
VMEM = pl.BlockSpec(memory_space=pltpu.VMEM)
ANY = pl.BlockSpec(memory_space=pl.ANY)
HBM = pl.BlockSpec(memory_space=pltpu.HBM)


def dot(left, right):
    return jnp.dot(left, right, preferred_element_type=f32)


def dot_rows(left, right):
    return lax.dot_general(left, right, (((1,), (1,)), ((), ())), preferred_element_type=f32)


def dot_tokens(left, right):
    return lax.dot_general(left, right, (((0,), (0,)), ((), ())), preferred_element_type=f32)


def where_am_i():
    tp, seq = lax.axis_index("tp"), lax.axis_index("seq")
    return tp >> 2, tp & 3, seq >> 1, seq & 1, lax.axis_index("grp")


def valid_rows():
    used = jnp.logical_or(lax.axis_index("grp") == 0, lax.axis_index("tp") * ROWS < LI)
    return jnp.where(used, 1.0, 0.0).astype(f32)


def load(sources, targets, sems):
    copies = [
        pltpu.make_async_copy(source, target, sems.at[i])
        for i, (source, target) in enumerate(zip(sources, targets))
    ]
    for copy in copies:
        copy.start()
    return copies


KCUT = 1024
KCUTS = WIDTH // KCUT


def dot_loaded(full, buffer, copies):
    total = None
    for i, copy in enumerate(copies):
        copy.wait()
        cut = slice(i * KCUT, (i + 1) * KCUT)
        part = dot(full[:, cut], buffer[cut])
        total = part if total is None else total + part
    return total


def k_cuts(ref):
    return [ref.at[pl.ds(i * KCUT, KCUT)] for i in range(KCUTS)]


def norm_kernel(x, gain, cot, n_left, n_right, grad, inv):
    x_float = x[...].astype(f32)
    scale = lax.rsqrt(jnp.mean(x_float * x_float, axis=1, keepdims=True) + 1e-05)
    normed = (x_float * scale * gain[...].astype(f32)).astype(bf16)
    n_left[...] = normed[:, :HALF]
    n_right[...] = normed[:, HALF:]
    grad[...] = (cot[...].astype(f32) * valid_rows()).astype(bf16)
    inv[...] = jnp.broadcast_to(scale, (ROWS, 128))


def norm_rows(x, gain, cot):
    part = sds((ROWS, HALF), bf16)
    return call(
        norm_kernel,
        [part, part, sds((ROWS, WIDTH), bf16), sds((ROWS, 128), f32)],
        vmem=4,
        nbytes=4 * ROWS * WIDTH * 2,
        in_specs=[VMEM] * 3,
        name="norm_rows",
    )(x, gain, cot)


def gather_blocks(left, right):
    right_pair = jnp.stack([right, lax.ppermute(right, "tp", X_SWAP)])
    left_four = [left] + [lax.ppermute(left, "tp", z_shift(k)) for k in STEPS[1:]]
    right_four = [right_pair] + [lax.ppermute(right_pair, "tp", z_shift(k)) for k in STEPS[1:]]
    left_own = jnp.stack(left_four)
    left_other = lax.ppermute(left_own, "tp", X_SWAP)
    return [left_own, left_other] + right_four


def place_pieces(pieces, whole_ref):
    left_own, left_other = pieces[:2]
    for slot in range(4):
        rows = pl.ds(slot * ROWS, ROWS)
        other = pl.ds((4 + slot) * ROWS, ROWS)
        whole_ref[rows, :HALF] = left_own[slot]
        whole_ref[other, :HALF] = left_other[slot]
        whole_ref[rows, HALF:] = pieces[2 + slot][0]
        whole_ref[other, HALF:] = pieces[2 + slot][1]


PIECE_SHAPES = [(4, ROWS, HALF)] * 2 + [(2, ROWS, HALF)] * 4


def sum_z_kernel(own, c1, c2, c3, *refs):
    kept, sent = refs[-2:]
    total = own[...].astype(f32)
    for came in (c1, c2, c3):
        total = total + came[...].astype(f32)
    kept[...] = total[0]
    sent[...] = total[1].astype(bf16)


def sum_z(own, came, after=()):
    shape = own.shape[1:]
    return call(
        sum_z_kernel,
        [sds(shape, f32), sds(shape, bf16)],
        vmem=6,
        nbytes=11 * shape[0] * shape[1] * 2,
        in_specs=[VMEM] * 4 + [ANY] * len(after),
        out_specs=[VMEM] * 2,
        name="sum_z",
    )(own, *came, *after)


def sum_left_kernel(own, c1, c2, c3, *refs):
    kept, sent, gain = refs[-3:]
    for part in range(2):
        total = own[part].astype(f32)
        for came in (c1, c2, c3):
            total = total + came[part].astype(f32)
        kept[pl.ds(part * 16, 16)] = total
        total = own[2 + part].astype(f32)
        for came in (c1, c2, c3):
            total = total + came[2 + part].astype(f32)
        sent[part] = total.astype(bf16)
    left, right = gain_from(own[4])
    for came in (c1, c2, c3):
        more_left, more_right = gain_from(came[4])
        left, right = left + more_left, right + more_right
    sent[2] = gain_rows_of(left, right)
    gain[0:1] = left
    gain[1:2] = right


def sum_left(own, came, after=()):
    return call(
        sum_left_kernel,
        [sds((ROWS, HALF), f32), sds((3, 16, HALF), bf16), sds((2, HALF), f32)],
        vmem=4,
        nbytes=11 * ROWS * HALF * 2,
        in_specs=[VMEM] * 4 + [ANY] * len(after),
        out_specs=[VMEM] * 3,
        name="sum_left",
    )(own, *came, *after)


def sum_gain_kernel(own, came, gain, out):
    left, right = gain_from(came[2])
    out[:, :HALF] = (own[0:1] + left) / gain[:, :HALF].astype(f32)
    out[:, HALF:] = (own[1:2] + right) / gain[:, HALF:].astype(f32)


def sum_gain(own, came, gain):
    return call(
        sum_gain_kernel,
        sds((1, WIDTH), f32),
        vmem=2,
        nbytes=10 * WIDTH * 2,
        in_specs=[VMEM] * 3,
        out_specs=VMEM,
        name="sum_gain",
    )(own, came, gain)


def sum_x_kernel(own, came, *refs):
    kept, sends = refs[-4], refs[-3:]
    kept[...] = own[0].astype(f32) + came[0].astype(f32)
    for slot, sent in enumerate(sends, 1):
        sent[...] = (own[slot].astype(f32) + came[slot].astype(f32)).astype(bf16)


def sum_x(own, came, after=()):
    shape = own.shape[1:]
    return call(
        sum_x_kernel,
        [sds(shape, f32)] + [sds(shape, bf16)] * 3,
        vmem=12,
        nbytes=13 * shape[0] * shape[1] * 2,
        in_specs=[VMEM] * 2 + [ANY] * len(after),
        out_specs=[VMEM] * 4,
        name="sum_x",
    )(own, came, *after)


def sum_rest_kernel(kept, c1, c2, c3, *refs):
    total = kept[...]
    for came in (c1, c2, c3):
        total = total + came[...].astype(f32)
    refs[-1][...] = total


def sum_rest(kept, came, after=()):
    return call(
        sum_rest_kernel,
        sds(kept.shape, f32),
        vmem=6,
        nbytes=14 * kept.size,
        in_specs=[VMEM] * 4 + [ANY] * len(after),
        out_specs=VMEM,
        name="sum_rest",
    )(kept, *came, *after)


def sum_keys_kernel(q_grad, own, came, *refs):
    out = refs[-1]
    out[0] = q_grad[...]
    out[1:] = (own[...] + came[...].astype(f32)).astype(bf16)


def sum_keys(q_grad, own, came, after=()):
    return call(
        sum_keys_kernel,
        sds((3, SLOTS, COLS), bf16),
        vmem=8,
        nbytes=10 * came.size,
        in_specs=[VMEM] * 3 + [ANY] * len(after),
        out_specs=VMEM,
        name="sum_keys",
    )(q_grad, own, came, *after)


def rows_kernel(x, grad, gain, inv, l_kept, l_came, r_kept, r1, r2, r3, *refs):
    out = refs[-1]
    left = l_kept[...] + l_came[0:2].reshape(ROWS, HALF).astype(f32)
    right = r_kept[...]
    for came in (r1, r2, r3):
        right = right + came[...].astype(f32)
    scale = inv[:, :1]
    halves = []
    dots = jnp.zeros((ROWS, 1), f32)
    for part, cols in ((left, slice(0, HALF)), (right, slice(HALF, WIDTH))):
        scaled = gain[:, cols].astype(f32) * part
        rows = x[:, cols].astype(f32)
        dots = dots + jnp.sum(scaled * rows, axis=1, keepdims=True)
        halves.append((scaled, rows, cols))
    mean = dots * (1.0 / WIDTH)
    for scaled, rows, cols in halves:
        total = grad[:, cols].astype(f32) + scale * scaled - rows * (scale * scale * scale) * mean
        out[:, cols] = total.astype(bf16)


def token_rows(x, grad, gain, inv, left, right, after=()):
    return call(
        rows_kernel,
        sds((ROWS, WIDTH), bf16),
        vmem=4,
        nbytes=6 * ROWS * WIDTH * 2,
        in_specs=[VMEM] * 10 + [ANY] * len(after),
        out_specs=VMEM,
        name="token_rows",
    )(x, grad, gain, inv, *left, *right, *after)


def key_value_kernel(*refs):
    pieces, weight = refs[:6], refs[6]
    full, out, buffer, sems = refs[-4:]
    copies = [
        load(k_cuts(weight.at[part + 1]), k_cuts(buffer.at[part]), sems.at[part])
        for part in range(2)
    ]
    place_pieces(pieces, full)
    for part in range(2):
        out[part] = dot_loaded(full, buffer.at[part], copies[part]).astype(bf16)


def key_value(pieces, weights, after):
    return call(
        key_value_kernel,
        [sds((SLOTS, WIDTH), bf16), sds((2, SLOTS, COLS), bf16)],
        vmem=20,
        flops=4 * SLOTS * WIDTH * COLS,
        nbytes=2 * WIDTH * COLS * 2 + 2 * SLOTS * WIDTH * 2,
        in_specs=[VMEM] * 6 + [HBM] + [ANY] * len(after),
        out_specs=[VMEM] * 2,
        scratch_shapes=[
            pltpu.VMEM((2, WIDTH, COLS), bf16),
            pltpu.SemaphoreType.DMA((2, KCUTS)),
        ],
        name="key_value",
    )(*pieces, weights, *after)


def query_kernel(full, weight, *refs):
    out, buffer, sems = refs[-3:]
    copies = load(k_cuts(weight.at[0]), k_cuts(buffer), sems)
    out[...] = dot_loaded(full, buffer, copies).astype(bf16)


DOT_SCRATCH = [pltpu.VMEM((WIDTH, COLS), bf16), pltpu.SemaphoreType.DMA((KCUTS,))]


def query_of(full, weights, after):
    return call(
        query_kernel,
        sds((SLOTS, COLS), bf16),
        vmem=12,
        flops=2 * SLOTS * WIDTH * COLS,
        nbytes=WIDTH * COLS * 2 + SLOTS * WIDTH * 2,
        in_specs=[VMEM, HBM] + [ANY] * len(after),
        out_specs=VMEM,
        scratch_shapes=DOT_SCRATCH,
        name="query",
    )(full, weights, *after)


def grad_mixed_kernel(p0, p1, p2, p3, weight, *refs):
    full, out, buffer, sems = refs[-4:]
    copies = load(k_cuts(weight.at[0]), k_cuts(buffer), sems)
    for slot, pair in enumerate((p0, p1, p2, p3)):
        full[pl.ds(slot * ROWS, ROWS)] = pair[0]
        full[pl.ds((4 + slot) * ROWS, ROWS)] = pair[1]
    out[...] = dot_loaded(full, buffer, copies).astype(bf16)


def grad_mixed_of(pairs, weights, after):
    return call(
        grad_mixed_kernel,
        [sds((SLOTS, WIDTH), bf16), sds((SLOTS, COLS), bf16)],
        vmem=16,
        flops=2 * SLOTS * WIDTH * COLS,
        nbytes=WIDTH * COLS * 2 + 2 * SLOTS * WIDTH * 2,
        in_specs=[VMEM] * 4 + [HBM] + [ANY] * len(after),
        out_specs=[VMEM] * 2,
        scratch_shapes=DOT_SCRATCH,
        name="grad_mixed",
    )(*pairs, weights, *after)


def gain_rows_of(left, right):
    row = lax.broadcasted_iota(jnp.int32, (16, left.shape[1]), 0)
    rows = jnp.zeros((16, left.shape[1]), f32)
    for first, part in ((0, left), (2, right)):
        high = part.astype(bf16).astype(f32)
        rows = jnp.where(row == first, high, rows)
        rows = jnp.where(row == first + 1, part - high, rows)
    return rows.astype(bf16)


def gain_from(rows):
    rows = rows.astype(f32)
    return rows[0:1] + rows[1:2], rows[2:3] + rows[3:4]


FCUT = 512
FCUTS = HALF // FCUT


def back_products(grads, weight, first, normed, buffer, sems):
    copies = [
        load(
            [weight.at[part, pl.ds(first + cut * FCUT, FCUT)] for part in range(3)],
            [buffer.at[part, pl.ds(cut * FCUT, FCUT)] for part in range(3)],
            sems.at[cut],
        )
        for cut in range(FCUTS)
    ]
    for cut in range(FCUTS):
        for copy in copies[cut]:
            copy.wait()
        rows = slice(cut * FCUT, (cut + 1) * FCUT)
        total = dot_rows(grads[0], buffer[0, rows])
        for part in range(1, 3):
            total = total + dot_rows(grads[part], buffer[part, rows])
        rounded = total.astype(bf16)
        terms = normed[:, first + cut * FCUT:first + (cut + 1) * FCUT].astype(f32)
        gain = jnp.sum(rounded.astype(f32) * terms, axis=0, keepdims=True)
        yield rows, rounded, gain


def back_right_kernel(waits, grads, weight, normed, *refs):
    own, sent, gain, buffer, sems = refs[waits:]
    for cols, rounded, terms in back_products(
        grads, weight, HALF, normed, buffer, sems
    ):
        gain[:, cols] = terms
        for xbit, out in enumerate((own, sent)):
            for slot in range(4):
                start = (xbit * 4 + slot) * ROWS
                out[slot, :, cols] = rounded[start:start + ROWS]


def back_left_kernel(waits, grads, weight, normed, gain_right, *refs):
    outs, buffer, sems = refs[waits:waits + 4], refs[-2], refs[-1]
    for cols, rounded, terms in back_products(
        grads, weight, 0, normed, buffer, sems
    ):
        gains = gain_rows_of(terms, gain_right[:, cols])
        for slot, out in enumerate(outs):
            for xbit in range(2):
                start = (xbit * 4 + slot) * ROWS
                out[2 * xbit, :, cols] = rounded[start:start + 16]
                out[2 * xbit + 1, :, cols] = rounded[start + 16:start + ROWS]
            out[4, :, cols] = gains


def back_dot(kernel, grads, weights, normed, extra, out_shape, after, name):
    return call(
        functools.partial(kernel, len(after)),
        out_shape,
        vmem=20,
        flops=2 * 3 * SLOTS * HALF * COLS,
        nbytes=3 * HALF * COLS * 2 + 2 * SLOTS * HALF * 2,
        in_specs=[VMEM, HBM, VMEM] + [VMEM] * len(extra) + [ANY] * len(after),
        out_specs=[VMEM] * len(out_shape),
        scratch_shapes=[
            pltpu.VMEM((3, HALF, COLS), bf16),
            pltpu.SemaphoreType.DMA((FCUTS, 3)),
        ],
        name=name,
    )(grads, weights, normed, *extra, *after)


def back_right(grads, weights, normed, after=()):
    out = [sds((4, ROWS, HALF), bf16)] * 2 + [sds((1, HALF), f32)]
    return back_dot(back_right_kernel, grads, weights, normed, [], out, after, "back_right")


def back_left(grads, weights, normed, gain_right, after=()):
    out = [sds((5, 16, HALF), bf16)] * 4
    return back_dot(back_left_kernel, grads, weights, normed, [gain_right], out, after, "back_left")


def proj_kernel(left, weight, *refs):
    outs, buffer, sems = refs[:4], refs[4], refs[5]
    copies = load(k_cuts(weight.at[0]), k_cuts(buffer), sems)
    for cut, copy in enumerate(copies):
        copy.wait()
        cols = slice(cut * KCUT, (cut + 1) * KCUT)
        rounded = dot_rows(left[...], buffer[cols]).astype(bf16)
        for slot in range(4):
            for xbit in range(2):
                start = (xbit * 4 + slot) * ROWS
                outs[slot][xbit, :, cols] = rounded[start:start + ROWS]


def proj_parts(mixed, weights):
    return call(
        proj_kernel,
        [sds((2, ROWS, WIDTH), bf16)] * 4,
        vmem=14,
        flops=2 * SLOTS * WIDTH * COLS,
        nbytes=WIDTH * COLS * 2 + SLOTS * WIDTH * 2,
        in_specs=[VMEM, HBM],
        out_specs=[VMEM] * 4,
        scratch_shapes=DOT_SCRATCH,
        name="proj_parts",
    )(mixed, weights)


def slot_of(row, x_index, z_index):
    block = row // ROWS
    xbit = block // 4
    slot = block - xbit * 4
    back = jnp.where(slot == 2, 3, jnp.where(slot == 3, 2, slot))
    x_from = jnp.where(xbit == 0, x_index, 1 - x_index)
    z_from = z_index - back
    z_from = jnp.where(z_from < 0, z_from + 4, z_from)
    return (x_from * 4 + z_from) * ROWS + (row - block * ROWS)


def places(gaps, runs, rows, is_text):
    x_index, z_index = where_am_i()[:2]
    slot = slot_of(rows, x_index, z_index)
    text = slot
    end = jnp.int32(0)
    for run in range(4):
        end = end + gaps[0, run]
        text = text + jnp.where(slot >= end, runs[0, run], 0)
    image = slot + gaps[0, 0]
    end = jnp.int32(0)
    for run in range(3):
        end = end + runs[0, run]
        image = image + jnp.where(slot >= end, gaps[0, run + 1], 0)
    image = jnp.where(slot < LI, image, FAR)
    return jnp.where(is_text, text, image)


def admitted(gaps, runs):
    group = lax.axis_index("grp")
    rows = lax.broadcasted_iota(jnp.int32, (SLOTS, 1), 0)
    query = places(gaps, runs, rows, group == 0)
    key_row = lax.broadcasted_iota(jnp.int32, (1, SLOTS), 1)
    own = places(gaps, runs, key_row, group == 0)
    other = places(gaps, runs, key_row, group != 0)
    return own <= query, other <= query


def head_attn(query, own_key, other_key, own_ok, other_ok):
    scale = HS ** (-0.5)
    own = jnp.where(own_ok, dot_rows(query, own_key) * scale, -1e30)
    other = jnp.where(other_ok, dot_rows(query, other_key) * scale, -1e30)
    row_max = jnp.maximum(
        jnp.max(own, axis=1, keepdims=True), jnp.max(other, axis=1, keepdims=True)
    )
    own = jnp.exp(own - row_max)
    other = jnp.exp(other - row_max)
    row_sum = jnp.sum(own, axis=1, keepdims=True) + jnp.sum(other, axis=1, keepdims=True)
    share = 1.0 / row_sum
    return own * share, other * share


def forward_kernel(gaps, runs, query, own_kv, other_kv, *refs):
    mixed = refs[-1]
    own_ok, other_ok = admitted(gaps, runs)
    for head in range(HEADS):
        cols = slice(head * HS, (head + 1) * HS)
        own, other = head_attn(
            query[:, cols], own_kv[0, :, cols], other_kv[0, :, cols], own_ok, other_ok
        )
        total = dot(own.astype(bf16), own_kv[1, :, cols])
        total = total + dot(other.astype(bf16), other_kv[1, :, cols])
        mixed[:, cols] = total.astype(bf16)


def backward_kernel(gaps, runs, query, own_kv, other_kv, mixed, grad, *refs):
    q_grad, own_grad, other_grad = refs[-3:]
    scale = HS ** (-0.5)
    own_ok, other_ok = admitted(gaps, runs)
    for head in range(HEADS):
        cols = slice(head * HS, (head + 1) * HS)
        q, g = query[:, cols], grad[:, cols]
        row_dot = jnp.sum(g.astype(f32) * mixed[:, cols].astype(f32), axis=1, keepdims=True)
        attns = head_attn(q, own_kv[0, :, cols], other_kv[0, :, cols], own_ok, other_ok)
        dq = None
        for attn, kv, kv_grad in zip(attns, (own_kv, other_kv), (own_grad, other_grad)):
            value_grad = dot_tokens(attn.astype(bf16), g)
            weight_grad = dot_rows(g, kv[1, :, cols])
            score_grad = (attn * (weight_grad - row_dot)).astype(bf16)
            part = dot(score_grad, kv[0, :, cols])
            dq = part if dq is None else dq + part
            key_grad = dot_tokens(score_grad, q) * scale
            kv_grad[0, :, cols] = key_grad.astype(kv_grad.dtype)
            kv_grad[1, :, cols] = value_grad.astype(kv_grad.dtype)
        q_grad[:, cols] = (dq * scale).astype(bf16)


ATTN_FLOPS = 2 * HEADS * SLOTS * 2 * SLOTS * HS


def attend_forward(spans, query, own_kv, other_kv, after):
    return call(
        forward_kernel,
        sds((SLOTS, COLS), bf16),
        vmem=10,
        flops=4 * ATTN_FLOPS,
        nbytes=6 * SLOTS * COLS * 2,
        in_specs=[SMEM] * 2 + [VMEM] * 3 + [ANY] * len(after),
        out_specs=VMEM,
        name="attend_forward",
    )(*spans, query, own_kv, other_kv, *after)


def attend_backward(spans, query, own_kv, other_kv, mixed, grad, after):
    kv = (2, SLOTS, COLS)
    return call(
        backward_kernel,
        [sds((SLOTS, COLS), bf16), sds(kv, f32), sds(kv, bf16)],
        vmem=14,
        flops=8 * ATTN_FLOPS,
        nbytes=12 * SLOTS * COLS * 2,
        in_specs=[SMEM] * 2 + [VMEM] * 5 + [ANY] * len(after),
        out_specs=[VMEM] * 3,
        name="attend_backward",
    )(*spans, query, own_kv, other_kv, mixed, grad, *after)


def out_kernel(grad, mixed, *refs):
    own, sent = refs[-2:]
    y_index, core = where_am_i()[2:4]
    for i in range(8):
        column = ((y_index - STEPS[i % 4]) & 3) * 2 + (1 - core if i < 4 else core)
        start = pl.multiple_of(column * COLS, COLS)
        share = dot_tokens(grad[:, pl.ds(start, COLS)], mixed[...]).astype(bf16)
        if i < 4:
            sent[i] = share
        else:
            own[i - 4] = share


def out_weight_parts(grad_full, mixed):
    return call(
        out_kernel,
        [sds((4, COLS, COLS), bf16)] * 2,
        vmem=12,
        flops=2 * SLOTS * WIDTH * COLS,
        nbytes=SLOTS * WIDTH * 2 + WIDTH * COLS * 2,
        in_specs=[VMEM] * 2,
        out_specs=[VMEM] * 2,
        name="out_weight_parts",
    )(grad_full, mixed)


def share_kernel(which, full, c1, c2, c3, g0, g1, g2, g3, g4, *refs):
    out, lefts = refs[-2:]
    y_index, core = where_am_i()[2:4]
    column = core if which else 1 - core
    start = pl.multiple_of((y_index * 2 + column) * COLS, COLS)
    lefts[0] = full[:, pl.ds(start, COLS)].T
    start = pl.multiple_of(column * COLS, COLS)
    for k, came in enumerate((c1, c2, c3), 1):
        lefts[k] = came[:, pl.ds(start, COLS)].T
    for part in range(3):
        total = dot(lefts[0], g0[part])
        for k, grad in enumerate((g1, g2), 1):
            total = total + dot(lefts[k], grad[part])
        total = total + dot(lefts[3, :, :SLOTS // 2], g3[part])
        total = total + dot(lefts[3, :, SLOTS // 2:], g4[part])
        out[part] = total.astype(out.dtype)


def weight_shares(which, full, came, grads, dtype, after=()):
    return call(
        functools.partial(share_kernel, which),
        sds((3, COLS, COLS), dtype),
        vmem=20,
        flops=3 * 4 * 2 * SLOTS * COLS * COLS,
        nbytes=16 * SLOTS * COLS * 2 + 3 * COLS * COLS * 4,
        in_specs=[VMEM] * 9 + [ANY] * len(after),
        out_specs=VMEM,
        scratch_shapes=[pltpu.VMEM((4, COLS, SLOTS), bf16)],
        name="weight_shares",
    )(full, *came, *grads, *after)


def chunk_kernel(full, *outs):
    y_index = where_am_i()[2]
    for k, out in zip(STEPS[1:], outs):
        start = pl.multiple_of(((y_index + k) & 3) * 1024, 1024)
        out[...] = full[:, pl.ds(start, 1024)]


def chunks_over_y(full):
    sends = call(
        chunk_kernel,
        [sds((SLOTS, 1024), bf16)] * 3,
        vmem=6,
        nbytes=6 * SLOTS * 1024 * 2,
        in_specs=[VMEM],
        out_specs=[VMEM] * 3,
        name="chunks",
    )(full)
    return [lax.ppermute(sent, "seq", y_shift(k)) for sent, k in zip(sends, STEPS[1:])]


def layer_kernel(x, kept, came, *refs):
    total = x[...].astype(f32) + (kept[...] + came[...].astype(f32))
    refs[-1][...] = (total * valid_rows()).astype(bf16)


def layer_rows(x, kept, came, after=()):
    return call(
        layer_kernel,
        sds((ROWS, WIDTH), bf16),
        vmem=4,
        nbytes=5 * ROWS * WIDTH * 2,
        in_specs=[VMEM] * 3 + [ANY] * len(after),
        out_specs=VMEM,
        name="layer_rows",
    )(x, kept, came, *after)


def per_device(tokens, text_gaps, image_runs, gains, w_qkv, w_out, cotangent):
    x_rows = tokens[0, 0]
    w_parts = jnp.transpose(w_qkv[0], (1, 0, 2))
    spans = (text_gaps, image_runs)

    n_left, n_right, grad_rows, inv = norm_rows(x_rows, gains, cotangent[0, 0])
    pieces = gather_blocks(n_left, n_right)
    grad_other = lax.ppermute(grad_rows, "tp", X_SWAP)
    grad_pair = jnp.stack([grad_rows, grad_other])
    grad_pairs = [grad_pair] + [lax.ppermute(grad_pair, "tp", z_shift(k)) for k in STEPS[1:]]
    normed_full, own_kv = key_value(pieces, w_parts, [grad_pair])
    other_kv = lax.ppermute(own_kv, "grp", GRP_SWAP)
    query = query_of(normed_full, w_parts, grad_pairs[1:3])
    chunks = chunks_over_y(normed_full)

    mixed = attend_forward(spans, query, own_kv, other_kv, [])
    proj = proj_parts(mixed, w_out)
    proj_came = [lax.ppermute(proj[i], "tp", z_shift(-STEPS[i])) for i in range(1, 4)]
    grad_full, grad_mixed = grad_mixed_of(grad_pairs, w_out, [proj[0]] + chunks[:2])
    q_grad, own_part, other_part = attend_backward(
        spans, query, own_kv, other_kv, mixed, grad_mixed, []
    )
    back = lax.ppermute(other_part, "grp", GRP_SWAP)
    out_own, out_sent = out_weight_parts(grad_full, mixed)
    out_came = lax.ppermute(out_sent, "seq", CORE_SWAP)
    out_kept, *out_sends = sum_x(out_own, out_came)
    out_terms = [lax.ppermute(v, "seq", y_shift(-k)) for v, k in zip(out_sends, STEPS[1:])]
    own_grads = sum_keys(q_grad, own_part, back, [out_own] + proj_came[:2])
    half = SLOTS // 2
    back_grads = lax.ppermute(own_grads, "seq", y_shift(1))
    next_grads = lax.ppermute(own_grads, "seq", y_shift(3))
    far_grads = [
        lax.ppermute(back_grads[:, :half], "seq", y_shift(1)),
        lax.ppermute(next_grads[:, half:], "seq", y_shift(3)),
    ]
    grads = [own_grads, back_grads, next_grads] + far_grads

    right = back_right(
        own_grads, w_parts, normed_full, chunks[2:] + proj_came[2:]
    )
    right_x = lax.ppermute(right[1], "tp", X_SWAP)
    left = back_left(own_grads, w_parts, normed_full, right[2], [out_sends[0]])
    left_came = [lax.ppermute(left[i], "tp", z_shift(-STEPS[i])) for i in range(1, 4)]
    left_kept, left_sent, gain_kept = sum_left(left[0], left_came, [right_x])
    left_x = lax.ppermute(left_sent, "tp", X_SWAP)
    gain_sum = sum_gain(gain_kept, left_x, gains)
    gain_sum = gain_sum + lax.ppermute(gain_sum, "seq", CORE_SWAP)
    gain_grad = gain_sum
    for k in STEPS[1:]:
        gain_grad = gain_grad + lax.ppermute(gain_sum, "seq", y_shift(k))
    shares = (normed_full, chunks, grads)
    qkv_sent = weight_shares(0, *shares, bf16)
    right_kept, *right_sends = sum_x(
        right[0], right_x, [left_x, qkv_sent] + out_terms[:2]
    )
    proj_kept, proj_sent = sum_z(proj[0], proj_came)
    right_came = [lax.ppermute(v, "tp", z_shift(-k)) for v, k in zip(right_sends, STEPS[1:])]
    tokens_grad = token_rows(
        x_rows, grad_rows, gains, inv, (left_kept, left_x), (right_kept, *right_came)
    )

    qkv_mine = weight_shares(1, *shares, f32, [qkv_sent, right_sends[0]])
    qkv_share = qkv_mine + lax.ppermute(qkv_sent, "seq", CORE_SWAP).astype(f32)
    proj_x = lax.ppermute(proj_sent, "tp", X_SWAP)
    layer_out = layer_rows(x_rows, proj_kept, proj_x)
    out_share = sum_rest(out_kept, out_terms, right_came[:1])
    return (
        layer_out[None, None],
        tokens_grad[None, None],
        gain_grad,
        jnp.transpose(qkv_share, (1, 0, 2))[None],
        out_share[None],
    )


def solution(mesh):
    in_specs = (
        P("grp", "seq", "tp", None),
        P("seq", None),
        P("seq", None),
        P("grp", None),
        P("grp", None, None, "tp"),
        P("grp", None, "tp"),
        P("grp", "seq", "tp", None),
    )
    out_specs = (
        P("grp", "seq", "tp", None),
        P("grp", "seq", "tp", None),
        P("grp", None),
        P("grp", "seq", None, "tp"),
        P("grp", "seq", "tp"),
    )
    return jax.shard_map(
        per_device, mesh=mesh, in_specs=in_specs, out_specs=out_specs, check_vma=False
    )
```

```python
import functools

import jax
import jax.numpy as jnp
from jax import lax
from jax.experimental import pallas as pl
from jax.experimental.pallas import tpu as pltpu
from jax.sharding import PartitionSpec as P

HS = 128
LI = 128
HEADS = 4
SLOTS = 256
ROWS = 32
WIDTH = 4096
HALF = 2048
COLS = 512
FAR = 1073741824
f32 = jnp.float32
bf16 = jnp.bfloat16
MIB = 1024 * 1024

STEPS = (0, 1, 3, 2)


def z_shift(k):
    return [(i, (i // 4) * 4 + (i + k) % 4) for i in range(8)]


X_SWAP = [(i, i ^ 4) for i in range(8)]


def y_shift(k):
    return [(i, (i + 2 * k) % 8) for i in range(8)]


CORE_SWAP = [(i, i ^ 1) for i in range(8)]
GRP_SWAP = [(0, 1), (1, 0)]


def sds(shape, dtype):
    return jax.ShapeDtypeStruct(shape, dtype)


def call(kernel, out_shape, vmem, flops=0, nbytes=0, **kwargs):
    return pl.pallas_call(
        kernel,
        out_shape=out_shape,
        compiler_params=pltpu.CompilerParams(vmem_limit_bytes=vmem * MIB),
        cost_estimate=pl.CostEstimate(flops=flops, bytes_accessed=nbytes, transcendentals=0),
        **kwargs,
    )


def whole(shape):
    return pl.BlockSpec(shape, lambda *_: (0,) * len(shape))


SMEM = pl.BlockSpec(memory_space=pltpu.SMEM)
VMEM = pl.BlockSpec(memory_space=pltpu.VMEM)
ANY = pl.BlockSpec(memory_space=pl.ANY)
HBM = pl.BlockSpec(memory_space=pltpu.HBM)


def dot(left, right):
    return jnp.dot(left, right, preferred_element_type=f32)


def dot_rows(left, right):
    return lax.dot_general(left, right, (((1,), (1,)), ((), ())), preferred_element_type=f32)


def dot_tokens(left, right):
    return lax.dot_general(left, right, (((0,), (0,)), ((), ())), preferred_element_type=f32)


def where_am_i():
    tp, seq = lax.axis_index("tp"), lax.axis_index("seq")
    return tp >> 2, tp & 3, seq >> 1, seq & 1, lax.axis_index("grp")


def valid_rows():
    used = jnp.logical_or(lax.axis_index("grp") == 0, lax.axis_index("tp") * ROWS < LI)
    return jnp.where(used, 1.0, 0.0).astype(f32)


def load(sources, targets, sems):
    copies = [
        pltpu.make_async_copy(source, target, sems.at[i])
        for i, (source, target) in enumerate(zip(sources, targets))
    ]
    for copy in copies:
        copy.start()
    return copies


KCUT = 1024
KCUTS = WIDTH // KCUT


def dot_loaded(full, buffer, copies):
    total = None
    for i, copy in enumerate(copies):
        copy.wait()
        cut = slice(i * KCUT, (i + 1) * KCUT)
        part = dot(full[:, cut], buffer[cut])
        total = part if total is None else total + part
    return total


def k_cuts(ref):
    return [ref.at[pl.ds(i * KCUT, KCUT)] for i in range(KCUTS)]


def norm_kernel(x, gain, cot, n_left, n_right, grad, inv):
    x_float = x[...].astype(f32)
    scale = lax.rsqrt(jnp.mean(x_float * x_float, axis=1, keepdims=True) + 1e-05)
    normed = (x_float * scale * gain[...].astype(f32)).astype(bf16)
    n_left[...] = normed[:, :HALF]
    n_right[...] = normed[:, HALF:]
    grad[...] = (cot[...].astype(f32) * valid_rows()).astype(bf16)
    inv[...] = jnp.broadcast_to(scale, (ROWS, 128))


def norm_rows(x, gain, cot):
    part = sds((ROWS, HALF), bf16)
    return call(
        norm_kernel,
        [part, part, sds((ROWS, WIDTH), bf16), sds((ROWS, 128), f32)],
        vmem=4,
        nbytes=4 * ROWS * WIDTH * 2,
        in_specs=[VMEM] * 3,
        name="norm_rows",
    )(x, gain, cot)


def gather_blocks(left, right):
    right_pair = jnp.stack([right, lax.ppermute(right, "tp", X_SWAP)])
    left_four = [left] + [lax.ppermute(left, "tp", z_shift(k)) for k in STEPS[1:]]
    right_four = [right_pair] + [lax.ppermute(right_pair, "tp", z_shift(k)) for k in STEPS[1:]]
    left_own = jnp.stack(left_four)
    left_other = lax.ppermute(left_own, "tp", X_SWAP)
    return [left_own, left_other] + right_four


def place_pieces(pieces, whole_ref):
    left_own, left_other = pieces[:2]
    for slot in range(4):
        rows = pl.ds(slot * ROWS, ROWS)
        other = pl.ds((4 + slot) * ROWS, ROWS)
        whole_ref[rows, :HALF] = left_own[slot]
        whole_ref[other, :HALF] = left_other[slot]
        whole_ref[rows, HALF:] = pieces[2 + slot][0]
        whole_ref[other, HALF:] = pieces[2 + slot][1]


PIECE_SHAPES = [(4, ROWS, HALF)] * 2 + [(2, ROWS, HALF)] * 4


def sum_z_kernel(own, c1, c2, c3, *refs):
    kept, sent = refs[-2:]
    total = own[...].astype(f32)
    for came in (c1, c2, c3):
        total = total + came[...].astype(f32)
    kept[...] = total[0]
    sent[...] = total[1].astype(bf16)


def sum_z(own, came, after=()):
    shape = own.shape[1:]
    return call(
        sum_z_kernel,
        [sds(shape, f32), sds(shape, bf16)],
        vmem=6,
        nbytes=11 * shape[0] * shape[1] * 2,
        in_specs=[VMEM] * 4 + [ANY] * len(after),
        out_specs=[VMEM] * 2,
        name="sum_z",
    )(own, *came, *after)


def sum_left_kernel(own, c1, c2, c3, *refs):
    kept, sent, gain = refs[-3:]
    for part in range(2):
        total = own[part].astype(f32)
        for came in (c1, c2, c3):
            total = total + came[part].astype(f32)
        kept[pl.ds(part * 16, 16)] = total
        total = own[2 + part].astype(f32)
        for came in (c1, c2, c3):
            total = total + came[2 + part].astype(f32)
        sent[part] = total.astype(bf16)
    left, right = gain_from(own[4])
    for came in (c1, c2, c3):
        more_left, more_right = gain_from(came[4])
        left, right = left + more_left, right + more_right
    sent[2] = gain_rows_of(left, right)
    gain[0:1] = left
    gain[1:2] = right


def sum_left(own, came, after=()):
    return call(
        sum_left_kernel,
        [sds((ROWS, HALF), f32), sds((3, 16, HALF), bf16), sds((2, HALF), f32)],
        vmem=4,
        nbytes=11 * ROWS * HALF * 2,
        in_specs=[VMEM] * 4 + [ANY] * len(after),
        out_specs=[VMEM] * 3,
        name="sum_left",
    )(own, *came, *after)


def sum_gain_kernel(own, came, gain, out):
    left, right = gain_from(came[2])
    out[:, :HALF] = (own[0:1] + left) / gain[:, :HALF].astype(f32)
    out[:, HALF:] = (own[1:2] + right) / gain[:, HALF:].astype(f32)


def sum_gain(own, came, gain):
    return call(
        sum_gain_kernel,
        sds((1, WIDTH), f32),
        vmem=2,
        nbytes=10 * WIDTH * 2,
        in_specs=[VMEM] * 3,
        out_specs=VMEM,
        name="sum_gain",
    )(own, came, gain)


def sum_x_kernel(waits, own, came, *refs):
    kept, sends = refs[waits], refs[waits + 1:]
    kept[...] = own[0].astype(f32) + came[0].astype(f32)
    for slot, sent in enumerate(sends, 1):
        sent[...] = (own[slot].astype(f32) + came[slot].astype(f32)).astype(bf16)


def sum_x(own, came, after=(), sends=3):
    shape = own.shape[1:]
    return call(
        functools.partial(sum_x_kernel, len(after)),
        [sds(shape, f32)] + [sds(shape, bf16)] * sends,
        vmem=12,
        nbytes=13 * shape[0] * shape[1] * 2,
        in_specs=[VMEM] * 2 + [ANY] * len(after),
        out_specs=[VMEM] * (1 + sends),
        name="sum_x",
    )(own, came, *after)


def halves_kernel(back, forth, *refs):
    half = SLOTS // 2
    refs[-2][...] = back[:, :half]
    refs[-1][...] = forth[:, half:]


def halves(back, forth, after):
    shape = (3, SLOTS // 2, COLS)
    return call(
        halves_kernel,
        [sds(shape, bf16)] * 2,
        vmem=6,
        nbytes=8 * back.size,
        in_specs=[VMEM] * 2 + [ANY] * len(after),
        out_specs=[VMEM] * 2,
        name="halves",
    )(back, forth, *after)


def sum_rest_kernel(kept, c1, c2, c3, *refs):
    total = kept[...]
    for came in (c1, c2, c3):
        total = total + came[...].astype(f32)
    refs[-1][...] = total


def sum_rest(kept, came, after=()):
    return call(
        sum_rest_kernel,
        sds(kept.shape, f32),
        vmem=6,
        nbytes=14 * kept.size,
        in_specs=[VMEM] * 4 + [ANY] * len(after),
        out_specs=VMEM,
        name="sum_rest",
    )(kept, *came, *after)


def sum_slot_kernel(slot, own, came, *refs):
    refs[-1][...] = (own[slot].astype(f32) + came[slot].astype(f32)).astype(bf16)


def sum_slot(slot, own, came, after):
    return call(
        functools.partial(sum_slot_kernel, slot),
        sds(own.shape[1:], bf16),
        vmem=8,
        nbytes=own.size * 2,
        in_specs=[VMEM] * 2 + [ANY] * len(after),
        out_specs=VMEM,
        name="sum_slot",
    )(own, came, *after)


def sum_keys_kernel(q_grad, own, came, *refs):
    out = refs[-1]
    out[0] = q_grad[...]
    out[1:] = (own[...] + came[...].astype(f32)).astype(bf16)


def sum_keys(q_grad, own, came, after=()):
    return call(
        sum_keys_kernel,
        sds((3, SLOTS, COLS), bf16),
        vmem=8,
        nbytes=10 * came.size,
        in_specs=[VMEM] * 3 + [ANY] * len(after),
        out_specs=VMEM,
        name="sum_keys",
    )(q_grad, own, came, *after)


def rows_kernel(x, grad, gain, inv, l_kept, l_came, r_kept, r1, r2, r3, *refs):
    out = refs[-1]
    left = l_kept[...] + l_came[0:2].reshape(ROWS, HALF).astype(f32)
    right = r_kept[...]
    for came in (r1, r2, r3):
        right = right + came[...].astype(f32)
    scale = inv[:, :1]
    halves = []
    dots = jnp.zeros((ROWS, 1), f32)
    for part, cols in ((left, slice(0, HALF)), (right, slice(HALF, WIDTH))):
        scaled = gain[:, cols].astype(f32) * part
        rows = x[:, cols].astype(f32)
        dots = dots + jnp.sum(scaled * rows, axis=1, keepdims=True)
        halves.append((scaled, rows, cols))
    mean = dots * (1.0 / WIDTH)
    for scaled, rows, cols in halves:
        total = grad[:, cols].astype(f32) + scale * scaled - rows * (scale * scale * scale) * mean
        out[:, cols] = total.astype(bf16)


def token_rows(x, grad, gain, inv, left, right, after=()):
    return call(
        rows_kernel,
        sds((ROWS, WIDTH), bf16),
        vmem=4,
        nbytes=6 * ROWS * WIDTH * 2,
        in_specs=[VMEM] * 10 + [ANY] * len(after),
        out_specs=VMEM,
        name="token_rows",
    )(x, grad, gain, inv, *left, *right, *after)


def key_value_kernel(*refs):
    pieces, weight = refs[:6], refs[6]
    full, out, buffer, sems = refs[-4:]
    copies = [
        load(k_cuts(weight.at[part + 1]), k_cuts(buffer.at[part]), sems.at[part])
        for part in range(2)
    ]
    place_pieces(pieces, full)
    for part in range(2):
        out[part] = dot_loaded(full, buffer.at[part], copies[part]).astype(bf16)


def key_value(pieces, weights, after):
    return call(
        key_value_kernel,
        [sds((SLOTS, WIDTH), bf16), sds((2, SLOTS, COLS), bf16)],
        vmem=20,
        flops=4 * SLOTS * WIDTH * COLS,
        nbytes=2 * WIDTH * COLS * 2 + 2 * SLOTS * WIDTH * 2,
        in_specs=[VMEM] * 6 + [HBM] + [ANY] * len(after),
        out_specs=[VMEM] * 2,
        scratch_shapes=[
            pltpu.VMEM((2, WIDTH, COLS), bf16),
            pltpu.SemaphoreType.DMA((2, KCUTS)),
        ],
        name="key_value",
    )(*pieces, weights, *after)


def query_kernel(full, weight, *refs):
    out, buffer, sems = refs[-3:]
    copies = load(k_cuts(weight.at[0]), k_cuts(buffer), sems)
    out[...] = dot_loaded(full, buffer, copies).astype(bf16)


DOT_SCRATCH = [pltpu.VMEM((WIDTH, COLS), bf16), pltpu.SemaphoreType.DMA((KCUTS,))]


def query_of(full, weights, after):
    return call(
        query_kernel,
        sds((SLOTS, COLS), bf16),
        vmem=12,
        flops=2 * SLOTS * WIDTH * COLS,
        nbytes=WIDTH * COLS * 2 + SLOTS * WIDTH * 2,
        in_specs=[VMEM, HBM] + [ANY] * len(after),
        out_specs=VMEM,
        scratch_shapes=DOT_SCRATCH,
        name="query",
    )(full, weights, *after)


def grad_mixed_kernel(p0, p1, p2, p3, weight, *refs):
    full, out, buffer, sems = refs[-4:]
    copies = load(k_cuts(weight.at[0]), k_cuts(buffer), sems)
    for slot, pair in enumerate((p0, p1, p2, p3)):
        full[pl.ds(slot * ROWS, ROWS)] = pair[0]
        full[pl.ds((4 + slot) * ROWS, ROWS)] = pair[1]
    out[...] = dot_loaded(full, buffer, copies).astype(bf16)


def grad_mixed_of(pairs, weights, after):
    return call(
        grad_mixed_kernel,
        [sds((SLOTS, WIDTH), bf16), sds((SLOTS, COLS), bf16)],
        vmem=16,
        flops=2 * SLOTS * WIDTH * COLS,
        nbytes=WIDTH * COLS * 2 + 2 * SLOTS * WIDTH * 2,
        in_specs=[VMEM] * 4 + [HBM] + [ANY] * len(after),
        out_specs=[VMEM] * 2,
        scratch_shapes=DOT_SCRATCH,
        name="grad_mixed",
    )(*pairs, weights, *after)


def gain_rows_of(left, right):
    row = lax.broadcasted_iota(jnp.int32, (16, left.shape[1]), 0)
    rows = jnp.zeros((16, left.shape[1]), f32)
    for first, part in ((0, left), (2, right)):
        high = part.astype(bf16).astype(f32)
        rows = jnp.where(row == first, high, rows)
        rows = jnp.where(row == first + 1, part - high, rows)
    return rows.astype(bf16)


def gain_from(rows):
    rows = rows.astype(f32)
    return rows[0:1] + rows[1:2], rows[2:3] + rows[3:4]


FCUT = 512
FCUTS = HALF // FCUT


def back_products(grads, weight, first, normed, buffer, sems):
    copies = [
        load(
            [weight.at[part, pl.ds(first + cut * FCUT, FCUT)] for part in range(3)],
            [buffer.at[part, pl.ds(cut * FCUT, FCUT)] for part in range(3)],
            sems.at[cut],
        )
        for cut in range(FCUTS)
    ]
    for cut in range(FCUTS):
        for copy in copies[cut]:
            copy.wait()
        rows = slice(cut * FCUT, (cut + 1) * FCUT)
        total = dot_rows(grads[0], buffer[0, rows])
        for part in range(1, 3):
            total = total + dot_rows(grads[part], buffer[part, rows])
        rounded = total.astype(bf16)
        terms = normed[:, first + cut * FCUT:first + (cut + 1) * FCUT].astype(f32)
        gain = jnp.sum(rounded.astype(f32) * terms, axis=0, keepdims=True)
        yield rows, rounded, gain


def back_right_kernel(waits, grads, weight, normed, *refs):
    own, sent, gain, buffer, sems = refs[waits:]
    for cols, rounded, terms in back_products(
        grads, weight, HALF, normed, buffer, sems
    ):
        gain[:, cols] = terms
        for xbit, out in enumerate((own, sent)):
            for slot in range(4):
                start = (xbit * 4 + slot) * ROWS
                out[slot, :, cols] = rounded[start:start + ROWS]


def back_left_kernel(waits, grads, weight, normed, gain_right, *refs):
    outs, buffer, sems = refs[waits:waits + 4], refs[-2], refs[-1]
    for cols, rounded, terms in back_products(
        grads, weight, 0, normed, buffer, sems
    ):
        gains = gain_rows_of(terms, gain_right[:, cols])
        for slot, out in enumerate(outs):
            for xbit in range(2):
                start = (xbit * 4 + slot) * ROWS
                out[2 * xbit, :, cols] = rounded[start:start + 16]
                out[2 * xbit + 1, :, cols] = rounded[start + 16:start + ROWS]
            out[4, :, cols] = gains


def back_dot(kernel, grads, weights, normed, extra, out_shape, after, name):
    return call(
        functools.partial(kernel, len(after)),
        out_shape,
        vmem=20,
        flops=2 * 3 * SLOTS * HALF * COLS,
        nbytes=3 * HALF * COLS * 2 + 2 * SLOTS * HALF * 2,
        in_specs=[VMEM, HBM, VMEM] + [VMEM] * len(extra) + [ANY] * len(after),
        out_specs=[VMEM] * len(out_shape),
        scratch_shapes=[
            pltpu.VMEM((3, HALF, COLS), bf16),
            pltpu.SemaphoreType.DMA((FCUTS, 3)),
        ],
        name=name,
    )(grads, weights, normed, *extra, *after)


def back_right(grads, weights, normed, after=()):
    out = [sds((4, ROWS, HALF), bf16)] * 2 + [sds((1, HALF), f32)]
    return back_dot(back_right_kernel, grads, weights, normed, [], out, after, "back_right")


def back_left(grads, weights, normed, gain_right, after=()):
    out = [sds((5, 16, HALF), bf16)] * 4
    return back_dot(back_left_kernel, grads, weights, normed, [gain_right], out, after, "back_left")


def proj_kernel(left, weight, *refs):
    outs, buffer, sems = refs[-6:-2], refs[-2], refs[-1]
    copies = load(k_cuts(weight.at[0]), k_cuts(buffer), sems)
    for cut, copy in enumerate(copies):
        copy.wait()
        cols = slice(cut * KCUT, (cut + 1) * KCUT)
        rounded = dot_rows(left[...], buffer[cols]).astype(bf16)
        for slot in range(4):
            for xbit in range(2):
                start = (xbit * 4 + slot) * ROWS
                outs[slot][xbit, :, cols] = rounded[start:start + ROWS]


def proj_parts(mixed, weights, after):
    return call(
        proj_kernel,
        [sds((2, ROWS, WIDTH), bf16)] * 4,
        vmem=14,
        flops=2 * SLOTS * WIDTH * COLS,
        nbytes=WIDTH * COLS * 2 + SLOTS * WIDTH * 2,
        in_specs=[VMEM, HBM] + [ANY] * len(after),
        out_specs=[VMEM] * 4,
        scratch_shapes=DOT_SCRATCH,
        name="proj_parts",
    )(mixed, weights, *after)


def slot_of(row, x_index, z_index):
    block = row // ROWS
    xbit = block // 4
    slot = block - xbit * 4
    back = jnp.where(slot == 2, 3, jnp.where(slot == 3, 2, slot))
    x_from = jnp.where(xbit == 0, x_index, 1 - x_index)
    z_from = z_index - back
    z_from = jnp.where(z_from < 0, z_from + 4, z_from)
    return (x_from * 4 + z_from) * ROWS + (row - block * ROWS)


def places(gaps, runs, rows, is_text):
    x_index, z_index = where_am_i()[:2]
    slot = slot_of(rows, x_index, z_index)
    text = slot
    end = jnp.int32(0)
    for run in range(4):
        end = end + gaps[0, run]
        text = text + jnp.where(slot >= end, runs[0, run], 0)
    image = slot + gaps[0, 0]
    end = jnp.int32(0)
    for run in range(3):
        end = end + runs[0, run]
        image = image + jnp.where(slot >= end, gaps[0, run + 1], 0)
    image = jnp.where(slot < LI, image, FAR)
    return jnp.where(is_text, text, image)


def admitted(gaps, runs):
    group = lax.axis_index("grp")
    rows = lax.broadcasted_iota(jnp.int32, (SLOTS, 1), 0)
    query = places(gaps, runs, rows, group == 0)
    key_row = lax.broadcasted_iota(jnp.int32, (1, SLOTS), 1)
    own = places(gaps, runs, key_row, group == 0)
    other = places(gaps, runs, key_row, group != 0)
    return own <= query, other <= query


def head_attn(query, own_key, other_key, own_ok, other_ok):
    scale = HS ** (-0.5)
    own = jnp.where(own_ok, dot_rows(query, own_key) * scale, -1e30)
    other = jnp.where(other_ok, dot_rows(query, other_key) * scale, -1e30)
    row_max = jnp.maximum(
        jnp.max(own, axis=1, keepdims=True), jnp.max(other, axis=1, keepdims=True)
    )
    own = jnp.exp(own - row_max)
    other = jnp.exp(other - row_max)
    row_sum = jnp.sum(own, axis=1, keepdims=True) + jnp.sum(other, axis=1, keepdims=True)
    share = 1.0 / row_sum
    return own * share, other * share


def forward_kernel(gaps, runs, query, own_kv, other_kv, *refs):
    mixed = refs[-1]
    own_ok, other_ok = admitted(gaps, runs)
    for head in range(HEADS):
        cols = slice(head * HS, (head + 1) * HS)
        own, other = head_attn(
            query[:, cols], own_kv[0, :, cols], other_kv[0, :, cols], own_ok, other_ok
        )
        total = dot(own.astype(bf16), own_kv[1, :, cols])
        total = total + dot(other.astype(bf16), other_kv[1, :, cols])
        mixed[:, cols] = total.astype(bf16)


def backward_kernel(gaps, runs, query, own_kv, other_kv, mixed, grad, *refs):
    q_grad, own_grad, other_grad = refs[-3:]
    scale = HS ** (-0.5)
    own_ok, other_ok = admitted(gaps, runs)
    for head in range(HEADS):
        cols = slice(head * HS, (head + 1) * HS)
        q, g = query[:, cols], grad[:, cols]
        row_dot = jnp.sum(g.astype(f32) * mixed[:, cols].astype(f32), axis=1, keepdims=True)
        attns = head_attn(q, own_kv[0, :, cols], other_kv[0, :, cols], own_ok, other_ok)
        dq = None
        for attn, kv, kv_grad in zip(attns, (own_kv, other_kv), (own_grad, other_grad)):
            value_grad = dot_tokens(attn.astype(bf16), g)
            weight_grad = dot_rows(g, kv[1, :, cols])
            score_grad = (attn * (weight_grad - row_dot)).astype(bf16)
            part = dot(score_grad, kv[0, :, cols])
            dq = part if dq is None else dq + part
            key_grad = dot_tokens(score_grad, q) * scale
            kv_grad[0, :, cols] = key_grad.astype(kv_grad.dtype)
            kv_grad[1, :, cols] = value_grad.astype(kv_grad.dtype)
        q_grad[:, cols] = (dq * scale).astype(bf16)


ATTN_FLOPS = 2 * HEADS * SLOTS * 2 * SLOTS * HS


def attend_forward(spans, query, own_kv, other_kv, after):
    return call(
        forward_kernel,
        sds((SLOTS, COLS), bf16),
        vmem=10,
        flops=4 * ATTN_FLOPS,
        nbytes=6 * SLOTS * COLS * 2,
        in_specs=[SMEM] * 2 + [VMEM] * 3 + [ANY] * len(after),
        out_specs=VMEM,
        name="attend_forward",
    )(*spans, query, own_kv, other_kv, *after)


def attend_backward(spans, query, own_kv, other_kv, mixed, grad, after):
    kv = (2, SLOTS, COLS)
    return call(
        backward_kernel,
        [sds((SLOTS, COLS), bf16), sds(kv, f32), sds(kv, bf16)],
        vmem=14,
        flops=8 * ATTN_FLOPS,
        nbytes=12 * SLOTS * COLS * 2,
        in_specs=[SMEM] * 2 + [VMEM] * 5 + [ANY] * len(after),
        out_specs=[VMEM] * 3,
        name="attend_backward",
    )(*spans, query, own_kv, other_kv, mixed, grad, *after)


def out_kernel(grad, mixed, *refs):
    own, sent = refs[-2:]
    y_index, core = where_am_i()[2:4]
    for i in range(8):
        column = ((y_index - STEPS[i % 4]) & 3) * 2 + (1 - core if i < 4 else core)
        start = pl.multiple_of(column * COLS, COLS)
        share = dot_tokens(grad[:, pl.ds(start, COLS)], mixed[...]).astype(bf16)
        if i < 4:
            sent[i] = share
        else:
            own[i - 4] = share


def out_weight_parts(grad_full, mixed, after):
    return call(
        out_kernel,
        [sds((4, COLS, COLS), bf16)] * 2,
        vmem=12,
        flops=2 * SLOTS * WIDTH * COLS,
        nbytes=SLOTS * WIDTH * 2 + WIDTH * COLS * 2,
        in_specs=[VMEM] * 2 + [ANY] * len(after),
        out_specs=[VMEM] * 2,
        name="out_weight_parts",
    )(grad_full, mixed, *after)


def share_kernel(which, full, c1, c2, c3, g0, g1, g2, g3, g4, *refs):
    out, lefts = refs[-2:]
    y_index, core = where_am_i()[2:4]
    column = core if which else 1 - core
    start = pl.multiple_of((y_index * 2 + column) * COLS, COLS)
    lefts[0] = full[:, pl.ds(start, COLS)].T
    start = pl.multiple_of(column * COLS, COLS)
    for k, came in enumerate((c1, c2, c3), 1):
        lefts[k] = came[:, pl.ds(start, COLS)].T
    for part in range(3):
        total = dot(lefts[0], g0[part])
        for k, grad in enumerate((g1, g2), 1):
            total = total + dot(lefts[k], grad[part])
        total = total + dot(lefts[3, :, :SLOTS // 2], g3[part])
        total = total + dot(lefts[3, :, SLOTS // 2:], g4[part])
        out[part] = total.astype(out.dtype)


def weight_shares(which, full, came, grads, dtype, after=()):
    return call(
        functools.partial(share_kernel, which),
        sds((3, COLS, COLS), dtype),
        vmem=20,
        flops=3 * 4 * 2 * SLOTS * COLS * COLS,
        nbytes=16 * SLOTS * COLS * 2 + 3 * COLS * COLS * 4,
        in_specs=[VMEM] * 9 + [ANY] * len(after),
        out_specs=VMEM,
        scratch_shapes=[pltpu.VMEM((4, COLS, SLOTS), bf16)],
        name="weight_shares",
    )(full, *came, *grads, *after)


def chunk_kernel(full, *outs):
    y_index = where_am_i()[2]
    for k, out in zip(STEPS[1:], outs):
        start = pl.multiple_of(((y_index + k) & 3) * 1024, 1024)
        out[...] = full[:, pl.ds(start, 1024)]


def chunks_over_y(full):
    sends = call(
        chunk_kernel,
        [sds((SLOTS, 1024), bf16)] * 3,
        vmem=6,
        nbytes=6 * SLOTS * 1024 * 2,
        in_specs=[VMEM],
        out_specs=[VMEM] * 3,
        name="chunks",
    )(full)
    return [lax.ppermute(sent, "seq", y_shift(k)) for sent, k in zip(sends, STEPS[1:])]


def layer_kernel(x, kept, came, *refs):
    total = x[...].astype(f32) + (kept[...] + came[...].astype(f32))
    refs[-1][...] = (total * valid_rows()).astype(bf16)


def layer_rows(x, kept, came, after=()):
    return call(
        layer_kernel,
        sds((ROWS, WIDTH), bf16),
        vmem=4,
        nbytes=5 * ROWS * WIDTH * 2,
        in_specs=[VMEM] * 3 + [ANY] * len(after),
        out_specs=VMEM,
        name="layer_rows",
    )(x, kept, came, *after)


def per_device(tokens, text_gaps, image_runs, gains, w_qkv, w_out, cotangent):
    x_rows = tokens[0, 0]
    w_parts = jnp.transpose(w_qkv[0], (1, 0, 2))
    spans = (text_gaps, image_runs)

    n_left, n_right, grad_rows, inv = norm_rows(x_rows, gains, cotangent[0, 0])
    pieces = gather_blocks(n_left, n_right)
    grad_other = lax.ppermute(grad_rows, "tp", X_SWAP)
    grad_pair = jnp.stack([grad_rows, grad_other])
    grad_pairs = [grad_pair] + [lax.ppermute(grad_pair, "tp", z_shift(k)) for k in STEPS[1:]]
    normed_full, own_kv = key_value(pieces, w_parts, [grad_pair])
    other_kv = lax.ppermute(own_kv, "grp", GRP_SWAP)
    query = query_of(normed_full, w_parts, grad_pairs[1:3])
    chunks = chunks_over_y(normed_full)

    mixed = attend_forward(spans, query, own_kv, other_kv, [])
    grad_full, grad_mixed = grad_mixed_of(grad_pairs, w_out, [mixed] + chunks[:2])
    q_grad, own_part, other_part = attend_backward(
        spans, query, own_kv, other_kv, mixed, grad_mixed, []
    )
    back = lax.ppermute(other_part, "grp", GRP_SWAP)
    proj = proj_parts(mixed, w_out, [q_grad])
    proj_came = [lax.ppermute(proj[i], "tp", z_shift(-STEPS[i])) for i in range(1, 4)]
    out_own, out_sent = out_weight_parts(grad_full, mixed, [q_grad])
    out_came = lax.ppermute(out_sent, "seq", CORE_SWAP)
    out_kept, *out_sends = sum_x(out_own, out_came, sends=2)
    out_terms = [lax.ppermute(v, "seq", y_shift(-k)) for v, k in zip(out_sends, STEPS[1:3])]
    own_grads = sum_keys(q_grad, own_part, back, [proj[0]])
    back_grads = lax.ppermute(own_grads, "seq", y_shift(1))
    next_grads = lax.ppermute(own_grads, "seq", y_shift(3))

    right = back_right(own_grads, w_parts, normed_full, [out_came] + chunks[2:])
    right_x = lax.ppermute(right[1], "tp", X_SWAP)
    left = back_left(own_grads, w_parts, normed_full, right[2], [out_sends[0]] + proj_came[:2])
    left_came = [lax.ppermute(left[i], "tp", z_shift(-STEPS[i])) for i in range(1, 4)]
    relayed = halves(back_grads, next_grads, left_came[:1] + [right_x])
    grads = [own_grads, back_grads, next_grads]
    grads += [lax.ppermute(v, "seq", y_shift(k)) for v, k in zip(relayed, (1, 3))]
    left_kept, left_sent, gain_kept = sum_left(left[0], left_came)
    left_x = lax.ppermute(left_sent, "tp", X_SWAP)
    gain_sum = sum_gain(gain_kept, left_x, gains)
    gain_sum = gain_sum + lax.ppermute(gain_sum, "seq", CORE_SWAP)
    out_far = sum_slot(3, out_own, out_came, [gain_sum])
    out_terms.append(lax.ppermute(out_far, "seq", y_shift(2)))
    gain_grad = gain_sum
    for k in STEPS[1:]:
        gain_grad = gain_grad + lax.ppermute(gain_sum, "seq", y_shift(k))
    shares = (normed_full, chunks, grads)
    qkv_sent = weight_shares(0, *shares, bf16)
    right_kept, *right_sends = sum_x(
        right[0], right_x, [left_sent]
    )
    right_came = [lax.ppermute(v, "tp", z_shift(-k)) for v, k in zip(right_sends, STEPS[1:])]
    tokens_grad = token_rows(
        x_rows, grad_rows, gains, inv, (left_kept, left_x), (right_kept, *right_came)
    )

    qkv_mine = weight_shares(1, *shares, f32, [qkv_sent] + out_terms[:2])
    qkv_share = qkv_mine + lax.ppermute(qkv_sent, "seq", CORE_SWAP).astype(f32)
    proj_kept, proj_sent = sum_z(proj[0], proj_came, right_came[:1])
    proj_x = lax.ppermute(proj_sent, "tp", X_SWAP)
    layer_out = layer_rows(x_rows, proj_kept, proj_x)
    out_share = sum_rest(out_kept, out_terms, right_came[:1])
    return (
        layer_out[None, None],
        tokens_grad[None, None],
        gain_grad,
        jnp.transpose(qkv_share, (1, 0, 2))[None],
        out_share[None],
    )


def solution(mesh):
    in_specs = (
        P("grp", "seq", "tp", None),
        P("seq", None),
        P("seq", None),
        P("grp", None),
        P("grp", None, None, "tp"),
        P("grp", None, "tp"),
        P("grp", "seq", "tp", None),
    )
    out_specs = (
        P("grp", "seq", "tp", None),
        P("grp", "seq", "tp", None),
        P("grp", None),
        P("grp", "seq", None, "tp"),
        P("grp", "seq", "tp"),
    )
    return jax.shard_map(
        per_device, mesh=mesh, in_specs=in_specs, out_specs=out_specs, check_vma=False
    )
```

```python
import functools

import jax
import jax.numpy as jnp
from jax import lax
from jax.experimental import pallas as pl
from jax.experimental.pallas import tpu as pltpu
from jax.sharding import PartitionSpec as P

HS = 128
LI = 128
HEADS = 4
SLOTS = 256
ROWS = 32
WIDTH = 4096
HALF = 2048
COLS = 512
FAR = 1073741824
f32 = jnp.float32
bf16 = jnp.bfloat16
MIB = 1024 * 1024

STEPS = (0, 1, 3, 2)


def z_shift(k):
    return [(i, (i // 4) * 4 + (i + k) % 4) for i in range(8)]


X_SWAP = [(i, i ^ 4) for i in range(8)]


def y_shift(k):
    return [(i, (i + 2 * k) % 8) for i in range(8)]


CORE_SWAP = [(i, i ^ 1) for i in range(8)]
GRP_SWAP = [(0, 1), (1, 0)]


def sds(shape, dtype):
    return jax.ShapeDtypeStruct(shape, dtype)


def call(kernel, out_shape, vmem, flops=0, nbytes=0, **kwargs):
    return pl.pallas_call(
        kernel,
        out_shape=out_shape,
        compiler_params=pltpu.CompilerParams(vmem_limit_bytes=vmem * MIB),
        cost_estimate=pl.CostEstimate(flops=flops, bytes_accessed=nbytes, transcendentals=0),
        **kwargs,
    )


def whole(shape):
    return pl.BlockSpec(shape, lambda *_: (0,) * len(shape))


SMEM = pl.BlockSpec(memory_space=pltpu.SMEM)
VMEM = pl.BlockSpec(memory_space=pltpu.VMEM)
ANY = pl.BlockSpec(memory_space=pl.ANY)
HBM = pl.BlockSpec(memory_space=pltpu.HBM)


def dot(left, right):
    return jnp.dot(left, right, preferred_element_type=f32)


def dot_rows(left, right):
    return lax.dot_general(left, right, (((1,), (1,)), ((), ())), preferred_element_type=f32)


def dot_tokens(left, right):
    return lax.dot_general(left, right, (((0,), (0,)), ((), ())), preferred_element_type=f32)


def where_am_i():
    tp, seq = lax.axis_index("tp"), lax.axis_index("seq")
    return tp >> 2, tp & 3, seq >> 1, seq & 1, lax.axis_index("grp")


def valid_rows():
    used = jnp.logical_or(lax.axis_index("grp") == 0, lax.axis_index("tp") * ROWS < LI)
    return jnp.where(used, 1.0, 0.0).astype(f32)


def load(sources, targets, sems):
    copies = [
        pltpu.make_async_copy(source, target, sems.at[i])
        for i, (source, target) in enumerate(zip(sources, targets))
    ]
    for copy in copies:
        copy.start()
    return copies


KCUT = 1024
KCUTS = WIDTH // KCUT


def dot_loaded(full, buffer, copies):
    total = None
    for i, copy in enumerate(copies):
        copy.wait()
        cut = slice(i * KCUT, (i + 1) * KCUT)
        part = dot(full[:, cut], buffer[cut])
        total = part if total is None else total + part
    return total


def k_cuts(ref):
    return [ref.at[pl.ds(i * KCUT, KCUT)] for i in range(KCUTS)]


def norm_kernel(x, gain, n_left, n_right, inv):
    x_float = x[...].astype(f32)
    scale = lax.rsqrt(jnp.mean(x_float * x_float, axis=1, keepdims=True) + 1e-05)
    normed = (x_float * scale * gain[...].astype(f32)).astype(bf16)
    n_left[...] = normed[:, :HALF]
    n_right[...] = normed[:, HALF:]
    inv[...] = jnp.broadcast_to(scale, (ROWS, 128))


def norm_rows(x, gain):
    part = sds((ROWS, HALF), bf16)
    return call(
        norm_kernel,
        [part, part, sds((ROWS, 128), f32)],
        vmem=4,
        nbytes=2 * ROWS * WIDTH * 2,
        in_specs=[VMEM] * 2,
        name="norm_rows",
    )(x, gain)


def grad_kernel(cot, *refs):
    refs[-1][...] = (cot[...].astype(f32) * valid_rows()).astype(bf16)


def grad_rows_of(cot, after):
    return call(
        grad_kernel,
        sds((ROWS, WIDTH), bf16),
        vmem=4,
        nbytes=2 * ROWS * WIDTH * 2,
        in_specs=[VMEM] + [ANY] * len(after),
        out_specs=VMEM,
        name="grad_rows",
    )(cot, *after)


def pair_kernel(own, other, *refs):
    refs[-1][0] = own[...]
    refs[-1][1] = other[...]


def pair_of(own, other, after):
    return call(
        pair_kernel,
        sds((2,) + own.shape, own.dtype),
        vmem=4,
        nbytes=own.size * 8,
        in_specs=[VMEM] * 2 + [ANY] * len(after),
        out_specs=VMEM,
        name="pair",
    )(own, other, *after)


def gather_blocks(left, right):
    right_pair = jnp.stack([right, lax.ppermute(right, "tp", X_SWAP)])
    left_four = [left] + [lax.ppermute(left, "tp", z_shift(k)) for k in STEPS[1:]]
    right_four = [right_pair] + [lax.ppermute(right_pair, "tp", z_shift(k)) for k in STEPS[1:]]
    left_own = jnp.stack(left_four)
    left_other = lax.ppermute(left_own, "tp", X_SWAP)
    return [left_own, left_other] + right_four


def place_pieces(pieces, whole_ref):
    left_own, left_other = pieces[:2]
    for slot in range(4):
        rows = pl.ds(slot * ROWS, ROWS)
        other = pl.ds((4 + slot) * ROWS, ROWS)
        whole_ref[rows, :HALF] = left_own[slot]
        whole_ref[other, :HALF] = left_other[slot]
        whole_ref[rows, HALF:] = pieces[2 + slot][0]
        whole_ref[other, HALF:] = pieces[2 + slot][1]


PIECE_SHAPES = [(4, ROWS, HALF)] * 2 + [(2, ROWS, HALF)] * 4


def sum_z_kernel(own, c1, c2, c3, *refs):
    kept, sent = refs[-2:]
    total = own[...].astype(f32)
    for came in (c1, c2, c3):
        total = total + came[...].astype(f32)
    kept[...] = total[0]
    sent[...] = total[1].astype(bf16)


def sum_z(own, came, after=()):
    shape = own.shape[1:]
    return call(
        sum_z_kernel,
        [sds(shape, f32), sds(shape, bf16)],
        vmem=6,
        nbytes=11 * shape[0] * shape[1] * 2,
        in_specs=[VMEM] * 4 + [ANY] * len(after),
        out_specs=[VMEM] * 2,
        name="sum_z",
    )(own, *came, *after)


def sum_left_kernel(own, c1, c2, *refs):
    kept, sent, gain = refs[-3:]
    for part in range(2):
        total = own[part].astype(f32)
        for came in (c1, c2):
            total = total + came[part].astype(f32)
        kept[pl.ds(part * 16, 16)] = total
        total = own[2 + part].astype(f32)
        for came in (c1, c2):
            total = total + came[2 + part].astype(f32)
        sent[part] = total.astype(bf16)
    left, right = gain_from(own[4])
    for came in (c1, c2):
        more_left, more_right = gain_from(came[4])
        left, right = left + more_left, right + more_right
    sent[2] = gain_rows_of(left, right)
    gain[0:1] = left
    gain[1:2] = right


def sum_left(own, came, after=()):
    return call(
        sum_left_kernel,
        [sds((ROWS, HALF), f32), sds((3, 16, HALF), bf16), sds((2, HALF), f32)],
        vmem=4,
        nbytes=11 * ROWS * HALF * 2,
        in_specs=[VMEM] * 3 + [ANY] * len(after),
        out_specs=[VMEM] * 3,
        name="sum_left",
    )(own, *came, *after)


def sum_gain_kernel(own, came, gain, out):
    left, right = gain_from(came[2])
    out[:, :HALF] = (own[0:1] + left) / gain[:, :HALF].astype(f32)
    out[:, HALF:] = (own[1:2] + right) / gain[:, HALF:].astype(f32)


def sum_gain(own, came, gain):
    return call(
        sum_gain_kernel,
        sds((1, WIDTH), f32),
        vmem=2,
        nbytes=10 * WIDTH * 2,
        in_specs=[VMEM] * 3,
        out_specs=VMEM,
        name="sum_gain",
    )(own, came, gain)


def pass_left_kernel(back, forth, far_a, far_b, *refs):
    out_back, out_forth = refs[-2:]
    out_forth[...] = forth[...]
    out_back[...] = back[...]
    for part in range(2):
        out_forth[part] = (forth[part].astype(f32) + far_a[part].astype(f32)).astype(bf16)
        total = back[2 + part].astype(f32) + far_b[part].astype(f32)
        out_back[2 + part] = total.astype(bf16)
    left, right = gain_from(forth[4])
    more_left, more_right = gain_from(far_a[2])
    out_forth[4] = gain_rows_of(left + more_left, right + more_right)


def pass_left(back, forth, far_a, far_b, after=()):
    return call(
        pass_left_kernel,
        [sds(back.shape, bf16)] * 2,
        vmem=6,
        nbytes=6 * back.size * 2,
        in_specs=[VMEM] * 4 + [ANY] * len(after),
        out_specs=[VMEM] * 2,
        name="pass_left",
    )(back, forth, far_a, far_b, *after)


def pass_out_kernel(back, forth, far_a, far_b, *refs):
    out_back, out_forth = refs[-2:]
    half = COLS // 2
    out_forth[half:] = forth[half:]
    out_forth[:half] = (forth[:half].astype(f32) + far_a[...].astype(f32)).astype(bf16)
    out_back[:half] = back[:half]
    out_back[half:] = (back[half:].astype(f32) + far_b[...].astype(f32)).astype(bf16)


def pass_out(back, forth, far_a, far_b, after=()):
    return call(
        pass_out_kernel,
        [sds(back.shape, bf16)] * 2,
        vmem=6,
        nbytes=6 * back.size * 2,
        in_specs=[VMEM] * 4 + [ANY] * len(after),
        out_specs=[VMEM] * 2,
        name="pass_out",
    )(back, forth, far_a, far_b, *after)


def sum_out_kernel(own, came, *refs):
    kept, back, forth, far_a, far_b = refs[-5:]
    half = COLS // 2

    def total(slot, rows=slice(None)):
        return own[slot, rows].astype(f32) + came[slot, rows].astype(f32)

    kept[...] = total(0)
    back[...] = total(1).astype(bf16)
    forth[...] = total(2).astype(bf16)
    far_a[...] = total(3, slice(0, half)).astype(bf16)
    far_b[...] = total(3, slice(half, COLS)).astype(bf16)


def sum_out(own, came, after=()):
    whole_share, half_share = sds((COLS, COLS), bf16), sds((COLS // 2, COLS), bf16)
    return call(
        sum_out_kernel,
        [sds((COLS, COLS), f32), whole_share, whole_share, half_share, half_share],
        vmem=12,
        nbytes=own.size * 6,
        in_specs=[VMEM] * 2 + [ANY] * len(after),
        out_specs=[VMEM] * 5,
        name="sum_out",
    )(own, came, *after)


def sum_x_kernel(waits, own, came, *refs):
    kept, sends = refs[waits], refs[waits + 1:]
    kept[...] = own[0].astype(f32) + came[0].astype(f32)
    for slot, sent in enumerate(sends, 1):
        sent[...] = (own[slot].astype(f32) + came[slot].astype(f32)).astype(bf16)


def sum_x(own, came, after=(), sends=3):
    shape = own.shape[1:]
    return call(
        functools.partial(sum_x_kernel, len(after)),
        [sds(shape, f32)] + [sds(shape, bf16)] * sends,
        vmem=12,
        nbytes=13 * shape[0] * shape[1] * 2,
        in_specs=[VMEM] * 2 + [ANY] * len(after),
        out_specs=[VMEM] * (1 + sends),
        name="sum_x",
    )(own, came, *after)


def halves_kernel(back, forth, *refs):
    half = SLOTS // 2
    refs[-2][...] = back[:, :half]
    refs[-1][...] = forth[:, half:]


def halves(back, forth, after):
    shape = (3, SLOTS // 2, COLS)
    return call(
        halves_kernel,
        [sds(shape, bf16)] * 2,
        vmem=6,
        nbytes=8 * back.size,
        in_specs=[VMEM] * 2 + [ANY] * len(after),
        out_specs=[VMEM] * 2,
        name="halves",
    )(back, forth, *after)


def late_kernel(count, *refs):
    for i in range(count):
        refs[i - count][...] = refs[i][...]


def late(arrays, after):
    count = len(arrays)
    return call(
        functools.partial(late_kernel, count),
        [sds(v.shape, v.dtype) for v in arrays],
        vmem=10,
        nbytes=sum(v.size * 4 for v in arrays),
        in_specs=[VMEM] * count + [ANY] * len(after),
        out_specs=[VMEM] * count,
        name="late",
    )(*arrays, *after)


def sum_rest_kernel(kept, c1, c2, *refs):
    total = kept[...]
    for came in (c1, c2):
        total = total + came[...].astype(f32)
    refs[-1][...] = total


def sum_rest(kept, came, after=()):
    return call(
        sum_rest_kernel,
        sds(kept.shape, f32),
        vmem=6,
        nbytes=14 * kept.size,
        in_specs=[VMEM] * 3 + [ANY] * len(after),
        out_specs=VMEM,
        name="sum_rest",
    )(kept, *came, *after)


def sum_keys_kernel(q_grad, own, came, *refs):
    out = refs[-1]
    out[0] = q_grad[...]
    out[1:] = (own[...] + came[...].astype(f32)).astype(bf16)


def sum_keys(q_grad, own, came, after=()):
    return call(
        sum_keys_kernel,
        sds((3, SLOTS, COLS), bf16),
        vmem=8,
        nbytes=10 * came.size,
        in_specs=[VMEM] * 3 + [ANY] * len(after),
        out_specs=VMEM,
        name="sum_keys",
    )(q_grad, own, came, *after)


def rows_kernel(x, grad, gain, inv, l_kept, l_came, r_kept, r1, r2, r3, *refs):
    out = refs[-1]
    left = l_kept[...] + l_came[0:2].reshape(ROWS, HALF).astype(f32)
    right = r_kept[...]
    for came in (r1, r2, r3):
        right = right + came[...].astype(f32)
    scale = inv[:, :1]
    halves = []
    dots = jnp.zeros((ROWS, 1), f32)
    for part, cols in ((left, slice(0, HALF)), (right, slice(HALF, WIDTH))):
        scaled = gain[:, cols].astype(f32) * part
        rows = x[:, cols].astype(f32)
        dots = dots + jnp.sum(scaled * rows, axis=1, keepdims=True)
        halves.append((scaled, rows, cols))
    mean = dots * (1.0 / WIDTH)
    for scaled, rows, cols in halves:
        total = grad[:, cols].astype(f32) + scale * scaled - rows * (scale * scale * scale) * mean
        out[:, cols] = total.astype(bf16)


def token_rows(x, grad, gain, inv, left, right, after=()):
    return call(
        rows_kernel,
        sds((ROWS, WIDTH), bf16),
        vmem=4,
        nbytes=6 * ROWS * WIDTH * 2,
        in_specs=[VMEM] * 10 + [ANY] * len(after),
        out_specs=VMEM,
        name="token_rows",
    )(x, grad, gain, inv, *left, *right, *after)


def key_value_kernel(*refs):
    pieces, weight = refs[:6], refs[6]
    full, out, buffer, sems = refs[-4:]
    copies = [
        load(k_cuts(weight.at[part + 1]), k_cuts(buffer.at[part]), sems.at[part])
        for part in range(2)
    ]
    place_pieces(pieces, full)
    for part in range(2):
        out[part] = dot_loaded(full, buffer.at[part], copies[part]).astype(bf16)


def key_value(pieces, weights, after):
    return call(
        key_value_kernel,
        [sds((SLOTS, WIDTH), bf16), sds((2, SLOTS, COLS), bf16)],
        vmem=20,
        flops=4 * SLOTS * WIDTH * COLS,
        nbytes=2 * WIDTH * COLS * 2 + 2 * SLOTS * WIDTH * 2,
        in_specs=[VMEM] * 6 + [HBM] + [ANY] * len(after),
        out_specs=[VMEM] * 2,
        scratch_shapes=[
            pltpu.VMEM((2, WIDTH, COLS), bf16),
            pltpu.SemaphoreType.DMA((2, KCUTS)),
        ],
        name="key_value",
    )(*pieces, weights, *after)


def query_kernel(full, weight, *refs):
    out, buffer, sems = refs[-3:]
    copies = load(k_cuts(weight.at[0]), k_cuts(buffer), sems)
    out[...] = dot_loaded(full, buffer, copies).astype(bf16)


DOT_SCRATCH = [pltpu.VMEM((WIDTH, COLS), bf16), pltpu.SemaphoreType.DMA((KCUTS,))]


def query_of(full, weights, after):
    return call(
        query_kernel,
        sds((SLOTS, COLS), bf16),
        vmem=12,
        flops=2 * SLOTS * WIDTH * COLS,
        nbytes=WIDTH * COLS * 2 + SLOTS * WIDTH * 2,
        in_specs=[VMEM, HBM] + [ANY] * len(after),
        out_specs=VMEM,
        scratch_shapes=DOT_SCRATCH,
        name="query",
    )(full, weights, *after)


def grad_mixed_kernel(p0, p1, p2, p3, weight, *refs):
    full, out, buffer, sems = refs[-4:]
    copies = load(k_cuts(weight.at[0]), k_cuts(buffer), sems)
    for slot, pair in enumerate((p0, p1, p2, p3)):
        full[pl.ds(slot * ROWS, ROWS)] = pair[0]
        full[pl.ds((4 + slot) * ROWS, ROWS)] = pair[1]
    out[...] = dot_loaded(full, buffer, copies).astype(bf16)


def grad_mixed_of(pairs, weights, after):
    return call(
        grad_mixed_kernel,
        [sds((SLOTS, WIDTH), bf16), sds((SLOTS, COLS), bf16)],
        vmem=16,
        flops=2 * SLOTS * WIDTH * COLS,
        nbytes=WIDTH * COLS * 2 + 2 * SLOTS * WIDTH * 2,
        in_specs=[VMEM] * 4 + [HBM] + [ANY] * len(after),
        out_specs=[VMEM] * 2,
        scratch_shapes=DOT_SCRATCH,
        name="grad_mixed",
    )(*pairs, weights, *after)


def gain_rows_of(left, right):
    row = lax.broadcasted_iota(jnp.int32, (16, left.shape[1]), 0)
    rows = jnp.zeros((16, left.shape[1]), f32)
    for first, part in ((0, left), (2, right)):
        high = part.astype(bf16).astype(f32)
        rows = jnp.where(row == first, high, rows)
        rows = jnp.where(row == first + 1, part - high, rows)
    return rows.astype(bf16)


def gain_from(rows):
    rows = rows.astype(f32)
    return rows[0:1] + rows[1:2], rows[2:3] + rows[3:4]


FCUT = 512
FCUTS = HALF // FCUT


def back_products(grads, weight, first, normed, buffer, sems):
    copies = [
        load(
            [weight.at[part, pl.ds(first + cut * FCUT, FCUT)] for part in range(3)],
            [buffer.at[part, pl.ds(cut * FCUT, FCUT)] for part in range(3)],
            sems.at[cut],
        )
        for cut in range(FCUTS)
    ]
    for cut in range(FCUTS):
        for copy in copies[cut]:
            copy.wait()
        rows = slice(cut * FCUT, (cut + 1) * FCUT)
        total = dot_rows(grads[0], buffer[0, rows])
        for part in range(1, 3):
            total = total + dot_rows(grads[part], buffer[part, rows])
        rounded = total.astype(bf16)
        terms = normed[:, first + cut * FCUT:first + (cut + 1) * FCUT].astype(f32)
        gain = jnp.sum(rounded.astype(f32) * terms, axis=0, keepdims=True)
        yield rows, rounded, gain


def back_right_kernel(waits, grads, weight, normed, *refs):
    own, sent, gain, buffer, sems = refs[waits:]
    for cols, rounded, terms in back_products(
        grads, weight, HALF, normed, buffer, sems
    ):
        gain[:, cols] = terms
        for xbit, out in enumerate((own, sent)):
            for slot in range(4):
                start = (xbit * 4 + slot) * ROWS
                out[slot, :, cols] = rounded[start:start + ROWS]


def back_left_kernel(waits, grads, weight, normed, gain_right, *refs):
    outs, far, buffer, sems = refs[waits:waits + 3], refs[-4:-2], refs[-2], refs[-1]
    for cols, rounded, terms in back_products(
        grads, weight, 0, normed, buffer, sems
    ):
        gains = gain_rows_of(terms, gain_right[:, cols])
        for slot, out in enumerate(outs):
            for xbit in range(2):
                start = (xbit * 4 + slot) * ROWS
                out[2 * xbit, :, cols] = rounded[start:start + 16]
                out[2 * xbit + 1, :, cols] = rounded[start + 16:start + ROWS]
            out[4, :, cols] = gains
        for xbit, out in enumerate(far):
            start = (xbit * 4 + 3) * ROWS
            out[0, :, cols] = rounded[start:start + 16]
            out[1, :, cols] = rounded[start + 16:start + ROWS]
        far[0][2, :, cols] = gains


def back_dot(kernel, grads, weights, normed, extra, out_shape, after, name):
    return call(
        functools.partial(kernel, len(after)),
        out_shape,
        vmem=20,
        flops=2 * 3 * SLOTS * HALF * COLS,
        nbytes=3 * HALF * COLS * 2 + 2 * SLOTS * HALF * 2,
        in_specs=[VMEM, HBM, VMEM] + [VMEM] * len(extra) + [ANY] * len(after),
        out_specs=[VMEM] * len(out_shape),
        scratch_shapes=[
            pltpu.VMEM((3, HALF, COLS), bf16),
            pltpu.SemaphoreType.DMA((FCUTS, 3)),
        ],
        name=name,
    )(grads, weights, normed, *extra, *after)


def back_right(grads, weights, normed, after=()):
    out = [sds((4, ROWS, HALF), bf16)] * 2 + [sds((1, HALF), f32)]
    return back_dot(back_right_kernel, grads, weights, normed, [], out, after, "back_right")


def back_left(grads, weights, normed, gain_right, after=()):
    out = [sds((5, 16, HALF), bf16)] * 3
    out += [sds((3, 16, HALF), bf16), sds((2, 16, HALF), bf16)]
    return back_dot(back_left_kernel, grads, weights, normed, [gain_right], out, after, "back_left")


def proj_kernel(left, weight, *refs):
    outs, buffer, sems = refs[-6:-2], refs[-2], refs[-1]
    copies = load(k_cuts(weight.at[0]), k_cuts(buffer), sems)
    for cut, copy in enumerate(copies):
        copy.wait()
        cols = slice(cut * KCUT, (cut + 1) * KCUT)
        rounded = dot_rows(left[...], buffer[cols]).astype(bf16)
        for slot in range(4):
            for xbit in range(2):
                start = (xbit * 4 + slot) * ROWS
                outs[slot][xbit, :, cols] = rounded[start:start + ROWS]


def proj_parts(mixed, weights, after):
    return call(
        proj_kernel,
        [sds((2, ROWS, WIDTH), bf16)] * 4,
        vmem=14,
        flops=2 * SLOTS * WIDTH * COLS,
        nbytes=WIDTH * COLS * 2 + SLOTS * WIDTH * 2,
        in_specs=[VMEM, HBM] + [ANY] * len(after),
        out_specs=[VMEM] * 4,
        scratch_shapes=DOT_SCRATCH,
        name="proj_parts",
    )(mixed, weights, *after)


def slot_of(row, x_index, z_index):
    block = row // ROWS
    xbit = block // 4
    slot = block - xbit * 4
    back = jnp.where(slot == 2, 3, jnp.where(slot == 3, 2, slot))
    x_from = jnp.where(xbit == 0, x_index, 1 - x_index)
    z_from = z_index - back
    z_from = jnp.where(z_from < 0, z_from + 4, z_from)
    return (x_from * 4 + z_from) * ROWS + (row - block * ROWS)


def places(gaps, runs, rows, is_text):
    x_index, z_index = where_am_i()[:2]
    slot = slot_of(rows, x_index, z_index)
    text = slot
    end = jnp.int32(0)
    for run in range(4):
        end = end + gaps[0, run]
        text = text + jnp.where(slot >= end, runs[0, run], 0)
    image = slot + gaps[0, 0]
    end = jnp.int32(0)
    for run in range(3):
        end = end + runs[0, run]
        image = image + jnp.where(slot >= end, gaps[0, run + 1], 0)
    image = jnp.where(slot < LI, image, FAR)
    return jnp.where(is_text, text, image)


def admitted(gaps, runs):
    group = lax.axis_index("grp")
    rows = lax.broadcasted_iota(jnp.int32, (SLOTS, 1), 0)
    query = places(gaps, runs, rows, group == 0)
    key_row = lax.broadcasted_iota(jnp.int32, (1, SLOTS), 1)
    own = places(gaps, runs, key_row, group == 0)
    other = places(gaps, runs, key_row, group != 0)
    return own <= query, other <= query


def head_attn(query, own_key, other_key, own_ok, other_ok):
    scale = HS ** (-0.5)
    own = jnp.where(own_ok, dot_rows(query, own_key) * scale, -1e30)
    other = jnp.where(other_ok, dot_rows(query, other_key) * scale, -1e30)
    row_max = jnp.maximum(
        jnp.max(own, axis=1, keepdims=True), jnp.max(other, axis=1, keepdims=True)
    )
    own = jnp.exp(own - row_max)
    other = jnp.exp(other - row_max)
    row_sum = jnp.sum(own, axis=1, keepdims=True) + jnp.sum(other, axis=1, keepdims=True)
    share = 1.0 / row_sum
    return own * share, other * share


def forward_kernel(gaps, runs, query, own_kv, other_kv, *refs):
    mixed = refs[-1]
    own_ok, other_ok = admitted(gaps, runs)
    for head in range(HEADS):
        cols = slice(head * HS, (head + 1) * HS)
        own, other = head_attn(
            query[:, cols], own_kv[0, :, cols], other_kv[0, :, cols], own_ok, other_ok
        )
        total = dot(own.astype(bf16), own_kv[1, :, cols])
        total = total + dot(other.astype(bf16), other_kv[1, :, cols])
        mixed[:, cols] = total.astype(bf16)


def backward_kernel(gaps, runs, query, own_kv, other_kv, mixed, grad, *refs):
    q_grad, own_grad, other_grad = refs[-3:]
    scale = HS ** (-0.5)
    own_ok, other_ok = admitted(gaps, runs)
    for head in range(HEADS):
        cols = slice(head * HS, (head + 1) * HS)
        q, g = query[:, cols], grad[:, cols]
        row_dot = jnp.sum(g.astype(f32) * mixed[:, cols].astype(f32), axis=1, keepdims=True)
        attns = head_attn(q, own_kv[0, :, cols], other_kv[0, :, cols], own_ok, other_ok)
        dq = None
        for attn, kv, kv_grad in zip(attns, (own_kv, other_kv), (own_grad, other_grad)):
            value_grad = dot_tokens(attn.astype(bf16), g)
            weight_grad = dot_rows(g, kv[1, :, cols])
            score_grad = (attn * (weight_grad - row_dot)).astype(bf16)
            part = dot(score_grad, kv[0, :, cols])
            dq = part if dq is None else dq + part
            key_grad = dot_tokens(score_grad, q) * scale
            kv_grad[0, :, cols] = key_grad.astype(kv_grad.dtype)
            kv_grad[1, :, cols] = value_grad.astype(kv_grad.dtype)
        q_grad[:, cols] = (dq * scale).astype(bf16)


ATTN_FLOPS = 2 * HEADS * SLOTS * 2 * SLOTS * HS


def attend_forward(spans, query, own_kv, other_kv, after):
    return call(
        forward_kernel,
        sds((SLOTS, COLS), bf16),
        vmem=10,
        flops=4 * ATTN_FLOPS,
        nbytes=6 * SLOTS * COLS * 2,
        in_specs=[SMEM] * 2 + [VMEM] * 3 + [ANY] * len(after),
        out_specs=VMEM,
        name="attend_forward",
    )(*spans, query, own_kv, other_kv, *after)


def attend_backward(spans, query, own_kv, other_kv, mixed, grad, after):
    kv = (2, SLOTS, COLS)
    return call(
        backward_kernel,
        [sds((SLOTS, COLS), bf16), sds(kv, f32), sds(kv, bf16)],
        vmem=14,
        flops=8 * ATTN_FLOPS,
        nbytes=12 * SLOTS * COLS * 2,
        in_specs=[SMEM] * 2 + [VMEM] * 5 + [ANY] * len(after),
        out_specs=[VMEM] * 3,
        name="attend_backward",
    )(*spans, query, own_kv, other_kv, mixed, grad, *after)


def out_kernel(grad, mixed, *refs):
    own, sent = refs[-2:]
    y_index, core = where_am_i()[2:4]
    for i in range(8):
        column = ((y_index - STEPS[i % 4]) & 3) * 2 + (1 - core if i < 4 else core)
        start = pl.multiple_of(column * COLS, COLS)
        share = dot_tokens(grad[:, pl.ds(start, COLS)], mixed[...]).astype(bf16)
        if i < 4:
            sent[i] = share
        else:
            own[i - 4] = share


def out_weight_parts(grad_full, mixed, after):
    return call(
        out_kernel,
        [sds((4, COLS, COLS), bf16)] * 2,
        vmem=12,
        flops=2 * SLOTS * WIDTH * COLS,
        nbytes=SLOTS * WIDTH * 2 + WIDTH * COLS * 2,
        in_specs=[VMEM] * 2 + [ANY] * len(after),
        out_specs=[VMEM] * 2,
        name="out_weight_parts",
    )(grad_full, mixed, *after)


def share_kernel(which, full, c1, c2, c3, g0, g1, g2, g3, g4, *refs):
    out, lefts = refs[-2:]
    y_index, core = where_am_i()[2:4]
    column = core if which else 1 - core
    start = pl.multiple_of((y_index * 2 + column) * COLS, COLS)
    lefts[0] = full[:, pl.ds(start, COLS)].T
    start = pl.multiple_of(column * COLS, COLS)
    for k, came in enumerate((c1, c2, c3), 1):
        lefts[k] = came[:, pl.ds(start, COLS)].T
    for part in range(3):
        total = dot(lefts[0], g0[part])
        for k, grad in enumerate((g1, g2), 1):
            total = total + dot(lefts[k], grad[part])
        total = total + dot(lefts[3, :, :SLOTS // 2], g3[part])
        total = total + dot(lefts[3, :, SLOTS // 2:], g4[part])
        out[part] = total.astype(out.dtype)


def weight_shares(which, full, came, grads, dtype, after=()):
    return call(
        functools.partial(share_kernel, which),
        sds((3, COLS, COLS), dtype),
        vmem=20,
        flops=3 * 4 * 2 * SLOTS * COLS * COLS,
        nbytes=16 * SLOTS * COLS * 2 + 3 * COLS * COLS * 4,
        in_specs=[VMEM] * 9 + [ANY] * len(after),
        out_specs=VMEM,
        scratch_shapes=[pltpu.VMEM((4, COLS, SLOTS), bf16)],
        name="weight_shares",
    )(full, *came, *grads, *after)


def chunk_kernel(full, *outs):
    y_index = where_am_i()[2]
    for k, out in zip(STEPS[1:], outs):
        start = pl.multiple_of(((y_index + k) & 3) * 1024, 1024)
        out[...] = full[:, pl.ds(start, 1024)]


def chunks_over_y(full):
    sends = call(
        chunk_kernel,
        [sds((SLOTS, 1024), bf16)] * 3,
        vmem=6,
        nbytes=6 * SLOTS * 1024 * 2,
        in_specs=[VMEM],
        out_specs=[VMEM] * 3,
        name="chunks",
    )(full)
    return [lax.ppermute(sent, "seq", y_shift(k)) for sent, k in zip(sends, STEPS[1:])]


def layer_kernel(x, kept, came, *refs):
    total = x[...].astype(f32) + (kept[...] + came[...].astype(f32))
    refs[-1][...] = (total * valid_rows()).astype(bf16)


def layer_rows(x, kept, came, after=()):
    return call(
        layer_kernel,
        sds((ROWS, WIDTH), bf16),
        vmem=4,
        nbytes=5 * ROWS * WIDTH * 2,
        in_specs=[VMEM] * 3 + [ANY] * len(after),
        out_specs=VMEM,
        name="layer_rows",
    )(x, kept, came, *after)


def per_device(tokens, text_gaps, image_runs, gains, w_qkv, w_out, cotangent):
    x_rows = tokens[0, 0]
    w_parts = jnp.transpose(w_qkv[0], (1, 0, 2))
    spans = (text_gaps, image_runs)

    n_left, n_right, inv = norm_rows(x_rows, gains)
    pieces = gather_blocks(n_left, n_right)
    grad_rows = grad_rows_of(cotangent[0, 0], pieces[2:3])
    grad_other = lax.ppermute(grad_rows, "tp", X_SWAP)
    grad_pair = pair_of(grad_rows, grad_other, pieces[3:4])
    grad_pairs = [grad_pair] + [lax.ppermute(grad_pair, "tp", z_shift(k)) for k in STEPS[1:]]
    normed_full, own_kv = key_value(pieces, w_parts, [grad_pair])
    other_kv = lax.ppermute(own_kv, "grp", GRP_SWAP)
    query = query_of(normed_full, w_parts, grad_pairs[1:3])
    chunks = chunks_over_y(normed_full)

    mixed = attend_forward(spans, query, own_kv, other_kv, [])
    proj = proj_parts(mixed, w_out, [])
    grad_full, grad_mixed = grad_mixed_of(grad_pairs, w_out, [proj[0]] + chunks[:2])
    q_grad, own_part, other_part = attend_backward(
        spans, query, own_kv, other_kv, mixed, grad_mixed, []
    )
    back = lax.ppermute(other_part, "grp", GRP_SWAP)
    sends = late(proj[1:3], [q_grad])
    proj_came = [lax.ppermute(v, "tp", z_shift(-k)) for v, k in zip(sends, (1, 3))]
    out_own, out_sent = out_weight_parts(grad_full, mixed, [q_grad])
    out_came = lax.ppermute(out_sent, "seq", CORE_SWAP)
    own_grads = sum_keys(q_grad, own_part, back, sends[:1])
    (far_sent,) = late(proj[3:], [own_grads])
    proj_came.append(lax.ppermute(far_sent, "tp", z_shift(2)))
    back_grads = lax.ppermute(own_grads, "seq", y_shift(1))
    next_grads = lax.ppermute(own_grads, "seq", y_shift(3))

    right = back_right(own_grads, w_parts, normed_full, [out_came] + chunks[2:])
    right_x = lax.ppermute(right[1], "tp", X_SWAP)
    left = back_left(own_grads, w_parts, normed_full, right[2], proj_came[:2])
    left_far_a = lax.ppermute(left[3], "tp", z_shift(1))
    left_far_b = lax.ppermute(left[4], "tp", z_shift(3))
    out_kept, *out_sends = sum_out(out_own, out_came, [left_far_a])
    out_far_a = lax.ppermute(out_sends[2], "seq", y_shift(1))
    out_far_b = lax.ppermute(out_sends[3], "seq", y_shift(3))
    left_back, left_forth = pass_left(
        left[1], left[2], left_far_a, left_far_b, [right_x]
    )
    left_came = [
        lax.ppermute(left_forth, "tp", z_shift(1)), lax.ppermute(left_back, "tp", z_shift(3))
    ]
    relayed = halves(back_grads, next_grads, [left_far_a, left_far_b, proj_came[2]])
    grads = [own_grads, back_grads, next_grads]
    grads += [lax.ppermute(v, "seq", y_shift(k)) for v, k in zip(relayed, (1, 3))]
    out_back, out_forth = pass_out(
        out_sends[0], out_sends[1], out_far_a, out_far_b, left_came[:1]
    )
    out_terms = [
        lax.ppermute(out_forth, "seq", y_shift(1)), lax.ppermute(out_back, "seq", y_shift(3))
    ]
    left_kept, left_sent, gain_kept = sum_left(left[0], left_came, [right_x])
    left_x = lax.ppermute(left_sent, "tp", X_SWAP)
    gain_sum = sum_gain(gain_kept, left_x, gains)
    gain_sum = gain_sum + lax.ppermute(gain_sum, "seq", CORE_SWAP)
    gain_grad = gain_sum
    for k in STEPS[1:]:
        gain_grad = gain_grad + lax.ppermute(gain_sum, "seq", y_shift(k))
    shares = (normed_full, chunks, grads)
    qkv_sent = weight_shares(0, *shares, bf16)
    right_kept, *right_sends = sum_x(
        right[0], right_x, [left_sent]
    )
    right_came = [lax.ppermute(v, "tp", z_shift(-k)) for v, k in zip(right_sends, STEPS[1:])]
    tokens_grad = token_rows(
        x_rows, grad_rows, gains, inv, (left_kept, left_x), (right_kept, *right_came)
    )

    qkv_mine = weight_shares(1, *shares, f32, [qkv_sent])
    qkv_share = qkv_mine + lax.ppermute(qkv_sent, "seq", CORE_SWAP).astype(f32)
    proj_kept, proj_sent = sum_z(proj[0], proj_came)
    proj_x = lax.ppermute(proj_sent, "tp", X_SWAP)
    layer_out = layer_rows(x_rows, proj_kept, proj_x)
    out_share = sum_rest(out_kept, out_terms, right_came[:1])
    return (
        layer_out[None, None],
        tokens_grad[None, None],
        gain_grad,
        jnp.transpose(qkv_share, (1, 0, 2))[None],
        out_share[None],
    )


def solution(mesh):
    in_specs = (
        P("grp", "seq", "tp", None),
        P("seq", None),
        P("seq", None),
        P("grp", None),
        P("grp", None, None, "tp"),
        P("grp", None, "tp"),
        P("grp", "seq", "tp", None),
    )
    out_specs = (
        P("grp", "seq", "tp", None),
        P("grp", "seq", "tp", None),
        P("grp", None),
        P("grp", "seq", None, "tp"),
        P("grp", "seq", "tp"),
    )
    return jax.shard_map(
        per_device, mesh=mesh, in_specs=in_specs, out_specs=out_specs, check_vma=False
    )
```

```python
import functools

import jax
import jax.numpy as jnp
from jax import lax
from jax.experimental import pallas as pl
from jax.experimental.pallas import tpu as pltpu
from jax.sharding import PartitionSpec as P

HS = 128
LI = 128
HEADS = 4
SLOTS = 256
ROWS = 32
WIDTH = 4096
HALF = 2048
COLS = 512
FAR = 1073741824
f32 = jnp.float32
bf16 = jnp.bfloat16
MIB = 1024 * 1024

STEPS = (0, 1, 3, 2)


def z_shift(k):
    return [(i, (i // 4) * 4 + (i + k) % 4) for i in range(8)]


X_SWAP = [(i, i ^ 4) for i in range(8)]


def y_shift(k):
    return [(i, (i + 2 * k) % 8) for i in range(8)]


CORE_SWAP = [(i, i ^ 1) for i in range(8)]
GRP_SWAP = [(0, 1), (1, 0)]


def sds(shape, dtype):
    return jax.ShapeDtypeStruct(shape, dtype)


def call(kernel, out_shape, vmem, flops=0, nbytes=0, **kwargs):
    return pl.pallas_call(
        kernel,
        out_shape=out_shape,
        compiler_params=pltpu.CompilerParams(vmem_limit_bytes=vmem * MIB),
        cost_estimate=pl.CostEstimate(flops=flops, bytes_accessed=nbytes, transcendentals=0),
        **kwargs,
    )


def whole(shape):
    return pl.BlockSpec(shape, lambda *_: (0,) * len(shape))


SMEM = pl.BlockSpec(memory_space=pltpu.SMEM)
VMEM = pl.BlockSpec(memory_space=pltpu.VMEM)
ANY = pl.BlockSpec(memory_space=pl.ANY)
HBM = pl.BlockSpec(memory_space=pltpu.HBM)


def dot(left, right):
    return jnp.dot(left, right, preferred_element_type=f32)


def dot_rows(left, right):
    return lax.dot_general(left, right, (((1,), (1,)), ((), ())), preferred_element_type=f32)


def dot_tokens(left, right):
    return lax.dot_general(left, right, (((0,), (0,)), ((), ())), preferred_element_type=f32)


def where_am_i():
    tp, seq = lax.axis_index("tp"), lax.axis_index("seq")
    return tp >> 2, tp & 3, seq >> 1, seq & 1, lax.axis_index("grp")


def valid_rows():
    used = jnp.logical_or(lax.axis_index("grp") == 0, lax.axis_index("tp") * ROWS < LI)
    return jnp.where(used, 1.0, 0.0).astype(f32)


def load(sources, targets, sems):
    copies = [
        pltpu.make_async_copy(source, target, sems.at[i])
        for i, (source, target) in enumerate(zip(sources, targets))
    ]
    for copy in copies:
        copy.start()
    return copies


KCUT = 1024
KCUTS = WIDTH // KCUT


def dot_loaded(full, buffer, copies):
    total = None
    for i, copy in enumerate(copies):
        copy.wait()
        cut = slice(i * KCUT, (i + 1) * KCUT)
        part = dot(full[:, cut], buffer[cut])
        total = part if total is None else total + part
    return total


def k_cuts(ref):
    return [ref.at[pl.ds(i * KCUT, KCUT)] for i in range(KCUTS)]


def touch_kernel(weight, pair, *refs):
    refs[-1][...] = pair[...]


def touch(pair, weight):
    return call(
        touch_kernel,
        sds(pair.shape, pair.dtype),
        vmem=4,
        nbytes=pair.size * 4,
        in_specs=[ANY, VMEM],
        out_specs=VMEM,
        name="touch",
    )(weight, pair)


def norm_kernel(x, gain, cot, n_left, n_right, grad, inv):
    x_float = x[...].astype(f32)
    scale = lax.rsqrt(jnp.mean(x_float * x_float, axis=1, keepdims=True) + 1e-05)
    normed = (x_float * scale * gain[...].astype(f32)).astype(bf16)
    n_left[...] = normed[:, :HALF]
    n_right[...] = normed[:, HALF:]
    grad[...] = (cot[...].astype(f32) * valid_rows()).astype(bf16)
    inv[...] = jnp.broadcast_to(scale, (ROWS, 128))


def norm_rows(x, gain, cot):
    part = sds((ROWS, HALF), bf16)
    return call(
        norm_kernel,
        [part, part, sds((ROWS, WIDTH), bf16), sds((ROWS, 128), f32)],
        vmem=4,
        nbytes=4 * ROWS * WIDTH * 2,
        in_specs=[VMEM] * 3,
        name="norm_rows",
    )(x, gain, cot)


def gather_blocks(left, right):
    right_pair = jnp.stack([right, lax.ppermute(right, "tp", X_SWAP)])
    left_four = [left] + [lax.ppermute(left, "tp", z_shift(k)) for k in STEPS[1:]]
    right_four = [right_pair] + [lax.ppermute(right_pair, "tp", z_shift(k)) for k in STEPS[1:]]
    left_own = jnp.stack(left_four)
    left_other = lax.ppermute(left_own, "tp", X_SWAP)
    return [left_own, left_other] + right_four


def place_pieces(pieces, whole_ref):
    left_own, left_other = pieces[:2]
    for slot in range(4):
        rows = pl.ds(slot * ROWS, ROWS)
        other = pl.ds((4 + slot) * ROWS, ROWS)
        whole_ref[rows, :HALF] = left_own[slot]
        whole_ref[other, :HALF] = left_other[slot]
        whole_ref[rows, HALF:] = pieces[2 + slot][0]
        whole_ref[other, HALF:] = pieces[2 + slot][1]


PIECE_SHAPES = [(4, ROWS, HALF)] * 2 + [(2, ROWS, HALF)] * 4


def sum_z_kernel(own, c1, c2, c3, *refs):
    kept, sent = refs[-2:]
    total = own[...].astype(f32)
    for came in (c1, c2, c3):
        total = total + came[...].astype(f32)
    kept[...] = total[0]
    sent[...] = total[1].astype(bf16)


def sum_z(own, came, after=()):
    shape = own.shape[1:]
    return call(
        sum_z_kernel,
        [sds(shape, f32), sds(shape, bf16)],
        vmem=6,
        nbytes=11 * shape[0] * shape[1] * 2,
        in_specs=[VMEM] * 4 + [ANY] * len(after),
        out_specs=[VMEM] * 2,
        name="sum_z",
    )(own, *came, *after)


def sum_left_kernel(own, c1, c2, *refs):
    kept, sent, gain = refs[-3:]
    for part in range(2):
        total = own[part].astype(f32)
        for came in (c1, c2):
            total = total + came[part].astype(f32)
        kept[pl.ds(part * 16, 16)] = total
        total = own[2 + part].astype(f32)
        for came in (c1, c2):
            total = total + came[2 + part].astype(f32)
        sent[part] = total.astype(bf16)
    left, right = gain_from(own[4])
    for came in (c1, c2):
        more_left, more_right = gain_from(came[4])
        left, right = left + more_left, right + more_right
    sent[2] = gain_rows_of(left, right)
    gain[0:1] = left
    gain[1:2] = right


def sum_left(own, came, after=()):
    return call(
        sum_left_kernel,
        [sds((ROWS, HALF), f32), sds((3, 16, HALF), bf16), sds((2, HALF), f32)],
        vmem=4,
        nbytes=11 * ROWS * HALF * 2,
        in_specs=[VMEM] * 3 + [ANY] * len(after),
        out_specs=[VMEM] * 3,
        name="sum_left",
    )(own, *came, *after)


def sum_gain_kernel(own, came, gain, out):
    left, right = gain_from(came[2])
    out[:, :HALF] = (own[0:1] + left) / gain[:, :HALF].astype(f32)
    out[:, HALF:] = (own[1:2] + right) / gain[:, HALF:].astype(f32)


def sum_gain(own, came, gain):
    return call(
        sum_gain_kernel,
        sds((1, WIDTH), f32),
        vmem=2,
        nbytes=10 * WIDTH * 2,
        in_specs=[VMEM] * 3,
        out_specs=VMEM,
        name="sum_gain",
    )(own, came, gain)


def pass_left_kernel(back, forth, far_a, far_b, *refs):
    out_back, out_forth = refs[-2:]
    out_forth[...] = forth[...]
    out_back[...] = back[...]
    for part in range(2):
        out_forth[part] = (forth[part].astype(f32) + far_a[part].astype(f32)).astype(bf16)
        total = back[2 + part].astype(f32) + far_b[part].astype(f32)
        out_back[2 + part] = total.astype(bf16)
    left, right = gain_from(forth[4])
    more_left, more_right = gain_from(far_a[2])
    out_forth[4] = gain_rows_of(left + more_left, right + more_right)


def pass_left(back, forth, far_a, far_b, after=()):
    return call(
        pass_left_kernel,
        [sds(back.shape, bf16)] * 2,
        vmem=6,
        nbytes=6 * back.size * 2,
        in_specs=[VMEM] * 4 + [ANY] * len(after),
        out_specs=[VMEM] * 2,
        name="pass_left",
    )(back, forth, far_a, far_b, *after)


def pass_out_kernel(back, forth, far_a, far_b, *refs):
    out_back, out_forth = refs[-2:]
    half = COLS // 2
    out_forth[half:] = forth[half:]
    out_forth[:half] = (forth[:half].astype(f32) + far_a[...].astype(f32)).astype(bf16)
    out_back[:half] = back[:half]
    out_back[half:] = (back[half:].astype(f32) + far_b[...].astype(f32)).astype(bf16)


def pass_out(back, forth, far_a, far_b, after=()):
    return call(
        pass_out_kernel,
        [sds(back.shape, bf16)] * 2,
        vmem=6,
        nbytes=6 * back.size * 2,
        in_specs=[VMEM] * 4 + [ANY] * len(after),
        out_specs=[VMEM] * 2,
        name="pass_out",
    )(back, forth, far_a, far_b, *after)


def sum_out_kernel(own, came, *refs):
    kept, back, forth, far_a, far_b = refs[-5:]
    half = COLS // 2

    def total(slot, rows=slice(None)):
        return own[slot, rows].astype(f32) + came[slot, rows].astype(f32)

    kept[...] = total(0)
    back[...] = total(1).astype(bf16)
    forth[...] = total(2).astype(bf16)
    far_a[...] = total(3, slice(0, half)).astype(bf16)
    far_b[...] = total(3, slice(half, COLS)).astype(bf16)


def sum_out(own, came, after=()):
    whole_share, half_share = sds((COLS, COLS), bf16), sds((COLS // 2, COLS), bf16)
    return call(
        sum_out_kernel,
        [sds((COLS, COLS), f32), whole_share, whole_share, half_share, half_share],
        vmem=12,
        nbytes=own.size * 6,
        in_specs=[VMEM] * 2 + [ANY] * len(after),
        out_specs=[VMEM] * 5,
        name="sum_out",
    )(own, came, *after)


def sum_x_kernel(waits, own, came, *refs):
    kept, sends = refs[waits], refs[waits + 1:]
    kept[...] = own[0].astype(f32) + came[0].astype(f32)
    for slot, sent in enumerate(sends, 1):
        sent[...] = (own[slot].astype(f32) + came[slot].astype(f32)).astype(bf16)


def sum_x(own, came, after=(), sends=3):
    shape = own.shape[1:]
    return call(
        functools.partial(sum_x_kernel, len(after)),
        [sds(shape, f32)] + [sds(shape, bf16)] * sends,
        vmem=12,
        nbytes=13 * shape[0] * shape[1] * 2,
        in_specs=[VMEM] * 2 + [ANY] * len(after),
        out_specs=[VMEM] * (1 + sends),
        name="sum_x",
    )(own, came, *after)


def halves_kernel(back, forth, *refs):
    half = SLOTS // 2
    refs[-2][...] = back[:, :half]
    refs[-1][...] = forth[:, half:]


def halves(back, forth, after):
    shape = (3, SLOTS // 2, COLS)
    return call(
        halves_kernel,
        [sds(shape, bf16)] * 2,
        vmem=6,
        nbytes=8 * back.size,
        in_specs=[VMEM] * 2 + [ANY] * len(after),
        out_specs=[VMEM] * 2,
        name="halves",
    )(back, forth, *after)


def late_kernel(count, *refs):
    for i in range(count):
        refs[i - count][...] = refs[i][...]


def late(arrays, after):
    count = len(arrays)
    return call(
        functools.partial(late_kernel, count),
        [sds(v.shape, v.dtype) for v in arrays],
        vmem=10,
        nbytes=sum(v.size * 4 for v in arrays),
        in_specs=[VMEM] * count + [ANY] * len(after),
        out_specs=[VMEM] * count,
        name="late",
    )(*arrays, *after)


def sum_rest_kernel(kept, c1, c2, *refs):
    total = kept[...]
    for came in (c1, c2):
        total = total + came[...].astype(f32)
    refs[-1][...] = total


def sum_rest(kept, came, after=()):
    return call(
        sum_rest_kernel,
        sds(kept.shape, f32),
        vmem=6,
        nbytes=14 * kept.size,
        in_specs=[VMEM] * 3 + [ANY] * len(after),
        out_specs=VMEM,
        name="sum_rest",
    )(kept, *came, *after)


def sum_keys_kernel(q_grad, own, came, *refs):
    out = refs[-1]
    out[0] = q_grad[...]
    out[1:] = (own[...] + came[...].astype(f32)).astype(bf16)


def sum_keys(q_grad, own, came, after=()):
    return call(
        sum_keys_kernel,
        sds((3, SLOTS, COLS), bf16),
        vmem=8,
        nbytes=10 * came.size,
        in_specs=[VMEM] * 3 + [ANY] * len(after),
        out_specs=VMEM,
        name="sum_keys",
    )(q_grad, own, came, *after)


def rows_kernel(x, grad, gain, inv, l_kept, l_came, r_kept, r1, r2, r3, *refs):
    out = refs[-1]
    left = l_kept[...] + l_came[0:2].reshape(ROWS, HALF).astype(f32)
    right = r_kept[...]
    for came in (r1, r2, r3):
        right = right + came[...].astype(f32)
    scale = inv[:, :1]
    halves = []
    dots = jnp.zeros((ROWS, 1), f32)
    for part, cols in ((left, slice(0, HALF)), (right, slice(HALF, WIDTH))):
        scaled = gain[:, cols].astype(f32) * part
        rows = x[:, cols].astype(f32)
        dots = dots + jnp.sum(scaled * rows, axis=1, keepdims=True)
        halves.append((scaled, rows, cols))
    mean = dots * (1.0 / WIDTH)
    for scaled, rows, cols in halves:
        total = grad[:, cols].astype(f32) + scale * scaled - rows * (scale * scale * scale) * mean
        out[:, cols] = total.astype(bf16)


def token_rows(x, grad, gain, inv, left, right, after=()):
    return call(
        rows_kernel,
        sds((ROWS, WIDTH), bf16),
        vmem=4,
        nbytes=6 * ROWS * WIDTH * 2,
        in_specs=[VMEM] * 10 + [ANY] * len(after),
        out_specs=VMEM,
        name="token_rows",
    )(x, grad, gain, inv, *left, *right, *after)


def key_value_kernel(*refs):
    pieces, weight = refs[:6], refs[6]
    full, out, buffer, sems = refs[-4:]
    copies = [
        load(k_cuts(weight.at[part + 1]), k_cuts(buffer.at[part]), sems.at[part])
        for part in range(2)
    ]
    place_pieces(pieces, full)
    for part in range(2):
        out[part] = dot_loaded(full, buffer.at[part], copies[part]).astype(bf16)


def key_value(pieces, weights, after):
    return call(
        key_value_kernel,
        [sds((SLOTS, WIDTH), bf16), sds((2, SLOTS, COLS), bf16)],
        vmem=20,
        flops=4 * SLOTS * WIDTH * COLS,
        nbytes=2 * WIDTH * COLS * 2 + 2 * SLOTS * WIDTH * 2,
        in_specs=[VMEM] * 6 + [HBM] + [ANY] * len(after),
        out_specs=[VMEM] * 2,
        scratch_shapes=[
            pltpu.VMEM((2, WIDTH, COLS), bf16),
            pltpu.SemaphoreType.DMA((2, KCUTS)),
        ],
        name="key_value",
    )(*pieces, weights, *after)


def query_kernel(full, weight, *refs):
    out, buffer, sems = refs[-3:]
    copies = load(k_cuts(weight.at[0]), k_cuts(buffer), sems)
    out[...] = dot_loaded(full, buffer, copies).astype(bf16)


DOT_SCRATCH = [pltpu.VMEM((WIDTH, COLS), bf16), pltpu.SemaphoreType.DMA((KCUTS,))]


def query_of(full, weights, after):
    return call(
        query_kernel,
        sds((SLOTS, COLS), bf16),
        vmem=12,
        flops=2 * SLOTS * WIDTH * COLS,
        nbytes=WIDTH * COLS * 2 + SLOTS * WIDTH * 2,
        in_specs=[VMEM, HBM] + [ANY] * len(after),
        out_specs=VMEM,
        scratch_shapes=DOT_SCRATCH,
        name="query",
    )(full, weights, *after)


def grad_mixed_kernel(p0, p1, p2, p3, weight, *refs):
    full, out, buffer, sems = refs[-4:]
    copies = load(k_cuts(weight.at[0]), k_cuts(buffer), sems)
    for slot, pair in enumerate((p0, p1, p2, p3)):
        full[pl.ds(slot * ROWS, ROWS)] = pair[0]
        full[pl.ds((4 + slot) * ROWS, ROWS)] = pair[1]
    out[...] = dot_loaded(full, buffer, copies).astype(bf16)


def grad_mixed_of(pairs, weights, after):
    return call(
        grad_mixed_kernel,
        [sds((SLOTS, WIDTH), bf16), sds((SLOTS, COLS), bf16)],
        vmem=16,
        flops=2 * SLOTS * WIDTH * COLS,
        nbytes=WIDTH * COLS * 2 + 2 * SLOTS * WIDTH * 2,
        in_specs=[VMEM] * 4 + [HBM] + [ANY] * len(after),
        out_specs=[VMEM] * 2,
        scratch_shapes=DOT_SCRATCH,
        name="grad_mixed",
    )(*pairs, weights, *after)


def gain_rows_of(left, right):
    row = lax.broadcasted_iota(jnp.int32, (16, left.shape[1]), 0)
    rows = jnp.zeros((16, left.shape[1]), f32)
    for first, part in ((0, left), (2, right)):
        high = part.astype(bf16).astype(f32)
        rows = jnp.where(row == first, high, rows)
        rows = jnp.where(row == first + 1, part - high, rows)
    return rows.astype(bf16)


def gain_from(rows):
    rows = rows.astype(f32)
    return rows[0:1] + rows[1:2], rows[2:3] + rows[3:4]


FCUT = 512
FCUTS = HALF // FCUT


def back_products(grads, weight, first, normed, buffer, sems):
    copies = [
        load(
            [weight.at[part, pl.ds(first + cut * FCUT, FCUT)] for part in range(3)],
            [buffer.at[part, pl.ds(cut * FCUT, FCUT)] for part in range(3)],
            sems.at[cut],
        )
        for cut in range(FCUTS)
    ]
    for cut in range(FCUTS):
        for copy in copies[cut]:
            copy.wait()
        rows = slice(cut * FCUT, (cut + 1) * FCUT)
        total = dot_rows(grads[0], buffer[0, rows])
        for part in range(1, 3):
            total = total + dot_rows(grads[part], buffer[part, rows])
        rounded = total.astype(bf16)
        terms = normed[:, first + cut * FCUT:first + (cut + 1) * FCUT].astype(f32)
        gain = jnp.sum(rounded.astype(f32) * terms, axis=0, keepdims=True)
        yield rows, rounded, gain


def back_right_kernel(waits, grads, weight, normed, *refs):
    own, sent, gain, buffer, sems = refs[waits:]
    for cols, rounded, terms in back_products(
        grads, weight, HALF, normed, buffer, sems
    ):
        gain[:, cols] = terms
        for xbit, out in enumerate((own, sent)):
            for slot in range(4):
                start = (xbit * 4 + slot) * ROWS
                out[slot, :, cols] = rounded[start:start + ROWS]


def back_left_kernel(waits, grads, weight, normed, gain_right, *refs):
    outs, far, buffer, sems = refs[waits:waits + 3], refs[-4:-2], refs[-2], refs[-1]
    for cols, rounded, terms in back_products(
        grads, weight, 0, normed, buffer, sems
    ):
        gains = gain_rows_of(terms, gain_right[:, cols])
        for slot, out in enumerate(outs):
            for xbit in range(2):
                start = (xbit * 4 + slot) * ROWS
                out[2 * xbit, :, cols] = rounded[start:start + 16]
                out[2 * xbit + 1, :, cols] = rounded[start + 16:start + ROWS]
            out[4, :, cols] = gains
        for xbit, out in enumerate(far):
            start = (xbit * 4 + 3) * ROWS
            out[0, :, cols] = rounded[start:start + 16]
            out[1, :, cols] = rounded[start + 16:start + ROWS]
        far[0][2, :, cols] = gains


def back_dot(kernel, grads, weights, normed, extra, out_shape, after, name):
    return call(
        functools.partial(kernel, len(after)),
        out_shape,
        vmem=20,
        flops=2 * 3 * SLOTS * HALF * COLS,
        nbytes=3 * HALF * COLS * 2 + 2 * SLOTS * HALF * 2,
        in_specs=[VMEM, HBM, VMEM] + [VMEM] * len(extra) + [ANY] * len(after),
        out_specs=[VMEM] * len(out_shape),
        scratch_shapes=[
            pltpu.VMEM((3, HALF, COLS), bf16),
            pltpu.SemaphoreType.DMA((FCUTS, 3)),
        ],
        name=name,
    )(grads, weights, normed, *extra, *after)


def back_right(grads, weights, normed, after=()):
    out = [sds((4, ROWS, HALF), bf16)] * 2 + [sds((1, HALF), f32)]
    return back_dot(back_right_kernel, grads, weights, normed, [], out, after, "back_right")


def back_left(grads, weights, normed, gain_right, after=()):
    out = [sds((5, 16, HALF), bf16)] * 3
    out += [sds((3, 16, HALF), bf16), sds((2, 16, HALF), bf16)]
    return back_dot(back_left_kernel, grads, weights, normed, [gain_right], out, after, "back_left")


def proj_kernel(left, weight, *refs):
    outs, buffer, sems = refs[-6:-2], refs[-2], refs[-1]
    copies = load(k_cuts(weight.at[0]), k_cuts(buffer), sems)
    for cut, copy in enumerate(copies):
        copy.wait()
        cols = slice(cut * KCUT, (cut + 1) * KCUT)
        rounded = dot_rows(left[...], buffer[cols]).astype(bf16)
        for slot in range(4):
            for xbit in range(2):
                start = (xbit * 4 + slot) * ROWS
                outs[slot][xbit, :, cols] = rounded[start:start + ROWS]


def proj_parts(mixed, weights, after):
    return call(
        proj_kernel,
        [sds((2, ROWS, WIDTH), bf16)] * 4,
        vmem=14,
        flops=2 * SLOTS * WIDTH * COLS,
        nbytes=WIDTH * COLS * 2 + SLOTS * WIDTH * 2,
        in_specs=[VMEM, HBM] + [ANY] * len(after),
        out_specs=[VMEM] * 4,
        scratch_shapes=DOT_SCRATCH,
        name="proj_parts",
    )(mixed, weights, *after)


def slot_of(row, x_index, z_index):
    block = row // ROWS
    xbit = block // 4
    slot = block - xbit * 4
    back = jnp.where(slot == 2, 3, jnp.where(slot == 3, 2, slot))
    x_from = jnp.where(xbit == 0, x_index, 1 - x_index)
    z_from = z_index - back
    z_from = jnp.where(z_from < 0, z_from + 4, z_from)
    return (x_from * 4 + z_from) * ROWS + (row - block * ROWS)


def places(gaps, runs, rows, is_text):
    x_index, z_index = where_am_i()[:2]
    slot = slot_of(rows, x_index, z_index)
    text = slot
    end = jnp.int32(0)
    for run in range(4):
        end = end + gaps[0, run]
        text = text + jnp.where(slot >= end, runs[0, run], 0)
    image = slot + gaps[0, 0]
    end = jnp.int32(0)
    for run in range(3):
        end = end + runs[0, run]
        image = image + jnp.where(slot >= end, gaps[0, run + 1], 0)
    image = jnp.where(slot < LI, image, FAR)
    return jnp.where(is_text, text, image)


def admitted(gaps, runs):
    group = lax.axis_index("grp")
    rows = lax.broadcasted_iota(jnp.int32, (SLOTS, 1), 0)
    query = places(gaps, runs, rows, group == 0)
    key_row = lax.broadcasted_iota(jnp.int32, (1, SLOTS), 1)
    own = places(gaps, runs, key_row, group == 0)
    other = places(gaps, runs, key_row, group != 0)
    return own <= query, other <= query


def head_attn(query, own_key, other_key, own_ok, other_ok):
    scale = HS ** (-0.5)
    own = jnp.where(own_ok, dot_rows(query, own_key) * scale, -1e30)
    other = jnp.where(other_ok, dot_rows(query, other_key) * scale, -1e30)
    row_max = jnp.maximum(
        jnp.max(own, axis=1, keepdims=True), jnp.max(other, axis=1, keepdims=True)
    )
    own = jnp.exp(own - row_max)
    other = jnp.exp(other - row_max)
    row_sum = jnp.sum(own, axis=1, keepdims=True) + jnp.sum(other, axis=1, keepdims=True)
    share = 1.0 / row_sum
    return own * share, other * share


def forward_kernel(gaps, runs, query, own_kv, other_kv, *refs):
    mixed = refs[-1]
    own_ok, other_ok = admitted(gaps, runs)
    for head in range(HEADS):
        cols = slice(head * HS, (head + 1) * HS)
        own, other = head_attn(
            query[:, cols], own_kv[0, :, cols], other_kv[0, :, cols], own_ok, other_ok
        )
        total = dot(own.astype(bf16), own_kv[1, :, cols])
        total = total + dot(other.astype(bf16), other_kv[1, :, cols])
        mixed[:, cols] = total.astype(bf16)


def backward_kernel(gaps, runs, query, own_kv, other_kv, mixed, grad, *refs):
    q_grad, own_grad, other_grad = refs[-3:]
    scale = HS ** (-0.5)
    own_ok, other_ok = admitted(gaps, runs)
    for head in range(HEADS):
        cols = slice(head * HS, (head + 1) * HS)
        q, g = query[:, cols], grad[:, cols]
        row_dot = jnp.sum(g.astype(f32) * mixed[:, cols].astype(f32), axis=1, keepdims=True)
        attns = head_attn(q, own_kv[0, :, cols], other_kv[0, :, cols], own_ok, other_ok)
        dq = None
        for attn, kv, kv_grad in zip(attns, (own_kv, other_kv), (own_grad, other_grad)):
            value_grad = dot_tokens(attn.astype(bf16), g)
            weight_grad = dot_rows(g, kv[1, :, cols])
            score_grad = (attn * (weight_grad - row_dot)).astype(bf16)
            part = dot(score_grad, kv[0, :, cols])
            dq = part if dq is None else dq + part
            key_grad = dot_tokens(score_grad, q) * scale
            kv_grad[0, :, cols] = key_grad.astype(kv_grad.dtype)
            kv_grad[1, :, cols] = value_grad.astype(kv_grad.dtype)
        q_grad[:, cols] = (dq * scale).astype(bf16)


ATTN_FLOPS = 2 * HEADS * SLOTS * 2 * SLOTS * HS


def attend_forward(spans, query, own_kv, other_kv, after):
    return call(
        forward_kernel,
        sds((SLOTS, COLS), bf16),
        vmem=10,
        flops=4 * ATTN_FLOPS,
        nbytes=6 * SLOTS * COLS * 2,
        in_specs=[SMEM] * 2 + [VMEM] * 3 + [ANY] * len(after),
        out_specs=VMEM,
        name="attend_forward",
    )(*spans, query, own_kv, other_kv, *after)


def attend_backward(spans, query, own_kv, other_kv, mixed, grad, after):
    kv = (2, SLOTS, COLS)
    return call(
        backward_kernel,
        [sds((SLOTS, COLS), bf16), sds(kv, f32), sds(kv, bf16)],
        vmem=14,
        flops=8 * ATTN_FLOPS,
        nbytes=12 * SLOTS * COLS * 2,
        in_specs=[SMEM] * 2 + [VMEM] * 5 + [ANY] * len(after),
        out_specs=[VMEM] * 3,
        name="attend_backward",
    )(*spans, query, own_kv, other_kv, mixed, grad, *after)


def out_kernel(grad, mixed, *refs):
    own, sent = refs[-2:]
    y_index, core = where_am_i()[2:4]
    for i in range(8):
        column = ((y_index - STEPS[i % 4]) & 3) * 2 + (1 - core if i < 4 else core)
        start = pl.multiple_of(column * COLS, COLS)
        share = dot_tokens(grad[:, pl.ds(start, COLS)], mixed[...]).astype(bf16)
        if i < 4:
            sent[i] = share
        else:
            own[i - 4] = share


def out_weight_parts(grad_full, mixed, after):
    return call(
        out_kernel,
        [sds((4, COLS, COLS), bf16)] * 2,
        vmem=12,
        flops=2 * SLOTS * WIDTH * COLS,
        nbytes=SLOTS * WIDTH * 2 + WIDTH * COLS * 2,
        in_specs=[VMEM] * 2 + [ANY] * len(after),
        out_specs=[VMEM] * 2,
        name="out_weight_parts",
    )(grad_full, mixed, *after)


def share_kernel(which, full, c1, c2, c3, g0, g1, g2, g3, g4, *refs):
    out, lefts = refs[-2:]
    y_index, core = where_am_i()[2:4]
    column = core if which else 1 - core
    start = pl.multiple_of((y_index * 2 + column) * COLS, COLS)
    lefts[0] = full[:, pl.ds(start, COLS)].T
    start = pl.multiple_of(column * COLS, COLS)
    for k, came in enumerate((c1, c2, c3), 1):
        lefts[k] = came[:, pl.ds(start, COLS)].T
    for part in range(3):
        total = dot(lefts[0], g0[part])
        for k, grad in enumerate((g1, g2), 1):
            total = total + dot(lefts[k], grad[part])
        total = total + dot(lefts[3, :, :SLOTS // 2], g3[part])
        total = total + dot(lefts[3, :, SLOTS // 2:], g4[part])
        out[part] = total.astype(out.dtype)


def weight_shares(which, full, came, grads, dtype, after=()):
    return call(
        functools.partial(share_kernel, which),
        sds((3, COLS, COLS), dtype),
        vmem=20,
        flops=3 * 4 * 2 * SLOTS * COLS * COLS,
        nbytes=16 * SLOTS * COLS * 2 + 3 * COLS * COLS * 4,
        in_specs=[VMEM] * 9 + [ANY] * len(after),
        out_specs=VMEM,
        scratch_shapes=[pltpu.VMEM((4, COLS, SLOTS), bf16)],
        name="weight_shares",
    )(full, *came, *grads, *after)


def chunk_kernel(full, *outs):
    y_index = where_am_i()[2]
    for k, out in zip(STEPS[1:], outs):
        start = pl.multiple_of(((y_index + k) & 3) * 1024, 1024)
        out[...] = full[:, pl.ds(start, 1024)]


def chunks_over_y(full):
    sends = call(
        chunk_kernel,
        [sds((SLOTS, 1024), bf16)] * 3,
        vmem=6,
        nbytes=6 * SLOTS * 1024 * 2,
        in_specs=[VMEM],
        out_specs=[VMEM] * 3,
        name="chunks",
    )(full)
    return [lax.ppermute(sent, "seq", y_shift(k)) for sent, k in zip(sends, STEPS[1:])]


def layer_kernel(x, kept, came, *refs):
    total = x[...].astype(f32) + (kept[...] + came[...].astype(f32))
    refs[-1][...] = (total * valid_rows()).astype(bf16)


def layer_rows(x, kept, came, after=()):
    return call(
        layer_kernel,
        sds((ROWS, WIDTH), bf16),
        vmem=4,
        nbytes=5 * ROWS * WIDTH * 2,
        in_specs=[VMEM] * 3 + [ANY] * len(after),
        out_specs=VMEM,
        name="layer_rows",
    )(x, kept, came, *after)


def per_device(tokens, text_gaps, image_runs, gains, w_qkv, w_out, cotangent):
    x_rows = tokens[0, 0]
    w_parts = jnp.transpose(w_qkv[0], (1, 0, 2))
    spans = (text_gaps, image_runs)

    n_left, n_right, grad_rows, inv = norm_rows(x_rows, gains, cotangent[0, 0])
    pieces = gather_blocks(n_left, n_right)
    grad_other = lax.ppermute(grad_rows, "tp", X_SWAP)
    grad_pair = touch(jnp.stack([grad_rows, grad_other]), w_parts)
    grad_pairs = [grad_pair] + [lax.ppermute(grad_pair, "tp", z_shift(k)) for k in STEPS[1:]]
    normed_full, own_kv = key_value(pieces, w_parts, [grad_pair])
    other_kv = lax.ppermute(own_kv, "grp", GRP_SWAP)
    query = query_of(normed_full, w_parts, grad_pairs[1:3])
    chunks = chunks_over_y(normed_full)

    mixed = attend_forward(spans, query, own_kv, other_kv, [])
    proj = proj_parts(mixed, w_out, [])
    grad_full, grad_mixed = grad_mixed_of(grad_pairs, w_out, [proj[0]] + chunks[:2])
    q_grad, own_part, other_part = attend_backward(
        spans, query, own_kv, other_kv, mixed, grad_mixed, []
    )
    back = lax.ppermute(other_part, "grp", GRP_SWAP)
    sends = late(proj[1:], [q_grad])
    proj_came = [lax.ppermute(v, "tp", z_shift(-k)) for v, k in zip(sends, STEPS[1:])]
    out_own, out_sent = out_weight_parts(grad_full, mixed, [q_grad])
    out_came = lax.ppermute(out_sent, "seq", CORE_SWAP)
    own_grads = sum_keys(q_grad, own_part, back, sends[:1])
    back_grads = lax.ppermute(own_grads, "seq", y_shift(1))
    next_grads = lax.ppermute(own_grads, "seq", y_shift(3))

    right = back_right(own_grads, w_parts, normed_full, [out_came] + chunks[2:])
    right_x = lax.ppermute(right[1], "tp", X_SWAP)
    left = back_left(own_grads, w_parts, normed_full, right[2], proj_came[:2])
    left_far_a = lax.ppermute(left[3], "tp", z_shift(1))
    left_far_b = lax.ppermute(left[4], "tp", z_shift(3))
    left_back, left_forth = pass_left(left[1], left[2], left_far_a, left_far_b, proj_came[2:])
    left_came = [
        lax.ppermute(left_forth, "tp", z_shift(1)), lax.ppermute(left_back, "tp", z_shift(3))
    ]
    out_kept, *out_sends = sum_out(
        out_own, out_came, [left_back, back_grads, next_grads, right_x]
    )
    out_far_a = lax.ppermute(out_sends[2], "seq", y_shift(1))
    out_far_b = lax.ppermute(out_sends[3], "seq", y_shift(3))
    out_back, out_forth = pass_out(
        out_sends[0], out_sends[1], out_far_a, out_far_b
    )
    out_terms = [
        lax.ppermute(out_forth, "seq", y_shift(1)), lax.ppermute(out_back, "seq", y_shift(3))
    ]
    left_kept, left_sent, gain_kept = sum_left(left[0], left_came, [out_back])
    left_x = lax.ppermute(left_sent, "tp", X_SWAP)
    gain_tp = sum_gain(gain_kept, left_x, gains)
    gain_sum = gain_tp + lax.ppermute(gain_tp, "seq", CORE_SWAP)
    gain_grad = gain_sum
    for k in STEPS[1:]:
        gain_grad = gain_grad + lax.ppermute(gain_sum, "seq", y_shift(k))
    right_kept, *right_sends = sum_x(
        right[0], right_x, [left_sent]
    )
    relayed = halves(
        back_grads, next_grads, [gain_tp, right_sends[0]] + out_terms
    )
    grads = [own_grads, back_grads, next_grads]
    grads += [lax.ppermute(v, "seq", y_shift(k)) for v, k in zip(relayed, (1, 3))]
    right_came = [lax.ppermute(v, "tp", z_shift(-k)) for v, k in zip(right_sends, STEPS[1:])]
    shares = (normed_full, chunks, grads)
    qkv_sent = weight_shares(0, *shares, bf16, right_came + [gain_sum])
    tokens_grad = token_rows(
        x_rows, grad_rows, gains, inv, (left_kept, left_x), (right_kept, *right_came)
    )

    qkv_mine = weight_shares(1, *shares, f32, [qkv_sent])
    qkv_share = qkv_mine + lax.ppermute(qkv_sent, "seq", CORE_SWAP).astype(f32)
    proj_kept, proj_sent = sum_z(proj[0], proj_came)
    proj_x = lax.ppermute(proj_sent, "tp", X_SWAP)
    layer_out = layer_rows(x_rows, proj_kept, proj_x)
    out_share = sum_rest(out_kept, out_terms, right_came[:1])
    return (
        layer_out[None, None],
        tokens_grad[None, None],
        gain_grad,
        jnp.transpose(qkv_share, (1, 0, 2))[None],
        out_share[None],
    )


def solution(mesh):
    in_specs = (
        P("grp", "seq", "tp", None),
        P("seq", None),
        P("seq", None),
        P("grp", None),
        P("grp", None, None, "tp"),
        P("grp", None, "tp"),
        P("grp", "seq", "tp", None),
    )
    out_specs = (
        P("grp", "seq", "tp", None),
        P("grp", "seq", "tp", None),
        P("grp", None),
        P("grp", "seq", None, "tp"),
        P("grp", "seq", "tp"),
    )
    return jax.shard_map(
        per_device, mesh=mesh, in_specs=in_specs, out_specs=out_specs, check_vma=False
    )
```

```python
import functools

import jax
import jax.numpy as jnp
from jax import lax
from jax.experimental import pallas as pl
from jax.experimental.pallas import tpu as pltpu
from jax.sharding import PartitionSpec as P

HS = 128
LI = 128
HEADS = 4
SLOTS = 256
ROWS = 32
WIDTH = 4096
HALF = 2048
COLS = 512
FAR = 1073741824
f32 = jnp.float32
bf16 = jnp.bfloat16
MIB = 1024 * 1024

STEPS = (0, 1, 3, 2)


def z_shift(k):
    return [(i, (i // 4) * 4 + (i + k) % 4) for i in range(8)]


X_SWAP = [(i, i ^ 4) for i in range(8)]


def y_shift(k):
    return [(i, (i + 2 * k) % 8) for i in range(8)]


CORE_SWAP = [(i, i ^ 1) for i in range(8)]
GRP_SWAP = [(0, 1), (1, 0)]


def sds(shape, dtype):
    return jax.ShapeDtypeStruct(shape, dtype)


def call(kernel, out_shape, vmem, flops=0, nbytes=0, **kwargs):
    return pl.pallas_call(
        kernel,
        out_shape=out_shape,
        compiler_params=pltpu.CompilerParams(vmem_limit_bytes=vmem * MIB),
        cost_estimate=pl.CostEstimate(flops=flops, bytes_accessed=nbytes, transcendentals=0),
        **kwargs,
    )


def whole(shape):
    return pl.BlockSpec(shape, lambda *_: (0,) * len(shape))


SMEM = pl.BlockSpec(memory_space=pltpu.SMEM)
VMEM = pl.BlockSpec(memory_space=pltpu.VMEM)
ANY = pl.BlockSpec(memory_space=pl.ANY)
HBM = pl.BlockSpec(memory_space=pltpu.HBM)


def dot(left, right):
    return jnp.dot(left, right, preferred_element_type=f32)


def dot_rows(left, right):
    return lax.dot_general(left, right, (((1,), (1,)), ((), ())), preferred_element_type=f32)


def dot_tokens(left, right):
    return lax.dot_general(left, right, (((0,), (0,)), ((), ())), preferred_element_type=f32)


def where_am_i():
    tp, seq = lax.axis_index("tp"), lax.axis_index("seq")
    return tp >> 2, tp & 3, seq >> 1, seq & 1, lax.axis_index("grp")


def valid_rows():
    used = jnp.logical_or(lax.axis_index("grp") == 0, lax.axis_index("tp") * ROWS < LI)
    return jnp.where(used, 1.0, 0.0).astype(f32)


def load(sources, targets, sems):
    copies = [
        pltpu.make_async_copy(source, target, sems.at[i])
        for i, (source, target) in enumerate(zip(sources, targets))
    ]
    for copy in copies:
        copy.start()
    return copies


KCUT = 1024
KCUTS = WIDTH // KCUT


def dot_loaded(full, buffer, copies):
    total = None
    for i, copy in enumerate(copies):
        copy.wait()
        cut = slice(i * KCUT, (i + 1) * KCUT)
        part = dot(full[:, cut], buffer[cut])
        total = part if total is None else total + part
    return total


def k_cuts(ref):
    return [ref.at[pl.ds(i * KCUT, KCUT)] for i in range(KCUTS)]


def touch_kernel(weight, pair, *refs):
    refs[-1][...] = pair[...]


def touch(pair, weight):
    return call(
        touch_kernel,
        sds(pair.shape, pair.dtype),
        vmem=4,
        nbytes=pair.size * 4,
        in_specs=[ANY, VMEM],
        out_specs=VMEM,
        name="touch",
    )(weight, pair)


def norm_kernel(x, gain, cot, n_left, n_right, grad, inv):
    x_float = x[...].astype(f32)
    scale = lax.rsqrt(jnp.mean(x_float * x_float, axis=1, keepdims=True) + 1e-05)
    normed = (x_float * scale * gain[...].astype(f32)).astype(bf16)
    n_left[...] = normed[:, :HALF]
    n_right[...] = normed[:, HALF:]
    grad[...] = (cot[...].astype(f32) * valid_rows()).astype(bf16)
    inv[...] = jnp.broadcast_to(scale, (ROWS, 128))


def norm_rows(x, gain, cot):
    part = sds((ROWS, HALF), bf16)
    return call(
        norm_kernel,
        [part, part, sds((ROWS, WIDTH), bf16), sds((ROWS, 128), f32)],
        vmem=4,
        nbytes=4 * ROWS * WIDTH * 2,
        in_specs=[VMEM] * 3,
        name="norm_rows",
    )(x, gain, cot)


def gather_blocks(left, right):
    right_pair = jnp.stack([right, lax.ppermute(right, "tp", X_SWAP)])
    left_four = [left] + [lax.ppermute(left, "tp", z_shift(k)) for k in STEPS[1:]]
    right_four = [right_pair] + [lax.ppermute(right_pair, "tp", z_shift(k)) for k in STEPS[1:]]
    left_own = jnp.stack(left_four)
    left_other = lax.ppermute(left_own, "tp", X_SWAP)
    return [left_own, left_other] + right_four


def place_pieces(pieces, whole_ref):
    left_own, left_other = pieces[:2]
    for slot in range(4):
        rows = pl.ds(slot * ROWS, ROWS)
        other = pl.ds((4 + slot) * ROWS, ROWS)
        whole_ref[rows, :HALF] = left_own[slot]
        whole_ref[other, :HALF] = left_other[slot]
        whole_ref[rows, HALF:] = pieces[2 + slot][0]
        whole_ref[other, HALF:] = pieces[2 + slot][1]


PIECE_SHAPES = [(4, ROWS, HALF)] * 2 + [(2, ROWS, HALF)] * 4


def sum_z_kernel(own, c1, c2, c3, *refs):
    kept, sent = refs[-2:]
    total = own[...].astype(f32)
    for came in (c1, c2, c3):
        total = total + came[...].astype(f32)
    kept[...] = total[0]
    sent[...] = total[1].astype(bf16)


def sum_z(own, came, after=()):
    shape = own.shape[1:]
    return call(
        sum_z_kernel,
        [sds(shape, f32), sds(shape, bf16)],
        vmem=6,
        nbytes=11 * shape[0] * shape[1] * 2,
        in_specs=[VMEM] * 4 + [ANY] * len(after),
        out_specs=[VMEM] * 2,
        name="sum_z",
    )(own, *came, *after)


def sum_left_kernel(own, c1, c2, *refs):
    kept, sent, gain = refs[-3:]
    for part in range(2):
        total = own[part].astype(f32)
        for came in (c1, c2):
            total = total + came[part].astype(f32)
        kept[pl.ds(part * 16, 16)] = total
        total = own[2 + part].astype(f32)
        for came in (c1, c2):
            total = total + came[2 + part].astype(f32)
        sent[part] = total.astype(bf16)
    left, right = gain_from(own[4])
    for came in (c1, c2):
        more_left, more_right = gain_from(came[4])
        left, right = left + more_left, right + more_right
    sent[2] = gain_rows_of(left, right)
    gain[0:1] = left
    gain[1:2] = right


def sum_left(own, came, after=()):
    return call(
        sum_left_kernel,
        [sds((ROWS, HALF), f32), sds((3, 16, HALF), bf16), sds((2, HALF), f32)],
        vmem=4,
        nbytes=11 * ROWS * HALF * 2,
        in_specs=[VMEM] * 3 + [ANY] * len(after),
        out_specs=[VMEM] * 3,
        name="sum_left",
    )(own, *came, *after)


def sum_gain_kernel(own, came, gain, out):
    left, right = gain_from(came[2])
    out[:, :HALF] = (own[0:1] + left) / gain[:, :HALF].astype(f32)
    out[:, HALF:] = (own[1:2] + right) / gain[:, HALF:].astype(f32)


def sum_gain(own, came, gain):
    return call(
        sum_gain_kernel,
        sds((1, WIDTH), f32),
        vmem=2,
        nbytes=10 * WIDTH * 2,
        in_specs=[VMEM] * 3,
        out_specs=VMEM,
        name="sum_gain",
    )(own, came, gain)


def pass_left_kernel(back, forth, far_a, far_b, *refs):
    out_back, out_forth = refs[-2:]
    out_forth[...] = forth[...]
    out_back[...] = back[...]
    for part in range(2):
        out_forth[part] = (forth[part].astype(f32) + far_a[part].astype(f32)).astype(bf16)
        total = back[2 + part].astype(f32) + far_b[part].astype(f32)
        out_back[2 + part] = total.astype(bf16)
    left, right = gain_from(forth[4])
    more_left, more_right = gain_from(far_a[2])
    out_forth[4] = gain_rows_of(left + more_left, right + more_right)


def pass_left(back, forth, far_a, far_b, after=()):
    return call(
        pass_left_kernel,
        [sds(back.shape, bf16)] * 2,
        vmem=6,
        nbytes=6 * back.size * 2,
        in_specs=[VMEM] * 4 + [ANY] * len(after),
        out_specs=[VMEM] * 2,
        name="pass_left",
    )(back, forth, far_a, far_b, *after)


def pass_out_kernel(back, forth, far_a, far_b, *refs):
    out_back, out_forth = refs[-2:]
    half = COLS // 2
    out_forth[half:] = forth[half:]
    out_forth[:half] = (forth[:half].astype(f32) + far_a[...].astype(f32)).astype(bf16)
    out_back[:half] = back[:half]
    out_back[half:] = (back[half:].astype(f32) + far_b[...].astype(f32)).astype(bf16)


def pass_out(back, forth, far_a, far_b, after=()):
    return call(
        pass_out_kernel,
        [sds(back.shape, bf16)] * 2,
        vmem=6,
        nbytes=6 * back.size * 2,
        in_specs=[VMEM] * 4 + [ANY] * len(after),
        out_specs=[VMEM] * 2,
        name="pass_out",
    )(back, forth, far_a, far_b, *after)


def sum_out_kernel(own, came, *refs):
    kept, back, forth, far_a, far_b = refs[-5:]
    half = COLS // 2

    def total(slot, rows=slice(None)):
        return own[slot, rows].astype(f32) + came[slot, rows].astype(f32)

    kept[...] = total(0)
    back[...] = total(1).astype(bf16)
    forth[...] = total(2).astype(bf16)
    far_a[...] = total(3, slice(0, half)).astype(bf16)
    far_b[...] = total(3, slice(half, COLS)).astype(bf16)


def sum_out(own, came, after=()):
    whole_share, half_share = sds((COLS, COLS), bf16), sds((COLS // 2, COLS), bf16)
    return call(
        sum_out_kernel,
        [sds((COLS, COLS), f32), whole_share, whole_share, half_share, half_share],
        vmem=12,
        nbytes=own.size * 6,
        in_specs=[VMEM] * 2 + [ANY] * len(after),
        out_specs=[VMEM] * 5,
        name="sum_out",
    )(own, came, *after)


def sum_x_kernel(waits, own, came, *refs):
    kept, sends = refs[waits], refs[waits + 1:]
    kept[...] = own[0].astype(f32) + came[0].astype(f32)
    for slot, sent in enumerate(sends, 1):
        sent[...] = (own[slot].astype(f32) + came[slot].astype(f32)).astype(bf16)


def sum_x(own, came, after=(), sends=3):
    shape = own.shape[1:]
    return call(
        functools.partial(sum_x_kernel, len(after)),
        [sds(shape, f32)] + [sds(shape, bf16)] * sends,
        vmem=12,
        nbytes=13 * shape[0] * shape[1] * 2,
        in_specs=[VMEM] * 2 + [ANY] * len(after),
        out_specs=[VMEM] * (1 + sends),
        name="sum_x",
    )(own, came, *after)


def halves_kernel(back, forth, *refs):
    half = SLOTS // 2
    refs[-2][...] = back[:, :half]
    refs[-1][...] = forth[:, half:]


def halves(back, forth, after):
    shape = (3, SLOTS // 2, COLS)
    return call(
        halves_kernel,
        [sds(shape, bf16)] * 2,
        vmem=6,
        nbytes=8 * back.size,
        in_specs=[VMEM] * 2 + [ANY] * len(after),
        out_specs=[VMEM] * 2,
        name="halves",
    )(back, forth, *after)


def late_kernel(count, *refs):
    for i in range(count):
        refs[i - count][...] = refs[i][...]


def late(arrays, after):
    count = len(arrays)
    return call(
        functools.partial(late_kernel, count),
        [sds(v.shape, v.dtype) for v in arrays],
        vmem=10,
        nbytes=sum(v.size * 4 for v in arrays),
        in_specs=[VMEM] * count + [ANY] * len(after),
        out_specs=[VMEM] * count,
        name="late",
    )(*arrays, *after)


def sum_rest_kernel(kept, c1, c2, *refs):
    total = kept[...]
    for came in (c1, c2):
        total = total + came[...].astype(f32)
    refs[-1][...] = total


def sum_rest(kept, came, after=()):
    return call(
        sum_rest_kernel,
        sds(kept.shape, f32),
        vmem=6,
        nbytes=14 * kept.size,
        in_specs=[VMEM] * 3 + [ANY] * len(after),
        out_specs=VMEM,
        name="sum_rest",
    )(kept, *came, *after)


def sum_keys_kernel(q_grad, own, came, *refs):
    out = refs[-1]
    out[0] = q_grad[...]
    out[1:] = (own[...] + came[...].astype(f32)).astype(bf16)


def sum_keys(q_grad, own, came, after=()):
    return call(
        sum_keys_kernel,
        sds((3, SLOTS, COLS), bf16),
        vmem=8,
        nbytes=10 * came.size,
        in_specs=[VMEM] * 3 + [ANY] * len(after),
        out_specs=VMEM,
        name="sum_keys",
    )(q_grad, own, came, *after)


def rows_kernel(x, grad, gain, inv, l_kept, l_came, r_kept, r1, r2, r3, *refs):
    out = refs[-1]
    left = l_kept[...] + l_came[0:2].reshape(ROWS, HALF).astype(f32)
    right = r_kept[...]
    for came in (r1, r2, r3):
        right = right + came[...].astype(f32)
    scale = inv[:, :1]
    halves = []
    dots = jnp.zeros((ROWS, 1), f32)
    for part, cols in ((left, slice(0, HALF)), (right, slice(HALF, WIDTH))):
        scaled = gain[:, cols].astype(f32) * part
        rows = x[:, cols].astype(f32)
        dots = dots + jnp.sum(scaled * rows, axis=1, keepdims=True)
        halves.append((scaled, rows, cols))
    mean = dots * (1.0 / WIDTH)
    for scaled, rows, cols in halves:
        total = grad[:, cols].astype(f32) + scale * scaled - rows * (scale * scale * scale) * mean
        out[:, cols] = total.astype(bf16)


def token_rows(x, grad, gain, inv, left, right, after=()):
    return call(
        rows_kernel,
        sds((ROWS, WIDTH), bf16),
        vmem=4,
        nbytes=6 * ROWS * WIDTH * 2,
        in_specs=[VMEM] * 10 + [ANY] * len(after),
        out_specs=VMEM,
        name="token_rows",
    )(x, grad, gain, inv, *left, *right, *after)


def key_value_kernel(*refs):
    pieces, weight = refs[:6], refs[6]
    full, out, buffer, sems = refs[-4:]
    copies = [
        load(k_cuts(weight.at[part + 1]), k_cuts(buffer.at[part]), sems.at[part])
        for part in range(2)
    ]
    place_pieces(pieces, full)
    for part in range(2):
        out[part] = dot_loaded(full, buffer.at[part], copies[part]).astype(bf16)


def key_value(pieces, weights, after):
    return call(
        key_value_kernel,
        [sds((SLOTS, WIDTH), bf16), sds((2, SLOTS, COLS), bf16)],
        vmem=20,
        flops=4 * SLOTS * WIDTH * COLS,
        nbytes=2 * WIDTH * COLS * 2 + 2 * SLOTS * WIDTH * 2,
        in_specs=[VMEM] * 6 + [HBM] + [ANY] * len(after),
        out_specs=[VMEM] * 2,
        scratch_shapes=[
            pltpu.VMEM((2, WIDTH, COLS), bf16),
            pltpu.SemaphoreType.DMA((2, KCUTS)),
        ],
        name="key_value",
    )(*pieces, weights, *after)


def query_kernel(full, weight, *refs):
    out, buffer, sems = refs[-3:]
    copies = load(k_cuts(weight.at[0]), k_cuts(buffer), sems)
    out[...] = dot_loaded(full, buffer, copies).astype(bf16)


DOT_SCRATCH = [pltpu.VMEM((WIDTH, COLS), bf16), pltpu.SemaphoreType.DMA((KCUTS,))]


def query_of(full, weights, after):
    return call(
        query_kernel,
        sds((SLOTS, COLS), bf16),
        vmem=12,
        flops=2 * SLOTS * WIDTH * COLS,
        nbytes=WIDTH * COLS * 2 + SLOTS * WIDTH * 2,
        in_specs=[VMEM, HBM] + [ANY] * len(after),
        out_specs=VMEM,
        scratch_shapes=DOT_SCRATCH,
        name="query",
    )(full, weights, *after)


def grad_mixed_kernel(p0, p1, p2, p3, weight, *refs):
    full, out, buffer, sems = refs[-4:]
    copies = load(k_cuts(weight.at[0]), k_cuts(buffer), sems)
    for slot, pair in enumerate((p0, p1, p2, p3)):
        full[pl.ds(slot * ROWS, ROWS)] = pair[0]
        full[pl.ds((4 + slot) * ROWS, ROWS)] = pair[1]
    out[...] = dot_loaded(full, buffer, copies).astype(bf16)


def grad_mixed_of(pairs, weights, after):
    return call(
        grad_mixed_kernel,
        [sds((SLOTS, WIDTH), bf16), sds((SLOTS, COLS), bf16)],
        vmem=16,
        flops=2 * SLOTS * WIDTH * COLS,
        nbytes=WIDTH * COLS * 2 + 2 * SLOTS * WIDTH * 2,
        in_specs=[VMEM] * 4 + [HBM] + [ANY] * len(after),
        out_specs=[VMEM] * 2,
        scratch_shapes=DOT_SCRATCH,
        name="grad_mixed",
    )(*pairs, weights, *after)


def gain_rows_of(left, right):
    row = lax.broadcasted_iota(jnp.int32, (16, left.shape[1]), 0)
    rows = jnp.zeros((16, left.shape[1]), f32)
    for first, part in ((0, left), (2, right)):
        high = part.astype(bf16).astype(f32)
        rows = jnp.where(row == first, high, rows)
        rows = jnp.where(row == first + 1, part - high, rows)
    return rows.astype(bf16)


def gain_from(rows):
    rows = rows.astype(f32)
    return rows[0:1] + rows[1:2], rows[2:3] + rows[3:4]


FCUT = 512
FCUTS = HALF // FCUT


def back_products(grads, weight, first, normed, buffer, sems):
    copies = [
        load(
            [weight.at[part, pl.ds(first + cut * FCUT, FCUT)] for part in range(3)],
            [buffer.at[part, pl.ds(cut * FCUT, FCUT)] for part in range(3)],
            sems.at[cut],
        )
        for cut in range(FCUTS)
    ]
    for cut in range(FCUTS):
        for copy in copies[cut]:
            copy.wait()
        rows = slice(cut * FCUT, (cut + 1) * FCUT)
        total = dot_rows(grads[0], buffer[0, rows])
        for part in range(1, 3):
            total = total + dot_rows(grads[part], buffer[part, rows])
        rounded = total.astype(bf16)
        terms = normed[:, first + cut * FCUT:first + (cut + 1) * FCUT].astype(f32)
        gain = jnp.sum(rounded.astype(f32) * terms, axis=0, keepdims=True)
        yield rows, rounded, gain


def back_right_kernel(waits, grads, weight, normed, *refs):
    own, sent, gain, buffer, sems = refs[waits:]
    for cols, rounded, terms in back_products(
        grads, weight, HALF, normed, buffer, sems
    ):
        gain[:, cols] = terms
        for xbit, out in enumerate((own, sent)):
            for slot in range(4):
                start = (xbit * 4 + slot) * ROWS
                out[slot, :, cols] = rounded[start:start + ROWS]


def back_left_kernel(waits, grads, weight, normed, gain_right, *refs):
    outs, far, buffer, sems = refs[waits:waits + 3], refs[-4:-2], refs[-2], refs[-1]
    for cols, rounded, terms in back_products(
        grads, weight, 0, normed, buffer, sems
    ):
        gains = gain_rows_of(terms, gain_right[:, cols])
        for slot, out in enumerate(outs):
            for xbit in range(2):
                start = (xbit * 4 + slot) * ROWS
                out[2 * xbit, :, cols] = rounded[start:start + 16]
                out[2 * xbit + 1, :, cols] = rounded[start + 16:start + ROWS]
            out[4, :, cols] = gains
        for xbit, out in enumerate(far):
            start = (xbit * 4 + 3) * ROWS
            out[0, :, cols] = rounded[start:start + 16]
            out[1, :, cols] = rounded[start + 16:start + ROWS]
        far[0][2, :, cols] = gains


def back_dot(kernel, grads, weights, normed, extra, out_shape, after, name):
    return call(
        functools.partial(kernel, len(after)),
        out_shape,
        vmem=20,
        flops=2 * 3 * SLOTS * HALF * COLS,
        nbytes=3 * HALF * COLS * 2 + 2 * SLOTS * HALF * 2,
        in_specs=[VMEM, HBM, VMEM] + [VMEM] * len(extra) + [ANY] * len(after),
        out_specs=[VMEM] * len(out_shape),
        scratch_shapes=[
            pltpu.VMEM((3, HALF, COLS), bf16),
            pltpu.SemaphoreType.DMA((FCUTS, 3)),
        ],
        name=name,
    )(grads, weights, normed, *extra, *after)


def back_right(grads, weights, normed, after=()):
    out = [sds((4, ROWS, HALF), bf16)] * 2 + [sds((1, HALF), f32)]
    return back_dot(back_right_kernel, grads, weights, normed, [], out, after, "back_right")


def back_left(grads, weights, normed, gain_right, after=()):
    out = [sds((5, 16, HALF), bf16)] * 3
    out += [sds((3, 16, HALF), bf16), sds((2, 16, HALF), bf16)]
    return back_dot(back_left_kernel, grads, weights, normed, [gain_right], out, after, "back_left")


def proj_kernel(left, weight, *refs):
    outs, buffer, sems = refs[-6:-2], refs[-2], refs[-1]
    copies = load(k_cuts(weight.at[0]), k_cuts(buffer), sems)
    for cut, copy in enumerate(copies):
        copy.wait()
        cols = slice(cut * KCUT, (cut + 1) * KCUT)
        rounded = dot_rows(left[...], buffer[cols]).astype(bf16)
        for slot in range(4):
            for xbit in range(2):
                start = (xbit * 4 + slot) * ROWS
                outs[slot][xbit, :, cols] = rounded[start:start + ROWS]


def proj_parts(mixed, weights, after):
    return call(
        proj_kernel,
        [sds((2, ROWS, WIDTH), bf16)] * 4,
        vmem=14,
        flops=2 * SLOTS * WIDTH * COLS,
        nbytes=WIDTH * COLS * 2 + SLOTS * WIDTH * 2,
        in_specs=[VMEM, HBM] + [ANY] * len(after),
        out_specs=[VMEM] * 4,
        scratch_shapes=DOT_SCRATCH,
        name="proj_parts",
    )(mixed, weights, *after)


def slot_of(row, x_index, z_index):
    block = row // ROWS
    xbit = block // 4
    slot = block - xbit * 4
    back = jnp.where(slot == 2, 3, jnp.where(slot == 3, 2, slot))
    x_from = jnp.where(xbit == 0, x_index, 1 - x_index)
    z_from = z_index - back
    z_from = jnp.where(z_from < 0, z_from + 4, z_from)
    return (x_from * 4 + z_from) * ROWS + (row - block * ROWS)


def places(gaps, runs, rows, is_text):
    x_index, z_index = where_am_i()[:2]
    slot = slot_of(rows, x_index, z_index)
    text = slot
    end = jnp.int32(0)
    for run in range(4):
        end = end + gaps[0, run]
        text = text + jnp.where(slot >= end, runs[0, run], 0)
    image = slot + gaps[0, 0]
    end = jnp.int32(0)
    for run in range(3):
        end = end + runs[0, run]
        image = image + jnp.where(slot >= end, gaps[0, run + 1], 0)
    image = jnp.where(slot < LI, image, FAR)
    return jnp.where(is_text, text, image)


def admitted(gaps, runs):
    group = lax.axis_index("grp")
    rows = lax.broadcasted_iota(jnp.int32, (SLOTS, 1), 0)
    query = places(gaps, runs, rows, group == 0)
    key_row = lax.broadcasted_iota(jnp.int32, (1, SLOTS), 1)
    own = places(gaps, runs, key_row, group == 0)
    other = places(gaps, runs, key_row, group != 0)
    return own <= query, other <= query


def head_attn(query, own_key, other_key, own_ok, other_ok):
    scale = HS ** (-0.5)
    own = jnp.where(own_ok, dot_rows(query, own_key) * scale, -1e30)
    other = jnp.where(other_ok, dot_rows(query, other_key) * scale, -1e30)
    row_max = jnp.maximum(
        jnp.max(own, axis=1, keepdims=True), jnp.max(other, axis=1, keepdims=True)
    )
    own = jnp.exp(own - row_max)
    other = jnp.exp(other - row_max)
    row_sum = jnp.sum(own, axis=1, keepdims=True) + jnp.sum(other, axis=1, keepdims=True)
    share = 1.0 / row_sum
    return own * share, other * share


def forward_kernel(gaps, runs, query, own_kv, other_kv, *refs):
    mixed = refs[-1]
    own_ok, other_ok = admitted(gaps, runs)
    for head in range(HEADS):
        cols = slice(head * HS, (head + 1) * HS)
        own, other = head_attn(
            query[:, cols], own_kv[0, :, cols], other_kv[0, :, cols], own_ok, other_ok
        )
        total = dot(own.astype(bf16), own_kv[1, :, cols])
        total = total + dot(other.astype(bf16), other_kv[1, :, cols])
        mixed[:, cols] = total.astype(bf16)


def backward_kernel(gaps, runs, query, own_kv, other_kv, mixed, grad, *refs):
    q_grad, own_grad, other_grad = refs[-3:]
    scale = HS ** (-0.5)
    own_ok, other_ok = admitted(gaps, runs)
    for head in range(HEADS):
        cols = slice(head * HS, (head + 1) * HS)
        q, g = query[:, cols], grad[:, cols]
        row_dot = jnp.sum(g.astype(f32) * mixed[:, cols].astype(f32), axis=1, keepdims=True)
        attns = head_attn(q, own_kv[0, :, cols], other_kv[0, :, cols], own_ok, other_ok)
        dq = None
        for attn, kv, kv_grad in zip(attns, (own_kv, other_kv), (own_grad, other_grad)):
            value_grad = dot_tokens(attn.astype(bf16), g)
            weight_grad = dot_rows(g, kv[1, :, cols])
            score_grad = (attn * (weight_grad - row_dot)).astype(bf16)
            part = dot(score_grad, kv[0, :, cols])
            dq = part if dq is None else dq + part
            key_grad = dot_tokens(score_grad, q) * scale
            kv_grad[0, :, cols] = key_grad.astype(kv_grad.dtype)
            kv_grad[1, :, cols] = value_grad.astype(kv_grad.dtype)
        q_grad[:, cols] = (dq * scale).astype(bf16)


ATTN_FLOPS = 2 * HEADS * SLOTS * 2 * SLOTS * HS


def attend_forward(spans, query, own_kv, other_kv, after):
    return call(
        forward_kernel,
        sds((SLOTS, COLS), bf16),
        vmem=10,
        flops=4 * ATTN_FLOPS,
        nbytes=6 * SLOTS * COLS * 2,
        in_specs=[SMEM] * 2 + [VMEM] * 3 + [ANY] * len(after),
        out_specs=VMEM,
        name="attend_forward",
    )(*spans, query, own_kv, other_kv, *after)


def attend_backward(spans, query, own_kv, other_kv, mixed, grad, after):
    kv = (2, SLOTS, COLS)
    return call(
        backward_kernel,
        [sds((SLOTS, COLS), bf16), sds(kv, f32), sds(kv, bf16)],
        vmem=14,
        flops=8 * ATTN_FLOPS,
        nbytes=12 * SLOTS * COLS * 2,
        in_specs=[SMEM] * 2 + [VMEM] * 5 + [ANY] * len(after),
        out_specs=[VMEM] * 3,
        name="attend_backward",
    )(*spans, query, own_kv, other_kv, mixed, grad, *after)


def out_kernel(grad, mixed, *refs):
    own, sent = refs[-2:]
    y_index, core = where_am_i()[2:4]
    for i in range(8):
        column = ((y_index - STEPS[i % 4]) & 3) * 2 + (1 - core if i < 4 else core)
        start = pl.multiple_of(column * COLS, COLS)
        share = dot_tokens(grad[:, pl.ds(start, COLS)], mixed[...]).astype(bf16)
        if i < 4:
            sent[i] = share
        else:
            own[i - 4] = share


def out_weight_parts(grad_full, mixed, after):
    return call(
        out_kernel,
        [sds((4, COLS, COLS), bf16)] * 2,
        vmem=12,
        flops=2 * SLOTS * WIDTH * COLS,
        nbytes=SLOTS * WIDTH * 2 + WIDTH * COLS * 2,
        in_specs=[VMEM] * 2 + [ANY] * len(after),
        out_specs=[VMEM] * 2,
        name="out_weight_parts",
    )(grad_full, mixed, *after)


def share_kernel(which, full, c1, c2, c3, g0, g1, g2, g3, g4, *refs):
    out, lefts = refs[-2:]
    y_index, core = where_am_i()[2:4]
    column = core if which else 1 - core
    start = pl.multiple_of((y_index * 2 + column) * COLS, COLS)
    lefts[0] = full[:, pl.ds(start, COLS)].T
    start = pl.multiple_of(column * COLS, COLS)
    for k, came in enumerate((c1, c2, c3), 1):
        lefts[k] = came[:, pl.ds(start, COLS)].T
    for part in range(3):
        total = dot(lefts[0], g0[part])
        for k, grad in enumerate((g1, g2), 1):
            total = total + dot(lefts[k], grad[part])
        total = total + dot(lefts[3, :, :SLOTS // 2], g3[part])
        total = total + dot(lefts[3, :, SLOTS // 2:], g4[part])
        out[part] = total.astype(out.dtype)


def weight_shares(which, full, came, grads, dtype, after=()):
    return call(
        functools.partial(share_kernel, which),
        sds((3, COLS, COLS), dtype),
        vmem=20,
        flops=3 * 4 * 2 * SLOTS * COLS * COLS,
        nbytes=16 * SLOTS * COLS * 2 + 3 * COLS * COLS * 4,
        in_specs=[VMEM] * 9 + [ANY] * len(after),
        out_specs=VMEM,
        scratch_shapes=[pltpu.VMEM((4, COLS, SLOTS), bf16)],
        name="weight_shares",
    )(full, *came, *grads, *after)


def chunk_kernel(full, *outs):
    y_index = where_am_i()[2]
    for k, out in zip(STEPS[1:], outs):
        start = pl.multiple_of(((y_index + k) & 3) * 1024, 1024)
        out[...] = full[:, pl.ds(start, 1024)]


def chunks_over_y(full):
    sends = call(
        chunk_kernel,
        [sds((SLOTS, 1024), bf16)] * 3,
        vmem=6,
        nbytes=6 * SLOTS * 1024 * 2,
        in_specs=[VMEM],
        out_specs=[VMEM] * 3,
        name="chunks",
    )(full)
    return [lax.ppermute(sent, "seq", y_shift(k)) for sent, k in zip(sends, STEPS[1:])]


def layer_kernel(x, kept, came, *refs):
    total = x[...].astype(f32) + (kept[...] + came[...].astype(f32))
    refs[-1][...] = (total * valid_rows()).astype(bf16)


def layer_rows(x, kept, came, after=()):
    return call(
        layer_kernel,
        sds((ROWS, WIDTH), bf16),
        vmem=4,
        nbytes=5 * ROWS * WIDTH * 2,
        in_specs=[VMEM] * 3 + [ANY] * len(after),
        out_specs=VMEM,
        name="layer_rows",
    )(x, kept, came, *after)


def per_device(tokens, text_gaps, image_runs, gains, w_qkv, w_out, cotangent):
    x_rows = tokens[0, 0]
    w_parts = jnp.transpose(w_qkv[0], (1, 0, 2))
    spans = (text_gaps, image_runs)

    n_left, n_right, grad_rows, inv = norm_rows(x_rows, gains, cotangent[0, 0])
    pieces = gather_blocks(n_left, n_right)
    grad_other = lax.ppermute(grad_rows, "tp", X_SWAP)
    grad_pair = touch(jnp.stack([grad_rows, grad_other]), w_parts)
    grad_pairs = [grad_pair] + [lax.ppermute(grad_pair, "tp", z_shift(k)) for k in STEPS[1:]]
    normed_full, own_kv = key_value(pieces, w_parts, [grad_pair])
    other_kv = lax.ppermute(own_kv, "grp", GRP_SWAP)
    query = query_of(normed_full, w_parts, grad_pairs[1:3])
    chunks = chunks_over_y(normed_full)

    mixed = attend_forward(spans, query, own_kv, other_kv, [])
    proj = proj_parts(mixed, w_out, [])
    grad_full, grad_mixed = grad_mixed_of(grad_pairs, w_out, [proj[0]] + chunks[:2])
    q_grad, own_part, other_part = attend_backward(
        spans, query, own_kv, other_kv, mixed, grad_mixed, []
    )
    back = lax.ppermute(other_part, "grp", GRP_SWAP)
    sends = late(proj[1:3], [q_grad])
    proj_came = [lax.ppermute(v, "tp", z_shift(-k)) for v, k in zip(sends, STEPS[1:3])]
    out_own, out_sent = out_weight_parts(grad_full, mixed, [q_grad])
    out_came = lax.ppermute(out_sent, "seq", CORE_SWAP)
    own_grads = sum_keys(q_grad, own_part, back, sends[:1])
    back_grads = lax.ppermute(own_grads, "seq", y_shift(1))
    next_grads = lax.ppermute(own_grads, "seq", y_shift(3))

    right = back_right(own_grads, w_parts, normed_full, [out_came] + chunks[2:])
    right_x = lax.ppermute(right[1], "tp", X_SWAP)
    left = back_left(own_grads, w_parts, normed_full, right[2], proj_came[:2])
    left_far_a = lax.ppermute(left[3], "tp", z_shift(1))
    left_far_b = lax.ppermute(left[4], "tp", z_shift(3))
    left_back, left_forth = pass_left(left[1], left[2], left_far_a, left_far_b)
    left_came = [
        lax.ppermute(left_forth, "tp", z_shift(1)), lax.ppermute(left_back, "tp", z_shift(3))
    ]
    out_kept, *out_sends = sum_out(
        out_own, out_came, [left_back, back_grads, next_grads, right_x]
    )
    out_far_a = lax.ppermute(out_sends[2], "seq", y_shift(1))
    out_far_b = lax.ppermute(out_sends[3], "seq", y_shift(3))
    out_back, out_forth = pass_out(
        out_sends[0], out_sends[1], out_far_a, out_far_b
    )
    out_terms = [
        lax.ppermute(out_forth, "seq", y_shift(1)), lax.ppermute(out_back, "seq", y_shift(3))
    ]
    left_kept, left_sent, gain_kept = sum_left(left[0], left_came, [out_back])
    left_x = lax.ppermute(left_sent, "tp", X_SWAP)
    gain_tp = sum_gain(gain_kept, left_x, gains)
    gain_sum = gain_tp + lax.ppermute(gain_tp, "seq", CORE_SWAP)
    gain_grad = gain_sum
    for k in STEPS[1:]:
        gain_grad = gain_grad + lax.ppermute(gain_sum, "seq", y_shift(k))
    right_kept, *right_sends = sum_x(
        right[0], right_x, [left_sent]
    )
    right_came = [lax.ppermute(v, "tp", z_shift(-k)) for v, k in zip(right_sends, STEPS[1:])]
    (far_sent,) = late(proj[3:], right_came[:1])
    proj_came.append(lax.ppermute(far_sent, "tp", z_shift(2)))
    relayed = halves(
        back_grads, next_grads, [gain_tp, far_sent] + right_came[:2] + out_terms
    )
    grads = [own_grads, back_grads, next_grads]
    grads += [lax.ppermute(v, "seq", y_shift(k)) for v, k in zip(relayed, (1, 3))]
    shares = (normed_full, chunks, grads)
    qkv_sent = weight_shares(0, *shares, bf16, [gain_sum])
    tokens_grad = token_rows(
        x_rows, grad_rows, gains, inv, (left_kept, left_x), (right_kept, *right_came)
    )

    qkv_mine = weight_shares(1, *shares, f32, [qkv_sent])
    qkv_share = qkv_mine + lax.ppermute(qkv_sent, "seq", CORE_SWAP).astype(f32)
    proj_kept, proj_sent = sum_z(proj[0], proj_came)
    proj_x = lax.ppermute(proj_sent, "tp", X_SWAP)
    layer_out = layer_rows(x_rows, proj_kept, proj_x, [qkv_mine])
    out_share = sum_rest(out_kept, out_terms, right_came[:1])
    return (
        layer_out[None, None],
        tokens_grad[None, None],
        gain_grad,
        jnp.transpose(qkv_share, (1, 0, 2))[None],
        out_share[None],
    )


def solution(mesh):
    in_specs = (
        P("grp", "seq", "tp", None),
        P("seq", None),
        P("seq", None),
        P("grp", None),
        P("grp", None, None, "tp"),
        P("grp", None, "tp"),
        P("grp", "seq", "tp", None),
    )
    out_specs = (
        P("grp", "seq", "tp", None),
        P("grp", "seq", "tp", None),
        P("grp", None),
        P("grp", "seq", None, "tp"),
        P("grp", "seq", "tp"),
    )
    return jax.shard_map(
        per_device, mesh=mesh, in_specs=in_specs, out_specs=out_specs, check_vma=False
    )
```

```python
import functools

import jax
import jax.numpy as jnp
from jax import lax
from jax.experimental import pallas as pl
from jax.experimental.pallas import tpu as pltpu
from jax.sharding import PartitionSpec as P

HS = 128
LI = 128
HEADS = 4
SLOTS = 256
ROWS = 32
WIDTH = 4096
HALF = 2048
COLS = 512
FAR = 1073741824
f32 = jnp.float32
bf16 = jnp.bfloat16
MIB = 1024 * 1024

STEPS = (0, 1, 3, 2)


def z_shift(k):
    return [(i, (i // 4) * 4 + (i + k) % 4) for i in range(8)]


X_SWAP = [(i, i ^ 4) for i in range(8)]


def y_shift(k):
    return [(i, (i + 2 * k) % 8) for i in range(8)]


CORE_SWAP = [(i, i ^ 1) for i in range(8)]
GRP_SWAP = [(0, 1), (1, 0)]


def sds(shape, dtype):
    return jax.ShapeDtypeStruct(shape, dtype)


def call(kernel, out_shape, vmem, flops=0, nbytes=0, **kwargs):
    return pl.pallas_call(
        kernel,
        out_shape=out_shape,
        compiler_params=pltpu.CompilerParams(vmem_limit_bytes=vmem * MIB),
        cost_estimate=pl.CostEstimate(flops=flops, bytes_accessed=nbytes, transcendentals=0),
        **kwargs,
    )


def whole(shape):
    return pl.BlockSpec(shape, lambda *_: (0,) * len(shape))


SMEM = pl.BlockSpec(memory_space=pltpu.SMEM)
VMEM = pl.BlockSpec(memory_space=pltpu.VMEM)
ANY = pl.BlockSpec(memory_space=pl.ANY)
HBM = pl.BlockSpec(memory_space=pltpu.HBM)


def dot(left, right):
    return jnp.dot(left, right, preferred_element_type=f32)


def dot_rows(left, right):
    return lax.dot_general(left, right, (((1,), (1,)), ((), ())), preferred_element_type=f32)


def dot_tokens(left, right):
    return lax.dot_general(left, right, (((0,), (0,)), ((), ())), preferred_element_type=f32)


def where_am_i():
    tp, seq = lax.axis_index("tp"), lax.axis_index("seq")
    return tp >> 2, tp & 3, seq >> 1, seq & 1, lax.axis_index("grp")


def valid_rows():
    used = jnp.logical_or(lax.axis_index("grp") == 0, lax.axis_index("tp") * ROWS < LI)
    return jnp.where(used, 1.0, 0.0).astype(f32)


def load(sources, targets, sems):
    copies = [
        pltpu.make_async_copy(source, target, sems.at[i])
        for i, (source, target) in enumerate(zip(sources, targets))
    ]
    for copy in copies:
        copy.start()
    return copies


KCUT = 1024
KCUTS = WIDTH // KCUT


def dot_loaded(full, buffer, copies):
    total = None
    for i, copy in enumerate(copies):
        copy.wait()
        cut = slice(i * KCUT, (i + 1) * KCUT)
        part = dot(full[:, cut], buffer[cut])
        total = part if total is None else total + part
    return total


def k_cuts(ref):
    return [ref.at[pl.ds(i * KCUT, KCUT)] for i in range(KCUTS)]


def touch_kernel(weight, pair, *refs):
    refs[-1][...] = pair[...]


def touch(pair, weight):
    return call(
        touch_kernel,
        sds(pair.shape, pair.dtype),
        vmem=4,
        nbytes=pair.size * 4,
        in_specs=[ANY, VMEM],
        out_specs=VMEM,
        name="touch",
    )(weight, pair)


def norm_kernel(x, gain, cot, n_left, n_right, grad, inv):
    x_float = x[...].astype(f32)
    scale = lax.rsqrt(jnp.mean(x_float * x_float, axis=1, keepdims=True) + 1e-05)
    normed = (x_float * scale * gain[...].astype(f32)).astype(bf16)
    n_left[...] = normed[:, :HALF]
    n_right[...] = normed[:, HALF:]
    grad[...] = (cot[...].astype(f32) * valid_rows()).astype(bf16)
    inv[...] = jnp.broadcast_to(scale, (ROWS, 128))


def norm_rows(x, gain, cot):
    part = sds((ROWS, HALF), bf16)
    return call(
        norm_kernel,
        [part, part, sds((ROWS, WIDTH), bf16), sds((ROWS, 128), f32)],
        vmem=4,
        nbytes=4 * ROWS * WIDTH * 2,
        in_specs=[VMEM] * 3,
        name="norm_rows",
    )(x, gain, cot)


def gather_blocks(left, right):
    right_pair = jnp.stack([right, lax.ppermute(right, "tp", X_SWAP)])
    left_four = [left] + [lax.ppermute(left, "tp", z_shift(k)) for k in STEPS[1:]]
    right_four = [right_pair] + [lax.ppermute(right_pair, "tp", z_shift(k)) for k in STEPS[1:]]
    left_own = jnp.stack(left_four)
    left_other = lax.ppermute(left_own, "tp", X_SWAP)
    return [left_own, left_other] + right_four


def place_pieces(pieces, whole_ref):
    left_own, left_other = pieces[:2]
    for slot in range(4):
        rows = pl.ds(slot * ROWS, ROWS)
        other = pl.ds((4 + slot) * ROWS, ROWS)
        whole_ref[rows, :HALF] = left_own[slot]
        whole_ref[other, :HALF] = left_other[slot]
        whole_ref[rows, HALF:] = pieces[2 + slot][0]
        whole_ref[other, HALF:] = pieces[2 + slot][1]


PIECE_SHAPES = [(4, ROWS, HALF)] * 2 + [(2, ROWS, HALF)] * 4


def sum_z_kernel(own, c1, c2, c3, *refs):
    kept, sent = refs[-2:]
    total = own[...].astype(f32)
    for came in (c1, c2, c3):
        total = total + came[...].astype(f32)
    kept[...] = total[0]
    sent[...] = total[1].astype(bf16)


def sum_z(own, came, after=()):
    shape = own.shape[1:]
    return call(
        sum_z_kernel,
        [sds(shape, f32), sds(shape, bf16)],
        vmem=6,
        nbytes=11 * shape[0] * shape[1] * 2,
        in_specs=[VMEM] * 4 + [ANY] * len(after),
        out_specs=[VMEM] * 2,
        name="sum_z",
    )(own, *came, *after)


def sum_left_kernel(own, c1, c2, *refs):
    kept, sent, gain = refs[-3:]
    for part in range(2):
        total = own[part].astype(f32)
        for came in (c1, c2):
            total = total + came[part].astype(f32)
        kept[pl.ds(part * 16, 16)] = total
        total = own[2 + part].astype(f32)
        for came in (c1, c2):
            total = total + came[2 + part].astype(f32)
        sent[part] = total.astype(bf16)
    left, right = gain_from(own[4])
    for came in (c1, c2):
        more_left, more_right = gain_from(came[4])
        left, right = left + more_left, right + more_right
    sent[2] = gain_rows_of(left, right)
    gain[0:1] = left
    gain[1:2] = right


def sum_left(own, came, after=()):
    return call(
        sum_left_kernel,
        [sds((ROWS, HALF), f32), sds((3, 16, HALF), bf16), sds((2, HALF), f32)],
        vmem=4,
        nbytes=11 * ROWS * HALF * 2,
        in_specs=[VMEM] * 3 + [ANY] * len(after),
        out_specs=[VMEM] * 3,
        name="sum_left",
    )(own, *came, *after)


def sum_gain_kernel(own, came, gain, out):
    left, right = gain_from(came[2])
    out[:, :HALF] = (own[0:1] + left) / gain[:, :HALF].astype(f32)
    out[:, HALF:] = (own[1:2] + right) / gain[:, HALF:].astype(f32)


def sum_gain(own, came, gain):
    return call(
        sum_gain_kernel,
        sds((1, WIDTH), f32),
        vmem=2,
        nbytes=10 * WIDTH * 2,
        in_specs=[VMEM] * 3,
        out_specs=VMEM,
        name="sum_gain",
    )(own, came, gain)


def pass_left_kernel(back, forth, far_a, far_b, *refs):
    out_back, out_forth = refs[-2:]
    out_forth[...] = forth[...]
    out_back[...] = back[...]
    for part in range(2):
        out_forth[part] = (forth[part].astype(f32) + far_a[part].astype(f32)).astype(bf16)
        total = back[2 + part].astype(f32) + far_b[part].astype(f32)
        out_back[2 + part] = total.astype(bf16)
    left, right = gain_from(forth[4])
    more_left, more_right = gain_from(far_a[2])
    out_forth[4] = gain_rows_of(left + more_left, right + more_right)


def pass_left(back, forth, far_a, far_b, after=()):
    return call(
        pass_left_kernel,
        [sds(back.shape, bf16)] * 2,
        vmem=6,
        nbytes=6 * back.size * 2,
        in_specs=[VMEM] * 4 + [ANY] * len(after),
        out_specs=[VMEM] * 2,
        name="pass_left",
    )(back, forth, far_a, far_b, *after)


def pass_out_kernel(back, forth, far_a, far_b, *refs):
    out_back, out_forth = refs[-2:]
    half = COLS // 2
    out_forth[half:] = forth[half:]
    out_forth[:half] = (forth[:half].astype(f32) + far_a[...].astype(f32)).astype(bf16)
    out_back[:half] = back[:half]
    out_back[half:] = (back[half:].astype(f32) + far_b[...].astype(f32)).astype(bf16)


def pass_out(back, forth, far_a, far_b, after=()):
    return call(
        pass_out_kernel,
        [sds(back.shape, bf16)] * 2,
        vmem=6,
        nbytes=6 * back.size * 2,
        in_specs=[VMEM] * 4 + [ANY] * len(after),
        out_specs=[VMEM] * 2,
        name="pass_out",
    )(back, forth, far_a, far_b, *after)


def sum_out_kernel(own, came, *refs):
    kept, back, forth, far_a, far_b = refs[-5:]
    half = COLS // 2

    def total(slot, rows=slice(None)):
        return own[slot, rows].astype(f32) + came[slot, rows].astype(f32)

    kept[...] = total(0)
    back[...] = total(1).astype(bf16)
    forth[...] = total(2).astype(bf16)
    far_a[...] = total(3, slice(0, half)).astype(bf16)
    far_b[...] = total(3, slice(half, COLS)).astype(bf16)


def sum_out(own, came, after=()):
    whole_share, half_share = sds((COLS, COLS), bf16), sds((COLS // 2, COLS), bf16)
    return call(
        sum_out_kernel,
        [sds((COLS, COLS), f32), whole_share, whole_share, half_share, half_share],
        vmem=12,
        nbytes=own.size * 6,
        in_specs=[VMEM] * 2 + [ANY] * len(after),
        out_specs=[VMEM] * 5,
        name="sum_out",
    )(own, came, *after)


def sum_x_kernel(waits, own, came, *refs):
    kept, sends = refs[waits], refs[waits + 1:]
    kept[...] = own[0].astype(f32) + came[0].astype(f32)
    for slot, sent in enumerate(sends, 1):
        sent[...] = (own[slot].astype(f32) + came[slot].astype(f32)).astype(bf16)


def sum_x(own, came, after=(), sends=3):
    shape = own.shape[1:]
    return call(
        functools.partial(sum_x_kernel, len(after)),
        [sds(shape, f32)] + [sds(shape, bf16)] * sends,
        vmem=12,
        nbytes=13 * shape[0] * shape[1] * 2,
        in_specs=[VMEM] * 2 + [ANY] * len(after),
        out_specs=[VMEM] * (1 + sends),
        name="sum_x",
    )(own, came, *after)


def halves_kernel(back, forth, *refs):
    half = SLOTS // 2
    refs[-2][...] = back[:, :half]
    refs[-1][...] = forth[:, half:]


def halves(back, forth, after):
    shape = (3, SLOTS // 2, COLS)
    return call(
        halves_kernel,
        [sds(shape, bf16)] * 2,
        vmem=6,
        nbytes=8 * back.size,
        in_specs=[VMEM] * 2 + [ANY] * len(after),
        out_specs=[VMEM] * 2,
        name="halves",
    )(back, forth, *after)


def late_kernel(count, *refs):
    for i in range(count):
        refs[i - count][...] = refs[i][...]


def late(arrays, after):
    count = len(arrays)
    return call(
        functools.partial(late_kernel, count),
        [sds(v.shape, v.dtype) for v in arrays],
        vmem=10,
        nbytes=sum(v.size * 4 for v in arrays),
        in_specs=[VMEM] * count + [ANY] * len(after),
        out_specs=[VMEM] * count,
        name="late",
    )(*arrays, *after)


def sum_rest_kernel(kept, c1, c2, *refs):
    total = kept[...]
    for came in (c1, c2):
        total = total + came[...].astype(f32)
    refs[-1][...] = total


def sum_rest(kept, came, after=()):
    return call(
        sum_rest_kernel,
        sds(kept.shape, f32),
        vmem=6,
        nbytes=14 * kept.size,
        in_specs=[VMEM] * 3 + [ANY] * len(after),
        out_specs=VMEM,
        name="sum_rest",
    )(kept, *came, *after)


def sum_keys_kernel(q_grad, own, came, *refs):
    out = refs[-1]
    out[0] = q_grad[...]
    out[1:] = (own[...] + came[...].astype(f32)).astype(bf16)


def sum_keys(q_grad, own, came, after=()):
    return call(
        sum_keys_kernel,
        sds((3, SLOTS, COLS), bf16),
        vmem=8,
        nbytes=10 * came.size,
        in_specs=[VMEM] * 3 + [ANY] * len(after),
        out_specs=VMEM,
        name="sum_keys",
    )(q_grad, own, came, *after)


def rows_kernel(x, grad, gain, inv, l_kept, l_came, r_kept, r1, r2, r3, *refs):
    out = refs[-1]
    left = l_kept[...] + l_came[0:2].reshape(ROWS, HALF).astype(f32)
    right = r_kept[...]
    for came in (r1, r2, r3):
        right = right + came[...].astype(f32)
    scale = inv[:, :1]
    halves = []
    dots = jnp.zeros((ROWS, 1), f32)
    for part, cols in ((left, slice(0, HALF)), (right, slice(HALF, WIDTH))):
        scaled = gain[:, cols].astype(f32) * part
        rows = x[:, cols].astype(f32)
        dots = dots + jnp.sum(scaled * rows, axis=1, keepdims=True)
        halves.append((scaled, rows, cols))
    mean = dots * (1.0 / WIDTH)
    for scaled, rows, cols in halves:
        total = grad[:, cols].astype(f32) + scale * scaled - rows * (scale * scale * scale) * mean
        out[:, cols] = total.astype(bf16)


def token_rows(x, grad, gain, inv, left, right, after=()):
    return call(
        rows_kernel,
        sds((ROWS, WIDTH), bf16),
        vmem=4,
        nbytes=6 * ROWS * WIDTH * 2,
        in_specs=[VMEM] * 10 + [ANY] * len(after),
        out_specs=VMEM,
        name="token_rows",
    )(x, grad, gain, inv, *left, *right, *after)


def key_value_kernel(*refs):
    pieces, weight = refs[:6], refs[6]
    full, out, buffer, sems = refs[-4:]
    copies = [
        load(k_cuts(weight.at[part + 1]), k_cuts(buffer.at[part]), sems.at[part])
        for part in range(2)
    ]
    place_pieces(pieces, full)
    for part in range(2):
        out[part] = dot_loaded(full, buffer.at[part], copies[part]).astype(bf16)


def key_value(pieces, weights, after):
    return call(
        key_value_kernel,
        [sds((SLOTS, WIDTH), bf16), sds((2, SLOTS, COLS), bf16)],
        vmem=20,
        flops=4 * SLOTS * WIDTH * COLS,
        nbytes=2 * WIDTH * COLS * 2 + 2 * SLOTS * WIDTH * 2,
        in_specs=[VMEM] * 6 + [HBM] + [ANY] * len(after),
        out_specs=[VMEM] * 2,
        scratch_shapes=[
            pltpu.VMEM((2, WIDTH, COLS), bf16),
            pltpu.SemaphoreType.DMA((2, KCUTS)),
        ],
        name="key_value",
    )(*pieces, weights, *after)


def query_kernel(full, weight, *refs):
    out, buffer, sems = refs[-3:]
    copies = load(k_cuts(weight.at[0]), k_cuts(buffer), sems)
    out[...] = dot_loaded(full, buffer, copies).astype(bf16)


DOT_SCRATCH = [pltpu.VMEM((WIDTH, COLS), bf16), pltpu.SemaphoreType.DMA((KCUTS,))]


def query_of(full, weights, after):
    return call(
        query_kernel,
        sds((SLOTS, COLS), bf16),
        vmem=12,
        flops=2 * SLOTS * WIDTH * COLS,
        nbytes=WIDTH * COLS * 2 + SLOTS * WIDTH * 2,
        in_specs=[VMEM, HBM] + [ANY] * len(after),
        out_specs=VMEM,
        scratch_shapes=DOT_SCRATCH,
        name="query",
    )(full, weights, *after)


def grad_mixed_kernel(p0, p1, p2, p3, weight, *refs):
    full, out, buffer, sems = refs[-4:]
    copies = load(k_cuts(weight.at[0]), k_cuts(buffer), sems)
    for slot, pair in enumerate((p0, p1, p2, p3)):
        full[pl.ds(slot * ROWS, ROWS)] = pair[0]
        full[pl.ds((4 + slot) * ROWS, ROWS)] = pair[1]
    out[...] = dot_loaded(full, buffer, copies).astype(bf16)


def grad_mixed_of(pairs, weights, after):
    return call(
        grad_mixed_kernel,
        [sds((SLOTS, WIDTH), bf16), sds((SLOTS, COLS), bf16)],
        vmem=16,
        flops=2 * SLOTS * WIDTH * COLS,
        nbytes=WIDTH * COLS * 2 + 2 * SLOTS * WIDTH * 2,
        in_specs=[VMEM] * 4 + [HBM] + [ANY] * len(after),
        out_specs=[VMEM] * 2,
        scratch_shapes=DOT_SCRATCH,
        name="grad_mixed",
    )(*pairs, weights, *after)


def gain_rows_of(left, right):
    row = lax.broadcasted_iota(jnp.int32, (16, left.shape[1]), 0)
    rows = jnp.zeros((16, left.shape[1]), f32)
    for first, part in ((0, left), (2, right)):
        high = part.astype(bf16).astype(f32)
        rows = jnp.where(row == first, high, rows)
        rows = jnp.where(row == first + 1, part - high, rows)
    return rows.astype(bf16)


def gain_from(rows):
    rows = rows.astype(f32)
    return rows[0:1] + rows[1:2], rows[2:3] + rows[3:4]


FCUT = 512
FCUTS = HALF // FCUT


def back_products(grads, weight, first, normed, buffer, sems):
    copies = [
        load(
            [weight.at[part, pl.ds(first + cut * FCUT, FCUT)] for part in range(3)],
            [buffer.at[part, pl.ds(cut * FCUT, FCUT)] for part in range(3)],
            sems.at[cut],
        )
        for cut in range(FCUTS)
    ]
    for cut in range(FCUTS):
        for copy in copies[cut]:
            copy.wait()
        rows = slice(cut * FCUT, (cut + 1) * FCUT)
        total = dot_rows(grads[0], buffer[0, rows])
        for part in range(1, 3):
            total = total + dot_rows(grads[part], buffer[part, rows])
        rounded = total.astype(bf16)
        terms = normed[:, first + cut * FCUT:first + (cut + 1) * FCUT].astype(f32)
        gain = jnp.sum(rounded.astype(f32) * terms, axis=0, keepdims=True)
        yield rows, rounded, gain


def back_right_kernel(waits, grads, weight, normed, *refs):
    own, sent, gain, buffer, sems = refs[waits:]
    for cols, rounded, terms in back_products(
        grads, weight, HALF, normed, buffer, sems
    ):
        gain[:, cols] = terms
        for xbit, out in enumerate((own, sent)):
            for slot in range(4):
                start = (xbit * 4 + slot) * ROWS
                out[slot, :, cols] = rounded[start:start + ROWS]


def back_left_kernel(waits, grads, weight, normed, gain_right, *refs):
    outs, far, buffer, sems = refs[waits:waits + 3], refs[-4:-2], refs[-2], refs[-1]
    for cols, rounded, terms in back_products(
        grads, weight, 0, normed, buffer, sems
    ):
        gains = gain_rows_of(terms, gain_right[:, cols])
        for slot, out in enumerate(outs):
            for xbit in range(2):
                start = (xbit * 4 + slot) * ROWS
                out[2 * xbit, :, cols] = rounded[start:start + 16]
                out[2 * xbit + 1, :, cols] = rounded[start + 16:start + ROWS]
            out[4, :, cols] = gains
        for xbit, out in enumerate(far):
            start = (xbit * 4 + 3) * ROWS
            out[0, :, cols] = rounded[start:start + 16]
            out[1, :, cols] = rounded[start + 16:start + ROWS]
        far[0][2, :, cols] = gains


def back_dot(kernel, grads, weights, normed, extra, out_shape, after, name):
    return call(
        functools.partial(kernel, len(after)),
        out_shape,
        vmem=20,
        flops=2 * 3 * SLOTS * HALF * COLS,
        nbytes=3 * HALF * COLS * 2 + 2 * SLOTS * HALF * 2,
        in_specs=[VMEM, HBM, VMEM] + [VMEM] * len(extra) + [ANY] * len(after),
        out_specs=[VMEM] * len(out_shape),
        scratch_shapes=[
            pltpu.VMEM((3, HALF, COLS), bf16),
            pltpu.SemaphoreType.DMA((FCUTS, 3)),
        ],
        name=name,
    )(grads, weights, normed, *extra, *after)


def back_right(grads, weights, normed, after=()):
    out = [sds((4, ROWS, HALF), bf16)] * 2 + [sds((1, HALF), f32)]
    return back_dot(back_right_kernel, grads, weights, normed, [], out, after, "back_right")


def back_left(grads, weights, normed, gain_right, after=()):
    out = [sds((5, 16, HALF), bf16)] * 3
    out += [sds((3, 16, HALF), bf16), sds((2, 16, HALF), bf16)]
    return back_dot(back_left_kernel, grads, weights, normed, [gain_right], out, after, "back_left")


def proj_kernel(left, weight, *refs):
    outs, buffer, sems = refs[-6:-2], refs[-2], refs[-1]
    copies = load(k_cuts(weight.at[0]), k_cuts(buffer), sems)
    for cut, copy in enumerate(copies):
        copy.wait()
        cols = slice(cut * KCUT, (cut + 1) * KCUT)
        rounded = dot_rows(left[...], buffer[cols]).astype(bf16)
        for slot in range(4):
            for xbit in range(2):
                start = (xbit * 4 + slot) * ROWS
                outs[slot][xbit, :, cols] = rounded[start:start + ROWS]


def proj_parts(mixed, weights, after):
    return call(
        proj_kernel,
        [sds((2, ROWS, WIDTH), bf16)] * 4,
        vmem=14,
        flops=2 * SLOTS * WIDTH * COLS,
        nbytes=WIDTH * COLS * 2 + SLOTS * WIDTH * 2,
        in_specs=[VMEM, HBM] + [ANY] * len(after),
        out_specs=[VMEM] * 4,
        scratch_shapes=DOT_SCRATCH,
        name="proj_parts",
    )(mixed, weights, *after)


def slot_of(row, x_index, z_index):
    block = row // ROWS
    xbit = block // 4
    slot = block - xbit * 4
    back = jnp.where(slot == 2, 3, jnp.where(slot == 3, 2, slot))
    x_from = jnp.where(xbit == 0, x_index, 1 - x_index)
    z_from = z_index - back
    z_from = jnp.where(z_from < 0, z_from + 4, z_from)
    return (x_from * 4 + z_from) * ROWS + (row - block * ROWS)


def places(gaps, runs, rows, is_text):
    x_index, z_index = where_am_i()[:2]
    slot = slot_of(rows, x_index, z_index)
    text = slot
    end = jnp.int32(0)
    for run in range(4):
        end = end + gaps[0, run]
        text = text + jnp.where(slot >= end, runs[0, run], 0)
    image = slot + gaps[0, 0]
    end = jnp.int32(0)
    for run in range(3):
        end = end + runs[0, run]
        image = image + jnp.where(slot >= end, gaps[0, run + 1], 0)
    image = jnp.where(slot < LI, image, FAR)
    return jnp.where(is_text, text, image)


def admitted(gaps, runs):
    group = lax.axis_index("grp")
    rows = lax.broadcasted_iota(jnp.int32, (SLOTS, 1), 0)
    query = places(gaps, runs, rows, group == 0)
    key_row = lax.broadcasted_iota(jnp.int32, (1, SLOTS), 1)
    own = places(gaps, runs, key_row, group == 0)
    other = places(gaps, runs, key_row, group != 0)
    return own <= query, other <= query


def head_attn(query, own_key, other_key, own_ok, other_ok):
    scale = HS ** (-0.5)
    own = jnp.where(own_ok, dot_rows(query, own_key) * scale, -1e30)
    other = jnp.where(other_ok, dot_rows(query, other_key) * scale, -1e30)
    row_max = jnp.maximum(
        jnp.max(own, axis=1, keepdims=True), jnp.max(other, axis=1, keepdims=True)
    )
    own = jnp.exp(own - row_max)
    other = jnp.exp(other - row_max)
    row_sum = jnp.sum(own, axis=1, keepdims=True) + jnp.sum(other, axis=1, keepdims=True)
    share = 1.0 / row_sum
    return own * share, other * share


def forward_kernel(gaps, runs, query, own_kv, other_kv, *refs):
    mixed = refs[-1]
    own_ok, other_ok = admitted(gaps, runs)
    for head in range(HEADS):
        cols = slice(head * HS, (head + 1) * HS)
        own, other = head_attn(
            query[:, cols], own_kv[0, :, cols], other_kv[0, :, cols], own_ok, other_ok
        )
        total = dot(own.astype(bf16), own_kv[1, :, cols])
        total = total + dot(other.astype(bf16), other_kv[1, :, cols])
        mixed[:, cols] = total.astype(bf16)


def backward_kernel(gaps, runs, query, own_kv, other_kv, mixed, grad, *refs):
    q_grad, own_grad, other_grad = refs[-3:]
    scale = HS ** (-0.5)
    own_ok, other_ok = admitted(gaps, runs)
    for head in range(HEADS):
        cols = slice(head * HS, (head + 1) * HS)
        q, g = query[:, cols], grad[:, cols]
        row_dot = jnp.sum(g.astype(f32) * mixed[:, cols].astype(f32), axis=1, keepdims=True)
        attns = head_attn(q, own_kv[0, :, cols], other_kv[0, :, cols], own_ok, other_ok)
        dq = None
        for attn, kv, kv_grad in zip(attns, (own_kv, other_kv), (own_grad, other_grad)):
            value_grad = dot_tokens(attn.astype(bf16), g)
            weight_grad = dot_rows(g, kv[1, :, cols])
            score_grad = (attn * (weight_grad - row_dot)).astype(bf16)
            part = dot(score_grad, kv[0, :, cols])
            dq = part if dq is None else dq + part
            key_grad = dot_tokens(score_grad, q) * scale
            kv_grad[0, :, cols] = key_grad.astype(kv_grad.dtype)
            kv_grad[1, :, cols] = value_grad.astype(kv_grad.dtype)
        q_grad[:, cols] = (dq * scale).astype(bf16)


ATTN_FLOPS = 2 * HEADS * SLOTS * 2 * SLOTS * HS


def attend_forward(spans, query, own_kv, other_kv, after):
    return call(
        forward_kernel,
        sds((SLOTS, COLS), bf16),
        vmem=10,
        flops=4 * ATTN_FLOPS,
        nbytes=6 * SLOTS * COLS * 2,
        in_specs=[SMEM] * 2 + [VMEM] * 3 + [ANY] * len(after),
        out_specs=VMEM,
        name="attend_forward",
    )(*spans, query, own_kv, other_kv, *after)


def attend_backward(spans, query, own_kv, other_kv, mixed, grad, after):
    kv = (2, SLOTS, COLS)
    return call(
        backward_kernel,
        [sds((SLOTS, COLS), bf16), sds(kv, f32), sds(kv, bf16)],
        vmem=14,
        flops=8 * ATTN_FLOPS,
        nbytes=12 * SLOTS * COLS * 2,
        in_specs=[SMEM] * 2 + [VMEM] * 5 + [ANY] * len(after),
        out_specs=[VMEM] * 3,
        name="attend_backward",
    )(*spans, query, own_kv, other_kv, mixed, grad, *after)


def out_kernel(grad, mixed, *refs):
    own, sent = refs[-2:]
    y_index, core = where_am_i()[2:4]
    for i in range(8):
        column = ((y_index - STEPS[i % 4]) & 3) * 2 + (1 - core if i < 4 else core)
        start = pl.multiple_of(column * COLS, COLS)
        share = dot_tokens(grad[:, pl.ds(start, COLS)], mixed[...]).astype(bf16)
        if i < 4:
            sent[i] = share
        else:
            own[i - 4] = share


def out_weight_parts(grad_full, mixed, after):
    return call(
        out_kernel,
        [sds((4, COLS, COLS), bf16)] * 2,
        vmem=12,
        flops=2 * SLOTS * WIDTH * COLS,
        nbytes=SLOTS * WIDTH * 2 + WIDTH * COLS * 2,
        in_specs=[VMEM] * 2 + [ANY] * len(after),
        out_specs=[VMEM] * 2,
        name="out_weight_parts",
    )(grad_full, mixed, *after)


def share_kernel(which, full, c1, c2, c3, g0, g1, g2, g3, g4, *refs):
    out, lefts = refs[-2:]
    y_index, core = where_am_i()[2:4]
    column = core if which else 1 - core
    start = pl.multiple_of((y_index * 2 + column) * COLS, COLS)
    lefts[0] = full[:, pl.ds(start, COLS)].T
    start = pl.multiple_of(column * COLS, COLS)
    for k, came in enumerate((c1, c2, c3), 1):
        lefts[k] = came[:, pl.ds(start, COLS)].T
    for part in range(3):
        total = dot(lefts[0], g0[part])
        for k, grad in enumerate((g1, g2), 1):
            total = total + dot(lefts[k], grad[part])
        total = total + dot(lefts[3, :, :SLOTS // 2], g3[part])
        total = total + dot(lefts[3, :, SLOTS // 2:], g4[part])
        out[part] = total.astype(out.dtype)


def weight_shares(which, full, came, grads, dtype, after=()):
    return call(
        functools.partial(share_kernel, which),
        sds((3, COLS, COLS), dtype),
        vmem=20,
        flops=3 * 4 * 2 * SLOTS * COLS * COLS,
        nbytes=16 * SLOTS * COLS * 2 + 3 * COLS * COLS * 4,
        in_specs=[VMEM] * 9 + [ANY] * len(after),
        out_specs=VMEM,
        scratch_shapes=[pltpu.VMEM((4, COLS, SLOTS), bf16)],
        name="weight_shares",
    )(full, *came, *grads, *after)


def chunk_kernel(full, *outs):
    y_index = where_am_i()[2]
    for k, out in zip(STEPS[1:], outs):
        start = pl.multiple_of(((y_index + k) & 3) * 1024, 1024)
        out[...] = full[:, pl.ds(start, 1024)]


def chunks_over_y(full):
    sends = call(
        chunk_kernel,
        [sds((SLOTS, 1024), bf16)] * 3,
        vmem=6,
        nbytes=6 * SLOTS * 1024 * 2,
        in_specs=[VMEM],
        out_specs=[VMEM] * 3,
        name="chunks",
    )(full)
    return [lax.ppermute(sent, "seq", y_shift(k)) for sent, k in zip(sends, STEPS[1:])]


def layer_kernel(x, kept, came, *refs):
    total = x[...].astype(f32) + (kept[...] + came[...].astype(f32))
    refs[-1][...] = (total * valid_rows()).astype(bf16)


def layer_rows(x, kept, came, after=()):
    return call(
        layer_kernel,
        sds((ROWS, WIDTH), bf16),
        vmem=4,
        nbytes=5 * ROWS * WIDTH * 2,
        in_specs=[VMEM] * 3 + [ANY] * len(after),
        out_specs=VMEM,
        name="layer_rows",
    )(x, kept, came, *after)


def per_device(tokens, text_gaps, image_runs, gains, w_qkv, w_out, cotangent):
    x_rows = tokens[0, 0]
    w_parts = jnp.transpose(w_qkv[0], (1, 0, 2))
    spans = (text_gaps, image_runs)

    n_left, n_right, grad_rows, inv = norm_rows(x_rows, gains, cotangent[0, 0])
    pieces = gather_blocks(n_left, n_right)
    grad_other = lax.ppermute(grad_rows, "tp", X_SWAP)
    grad_pair = touch(jnp.stack([grad_rows, grad_other]), w_parts)
    grad_pairs = [grad_pair] + [lax.ppermute(grad_pair, "tp", z_shift(k)) for k in STEPS[1:]]
    normed_full, own_kv = key_value(pieces, w_parts, [grad_pair])
    other_kv = lax.ppermute(own_kv, "grp", GRP_SWAP)
    query = query_of(normed_full, w_parts, grad_pairs[1:3])
    chunks = chunks_over_y(normed_full)

    mixed = attend_forward(spans, query, own_kv, other_kv, [])
    proj = proj_parts(mixed, w_out, [])
    grad_full, grad_mixed = grad_mixed_of(grad_pairs, w_out, [proj[0]] + chunks[:2])
    q_grad, own_part, other_part = attend_backward(
        spans, query, own_kv, other_kv, mixed, grad_mixed, []
    )
    back = lax.ppermute(other_part, "grp", GRP_SWAP)
    sends = late(proj[1:3], [q_grad])
    proj_came = [lax.ppermute(v, "tp", z_shift(-k)) for v, k in zip(sends, STEPS[1:3])]
    out_own, out_sent = out_weight_parts(grad_full, mixed, [q_grad])
    out_came = lax.ppermute(out_sent, "seq", CORE_SWAP)
    own_grads = sum_keys(q_grad, own_part, back, sends[:1])
    back_grads = lax.ppermute(own_grads, "seq", y_shift(1))
    next_grads = lax.ppermute(own_grads, "seq", y_shift(3))

    right = back_right(own_grads, w_parts, normed_full, [out_came] + chunks[2:])
    right_x = lax.ppermute(right[1], "tp", X_SWAP)
    left = back_left(own_grads, w_parts, normed_full, right[2], proj_came[:2])
    left_far_a = lax.ppermute(left[3], "tp", z_shift(1))
    left_far_b = lax.ppermute(left[4], "tp", z_shift(3))
    left_back, left_forth = pass_left(left[1], left[2], left_far_a, left_far_b)
    left_came = [
        lax.ppermute(left_forth, "tp", z_shift(1)), lax.ppermute(left_back, "tp", z_shift(3))
    ]
    out_kept, *out_sends = sum_out(
        out_own, out_came, [left_back, back_grads, next_grads, right_x]
    )
    out_far_a = lax.ppermute(out_sends[2], "seq", y_shift(1))
    out_far_b = lax.ppermute(out_sends[3], "seq", y_shift(3))
    out_back, out_forth = pass_out(
        out_sends[0], out_sends[1], out_far_a, out_far_b
    )
    out_terms = [
        lax.ppermute(out_forth, "seq", y_shift(1)), lax.ppermute(out_back, "seq", y_shift(3))
    ]
    left_kept, left_sent, gain_kept = sum_left(left[0], left_came, [out_back])
    left_x = lax.ppermute(left_sent, "tp", X_SWAP)
    gain_tp = sum_gain(gain_kept, left_x, gains)
    gain_sum = gain_tp + lax.ppermute(gain_tp, "seq", CORE_SWAP)
    gain_grad = gain_sum
    for k in STEPS[1:]:
        gain_grad = gain_grad + lax.ppermute(gain_sum, "seq", y_shift(k))
    right_kept, *right_sends = sum_x(
        right[0], right_x, [left_sent]
    )
    right_came = [lax.ppermute(v, "tp", z_shift(-k)) for v, k in zip(right_sends, STEPS[1:])]
    (far_sent,) = late(proj[3:], right_came[:1])
    proj_came.append(lax.ppermute(far_sent, "tp", z_shift(2)))
    relayed = halves(
        back_grads, next_grads, [gain_tp, far_sent] + right_came + out_terms
    )
    grads = [own_grads, back_grads, next_grads]
    grads += [lax.ppermute(v, "seq", y_shift(k)) for v, k in zip(relayed, (1, 3))]
    shares = (normed_full, chunks, grads)
    proj_kept, proj_sent = sum_z(proj[0], proj_came)
    proj_x = lax.ppermute(proj_sent, "tp", X_SWAP)
    qkv_sent = weight_shares(0, *shares, bf16, [gain_grad, proj_kept])
    qkv_mine = weight_shares(1, *shares, f32, [qkv_sent])
    tokens_grad = token_rows(
        x_rows, grad_rows, gains, inv, (left_kept, left_x), (right_kept, *right_came), [qkv_mine]
    )

    qkv_share = qkv_mine + lax.ppermute(qkv_sent, "seq", CORE_SWAP).astype(f32)
    layer_out = layer_rows(x_rows, proj_kept, proj_x, [qkv_mine])
    out_share = sum_rest(out_kept, out_terms, [qkv_sent])
    return (
        layer_out[None, None],
        tokens_grad[None, None],
        gain_grad,
        jnp.transpose(qkv_share, (1, 0, 2))[None],
        out_share[None],
    )


def solution(mesh):
    in_specs = (
        P("grp", "seq", "tp", None),
        P("seq", None),
        P("seq", None),
        P("grp", None),
        P("grp", None, None, "tp"),
        P("grp", None, "tp"),
        P("grp", "seq", "tp", None),
    )
    out_specs = (
        P("grp", "seq", "tp", None),
        P("grp", "seq", "tp", None),
        P("grp", None),
        P("grp", "seq", None, "tp"),
        P("grp", "seq", "tp"),
    )
    return jax.shard_map(
        per_device, mesh=mesh, in_specs=in_specs, out_specs=out_specs, check_vma=False
    )
```

```python
import functools

import jax
import jax.numpy as jnp
from jax import lax
from jax.experimental import pallas as pl
from jax.experimental.pallas import tpu as pltpu
from jax.sharding import PartitionSpec as P

HS = 128
LI = 128
HEADS = 4
SLOTS = 256
ROWS = 32
WIDTH = 4096
HALF = 2048
COLS = 512
FAR = 1073741824
f32 = jnp.float32
bf16 = jnp.bfloat16
MIB = 1024 * 1024

STEPS = (0, 1, 3, 2)


def z_shift(k):
    return [(i, (i // 4) * 4 + (i + k) % 4) for i in range(8)]


X_SWAP = [(i, i ^ 4) for i in range(8)]


def y_shift(k):
    return [(i, (i + 2 * k) % 8) for i in range(8)]


CORE_SWAP = [(i, i ^ 1) for i in range(8)]
GRP_SWAP = [(0, 1), (1, 0)]


def sds(shape, dtype):
    return jax.ShapeDtypeStruct(shape, dtype)


def call(kernel, out_shape, vmem, flops=0, nbytes=0, **kwargs):
    return pl.pallas_call(
        kernel,
        out_shape=out_shape,
        compiler_params=pltpu.CompilerParams(vmem_limit_bytes=vmem * MIB),
        cost_estimate=pl.CostEstimate(flops=flops, bytes_accessed=nbytes, transcendentals=0),
        **kwargs,
    )


def whole(shape):
    return pl.BlockSpec(shape, lambda *_: (0,) * len(shape))


SMEM = pl.BlockSpec(memory_space=pltpu.SMEM)
VMEM = pl.BlockSpec(memory_space=pltpu.VMEM)
ANY = pl.BlockSpec(memory_space=pl.ANY)
HBM = pl.BlockSpec(memory_space=pltpu.HBM)


def dot(left, right):
    return jnp.dot(left, right, preferred_element_type=f32)


def dot_rows(left, right):
    return lax.dot_general(left, right, (((1,), (1,)), ((), ())), preferred_element_type=f32)


def dot_tokens(left, right):
    return lax.dot_general(left, right, (((0,), (0,)), ((), ())), preferred_element_type=f32)


def where_am_i():
    tp, seq = lax.axis_index("tp"), lax.axis_index("seq")
    return tp >> 2, tp & 3, seq >> 1, seq & 1, lax.axis_index("grp")


def valid_rows():
    used = jnp.logical_or(lax.axis_index("grp") == 0, lax.axis_index("tp") * ROWS < LI)
    return jnp.where(used, 1.0, 0.0).astype(f32)


def load(sources, targets, sems):
    copies = [
        pltpu.make_async_copy(source, target, sems.at[i])
        for i, (source, target) in enumerate(zip(sources, targets))
    ]
    for copy in copies:
        copy.start()
    return copies


KCUT = 1024
KCUTS = WIDTH // KCUT


def dot_loaded(full, buffer, copies):
    total = None
    for i, copy in enumerate(copies):
        copy.wait()
        cut = slice(i * KCUT, (i + 1) * KCUT)
        part = dot(full[:, cut], buffer[cut])
        total = part if total is None else total + part
    return total


def k_cuts(ref):
    return [ref.at[pl.ds(i * KCUT, KCUT)] for i in range(KCUTS)]


def touch_kernel(weight, pair, *refs):
    refs[-1][...] = pair[...]


def touch(pair, weight):
    return call(
        touch_kernel,
        sds(pair.shape, pair.dtype),
        vmem=4,
        nbytes=pair.size * 4,
        in_specs=[ANY, VMEM],
        out_specs=VMEM,
        name="touch",
    )(weight, pair)


def norm_kernel(x, gain, cot, n_left, n_right, grad, inv):
    x_float = x[...].astype(f32)
    scale = lax.rsqrt(jnp.mean(x_float * x_float, axis=1, keepdims=True) + 1e-05)
    normed = (x_float * scale * gain[...].astype(f32)).astype(bf16)
    n_left[...] = normed[:, :HALF]
    n_right[...] = normed[:, HALF:]
    grad[...] = (cot[...].astype(f32) * valid_rows()).astype(bf16)
    inv[...] = jnp.broadcast_to(scale, (ROWS, 128))


def norm_rows(x, gain, cot):
    part = sds((ROWS, HALF), bf16)
    return call(
        norm_kernel,
        [part, part, sds((ROWS, WIDTH), bf16), sds((ROWS, 128), f32)],
        vmem=4,
        nbytes=4 * ROWS * WIDTH * 2,
        in_specs=[VMEM] * 3,
        name="norm_rows",
    )(x, gain, cot)


def gather_blocks(left, right):
    right_pair = jnp.stack([right, lax.ppermute(right, "tp", X_SWAP)])
    left_four = [left] + [lax.ppermute(left, "tp", z_shift(k)) for k in STEPS[1:]]
    right_four = [right_pair] + [lax.ppermute(right_pair, "tp", z_shift(k)) for k in STEPS[1:]]
    left_own = jnp.stack(left_four)
    left_other = lax.ppermute(left_own, "tp", X_SWAP)
    return [left_own, left_other] + right_four


def place_pieces(pieces, whole_ref):
    left_own, left_other = pieces[:2]
    for slot in range(4):
        rows = pl.ds(slot * ROWS, ROWS)
        other = pl.ds((4 + slot) * ROWS, ROWS)
        whole_ref[rows, :HALF] = left_own[slot]
        whole_ref[other, :HALF] = left_other[slot]
        whole_ref[rows, HALF:] = pieces[2 + slot][0]
        whole_ref[other, HALF:] = pieces[2 + slot][1]


PIECE_SHAPES = [(4, ROWS, HALF)] * 2 + [(2, ROWS, HALF)] * 4


def sum_z_kernel(own, c1, c2, c3, *refs):
    kept, sent = refs[-2:]
    total = own[...].astype(f32)
    for came in (c1, c2, c3):
        total = total + came[...].astype(f32)
    kept[...] = total[0]
    sent[...] = total[1].astype(bf16)


def sum_z(own, came, after=()):
    shape = own.shape[1:]
    return call(
        sum_z_kernel,
        [sds(shape, f32), sds(shape, bf16)],
        vmem=6,
        nbytes=11 * shape[0] * shape[1] * 2,
        in_specs=[VMEM] * 4 + [ANY] * len(after),
        out_specs=[VMEM] * 2,
        name="sum_z",
    )(own, *came, *after)


def sum_left_kernel(own, c1, c2, *refs):
    kept, sent, gain = refs[-3:]
    for part in range(2):
        total = own[part].astype(f32)
        for came in (c1, c2):
            total = total + came[part].astype(f32)
        kept[pl.ds(part * 16, 16)] = total
        total = own[2 + part].astype(f32)
        for came in (c1, c2):
            total = total + came[2 + part].astype(f32)
        sent[part] = total.astype(bf16)
    left, right = gain_from(own[4])
    for came in (c1, c2):
        more_left, more_right = gain_from(came[4])
        left, right = left + more_left, right + more_right
    sent[2] = gain_rows_of(left, right)
    gain[0:1] = left
    gain[1:2] = right


def sum_left(own, came, after=()):
    return call(
        sum_left_kernel,
        [sds((ROWS, HALF), f32), sds((3, 16, HALF), bf16), sds((2, HALF), f32)],
        vmem=4,
        nbytes=11 * ROWS * HALF * 2,
        in_specs=[VMEM] * 3 + [ANY] * len(after),
        out_specs=[VMEM] * 3,
        name="sum_left",
    )(own, *came, *after)


def sum_gain_kernel(own, came, gain, out):
    left, right = gain_from(came[2])
    out[:, :HALF] = (own[0:1] + left) / gain[:, :HALF].astype(f32)
    out[:, HALF:] = (own[1:2] + right) / gain[:, HALF:].astype(f32)


def sum_gain(own, came, gain):
    return call(
        sum_gain_kernel,
        sds((1, WIDTH), f32),
        vmem=2,
        nbytes=10 * WIDTH * 2,
        in_specs=[VMEM] * 3,
        out_specs=VMEM,
        name="sum_gain",
    )(own, came, gain)


def pass_left_kernel(back, forth, far_a, far_b, *refs):
    out_back, out_forth = refs[-2:]
    out_forth[...] = forth[...]
    out_back[...] = back[...]
    for part in range(2):
        out_forth[part] = (forth[part].astype(f32) + far_a[part].astype(f32)).astype(bf16)
        total = back[2 + part].astype(f32) + far_b[part].astype(f32)
        out_back[2 + part] = total.astype(bf16)
    left, right = gain_from(forth[4])
    more_left, more_right = gain_from(far_a[2])
    out_forth[4] = gain_rows_of(left + more_left, right + more_right)


def pass_left(back, forth, far_a, far_b, after=()):
    return call(
        pass_left_kernel,
        [sds(back.shape, bf16)] * 2,
        vmem=6,
        nbytes=6 * back.size * 2,
        in_specs=[VMEM] * 4 + [ANY] * len(after),
        out_specs=[VMEM] * 2,
        name="pass_left",
    )(back, forth, far_a, far_b, *after)


def pass_out_kernel(back, forth, far_a, far_b, *refs):
    out_back, out_forth = refs[-2:]
    half = COLS // 2
    out_forth[half:] = forth[half:]
    out_forth[:half] = (forth[:half].astype(f32) + far_a[...].astype(f32)).astype(bf16)
    out_back[:half] = back[:half]
    out_back[half:] = (back[half:].astype(f32) + far_b[...].astype(f32)).astype(bf16)


def pass_out(back, forth, far_a, far_b, after=()):
    return call(
        pass_out_kernel,
        [sds(back.shape, bf16)] * 2,
        vmem=6,
        nbytes=6 * back.size * 2,
        in_specs=[VMEM] * 4 + [ANY] * len(after),
        out_specs=[VMEM] * 2,
        name="pass_out",
    )(back, forth, far_a, far_b, *after)


def sum_out_kernel(own, came, *refs):
    kept, back, forth, far_a, far_b = refs[-5:]
    half = COLS // 2

    def total(slot, rows=slice(None)):
        return own[slot, rows].astype(f32) + came[slot, rows].astype(f32)

    kept[...] = total(0)
    back[...] = total(1).astype(bf16)
    forth[...] = total(2).astype(bf16)
    far_a[...] = total(3, slice(0, half)).astype(bf16)
    far_b[...] = total(3, slice(half, COLS)).astype(bf16)


def sum_out(own, came, after=()):
    whole_share, half_share = sds((COLS, COLS), bf16), sds((COLS // 2, COLS), bf16)
    return call(
        sum_out_kernel,
        [sds((COLS, COLS), f32), whole_share, whole_share, half_share, half_share],
        vmem=12,
        nbytes=own.size * 6,
        in_specs=[VMEM] * 2 + [ANY] * len(after),
        out_specs=[VMEM] * 5,
        name="sum_out",
    )(own, came, *after)


def sum_x_kernel(waits, own, came, *refs):
    kept, sends = refs[waits], refs[waits + 1:]
    kept[...] = own[0].astype(f32) + came[0].astype(f32)
    for slot, sent in enumerate(sends, 1):
        sent[...] = (own[slot].astype(f32) + came[slot].astype(f32)).astype(bf16)


def sum_x(own, came, after=(), sends=3):
    shape = own.shape[1:]
    return call(
        functools.partial(sum_x_kernel, len(after)),
        [sds(shape, f32)] + [sds(shape, bf16)] * sends,
        vmem=12,
        nbytes=13 * shape[0] * shape[1] * 2,
        in_specs=[VMEM] * 2 + [ANY] * len(after),
        out_specs=[VMEM] * (1 + sends),
        name="sum_x",
    )(own, came, *after)


def halves_kernel(back, forth, *refs):
    half = SLOTS // 2
    refs[-2][...] = back[:, :half]
    refs[-1][...] = forth[:, half:]


def halves(back, forth, after):
    shape = (3, SLOTS // 2, COLS)
    return call(
        halves_kernel,
        [sds(shape, bf16)] * 2,
        vmem=6,
        nbytes=8 * back.size,
        in_specs=[VMEM] * 2 + [ANY] * len(after),
        out_specs=[VMEM] * 2,
        name="halves",
    )(back, forth, *after)


def late_kernel(count, *refs):
    for i in range(count):
        refs[i - count][...] = refs[i][...]


def late(arrays, after):
    count = len(arrays)
    return call(
        functools.partial(late_kernel, count),
        [sds(v.shape, v.dtype) for v in arrays],
        vmem=10,
        nbytes=sum(v.size * 4 for v in arrays),
        in_specs=[VMEM] * count + [ANY] * len(after),
        out_specs=[VMEM] * count,
        name="late",
    )(*arrays, *after)


def sum_rest_kernel(kept, c1, c2, *refs):
    total = kept[...]
    for came in (c1, c2):
        total = total + came[...].astype(f32)
    refs[-1][...] = total


def sum_rest(kept, came, after=()):
    return call(
        sum_rest_kernel,
        sds(kept.shape, f32),
        vmem=6,
        nbytes=14 * kept.size,
        in_specs=[VMEM] * 3 + [ANY] * len(after),
        out_specs=VMEM,
        name="sum_rest",
    )(kept, *came, *after)


def sum_keys_kernel(q_grad, own, came, *refs):
    out = refs[-1]
    out[0] = q_grad[...]
    out[1:] = (own[...] + came[...].astype(f32)).astype(bf16)


def sum_keys(q_grad, own, came, after=()):
    return call(
        sum_keys_kernel,
        sds((3, SLOTS, COLS), bf16),
        vmem=8,
        nbytes=10 * came.size,
        in_specs=[VMEM] * 3 + [ANY] * len(after),
        out_specs=VMEM,
        name="sum_keys",
    )(q_grad, own, came, *after)


def rows_kernel(x, grad, gain, inv, l_kept, l_came, r_kept, r1, r2, r3, *refs):
    out = refs[-1]
    left = l_kept[...] + l_came[0:2].reshape(ROWS, HALF).astype(f32)
    right = r_kept[...]
    for came in (r1, r2, r3):
        right = right + came[...].astype(f32)
    scale = inv[:, :1]
    halves = []
    dots = jnp.zeros((ROWS, 1), f32)
    for part, cols in ((left, slice(0, HALF)), (right, slice(HALF, WIDTH))):
        scaled = gain[:, cols].astype(f32) * part
        rows = x[:, cols].astype(f32)
        dots = dots + jnp.sum(scaled * rows, axis=1, keepdims=True)
        halves.append((scaled, rows, cols))
    mean = dots * (1.0 / WIDTH)
    for scaled, rows, cols in halves:
        total = grad[:, cols].astype(f32) + scale * scaled - rows * (scale * scale * scale) * mean
        out[:, cols] = total.astype(bf16)


def token_rows(x, grad, gain, inv, left, right, after=()):
    return call(
        rows_kernel,
        sds((ROWS, WIDTH), bf16),
        vmem=4,
        nbytes=6 * ROWS * WIDTH * 2,
        in_specs=[VMEM] * 10 + [ANY] * len(after),
        out_specs=VMEM,
        name="token_rows",
    )(x, grad, gain, inv, *left, *right, *after)


def key_value_kernel(*refs):
    pieces, weight = refs[:6], refs[6]
    full, out, buffer, sems = refs[-4:]
    copies = [
        load(k_cuts(weight.at[part + 1]), k_cuts(buffer.at[part]), sems.at[part])
        for part in range(2)
    ]
    place_pieces(pieces, full)
    for part in range(2):
        out[part] = dot_loaded(full, buffer.at[part], copies[part]).astype(bf16)


def key_value(pieces, weights, after):
    return call(
        key_value_kernel,
        [sds((SLOTS, WIDTH), bf16), sds((2, SLOTS, COLS), bf16)],
        vmem=20,
        flops=4 * SLOTS * WIDTH * COLS,
        nbytes=2 * WIDTH * COLS * 2 + 2 * SLOTS * WIDTH * 2,
        in_specs=[VMEM] * 6 + [HBM] + [ANY] * len(after),
        out_specs=[VMEM] * 2,
        scratch_shapes=[
            pltpu.VMEM((2, WIDTH, COLS), bf16),
            pltpu.SemaphoreType.DMA((2, KCUTS)),
        ],
        name="key_value",
    )(*pieces, weights, *after)


def query_kernel(full, weight, *refs):
    out, buffer, sems = refs[-3:]
    copies = load(k_cuts(weight.at[0]), k_cuts(buffer), sems)
    out[...] = dot_loaded(full, buffer, copies).astype(bf16)


DOT_SCRATCH = [pltpu.VMEM((WIDTH, COLS), bf16), pltpu.SemaphoreType.DMA((KCUTS,))]


def query_of(full, weights, after):
    return call(
        query_kernel,
        sds((SLOTS, COLS), bf16),
        vmem=12,
        flops=2 * SLOTS * WIDTH * COLS,
        nbytes=WIDTH * COLS * 2 + SLOTS * WIDTH * 2,
        in_specs=[VMEM, HBM] + [ANY] * len(after),
        out_specs=VMEM,
        scratch_shapes=DOT_SCRATCH,
        name="query",
    )(full, weights, *after)


def grad_mixed_kernel(p0, p1, p2, p3, weight, *refs):
    full, out, buffer, sems = refs[-4:]
    copies = load(k_cuts(weight.at[0]), k_cuts(buffer), sems)
    for slot, pair in enumerate((p0, p1, p2, p3)):
        full[pl.ds(slot * ROWS, ROWS)] = pair[0]
        full[pl.ds((4 + slot) * ROWS, ROWS)] = pair[1]
    out[...] = dot_loaded(full, buffer, copies).astype(bf16)


def grad_mixed_of(pairs, weights, after):
    return call(
        grad_mixed_kernel,
        [sds((SLOTS, WIDTH), bf16), sds((SLOTS, COLS), bf16)],
        vmem=16,
        flops=2 * SLOTS * WIDTH * COLS,
        nbytes=WIDTH * COLS * 2 + 2 * SLOTS * WIDTH * 2,
        in_specs=[VMEM] * 4 + [HBM] + [ANY] * len(after),
        out_specs=[VMEM] * 2,
        scratch_shapes=DOT_SCRATCH,
        name="grad_mixed",
    )(*pairs, weights, *after)


def gain_rows_of(left, right):
    row = lax.broadcasted_iota(jnp.int32, (16, left.shape[1]), 0)
    rows = jnp.zeros((16, left.shape[1]), f32)
    for first, part in ((0, left), (2, right)):
        high = part.astype(bf16).astype(f32)
        rows = jnp.where(row == first, high, rows)
        rows = jnp.where(row == first + 1, part - high, rows)
    return rows.astype(bf16)


def gain_from(rows):
    rows = rows.astype(f32)
    return rows[0:1] + rows[1:2], rows[2:3] + rows[3:4]


FCUT = 512
FCUTS = HALF // FCUT


def back_products(grads, weight, first, normed, buffer, sems):
    copies = [
        load(
            [weight.at[part, pl.ds(first + cut * FCUT, FCUT)] for part in range(3)],
            [buffer.at[part, pl.ds(cut * FCUT, FCUT)] for part in range(3)],
            sems.at[cut],
        )
        for cut in range(FCUTS)
    ]
    for cut in range(FCUTS):
        for copy in copies[cut]:
            copy.wait()
        rows = slice(cut * FCUT, (cut + 1) * FCUT)
        total = dot_rows(grads[0], buffer[0, rows])
        for part in range(1, 3):
            total = total + dot_rows(grads[part], buffer[part, rows])
        rounded = total.astype(bf16)
        terms = normed[:, first + cut * FCUT:first + (cut + 1) * FCUT].astype(f32)
        gain = jnp.sum(rounded.astype(f32) * terms, axis=0, keepdims=True)
        yield rows, rounded, gain


def back_right_kernel(waits, grads, weight, normed, *refs):
    own, sent, gain, buffer, sems = refs[waits:]
    for cols, rounded, terms in back_products(
        grads, weight, HALF, normed, buffer, sems
    ):
        gain[:, cols] = terms
        for xbit, out in enumerate((own, sent)):
            for slot in range(4):
                start = (xbit * 4 + slot) * ROWS
                out[slot, :, cols] = rounded[start:start + ROWS]


def back_left_kernel(waits, grads, weight, normed, gain_right, *refs):
    outs, far, buffer, sems = refs[waits:waits + 3], refs[-4:-2], refs[-2], refs[-1]
    for cols, rounded, terms in back_products(
        grads, weight, 0, normed, buffer, sems
    ):
        gains = gain_rows_of(terms, gain_right[:, cols])
        for slot, out in enumerate(outs):
            for xbit in range(2):
                start = (xbit * 4 + slot) * ROWS
                out[2 * xbit, :, cols] = rounded[start:start + 16]
                out[2 * xbit + 1, :, cols] = rounded[start + 16:start + ROWS]
            out[4, :, cols] = gains
        for xbit, out in enumerate(far):
            start = (xbit * 4 + 3) * ROWS
            out[0, :, cols] = rounded[start:start + 16]
            out[1, :, cols] = rounded[start + 16:start + ROWS]
        far[0][2, :, cols] = gains


def back_dot(kernel, grads, weights, normed, extra, out_shape, after, name):
    return call(
        functools.partial(kernel, len(after)),
        out_shape,
        vmem=20,
        flops=2 * 3 * SLOTS * HALF * COLS,
        nbytes=3 * HALF * COLS * 2 + 2 * SLOTS * HALF * 2,
        in_specs=[VMEM, HBM, VMEM] + [VMEM] * len(extra) + [ANY] * len(after),
        out_specs=[VMEM] * len(out_shape),
        scratch_shapes=[
            pltpu.VMEM((3, HALF, COLS), bf16),
            pltpu.SemaphoreType.DMA((FCUTS, 3)),
        ],
        name=name,
    )(grads, weights, normed, *extra, *after)


def back_right(grads, weights, normed, after=()):
    out = [sds((4, ROWS, HALF), bf16)] * 2 + [sds((1, HALF), f32)]
    return back_dot(back_right_kernel, grads, weights, normed, [], out, after, "back_right")


def back_left(grads, weights, normed, gain_right, after=()):
    out = [sds((5, 16, HALF), bf16)] * 3
    out += [sds((3, 16, HALF), bf16), sds((2, 16, HALF), bf16)]
    return back_dot(back_left_kernel, grads, weights, normed, [gain_right], out, after, "back_left")


def proj_kernel(left, weight, *refs):
    outs, buffer, sems = refs[-6:-2], refs[-2], refs[-1]
    copies = load(k_cuts(weight.at[0]), k_cuts(buffer), sems)
    for cut, copy in enumerate(copies):
        copy.wait()
        cols = slice(cut * KCUT, (cut + 1) * KCUT)
        rounded = dot_rows(left[...], buffer[cols]).astype(bf16)
        for slot in range(4):
            for xbit in range(2):
                start = (xbit * 4 + slot) * ROWS
                outs[slot][xbit, :, cols] = rounded[start:start + ROWS]


def proj_parts(mixed, weights, after):
    return call(
        proj_kernel,
        [sds((2, ROWS, WIDTH), bf16)] * 4,
        vmem=14,
        flops=2 * SLOTS * WIDTH * COLS,
        nbytes=WIDTH * COLS * 2 + SLOTS * WIDTH * 2,
        in_specs=[VMEM, HBM] + [ANY] * len(after),
        out_specs=[VMEM] * 4,
        scratch_shapes=DOT_SCRATCH,
        name="proj_parts",
    )(mixed, weights, *after)


def slot_of(row, x_index, z_index):
    block = row // ROWS
    xbit = block // 4
    slot = block - xbit * 4
    back = jnp.where(slot == 2, 3, jnp.where(slot == 3, 2, slot))
    x_from = jnp.where(xbit == 0, x_index, 1 - x_index)
    z_from = z_index - back
    z_from = jnp.where(z_from < 0, z_from + 4, z_from)
    return (x_from * 4 + z_from) * ROWS + (row - block * ROWS)


def places(gaps, runs, rows, is_text):
    x_index, z_index = where_am_i()[:2]
    slot = slot_of(rows, x_index, z_index)
    text = slot
    end = jnp.int32(0)
    for run in range(4):
        end = end + gaps[0, run]
        text = text + jnp.where(slot >= end, runs[0, run], 0)
    image = slot + gaps[0, 0]
    end = jnp.int32(0)
    for run in range(3):
        end = end + runs[0, run]
        image = image + jnp.where(slot >= end, gaps[0, run + 1], 0)
    image = jnp.where(slot < LI, image, FAR)
    return jnp.where(is_text, text, image)


def admitted(gaps, runs):
    group = lax.axis_index("grp")
    rows = lax.broadcasted_iota(jnp.int32, (SLOTS, 1), 0)
    query = places(gaps, runs, rows, group == 0)
    key_row = lax.broadcasted_iota(jnp.int32, (1, SLOTS), 1)
    own = places(gaps, runs, key_row, group == 0)
    other = places(gaps, runs, key_row, group != 0)
    return own <= query, other <= query


def head_attn(query, own_key, other_key, own_ok, other_ok):
    scale = HS ** (-0.5)
    own = jnp.where(own_ok, dot_rows(query, own_key) * scale, -1e30)
    other = jnp.where(other_ok, dot_rows(query, other_key) * scale, -1e30)
    row_max = jnp.maximum(
        jnp.max(own, axis=1, keepdims=True), jnp.max(other, axis=1, keepdims=True)
    )
    own = jnp.exp(own - row_max)
    other = jnp.exp(other - row_max)
    row_sum = jnp.sum(own, axis=1, keepdims=True) + jnp.sum(other, axis=1, keepdims=True)
    share = 1.0 / row_sum
    return own * share, other * share


def forward_kernel(gaps, runs, query, own_kv, other_kv, *refs):
    mixed = refs[-1]
    own_ok, other_ok = admitted(gaps, runs)
    for head in range(HEADS):
        cols = slice(head * HS, (head + 1) * HS)
        own, other = head_attn(
            query[:, cols], own_kv[0, :, cols], other_kv[0, :, cols], own_ok, other_ok
        )
        total = dot(own.astype(bf16), own_kv[1, :, cols])
        total = total + dot(other.astype(bf16), other_kv[1, :, cols])
        mixed[:, cols] = total.astype(bf16)


def backward_kernel(gaps, runs, query, own_kv, other_kv, mixed, grad, *refs):
    q_grad, own_grad, other_grad = refs[-3:]
    scale = HS ** (-0.5)
    own_ok, other_ok = admitted(gaps, runs)
    for head in range(HEADS):
        cols = slice(head * HS, (head + 1) * HS)
        q, g = query[:, cols], grad[:, cols]
        row_dot = jnp.sum(g.astype(f32) * mixed[:, cols].astype(f32), axis=1, keepdims=True)
        attns = head_attn(q, own_kv[0, :, cols], other_kv[0, :, cols], own_ok, other_ok)
        dq = None
        for attn, kv, kv_grad in zip(attns, (own_kv, other_kv), (own_grad, other_grad)):
            value_grad = dot_tokens(attn.astype(bf16), g)
            weight_grad = dot_rows(g, kv[1, :, cols])
            score_grad = (attn * (weight_grad - row_dot)).astype(bf16)
            part = dot(score_grad, kv[0, :, cols])
            dq = part if dq is None else dq + part
            key_grad = dot_tokens(score_grad, q) * scale
            kv_grad[0, :, cols] = key_grad.astype(kv_grad.dtype)
            kv_grad[1, :, cols] = value_grad.astype(kv_grad.dtype)
        q_grad[:, cols] = (dq * scale).astype(bf16)


ATTN_FLOPS = 2 * HEADS * SLOTS * 2 * SLOTS * HS


def attend_forward(spans, query, own_kv, other_kv, after):
    return call(
        forward_kernel,
        sds((SLOTS, COLS), bf16),
        vmem=10,
        flops=4 * ATTN_FLOPS,
        nbytes=6 * SLOTS * COLS * 2,
        in_specs=[SMEM] * 2 + [VMEM] * 3 + [ANY] * len(after),
        out_specs=VMEM,
        name="attend_forward",
    )(*spans, query, own_kv, other_kv, *after)


def attend_backward(spans, query, own_kv, other_kv, mixed, grad, after):
    kv = (2, SLOTS, COLS)
    return call(
        backward_kernel,
        [sds((SLOTS, COLS), bf16), sds(kv, f32), sds(kv, bf16)],
        vmem=14,
        flops=8 * ATTN_FLOPS,
        nbytes=12 * SLOTS * COLS * 2,
        in_specs=[SMEM] * 2 + [VMEM] * 5 + [ANY] * len(after),
        out_specs=[VMEM] * 3,
        name="attend_backward",
    )(*spans, query, own_kv, other_kv, mixed, grad, *after)


def out_kernel(grad, mixed, *refs):
    own, sent = refs[-2:]
    y_index, core = where_am_i()[2:4]
    for i in range(8):
        column = ((y_index - STEPS[i % 4]) & 3) * 2 + (1 - core if i < 4 else core)
        start = pl.multiple_of(column * COLS, COLS)
        share = dot_tokens(grad[:, pl.ds(start, COLS)], mixed[...]).astype(bf16)
        if i < 4:
            sent[i] = share
        else:
            own[i - 4] = share


def out_weight_parts(grad_full, mixed, after):
    return call(
        out_kernel,
        [sds((4, COLS, COLS), bf16)] * 2,
        vmem=12,
        flops=2 * SLOTS * WIDTH * COLS,
        nbytes=SLOTS * WIDTH * 2 + WIDTH * COLS * 2,
        in_specs=[VMEM] * 2 + [ANY] * len(after),
        out_specs=[VMEM] * 2,
        name="out_weight_parts",
    )(grad_full, mixed, *after)


def share_kernel(which, full, c1, c2, c3, g0, g1, g2, g3, g4, *refs):
    out, lefts = refs[-2:]
    y_index, core = where_am_i()[2:4]
    column = core if which else 1 - core
    start = pl.multiple_of((y_index * 2 + column) * COLS, COLS)
    lefts[0] = full[:, pl.ds(start, COLS)].T
    start = pl.multiple_of(column * COLS, COLS)
    for k, came in enumerate((c1, c2, c3), 1):
        lefts[k] = came[:, pl.ds(start, COLS)].T
    for part in range(3):
        total = dot(lefts[0], g0[part])
        for k, grad in enumerate((g1, g2), 1):
            total = total + dot(lefts[k], grad[part])
        total = total + dot(lefts[3, :, :SLOTS // 2], g3[part])
        total = total + dot(lefts[3, :, SLOTS // 2:], g4[part])
        out[part] = total.astype(out.dtype)


def weight_shares(which, full, came, grads, dtype, after=()):
    return call(
        functools.partial(share_kernel, which),
        sds((3, COLS, COLS), dtype),
        vmem=20,
        flops=3 * 4 * 2 * SLOTS * COLS * COLS,
        nbytes=16 * SLOTS * COLS * 2 + 3 * COLS * COLS * 4,
        in_specs=[VMEM] * 9 + [ANY] * len(after),
        out_specs=VMEM,
        scratch_shapes=[pltpu.VMEM((4, COLS, SLOTS), bf16)],
        name="weight_shares",
    )(full, *came, *grads, *after)


def chunk_kernel(full, *outs):
    y_index = where_am_i()[2]
    for k, out in zip(STEPS[1:], outs):
        start = pl.multiple_of(((y_index + k) & 3) * 1024, 1024)
        out[...] = full[:, pl.ds(start, 1024)]


def chunks_over_y(full):
    sends = call(
        chunk_kernel,
        [sds((SLOTS, 1024), bf16)] * 3,
        vmem=6,
        nbytes=6 * SLOTS * 1024 * 2,
        in_specs=[VMEM],
        out_specs=[VMEM] * 3,
        name="chunks",
    )(full)
    return [lax.ppermute(sent, "seq", y_shift(k)) for sent, k in zip(sends, STEPS[1:])]


def layer_kernel(x, kept, came, *refs):
    total = x[...].astype(f32) + (kept[...] + came[...].astype(f32))
    refs[-1][...] = (total * valid_rows()).astype(bf16)


def layer_rows(x, kept, came, after=()):
    return call(
        layer_kernel,
        sds((ROWS, WIDTH), bf16),
        vmem=4,
        nbytes=5 * ROWS * WIDTH * 2,
        in_specs=[VMEM] * 3 + [ANY] * len(after),
        out_specs=VMEM,
        name="layer_rows",
    )(x, kept, came, *after)


def per_device(tokens, text_gaps, image_runs, gains, w_qkv, w_out, cotangent):
    x_rows = tokens[0, 0]
    w_parts = jnp.transpose(w_qkv[0], (1, 0, 2))
    spans = (text_gaps, image_runs)

    n_left, n_right, grad_rows, inv = norm_rows(x_rows, gains, cotangent[0, 0])
    pieces = gather_blocks(n_left, n_right)
    grad_other = lax.ppermute(grad_rows, "tp", X_SWAP)
    grad_pair = touch(jnp.stack([grad_rows, grad_other]), w_parts)
    grad_pairs = [grad_pair] + [lax.ppermute(grad_pair, "tp", z_shift(k)) for k in STEPS[1:]]
    normed_full, own_kv = key_value(pieces, w_parts, [grad_pair])
    other_kv = lax.ppermute(own_kv, "grp", GRP_SWAP)
    query = query_of(normed_full, w_parts, grad_pairs[1:3])
    chunks = chunks_over_y(normed_full)

    mixed = attend_forward(spans, query, own_kv, other_kv, [])
    proj = proj_parts(mixed, w_out, [])
    grad_full, grad_mixed = grad_mixed_of(grad_pairs, w_out, [proj[0]] + chunks[:2])
    q_grad, own_part, other_part = attend_backward(
        spans, query, own_kv, other_kv, mixed, grad_mixed, []
    )
    back = lax.ppermute(other_part, "grp", GRP_SWAP)
    sends = late(proj[1:], [q_grad])
    proj_came = [lax.ppermute(v, "tp", z_shift(-k)) for v, k in zip(sends, STEPS[1:])]
    out_own, out_sent = out_weight_parts(grad_full, mixed, [q_grad])
    out_came = lax.ppermute(out_sent, "seq", CORE_SWAP)
    own_grads = sum_keys(q_grad, own_part, back, sends[:1])
    back_grads = lax.ppermute(own_grads, "seq", y_shift(1))
    next_grads = lax.ppermute(own_grads, "seq", y_shift(3))

    right = back_right(own_grads, w_parts, normed_full, [out_came] + chunks[2:])
    right_x = lax.ppermute(right[1], "tp", X_SWAP)
    left = back_left(own_grads, w_parts, normed_full, right[2], proj_came[:2])
    left_far_a = lax.ppermute(left[3], "tp", z_shift(1))
    left_far_b = lax.ppermute(left[4], "tp", z_shift(3))
    left_back, left_forth = pass_left(left[1], left[2], left_far_a, left_far_b)
    left_came = [
        lax.ppermute(left_forth, "tp", z_shift(1)), lax.ppermute(left_back, "tp", z_shift(3))
    ]
    proj_kept, proj_sent = sum_z(proj[0], proj_came)
    proj_x = lax.ppermute(proj_sent, "tp", X_SWAP)
    layer_out = layer_rows(x_rows, proj_kept, proj_x)
    out_kept, *out_sends = sum_out(
        out_own, out_came, [left_back, back_grads, next_grads, right_x, proj_kept]
    )
    out_far_a = lax.ppermute(out_sends[2], "seq", y_shift(1))
    out_far_b = lax.ppermute(out_sends[3], "seq", y_shift(3))
    out_back, out_forth = pass_out(
        out_sends[0], out_sends[1], out_far_a, out_far_b
    )
    out_terms = [
        lax.ppermute(out_forth, "seq", y_shift(1)), lax.ppermute(out_back, "seq", y_shift(3))
    ]
    left_kept, left_sent, gain_kept = sum_left(left[0], left_came, [out_back])
    left_x = lax.ppermute(left_sent, "tp", X_SWAP)
    gain_tp = sum_gain(gain_kept, left_x, gains)
    gain_sum = gain_tp + lax.ppermute(gain_tp, "seq", CORE_SWAP)
    gain_grad = gain_sum
    for k in STEPS[1:]:
        gain_grad = gain_grad + lax.ppermute(gain_sum, "seq", y_shift(k))
    right_kept, *right_sends = sum_x(
        right[0], right_x, [left_sent]
    )
    right_came = [lax.ppermute(v, "tp", z_shift(-k)) for v, k in zip(right_sends, STEPS[1:])]
    relayed = halves(
        back_grads, next_grads, [gain_tp] + right_came[:2] + out_terms
    )
    grads = [own_grads, back_grads, next_grads]
    grads += [lax.ppermute(v, "seq", y_shift(k)) for v, k in zip(relayed, (1, 3))]
    shares = (normed_full, chunks, grads)
    qkv_sent = weight_shares(0, *shares, bf16, [gain_sum, right_came[2], layer_out])
    qkv_mine = weight_shares(1, *shares, f32, [qkv_sent])
    tokens_grad = token_rows(
        x_rows, grad_rows, gains, inv, (left_kept, left_x), (right_kept, *right_came), [qkv_mine]
    )

    qkv_share = qkv_mine + lax.ppermute(qkv_sent, "seq", CORE_SWAP).astype(f32)
    out_share = sum_rest(out_kept, out_terms, [qkv_sent])
    return (
        layer_out[None, None],
        tokens_grad[None, None],
        gain_grad,
        jnp.transpose(qkv_share, (1, 0, 2))[None],
        out_share[None],
    )


def solution(mesh):
    in_specs = (
        P("grp", "seq", "tp", None),
        P("seq", None),
        P("seq", None),
        P("grp", None),
        P("grp", None, None, "tp"),
        P("grp", None, "tp"),
        P("grp", "seq", "tp", None),
    )
    out_specs = (
        P("grp", "seq", "tp", None),
        P("grp", "seq", "tp", None),
        P("grp", None),
        P("grp", "seq", None, "tp"),
        P("grp", "seq", "tp"),
    )
    return jax.shard_map(
        per_device, mesh=mesh, in_specs=in_specs, out_specs=out_specs, check_vma=False
    )
```

```python
import functools

import jax
import jax.numpy as jnp
from jax import lax
from jax.experimental import pallas as pl
from jax.experimental.pallas import tpu as pltpu
from jax.sharding import PartitionSpec as P

HS = 128
LI = 128
HEADS = 4
SLOTS = 256
ROWS = 32
WIDTH = 4096
HALF = 2048
COLS = 512
FAR = 1073741824
f32 = jnp.float32
bf16 = jnp.bfloat16
MIB = 1024 * 1024

STEPS = (0, 1, 3, 2)


def z_shift(k):
    return [(i, (i // 4) * 4 + (i + k) % 4) for i in range(8)]


X_SWAP = [(i, i ^ 4) for i in range(8)]


def y_shift(k):
    return [(i, (i + 2 * k) % 8) for i in range(8)]


CORE_SWAP = [(i, i ^ 1) for i in range(8)]
GRP_SWAP = [(0, 1), (1, 0)]


def sds(shape, dtype):
    return jax.ShapeDtypeStruct(shape, dtype)


def call(kernel, out_shape, vmem, flops=0, nbytes=0, **kwargs):
    return pl.pallas_call(
        kernel,
        out_shape=out_shape,
        compiler_params=pltpu.CompilerParams(vmem_limit_bytes=vmem * MIB),
        cost_estimate=pl.CostEstimate(flops=flops, bytes_accessed=nbytes, transcendentals=0),
        **kwargs,
    )


def whole(shape):
    return pl.BlockSpec(shape, lambda *_: (0,) * len(shape))


SMEM = pl.BlockSpec(memory_space=pltpu.SMEM)
VMEM = pl.BlockSpec(memory_space=pltpu.VMEM)
ANY = pl.BlockSpec(memory_space=pl.ANY)
HBM = pl.BlockSpec(memory_space=pltpu.HBM)


def dot(left, right):
    return jnp.dot(left, right, preferred_element_type=f32)


def dot_rows(left, right):
    return lax.dot_general(left, right, (((1,), (1,)), ((), ())), preferred_element_type=f32)


def dot_tokens(left, right):
    return lax.dot_general(left, right, (((0,), (0,)), ((), ())), preferred_element_type=f32)


def where_am_i():
    tp, seq = lax.axis_index("tp"), lax.axis_index("seq")
    return tp >> 2, tp & 3, seq >> 1, seq & 1, lax.axis_index("grp")


def valid_rows():
    used = jnp.logical_or(lax.axis_index("grp") == 0, lax.axis_index("tp") * ROWS < LI)
    return jnp.where(used, 1.0, 0.0).astype(f32)


def load(sources, targets, sems):
    copies = [
        pltpu.make_async_copy(source, target, sems.at[i])
        for i, (source, target) in enumerate(zip(sources, targets))
    ]
    for copy in copies:
        copy.start()
    return copies


KCUT = 1024
KCUTS = WIDTH // KCUT


def dot_loaded(full, buffer, copies):
    total = None
    for i, copy in enumerate(copies):
        copy.wait()
        cut = slice(i * KCUT, (i + 1) * KCUT)
        part = dot(full[:, cut], buffer[cut])
        total = part if total is None else total + part
    return total


def k_cuts(ref):
    return [ref.at[pl.ds(i * KCUT, KCUT)] for i in range(KCUTS)]


def touch_kernel(weight, pair, *refs):
    refs[-1][...] = pair[...]


def touch(pair, weight):
    return call(
        touch_kernel,
        sds(pair.shape, pair.dtype),
        vmem=4,
        nbytes=pair.size * 4,
        in_specs=[ANY, VMEM],
        out_specs=VMEM,
        name="touch",
    )(weight, pair)


def norm_kernel(x, gain, cot, n_left, n_right, grad, inv):
    x_float = x[...].astype(f32)
    scale = lax.rsqrt(jnp.mean(x_float * x_float, axis=1, keepdims=True) + 1e-05)
    normed = (x_float * scale * gain[...].astype(f32)).astype(bf16)
    n_left[...] = normed[:, :HALF]
    n_right[...] = normed[:, HALF:]
    grad[...] = (cot[...].astype(f32) * valid_rows()).astype(bf16)
    inv[...] = jnp.broadcast_to(scale, (ROWS, 128))


def norm_rows(x, gain, cot):
    part = sds((ROWS, HALF), bf16)
    return call(
        norm_kernel,
        [part, part, sds((ROWS, WIDTH), bf16), sds((ROWS, 128), f32)],
        vmem=4,
        nbytes=4 * ROWS * WIDTH * 2,
        in_specs=[VMEM] * 3,
        name="norm_rows",
    )(x, gain, cot)


def gather_blocks(left, right):
    right_pair = jnp.stack([right, lax.ppermute(right, "tp", X_SWAP)])
    left_four = [left] + [lax.ppermute(left, "tp", z_shift(k)) for k in STEPS[1:]]
    right_four = [right_pair] + [lax.ppermute(right_pair, "tp", z_shift(k)) for k in STEPS[1:]]
    left_own = jnp.stack(left_four)
    left_other = lax.ppermute(left_own, "tp", X_SWAP)
    return [left_own, left_other] + right_four


def place_pieces(pieces, whole_ref):
    left_own, left_other = pieces[:2]
    for slot in range(4):
        rows = pl.ds(slot * ROWS, ROWS)
        other = pl.ds((4 + slot) * ROWS, ROWS)
        whole_ref[rows, :HALF] = left_own[slot]
        whole_ref[other, :HALF] = left_other[slot]
        whole_ref[rows, HALF:] = pieces[2 + slot][0]
        whole_ref[other, HALF:] = pieces[2 + slot][1]


PIECE_SHAPES = [(4, ROWS, HALF)] * 2 + [(2, ROWS, HALF)] * 4


def sum_z_kernel(own, c1, c2, c3, *refs):
    kept, sent = refs[-2:]
    total = own[...].astype(f32)
    for came in (c1, c2, c3):
        total = total + came[...].astype(f32)
    kept[...] = total[0]
    sent[...] = total[1].astype(bf16)


def sum_z(own, came, after=()):
    shape = own.shape[1:]
    return call(
        sum_z_kernel,
        [sds(shape, f32), sds(shape, bf16)],
        vmem=6,
        nbytes=11 * shape[0] * shape[1] * 2,
        in_specs=[VMEM] * 4 + [ANY] * len(after),
        out_specs=[VMEM] * 2,
        name="sum_z",
    )(own, *came, *after)


def sum_left_kernel(own, c1, c2, *refs):
    kept, sent, gain = refs[-3:]
    for part in range(2):
        total = own[part].astype(f32)
        for came in (c1, c2):
            total = total + came[part].astype(f32)
        kept[pl.ds(part * 16, 16)] = total
        total = own[2 + part].astype(f32)
        for came in (c1, c2):
            total = total + came[2 + part].astype(f32)
        sent[part] = total.astype(bf16)
    left, right = gain_from(own[4])
    for came in (c1, c2):
        more_left, more_right = gain_from(came[4])
        left, right = left + more_left, right + more_right
    sent[2] = gain_rows_of(left, right)
    gain[0:1] = left
    gain[1:2] = right


def sum_left(own, came, after=()):
    return call(
        sum_left_kernel,
        [sds((ROWS, HALF), f32), sds((3, 16, HALF), bf16), sds((2, HALF), f32)],
        vmem=4,
        nbytes=11 * ROWS * HALF * 2,
        in_specs=[VMEM] * 3 + [ANY] * len(after),
        out_specs=[VMEM] * 3,
        name="sum_left",
    )(own, *came, *after)


def sum_gain_kernel(own, came, gain, out):
    left, right = gain_from(came[2])
    out[:, :HALF] = (own[0:1] + left) / gain[:, :HALF].astype(f32)
    out[:, HALF:] = (own[1:2] + right) / gain[:, HALF:].astype(f32)


def sum_gain(own, came, gain):
    return call(
        sum_gain_kernel,
        sds((1, WIDTH), f32),
        vmem=2,
        nbytes=10 * WIDTH * 2,
        in_specs=[VMEM] * 3,
        out_specs=VMEM,
        name="sum_gain",
    )(own, came, gain)


def pass_left_kernel(back, forth, far_a, far_b, *refs):
    out_back, out_forth = refs[-2:]
    out_forth[...] = forth[...]
    out_back[...] = back[...]
    for part in range(2):
        out_forth[part] = (forth[part].astype(f32) + far_a[part].astype(f32)).astype(bf16)
        total = back[2 + part].astype(f32) + far_b[part].astype(f32)
        out_back[2 + part] = total.astype(bf16)
    left, right = gain_from(forth[4])
    more_left, more_right = gain_from(far_a[2])
    out_forth[4] = gain_rows_of(left + more_left, right + more_right)


def pass_left(back, forth, far_a, far_b, after=()):
    return call(
        pass_left_kernel,
        [sds(back.shape, bf16)] * 2,
        vmem=6,
        nbytes=6 * back.size * 2,
        in_specs=[VMEM] * 4 + [ANY] * len(after),
        out_specs=[VMEM] * 2,
        name="pass_left",
    )(back, forth, far_a, far_b, *after)


def pass_out_kernel(back, forth, far_a, far_b, *refs):
    out_back, out_forth = refs[-2:]
    half = COLS // 2
    out_forth[half:] = forth[half:]
    out_forth[:half] = (forth[:half].astype(f32) + far_a[...].astype(f32)).astype(bf16)
    out_back[:half] = back[:half]
    out_back[half:] = (back[half:].astype(f32) + far_b[...].astype(f32)).astype(bf16)


def pass_out(back, forth, far_a, far_b, after=()):
    return call(
        pass_out_kernel,
        [sds(back.shape, bf16)] * 2,
        vmem=6,
        nbytes=6 * back.size * 2,
        in_specs=[VMEM] * 4 + [ANY] * len(after),
        out_specs=[VMEM] * 2,
        name="pass_out",
    )(back, forth, far_a, far_b, *after)


def sum_out_kernel(own, came, *refs):
    kept, back, forth, far_a, far_b = refs[-5:]
    half = COLS // 2

    def total(slot, rows=slice(None)):
        return own[slot, rows].astype(f32) + came[slot, rows].astype(f32)

    kept[...] = total(0)
    back[...] = total(1).astype(bf16)
    forth[...] = total(2).astype(bf16)
    far_a[...] = total(3, slice(0, half)).astype(bf16)
    far_b[...] = total(3, slice(half, COLS)).astype(bf16)


def sum_out(own, came, after=()):
    whole_share, half_share = sds((COLS, COLS), bf16), sds((COLS // 2, COLS), bf16)
    return call(
        sum_out_kernel,
        [sds((COLS, COLS), f32), whole_share, whole_share, half_share, half_share],
        vmem=12,
        nbytes=own.size * 6,
        in_specs=[VMEM] * 2 + [ANY] * len(after),
        out_specs=[VMEM] * 5,
        name="sum_out",
    )(own, came, *after)


def sum_x_kernel(waits, own, came, *refs):
    kept, sends = refs[waits], refs[waits + 1:]
    kept[...] = own[0].astype(f32) + came[0].astype(f32)
    for slot, sent in enumerate(sends, 1):
        sent[...] = (own[slot].astype(f32) + came[slot].astype(f32)).astype(bf16)


def sum_x(own, came, after=(), sends=3):
    shape = own.shape[1:]
    return call(
        functools.partial(sum_x_kernel, len(after)),
        [sds(shape, f32)] + [sds(shape, bf16)] * sends,
        vmem=12,
        nbytes=13 * shape[0] * shape[1] * 2,
        in_specs=[VMEM] * 2 + [ANY] * len(after),
        out_specs=[VMEM] * (1 + sends),
        name="sum_x",
    )(own, came, *after)


def halves_kernel(back, forth, *refs):
    half = SLOTS // 2
    refs[-2][...] = back[:, :half]
    refs[-1][...] = forth[:, half:]


def halves(back, forth, after):
    shape = (3, SLOTS // 2, COLS)
    return call(
        halves_kernel,
        [sds(shape, bf16)] * 2,
        vmem=6,
        nbytes=8 * back.size,
        in_specs=[VMEM] * 2 + [ANY] * len(after),
        out_specs=[VMEM] * 2,
        name="halves",
    )(back, forth, *after)


def late_kernel(count, *refs):
    for i in range(count):
        refs[i - count][...] = refs[i][...]


def late(arrays, after):
    count = len(arrays)
    return call(
        functools.partial(late_kernel, count),
        [sds(v.shape, v.dtype) for v in arrays],
        vmem=10,
        nbytes=sum(v.size * 4 for v in arrays),
        in_specs=[VMEM] * count + [ANY] * len(after),
        out_specs=[VMEM] * count,
        name="late",
    )(*arrays, *after)


def sum_rest_kernel(kept, c1, c2, *refs):
    total = kept[...]
    for came in (c1, c2):
        total = total + came[...].astype(f32)
    refs[-1][...] = total


def sum_rest(kept, came, after=()):
    return call(
        sum_rest_kernel,
        sds(kept.shape, f32),
        vmem=6,
        nbytes=14 * kept.size,
        in_specs=[VMEM] * 3 + [ANY] * len(after),
        out_specs=VMEM,
        name="sum_rest",
    )(kept, *came, *after)


def sum_keys_kernel(q_grad, own, came, *refs):
    out = refs[-1]
    out[0] = q_grad[...]
    out[1:] = (own[...] + came[...].astype(f32)).astype(bf16)


def sum_keys(q_grad, own, came, after=()):
    return call(
        sum_keys_kernel,
        sds((3, SLOTS, COLS), bf16),
        vmem=8,
        nbytes=10 * came.size,
        in_specs=[VMEM] * 3 + [ANY] * len(after),
        out_specs=VMEM,
        name="sum_keys",
    )(q_grad, own, came, *after)


def rows_kernel(x, grad, gain, inv, l_kept, l_came, r_kept, r1, r2, r3, *refs):
    out = refs[-1]
    left = l_kept[...] + l_came[0:2].reshape(ROWS, HALF).astype(f32)
    right = r_kept[...]
    for came in (r1, r2, r3):
        right = right + came[...].astype(f32)
    scale = inv[:, :1]
    halves = []
    dots = jnp.zeros((ROWS, 1), f32)
    for part, cols in ((left, slice(0, HALF)), (right, slice(HALF, WIDTH))):
        scaled = gain[:, cols].astype(f32) * part
        rows = x[:, cols].astype(f32)
        dots = dots + jnp.sum(scaled * rows, axis=1, keepdims=True)
        halves.append((scaled, rows, cols))
    mean = dots * (1.0 / WIDTH)
    for scaled, rows, cols in halves:
        total = grad[:, cols].astype(f32) + scale * scaled - rows * (scale * scale * scale) * mean
        out[:, cols] = total.astype(bf16)


def token_rows(x, grad, gain, inv, left, right, after=()):
    return call(
        rows_kernel,
        sds((ROWS, WIDTH), bf16),
        vmem=4,
        nbytes=6 * ROWS * WIDTH * 2,
        in_specs=[VMEM] * 10 + [ANY] * len(after),
        out_specs=VMEM,
        name="token_rows",
    )(x, grad, gain, inv, *left, *right, *after)


def key_value_kernel(*refs):
    pieces, weight = refs[:6], refs[6]
    full, out, buffer, sems = refs[-4:]
    copies = [
        load(k_cuts(weight.at[part + 1]), k_cuts(buffer.at[part]), sems.at[part])
        for part in range(2)
    ]
    place_pieces(pieces, full)
    for part in range(2):
        out[part] = dot_loaded(full, buffer.at[part], copies[part]).astype(bf16)


def key_value(pieces, weights, after):
    return call(
        key_value_kernel,
        [sds((SLOTS, WIDTH), bf16), sds((2, SLOTS, COLS), bf16)],
        vmem=20,
        flops=4 * SLOTS * WIDTH * COLS,
        nbytes=2 * WIDTH * COLS * 2 + 2 * SLOTS * WIDTH * 2,
        in_specs=[VMEM] * 6 + [HBM] + [ANY] * len(after),
        out_specs=[VMEM] * 2,
        scratch_shapes=[
            pltpu.VMEM((2, WIDTH, COLS), bf16),
            pltpu.SemaphoreType.DMA((2, KCUTS)),
        ],
        name="key_value",
    )(*pieces, weights, *after)


def query_kernel(full, weight, *refs):
    out, buffer, sems = refs[-3:]
    copies = load(k_cuts(weight.at[0]), k_cuts(buffer), sems)
    out[...] = dot_loaded(full, buffer, copies).astype(bf16)


DOT_SCRATCH = [pltpu.VMEM((WIDTH, COLS), bf16), pltpu.SemaphoreType.DMA((KCUTS,))]


def query_of(full, weights, after):
    return call(
        query_kernel,
        sds((SLOTS, COLS), bf16),
        vmem=12,
        flops=2 * SLOTS * WIDTH * COLS,
        nbytes=WIDTH * COLS * 2 + SLOTS * WIDTH * 2,
        in_specs=[VMEM, HBM] + [ANY] * len(after),
        out_specs=VMEM,
        scratch_shapes=DOT_SCRATCH,
        name="query",
    )(full, weights, *after)


def grad_mixed_kernel(p0, p1, p2, p3, weight, *refs):
    full, out, buffer, sems = refs[-4:]
    copies = load(k_cuts(weight.at[0]), k_cuts(buffer), sems)
    for slot, pair in enumerate((p0, p1, p2, p3)):
        full[pl.ds(slot * ROWS, ROWS)] = pair[0]
        full[pl.ds((4 + slot) * ROWS, ROWS)] = pair[1]
    out[...] = dot_loaded(full, buffer, copies).astype(bf16)


def grad_mixed_of(pairs, weights, after):
    return call(
        grad_mixed_kernel,
        [sds((SLOTS, WIDTH), bf16), sds((SLOTS, COLS), bf16)],
        vmem=16,
        flops=2 * SLOTS * WIDTH * COLS,
        nbytes=WIDTH * COLS * 2 + 2 * SLOTS * WIDTH * 2,
        in_specs=[VMEM] * 4 + [HBM] + [ANY] * len(after),
        out_specs=[VMEM] * 2,
        scratch_shapes=DOT_SCRATCH,
        name="grad_mixed",
    )(*pairs, weights, *after)


def gain_rows_of(left, right):
    row = lax.broadcasted_iota(jnp.int32, (16, left.shape[1]), 0)
    rows = jnp.zeros((16, left.shape[1]), f32)
    for first, part in ((0, left), (2, right)):
        high = part.astype(bf16).astype(f32)
        rows = jnp.where(row == first, high, rows)
        rows = jnp.where(row == first + 1, part - high, rows)
    return rows.astype(bf16)


def gain_from(rows):
    rows = rows.astype(f32)
    return rows[0:1] + rows[1:2], rows[2:3] + rows[3:4]


FCUT = 512
FCUTS = HALF // FCUT


def back_products(grads, weight, first, normed, buffer, sems):
    copies = [
        load(
            [weight.at[part, pl.ds(first + cut * FCUT, FCUT)] for part in range(3)],
            [buffer.at[part, pl.ds(cut * FCUT, FCUT)] for part in range(3)],
            sems.at[cut],
        )
        for cut in range(FCUTS)
    ]
    for cut in range(FCUTS):
        for copy in copies[cut]:
            copy.wait()
        rows = slice(cut * FCUT, (cut + 1) * FCUT)
        total = dot_rows(grads[0], buffer[0, rows])
        for part in range(1, 3):
            total = total + dot_rows(grads[part], buffer[part, rows])
        rounded = total.astype(bf16)
        terms = normed[:, first + cut * FCUT:first + (cut + 1) * FCUT].astype(f32)
        gain = jnp.sum(rounded.astype(f32) * terms, axis=0, keepdims=True)
        yield rows, rounded, gain


def back_right_kernel(waits, grads, weight, normed, *refs):
    own, sent, gain, buffer, sems = refs[waits:]
    for cols, rounded, terms in back_products(
        grads, weight, HALF, normed, buffer, sems
    ):
        gain[:, cols] = terms
        for xbit, out in enumerate((own, sent)):
            for slot in range(4):
                start = (xbit * 4 + slot) * ROWS
                out[slot, :, cols] = rounded[start:start + ROWS]


def back_left_kernel(waits, grads, weight, normed, gain_right, *refs):
    outs, far, buffer, sems = refs[waits:waits + 3], refs[-4:-2], refs[-2], refs[-1]
    for cols, rounded, terms in back_products(
        grads, weight, 0, normed, buffer, sems
    ):
        gains = gain_rows_of(terms, gain_right[:, cols])
        for slot, out in enumerate(outs):
            for xbit in range(2):
                start = (xbit * 4 + slot) * ROWS
                out[2 * xbit, :, cols] = rounded[start:start + 16]
                out[2 * xbit + 1, :, cols] = rounded[start + 16:start + ROWS]
            out[4, :, cols] = gains
        for xbit, out in enumerate(far):
            start = (xbit * 4 + 3) * ROWS
            out[0, :, cols] = rounded[start:start + 16]
            out[1, :, cols] = rounded[start + 16:start + ROWS]
        far[0][2, :, cols] = gains


def back_dot(kernel, grads, weights, normed, extra, out_shape, after, name):
    return call(
        functools.partial(kernel, len(after)),
        out_shape,
        vmem=20,
        flops=2 * 3 * SLOTS * HALF * COLS,
        nbytes=3 * HALF * COLS * 2 + 2 * SLOTS * HALF * 2,
        in_specs=[VMEM, HBM, VMEM] + [VMEM] * len(extra) + [ANY] * len(after),
        out_specs=[VMEM] * len(out_shape),
        scratch_shapes=[
            pltpu.VMEM((3, HALF, COLS), bf16),
            pltpu.SemaphoreType.DMA((FCUTS, 3)),
        ],
        name=name,
    )(grads, weights, normed, *extra, *after)


def back_right(grads, weights, normed, after=()):
    out = [sds((4, ROWS, HALF), bf16)] * 2 + [sds((1, HALF), f32)]
    return back_dot(back_right_kernel, grads, weights, normed, [], out, after, "back_right")


def back_left(grads, weights, normed, gain_right, after=()):
    out = [sds((5, 16, HALF), bf16)] * 3
    out += [sds((3, 16, HALF), bf16), sds((2, 16, HALF), bf16)]
    return back_dot(back_left_kernel, grads, weights, normed, [gain_right], out, after, "back_left")


def proj_kernel(left, weight, *refs):
    outs, buffer, sems = refs[-6:-2], refs[-2], refs[-1]
    copies = load(k_cuts(weight.at[0]), k_cuts(buffer), sems)
    for cut, copy in enumerate(copies):
        copy.wait()
        cols = slice(cut * KCUT, (cut + 1) * KCUT)
        rounded = dot_rows(left[...], buffer[cols]).astype(bf16)
        for slot in range(4):
            for xbit in range(2):
                start = (xbit * 4 + slot) * ROWS
                outs[slot][xbit, :, cols] = rounded[start:start + ROWS]


def proj_parts(mixed, weights, after):
    return call(
        proj_kernel,
        [sds((2, ROWS, WIDTH), bf16)] * 4,
        vmem=14,
        flops=2 * SLOTS * WIDTH * COLS,
        nbytes=WIDTH * COLS * 2 + SLOTS * WIDTH * 2,
        in_specs=[VMEM, HBM] + [ANY] * len(after),
        out_specs=[VMEM] * 4,
        scratch_shapes=DOT_SCRATCH,
        name="proj_parts",
    )(mixed, weights, *after)


def slot_of(row, x_index, z_index):
    block = row // ROWS
    xbit = block // 4
    slot = block - xbit * 4
    back = jnp.where(slot == 2, 3, jnp.where(slot == 3, 2, slot))
    x_from = jnp.where(xbit == 0, x_index, 1 - x_index)
    z_from = z_index - back
    z_from = jnp.where(z_from < 0, z_from + 4, z_from)
    return (x_from * 4 + z_from) * ROWS + (row - block * ROWS)


def places(gaps, runs, rows, is_text):
    x_index, z_index = where_am_i()[:2]
    slot = slot_of(rows, x_index, z_index)
    text = slot
    end = jnp.int32(0)
    for run in range(4):
        end = end + gaps[0, run]
        text = text + jnp.where(slot >= end, runs[0, run], 0)
    image = slot + gaps[0, 0]
    end = jnp.int32(0)
    for run in range(3):
        end = end + runs[0, run]
        image = image + jnp.where(slot >= end, gaps[0, run + 1], 0)
    image = jnp.where(slot < LI, image, FAR)
    return jnp.where(is_text, text, image)


def admitted(gaps, runs):
    group = lax.axis_index("grp")
    rows = lax.broadcasted_iota(jnp.int32, (SLOTS, 1), 0)
    query = places(gaps, runs, rows, group == 0)
    key_row = lax.broadcasted_iota(jnp.int32, (1, SLOTS), 1)
    own = places(gaps, runs, key_row, group == 0)
    other = places(gaps, runs, key_row, group != 0)
    return own <= query, other <= query


def head_attn(query, own_key, other_key, own_ok, other_ok):
    scale = HS ** (-0.5)
    own = jnp.where(own_ok, dot_rows(query, own_key) * scale, -1e30)
    other = jnp.where(other_ok, dot_rows(query, other_key) * scale, -1e30)
    row_max = jnp.maximum(
        jnp.max(own, axis=1, keepdims=True), jnp.max(other, axis=1, keepdims=True)
    )
    own = jnp.exp(own - row_max)
    other = jnp.exp(other - row_max)
    row_sum = jnp.sum(own, axis=1, keepdims=True) + jnp.sum(other, axis=1, keepdims=True)
    share = 1.0 / row_sum
    return own * share, other * share


def forward_kernel(gaps, runs, query, own_kv, other_kv, *refs):
    mixed = refs[-1]
    own_ok, other_ok = admitted(gaps, runs)
    for head in range(HEADS):
        cols = slice(head * HS, (head + 1) * HS)
        own, other = head_attn(
            query[:, cols], own_kv[0, :, cols], other_kv[0, :, cols], own_ok, other_ok
        )
        total = dot(own.astype(bf16), own_kv[1, :, cols])
        total = total + dot(other.astype(bf16), other_kv[1, :, cols])
        mixed[:, cols] = total.astype(bf16)


def backward_kernel(gaps, runs, query, own_kv, other_kv, mixed, grad, *refs):
    q_grad, own_grad, other_grad = refs[-3:]
    scale = HS ** (-0.5)
    own_ok, other_ok = admitted(gaps, runs)
    for head in range(HEADS):
        cols = slice(head * HS, (head + 1) * HS)
        q, g = query[:, cols], grad[:, cols]
        row_dot = jnp.sum(g.astype(f32) * mixed[:, cols].astype(f32), axis=1, keepdims=True)
        attns = head_attn(q, own_kv[0, :, cols], other_kv[0, :, cols], own_ok, other_ok)
        dq = None
        for attn, kv, kv_grad in zip(attns, (own_kv, other_kv), (own_grad, other_grad)):
            value_grad = dot_tokens(attn.astype(bf16), g)
            weight_grad = dot_rows(g, kv[1, :, cols])
            score_grad = (attn * (weight_grad - row_dot)).astype(bf16)
            part = dot(score_grad, kv[0, :, cols])
            dq = part if dq is None else dq + part
            key_grad = dot_tokens(score_grad, q) * scale
            kv_grad[0, :, cols] = key_grad.astype(kv_grad.dtype)
            kv_grad[1, :, cols] = value_grad.astype(kv_grad.dtype)
        q_grad[:, cols] = (dq * scale).astype(bf16)


ATTN_FLOPS = 2 * HEADS * SLOTS * 2 * SLOTS * HS


def attend_forward(spans, query, own_kv, other_kv, after):
    return call(
        forward_kernel,
        sds((SLOTS, COLS), bf16),
        vmem=10,
        flops=4 * ATTN_FLOPS,
        nbytes=6 * SLOTS * COLS * 2,
        in_specs=[SMEM] * 2 + [VMEM] * 3 + [ANY] * len(after),
        out_specs=VMEM,
        name="attend_forward",
    )(*spans, query, own_kv, other_kv, *after)


def attend_backward(spans, query, own_kv, other_kv, mixed, grad, after):
    kv = (2, SLOTS, COLS)
    return call(
        backward_kernel,
        [sds((SLOTS, COLS), bf16), sds(kv, f32), sds(kv, bf16)],
        vmem=14,
        flops=8 * ATTN_FLOPS,
        nbytes=12 * SLOTS * COLS * 2,
        in_specs=[SMEM] * 2 + [VMEM] * 5 + [ANY] * len(after),
        out_specs=[VMEM] * 3,
        name="attend_backward",
    )(*spans, query, own_kv, other_kv, mixed, grad, *after)


def out_kernel(grad, mixed, *refs):
    own, sent = refs[-2:]
    y_index, core = where_am_i()[2:4]
    for i in range(8):
        column = ((y_index - STEPS[i % 4]) & 3) * 2 + (1 - core if i < 4 else core)
        start = pl.multiple_of(column * COLS, COLS)
        share = dot_tokens(grad[:, pl.ds(start, COLS)], mixed[...]).astype(bf16)
        if i < 4:
            sent[i] = share
        else:
            own[i - 4] = share


def out_weight_parts(grad_full, mixed, after):
    return call(
        out_kernel,
        [sds((4, COLS, COLS), bf16)] * 2,
        vmem=12,
        flops=2 * SLOTS * WIDTH * COLS,
        nbytes=SLOTS * WIDTH * 2 + WIDTH * COLS * 2,
        in_specs=[VMEM] * 2 + [ANY] * len(after),
        out_specs=[VMEM] * 2,
        name="out_weight_parts",
    )(grad_full, mixed, *after)


def share_kernel(which, full, c1, c2, c3, g0, g1, g2, g3, g4, *refs):
    out, lefts = refs[-2:]
    y_index, core = where_am_i()[2:4]
    column = core if which else 1 - core
    start = pl.multiple_of((y_index * 2 + column) * COLS, COLS)
    lefts[0] = full[:, pl.ds(start, COLS)].T
    start = pl.multiple_of(column * COLS, COLS)
    for k, came in enumerate((c1, c2, c3), 1):
        lefts[k] = came[:, pl.ds(start, COLS)].T
    for part in range(3):
        total = dot(lefts[0], g0[part])
        for k, grad in enumerate((g1, g2), 1):
            total = total + dot(lefts[k], grad[part])
        total = total + dot(lefts[3, :, :SLOTS // 2], g3[part])
        total = total + dot(lefts[3, :, SLOTS // 2:], g4[part])
        out[part] = total.astype(out.dtype)


def weight_shares(which, full, came, grads, dtype, after=()):
    return call(
        functools.partial(share_kernel, which),
        sds((3, COLS, COLS), dtype),
        vmem=20,
        flops=3 * 4 * 2 * SLOTS * COLS * COLS,
        nbytes=16 * SLOTS * COLS * 2 + 3 * COLS * COLS * 4,
        in_specs=[VMEM] * 9 + [ANY] * len(after),
        out_specs=VMEM,
        scratch_shapes=[pltpu.VMEM((4, COLS, SLOTS), bf16)],
        name="weight_shares",
    )(full, *came, *grads, *after)


def chunk_kernel(full, *outs):
    y_index = where_am_i()[2]
    for k, out in zip(STEPS[1:], outs):
        start = pl.multiple_of(((y_index + k) & 3) * 1024, 1024)
        out[...] = full[:, pl.ds(start, 1024)]


def chunks_over_y(full):
    sends = call(
        chunk_kernel,
        [sds((SLOTS, 1024), bf16)] * 3,
        vmem=6,
        nbytes=6 * SLOTS * 1024 * 2,
        in_specs=[VMEM],
        out_specs=[VMEM] * 3,
        name="chunks",
    )(full)
    return [lax.ppermute(sent, "seq", y_shift(k)) for sent, k in zip(sends, STEPS[1:])]


def layer_kernel(x, kept, came, *refs):
    total = x[...].astype(f32) + (kept[...] + came[...].astype(f32))
    refs[-1][...] = (total * valid_rows()).astype(bf16)


def layer_rows(x, kept, came, after=()):
    return call(
        layer_kernel,
        sds((ROWS, WIDTH), bf16),
        vmem=4,
        nbytes=5 * ROWS * WIDTH * 2,
        in_specs=[VMEM] * 3 + [ANY] * len(after),
        out_specs=VMEM,
        name="layer_rows",
    )(x, kept, came, *after)


def per_device(tokens, text_gaps, image_runs, gains, w_qkv, w_out, cotangent):
    x_rows = tokens[0, 0]
    w_parts = jnp.transpose(w_qkv[0], (1, 0, 2))
    spans = (text_gaps, image_runs)

    n_left, n_right, grad_rows, inv = norm_rows(x_rows, gains, cotangent[0, 0])
    pieces = gather_blocks(n_left, n_right)
    grad_other = lax.ppermute(grad_rows, "tp", X_SWAP)
    grad_pair = touch(jnp.stack([grad_rows, grad_other]), w_parts)
    grad_pairs = [grad_pair] + [lax.ppermute(grad_pair, "tp", z_shift(k)) for k in STEPS[1:]]
    normed_full, own_kv = key_value(pieces, w_parts, [grad_pair])
    other_kv = lax.ppermute(own_kv, "grp", GRP_SWAP)
    query = query_of(normed_full, w_parts, grad_pairs[1:3])
    chunks = chunks_over_y(normed_full)

    mixed = attend_forward(spans, query, own_kv, other_kv, [])
    proj = proj_parts(mixed, w_out, [])
    grad_full, grad_mixed = grad_mixed_of(grad_pairs, w_out, [proj[0]] + chunks[:2])
    q_grad, own_part, other_part = attend_backward(
        spans, query, own_kv, other_kv, mixed, grad_mixed, []
    )
    back = lax.ppermute(other_part, "grp", GRP_SWAP)
    sends = late(proj[1:3], [q_grad])
    proj_came = [lax.ppermute(v, "tp", z_shift(-k)) for v, k in zip(sends, STEPS[1:3])]
    out_own, out_sent = out_weight_parts(grad_full, mixed, [q_grad])
    out_came = lax.ppermute(out_sent, "seq", CORE_SWAP)
    own_grads = sum_keys(q_grad, own_part, back, sends[:1])
    back_grads = lax.ppermute(own_grads, "seq", y_shift(1))
    next_grads = lax.ppermute(own_grads, "seq", y_shift(3))

    right = back_right(own_grads, w_parts, normed_full, [out_came] + chunks[2:])
    right_x = lax.ppermute(right[1], "tp", X_SWAP)
    left = back_left(own_grads, w_parts, normed_full, right[2], proj_came[:2])
    left_far_a = lax.ppermute(left[3], "tp", z_shift(1))
    left_far_b = lax.ppermute(left[4], "tp", z_shift(3))
    left_back, left_forth = pass_left(left[1], left[2], left_far_a, left_far_b)
    left_came = [
        lax.ppermute(left_forth, "tp", z_shift(1)), lax.ppermute(left_back, "tp", z_shift(3))
    ]
    out_kept, *out_sends = sum_out(
        out_own, out_came, [left_back, back_grads, next_grads, right_x]
    )
    out_far_a = lax.ppermute(out_sends[2], "seq", y_shift(1))
    out_far_b = lax.ppermute(out_sends[3], "seq", y_shift(3))
    out_back, out_forth = pass_out(
        out_sends[0], out_sends[1], out_far_a, out_far_b
    )
    out_terms = [
        lax.ppermute(out_forth, "seq", y_shift(1)), lax.ppermute(out_back, "seq", y_shift(3))
    ]
    left_kept, left_sent, gain_kept = sum_left(left[0], left_came, [out_back])
    left_x = lax.ppermute(left_sent, "tp", X_SWAP)
    gain_tp = sum_gain(gain_kept, left_x, gains)
    gain_sum = gain_tp + lax.ppermute(gain_tp, "seq", CORE_SWAP)
    gain_grad = gain_sum
    for k in STEPS[1:]:
        gain_grad = gain_grad + lax.ppermute(gain_sum, "seq", y_shift(k))
    right_kept, *right_sends = sum_x(
        right[0], right_x, [left_sent]
    )
    right_came = [lax.ppermute(v, "tp", z_shift(-k)) for v, k in zip(right_sends, STEPS[1:])]
    (far_sent,) = late(proj[3:], right_came[:1])
    proj_came.append(lax.ppermute(far_sent, "tp", z_shift(2)))
    relayed = halves(
        back_grads, next_grads, [gain_tp, far_sent] + right_came + out_terms
    )
    grads = [own_grads, back_grads, next_grads]
    grads += [lax.ppermute(v, "seq", y_shift(k)) for v, k in zip(relayed, (1, 3))]
    shares = (normed_full, chunks, grads)
    qkv_sent = weight_shares(0, *shares, bf16, [gain_sum])
    qkv_mine = weight_shares(1, *shares, f32, [qkv_sent])
    out_share = sum_rest(out_kept, out_terms, [qkv_sent])
    tokens_grad = token_rows(
        x_rows, grad_rows, gains, inv, (left_kept, left_x), (right_kept, *right_came), [qkv_mine, out_share]
    )

    qkv_share = qkv_mine + lax.ppermute(qkv_sent, "seq", CORE_SWAP).astype(f32)
    proj_kept, proj_sent = sum_z(proj[0], proj_came)
    proj_x = lax.ppermute(proj_sent, "tp", X_SWAP)
    layer_out = layer_rows(x_rows, proj_kept, proj_x, [tokens_grad])
    return (
        layer_out[None, None],
        tokens_grad[None, None],
        gain_grad,
        jnp.transpose(qkv_share, (1, 0, 2))[None],
        out_share[None],
    )


def solution(mesh):
    in_specs = (
        P("grp", "seq", "tp", None),
        P("seq", None),
        P("seq", None),
        P("grp", None),
        P("grp", None, None, "tp"),
        P("grp", None, "tp"),
        P("grp", "seq", "tp", None),
    )
    out_specs = (
        P("grp", "seq", "tp", None),
        P("grp", "seq", "tp", None),
        P("grp", None),
        P("grp", "seq", None, "tp"),
        P("grp", "seq", "tp"),
    )
    return jax.shard_map(
        per_device, mesh=mesh, in_specs=in_specs, out_specs=out_specs, check_vma=False
    )
```

```python
import functools

import jax
import jax.numpy as jnp
from jax import lax
from jax.experimental import pallas as pl
from jax.experimental.pallas import tpu as pltpu
from jax.sharding import PartitionSpec as P

HS = 128
LI = 128
HEADS = 4
SLOTS = 256
ROWS = 32
WIDTH = 4096
HALF = 2048
COLS = 512
FAR = 1073741824
f32 = jnp.float32
bf16 = jnp.bfloat16
MIB = 1024 * 1024

STEPS = (0, 1, 3, 2)


def z_shift(k):
    return [(i, (i // 4) * 4 + (i + k) % 4) for i in range(8)]


X_SWAP = [(i, i ^ 4) for i in range(8)]


def y_shift(k):
    return [(i, (i + 2 * k) % 8) for i in range(8)]


CORE_SWAP = [(i, i ^ 1) for i in range(8)]
GRP_SWAP = [(0, 1), (1, 0)]


def sds(shape, dtype):
    return jax.ShapeDtypeStruct(shape, dtype)


def call(kernel, out_shape, vmem, flops=0, nbytes=0, **kwargs):
    return pl.pallas_call(
        kernel,
        out_shape=out_shape,
        compiler_params=pltpu.CompilerParams(vmem_limit_bytes=vmem * MIB),
        cost_estimate=pl.CostEstimate(flops=flops, bytes_accessed=nbytes, transcendentals=0),
        **kwargs,
    )


def whole(shape):
    return pl.BlockSpec(shape, lambda *_: (0,) * len(shape))


SMEM = pl.BlockSpec(memory_space=pltpu.SMEM)
VMEM = pl.BlockSpec(memory_space=pltpu.VMEM)
ANY = pl.BlockSpec(memory_space=pl.ANY)
HBM = pl.BlockSpec(memory_space=pltpu.HBM)


def dot(left, right):
    return jnp.dot(left, right, preferred_element_type=f32)


def dot_rows(left, right):
    return lax.dot_general(left, right, (((1,), (1,)), ((), ())), preferred_element_type=f32)


def dot_tokens(left, right):
    return lax.dot_general(left, right, (((0,), (0,)), ((), ())), preferred_element_type=f32)


def where_am_i():
    tp, seq = lax.axis_index("tp"), lax.axis_index("seq")
    return tp >> 2, tp & 3, seq >> 1, seq & 1, lax.axis_index("grp")


def valid_rows():
    used = jnp.logical_or(lax.axis_index("grp") == 0, lax.axis_index("tp") * ROWS < LI)
    return jnp.where(used, 1.0, 0.0).astype(f32)


def load(sources, targets, sems):
    copies = [
        pltpu.make_async_copy(source, target, sems.at[i])
        for i, (source, target) in enumerate(zip(sources, targets))
    ]
    for copy in copies:
        copy.start()
    return copies


KCUT = 1024
KCUTS = WIDTH // KCUT


def dot_loaded(full, buffer, copies):
    total = None
    for i, copy in enumerate(copies):
        copy.wait()
        cut = slice(i * KCUT, (i + 1) * KCUT)
        part = dot(full[:, cut], buffer[cut])
        total = part if total is None else total + part
    return total


def k_cuts(ref):
    return [ref.at[pl.ds(i * KCUT, KCUT)] for i in range(KCUTS)]


def touch_kernel(weight, pair, *refs):
    refs[-1][...] = pair[...]


def touch(pair, weight):
    return call(
        touch_kernel,
        sds(pair.shape, pair.dtype),
        vmem=4,
        nbytes=pair.size * 4,
        in_specs=[ANY, VMEM],
        out_specs=VMEM,
        name="touch",
    )(weight, pair)


def norm_kernel(x, gain, cot, n_left, n_right, grad, inv):
    x_float = x[...].astype(f32)
    scale = lax.rsqrt(jnp.mean(x_float * x_float, axis=1, keepdims=True) + 1e-05)
    normed = (x_float * scale * gain[...].astype(f32)).astype(bf16)
    n_left[...] = normed[:, :HALF]
    n_right[...] = normed[:, HALF:]
    grad[...] = (cot[...].astype(f32) * valid_rows()).astype(bf16)
    inv[...] = jnp.broadcast_to(scale, (ROWS, 128))


def norm_rows(x, gain, cot):
    part = sds((ROWS, HALF), bf16)
    return call(
        norm_kernel,
        [part, part, sds((ROWS, WIDTH), bf16), sds((ROWS, 128), f32)],
        vmem=4,
        nbytes=4 * ROWS * WIDTH * 2,
        in_specs=[VMEM] * 3,
        name="norm_rows",
    )(x, gain, cot)


def gather_blocks(left, right):
    right_pair = jnp.stack([right, lax.ppermute(right, "tp", X_SWAP)])
    left_four = [left] + [lax.ppermute(left, "tp", z_shift(k)) for k in STEPS[1:]]
    right_four = [right_pair] + [lax.ppermute(right_pair, "tp", z_shift(k)) for k in STEPS[1:]]
    left_own = jnp.stack(left_four)
    left_other = lax.ppermute(left_own, "tp", X_SWAP)
    return [left_own, left_other] + right_four


def place_pieces(pieces, whole_ref):
    left_own, left_other = pieces[:2]
    for slot in range(4):
        rows = pl.ds(slot * ROWS, ROWS)
        other = pl.ds((4 + slot) * ROWS, ROWS)
        whole_ref[rows, :HALF] = left_own[slot]
        whole_ref[other, :HALF] = left_other[slot]
        whole_ref[rows, HALF:] = pieces[2 + slot][0]
        whole_ref[other, HALF:] = pieces[2 + slot][1]


PIECE_SHAPES = [(4, ROWS, HALF)] * 2 + [(2, ROWS, HALF)] * 4


def sum_z_kernel(own, c1, c2, c3, *refs):
    kept, sent = refs[-2:]
    total = own[...].astype(f32)
    for came in (c1, c2, c3):
        total = total + came[...].astype(f32)
    kept[...] = total[0]
    sent[...] = total[1].astype(bf16)


def sum_z(own, came, after=()):
    shape = own.shape[1:]
    return call(
        sum_z_kernel,
        [sds(shape, f32), sds(shape, bf16)],
        vmem=6,
        nbytes=11 * shape[0] * shape[1] * 2,
        in_specs=[VMEM] * 4 + [ANY] * len(after),
        out_specs=[VMEM] * 2,
        name="sum_z",
    )(own, *came, *after)


def sum_left_kernel(own, c1, c2, *refs):
    kept, sent, gain = refs[-3:]
    for part in range(2):
        total = own[part].astype(f32)
        for came in (c1, c2):
            total = total + came[part].astype(f32)
        kept[pl.ds(part * 16, 16)] = total
        total = own[2 + part].astype(f32)
        for came in (c1, c2):
            total = total + came[2 + part].astype(f32)
        sent[part] = total.astype(bf16)
    left, right = gain_from(own[4])
    for came in (c1, c2):
        more_left, more_right = gain_from(came[4])
        left, right = left + more_left, right + more_right
    sent[2] = gain_rows_of(left, right)
    gain[0:1] = left
    gain[1:2] = right


def sum_left(own, came, after=()):
    return call(
        sum_left_kernel,
        [sds((ROWS, HALF), f32), sds((3, 16, HALF), bf16), sds((2, HALF), f32)],
        vmem=4,
        nbytes=11 * ROWS * HALF * 2,
        in_specs=[VMEM] * 3 + [ANY] * len(after),
        out_specs=[VMEM] * 3,
        name="sum_left",
    )(own, *came, *after)


def sum_gain_kernel(own, came, gain, out):
    left, right = gain_from(came[2])
    out[:, :HALF] = (own[0:1] + left) / gain[:, :HALF].astype(f32)
    out[:, HALF:] = (own[1:2] + right) / gain[:, HALF:].astype(f32)


def sum_gain(own, came, gain):
    return call(
        sum_gain_kernel,
        sds((1, WIDTH), f32),
        vmem=2,
        nbytes=10 * WIDTH * 2,
        in_specs=[VMEM] * 3,
        out_specs=VMEM,
        name="sum_gain",
    )(own, came, gain)


def pass_left_kernel(back, forth, far_a, far_b, *refs):
    out_back, out_forth = refs[-2:]
    out_forth[...] = forth[...]
    out_back[...] = back[...]
    for part in range(2):
        out_forth[part] = (forth[part].astype(f32) + far_a[part].astype(f32)).astype(bf16)
        total = back[2 + part].astype(f32) + far_b[part].astype(f32)
        out_back[2 + part] = total.astype(bf16)
    left, right = gain_from(forth[4])
    more_left, more_right = gain_from(far_a[2])
    out_forth[4] = gain_rows_of(left + more_left, right + more_right)


def pass_left(back, forth, far_a, far_b, after=()):
    return call(
        pass_left_kernel,
        [sds(back.shape, bf16)] * 2,
        vmem=6,
        nbytes=6 * back.size * 2,
        in_specs=[VMEM] * 4 + [ANY] * len(after),
        out_specs=[VMEM] * 2,
        name="pass_left",
    )(back, forth, far_a, far_b, *after)


def pass_out_kernel(back, forth, far_a, far_b, *refs):
    out_back, out_forth = refs[-2:]
    half = COLS // 2
    out_forth[half:] = forth[half:]
    out_forth[:half] = (forth[:half].astype(f32) + far_a[...].astype(f32)).astype(bf16)
    out_back[:half] = back[:half]
    out_back[half:] = (back[half:].astype(f32) + far_b[...].astype(f32)).astype(bf16)


def pass_out(back, forth, far_a, far_b, after=()):
    return call(
        pass_out_kernel,
        [sds(back.shape, bf16)] * 2,
        vmem=6,
        nbytes=6 * back.size * 2,
        in_specs=[VMEM] * 4 + [ANY] * len(after),
        out_specs=[VMEM] * 2,
        name="pass_out",
    )(back, forth, far_a, far_b, *after)


def sum_out_kernel(own, came, *refs):
    kept, back, forth, far_a, far_b = refs[-5:]
    half = COLS // 2

    def total(slot, rows=slice(None)):
        return own[slot, rows].astype(f32) + came[slot, rows].astype(f32)

    kept[...] = total(0)
    back[...] = total(1).astype(bf16)
    forth[...] = total(2).astype(bf16)
    far_a[...] = total(3, slice(0, half)).astype(bf16)
    far_b[...] = total(3, slice(half, COLS)).astype(bf16)


def sum_out(own, came, after=()):
    whole_share, half_share = sds((COLS, COLS), bf16), sds((COLS // 2, COLS), bf16)
    return call(
        sum_out_kernel,
        [sds((COLS, COLS), f32), whole_share, whole_share, half_share, half_share],
        vmem=12,
        nbytes=own.size * 6,
        in_specs=[VMEM] * 2 + [ANY] * len(after),
        out_specs=[VMEM] * 5,
        name="sum_out",
    )(own, came, *after)


def sum_x_kernel(waits, own, came, *refs):
    kept, sends = refs[waits], refs[waits + 1:]
    kept[...] = own[0].astype(f32) + came[0].astype(f32)
    for slot, sent in enumerate(sends, 1):
        sent[...] = (own[slot].astype(f32) + came[slot].astype(f32)).astype(bf16)


def sum_x(own, came, after=(), sends=3):
    shape = own.shape[1:]
    return call(
        functools.partial(sum_x_kernel, len(after)),
        [sds(shape, f32)] + [sds(shape, bf16)] * sends,
        vmem=12,
        nbytes=13 * shape[0] * shape[1] * 2,
        in_specs=[VMEM] * 2 + [ANY] * len(after),
        out_specs=[VMEM] * (1 + sends),
        name="sum_x",
    )(own, came, *after)


def halves_kernel(back, forth, *refs):
    half = SLOTS // 2
    refs[-2][...] = back[:, :half]
    refs[-1][...] = forth[:, half:]


def halves(back, forth, after):
    shape = (3, SLOTS // 2, COLS)
    return call(
        halves_kernel,
        [sds(shape, bf16)] * 2,
        vmem=6,
        nbytes=8 * back.size,
        in_specs=[VMEM] * 2 + [ANY] * len(after),
        out_specs=[VMEM] * 2,
        name="halves",
    )(back, forth, *after)


def late_kernel(count, *refs):
    for i in range(count):
        refs[i - count][...] = refs[i][...]


def late(arrays, after):
    count = len(arrays)
    return call(
        functools.partial(late_kernel, count),
        [sds(v.shape, v.dtype) for v in arrays],
        vmem=10,
        nbytes=sum(v.size * 4 for v in arrays),
        in_specs=[VMEM] * count + [ANY] * len(after),
        out_specs=[VMEM] * count,
        name="late",
    )(*arrays, *after)


def sum_rest_kernel(kept, c1, c2, *refs):
    total = kept[...]
    for came in (c1, c2):
        total = total + came[...].astype(f32)
    refs[-1][...] = total


def sum_rest(kept, came, after=()):
    return call(
        sum_rest_kernel,
        sds(kept.shape, f32),
        vmem=6,
        nbytes=14 * kept.size,
        in_specs=[VMEM] * 3 + [ANY] * len(after),
        out_specs=VMEM,
        name="sum_rest",
    )(kept, *came, *after)


def sum_keys_kernel(q_grad, own, came, *refs):
    out = refs[-1]
    out[0] = q_grad[...]
    out[1:] = (own[...] + came[...].astype(f32)).astype(bf16)


def sum_keys(q_grad, own, came, after=()):
    return call(
        sum_keys_kernel,
        sds((3, SLOTS, COLS), bf16),
        vmem=8,
        nbytes=10 * came.size,
        in_specs=[VMEM] * 3 + [ANY] * len(after),
        out_specs=VMEM,
        name="sum_keys",
    )(q_grad, own, came, *after)


def rows_kernel(x, grad, gain, inv, l_kept, l_came, r_kept, r1, r2, r3, *refs):
    out = refs[-1]
    left = l_kept[...] + l_came[0:2].reshape(ROWS, HALF).astype(f32)
    right = r_kept[...]
    for came in (r1, r2, r3):
        right = right + came[...].astype(f32)
    scale = inv[:, :1]
    halves = []
    dots = jnp.zeros((ROWS, 1), f32)
    for part, cols in ((left, slice(0, HALF)), (right, slice(HALF, WIDTH))):
        scaled = gain[:, cols].astype(f32) * part
        rows = x[:, cols].astype(f32)
        dots = dots + jnp.sum(scaled * rows, axis=1, keepdims=True)
        halves.append((scaled, rows, cols))
    mean = dots * (1.0 / WIDTH)
    for scaled, rows, cols in halves:
        total = grad[:, cols].astype(f32) + scale * scaled - rows * (scale * scale * scale) * mean
        out[:, cols] = total.astype(bf16)


def token_rows(x, grad, gain, inv, left, right, after=()):
    return call(
        rows_kernel,
        sds((ROWS, WIDTH), bf16),
        vmem=4,
        nbytes=6 * ROWS * WIDTH * 2,
        in_specs=[VMEM] * 10 + [ANY] * len(after),
        out_specs=VMEM,
        name="token_rows",
    )(x, grad, gain, inv, *left, *right, *after)


def key_value_kernel(*refs):
    pieces, weight = refs[:6], refs[6]
    full, out, buffer, sems = refs[-4:]
    copies = [
        load(k_cuts(weight.at[part + 1]), k_cuts(buffer.at[part]), sems.at[part])
        for part in range(2)
    ]
    place_pieces(pieces, full)
    for part in range(2):
        out[part] = dot_loaded(full, buffer.at[part], copies[part]).astype(bf16)


def key_value(pieces, weights, after):
    return call(
        key_value_kernel,
        [sds((SLOTS, WIDTH), bf16), sds((2, SLOTS, COLS), bf16)],
        vmem=20,
        flops=4 * SLOTS * WIDTH * COLS,
        nbytes=2 * WIDTH * COLS * 2 + 2 * SLOTS * WIDTH * 2,
        in_specs=[VMEM] * 6 + [HBM] + [ANY] * len(after),
        out_specs=[VMEM] * 2,
        scratch_shapes=[
            pltpu.VMEM((2, WIDTH, COLS), bf16),
            pltpu.SemaphoreType.DMA((2, KCUTS)),
        ],
        name="key_value",
    )(*pieces, weights, *after)


def query_kernel(full, weight, *refs):
    out, buffer, sems = refs[-3:]
    copies = load(k_cuts(weight.at[0]), k_cuts(buffer), sems)
    out[...] = dot_loaded(full, buffer, copies).astype(bf16)


DOT_SCRATCH = [pltpu.VMEM((WIDTH, COLS), bf16), pltpu.SemaphoreType.DMA((KCUTS,))]


def query_of(full, weights, after):
    return call(
        query_kernel,
        sds((SLOTS, COLS), bf16),
        vmem=12,
        flops=2 * SLOTS * WIDTH * COLS,
        nbytes=WIDTH * COLS * 2 + SLOTS * WIDTH * 2,
        in_specs=[VMEM, HBM] + [ANY] * len(after),
        out_specs=VMEM,
        scratch_shapes=DOT_SCRATCH,
        name="query",
    )(full, weights, *after)


def grad_mixed_kernel(p0, p1, p2, p3, weight, *refs):
    full, out, buffer, sems = refs[-4:]
    copies = load(k_cuts(weight.at[0]), k_cuts(buffer), sems)
    for slot, pair in enumerate((p0, p1, p2, p3)):
        full[pl.ds(slot * ROWS, ROWS)] = pair[0]
        full[pl.ds((4 + slot) * ROWS, ROWS)] = pair[1]
    out[...] = dot_loaded(full, buffer, copies).astype(bf16)


def grad_mixed_of(pairs, weights, after):
    return call(
        grad_mixed_kernel,
        [sds((SLOTS, WIDTH), bf16), sds((SLOTS, COLS), bf16)],
        vmem=16,
        flops=2 * SLOTS * WIDTH * COLS,
        nbytes=WIDTH * COLS * 2 + 2 * SLOTS * WIDTH * 2,
        in_specs=[VMEM] * 4 + [HBM] + [ANY] * len(after),
        out_specs=[VMEM] * 2,
        scratch_shapes=DOT_SCRATCH,
        name="grad_mixed",
    )(*pairs, weights, *after)


def gain_rows_of(left, right):
    row = lax.broadcasted_iota(jnp.int32, (16, left.shape[1]), 0)
    rows = jnp.zeros((16, left.shape[1]), f32)
    for first, part in ((0, left), (2, right)):
        high = part.astype(bf16).astype(f32)
        rows = jnp.where(row == first, high, rows)
        rows = jnp.where(row == first + 1, part - high, rows)
    return rows.astype(bf16)


def gain_from(rows):
    rows = rows.astype(f32)
    return rows[0:1] + rows[1:2], rows[2:3] + rows[3:4]


FCUT = 512
FCUTS = HALF // FCUT


def back_products(grads, weight, first, normed, buffer, sems):
    copies = [
        load(
            [weight.at[part, pl.ds(first + cut * FCUT, FCUT)] for part in range(3)],
            [buffer.at[part, pl.ds(cut * FCUT, FCUT)] for part in range(3)],
            sems.at[cut],
        )
        for cut in range(FCUTS)
    ]
    for cut in range(FCUTS):
        for copy in copies[cut]:
            copy.wait()
        rows = slice(cut * FCUT, (cut + 1) * FCUT)
        total = dot_rows(grads[0], buffer[0, rows])
        for part in range(1, 3):
            total = total + dot_rows(grads[part], buffer[part, rows])
        rounded = total.astype(bf16)
        terms = normed[:, first + cut * FCUT:first + (cut + 1) * FCUT].astype(f32)
        gain = jnp.sum(rounded.astype(f32) * terms, axis=0, keepdims=True)
        yield rows, rounded, gain


def back_right_kernel(waits, grads, weight, normed, *refs):
    own, sent, gain, buffer, sems = refs[waits:]
    for cols, rounded, terms in back_products(
        grads, weight, HALF, normed, buffer, sems
    ):
        gain[:, cols] = terms
        for xbit, out in enumerate((own, sent)):
            for slot in range(4):
                start = (xbit * 4 + slot) * ROWS
                out[slot, :, cols] = rounded[start:start + ROWS]


def back_left_kernel(waits, grads, weight, normed, gain_right, *refs):
    outs, far, buffer, sems = refs[waits:waits + 3], refs[-4:-2], refs[-2], refs[-1]
    for cols, rounded, terms in back_products(
        grads, weight, 0, normed, buffer, sems
    ):
        gains = gain_rows_of(terms, gain_right[:, cols])
        for slot, out in enumerate(outs):
            for xbit in range(2):
                start = (xbit * 4 + slot) * ROWS
                out[2 * xbit, :, cols] = rounded[start:start + 16]
                out[2 * xbit + 1, :, cols] = rounded[start + 16:start + ROWS]
            out[4, :, cols] = gains
        for xbit, out in enumerate(far):
            start = (xbit * 4 + 3) * ROWS
            out[0, :, cols] = rounded[start:start + 16]
            out[1, :, cols] = rounded[start + 16:start + ROWS]
        far[0][2, :, cols] = gains


def back_dot(kernel, grads, weights, normed, extra, out_shape, after, name):
    return call(
        functools.partial(kernel, len(after)),
        out_shape,
        vmem=20,
        flops=2 * 3 * SLOTS * HALF * COLS,
        nbytes=3 * HALF * COLS * 2 + 2 * SLOTS * HALF * 2,
        in_specs=[VMEM, HBM, VMEM] + [VMEM] * len(extra) + [ANY] * len(after),
        out_specs=[VMEM] * len(out_shape),
        scratch_shapes=[
            pltpu.VMEM((3, HALF, COLS), bf16),
            pltpu.SemaphoreType.DMA((FCUTS, 3)),
        ],
        name=name,
    )(grads, weights, normed, *extra, *after)


def back_right(grads, weights, normed, after=()):
    out = [sds((4, ROWS, HALF), bf16)] * 2 + [sds((1, HALF), f32)]
    return back_dot(back_right_kernel, grads, weights, normed, [], out, after, "back_right")


def back_left(grads, weights, normed, gain_right, after=()):
    out = [sds((5, 16, HALF), bf16)] * 3
    out += [sds((3, 16, HALF), bf16), sds((2, 16, HALF), bf16)]
    return back_dot(back_left_kernel, grads, weights, normed, [gain_right], out, after, "back_left")


def proj_kernel(left, weight, *refs):
    outs, buffer, sems = refs[-6:-2], refs[-2], refs[-1]
    copies = load(k_cuts(weight.at[0]), k_cuts(buffer), sems)
    for cut, copy in enumerate(copies):
        copy.wait()
        cols = slice(cut * KCUT, (cut + 1) * KCUT)
        rounded = dot_rows(left[...], buffer[cols]).astype(bf16)
        for slot in range(4):
            for xbit in range(2):
                start = (xbit * 4 + slot) * ROWS
                outs[slot][xbit, :, cols] = rounded[start:start + ROWS]


def proj_parts(mixed, weights, after):
    return call(
        proj_kernel,
        [sds((2, ROWS, WIDTH), bf16)] * 4,
        vmem=14,
        flops=2 * SLOTS * WIDTH * COLS,
        nbytes=WIDTH * COLS * 2 + SLOTS * WIDTH * 2,
        in_specs=[VMEM, HBM] + [ANY] * len(after),
        out_specs=[VMEM] * 4,
        scratch_shapes=DOT_SCRATCH,
        name="proj_parts",
    )(mixed, weights, *after)


def slot_of(row, x_index, z_index):
    block = row // ROWS
    xbit = block // 4
    slot = block - xbit * 4
    back = jnp.where(slot == 2, 3, jnp.where(slot == 3, 2, slot))
    x_from = jnp.where(xbit == 0, x_index, 1 - x_index)
    z_from = z_index - back
    z_from = jnp.where(z_from < 0, z_from + 4, z_from)
    return (x_from * 4 + z_from) * ROWS + (row - block * ROWS)


def places(gaps, runs, rows, is_text):
    x_index, z_index = where_am_i()[:2]
    slot = slot_of(rows, x_index, z_index)
    text = slot
    end = jnp.int32(0)
    for run in range(4):
        end = end + gaps[0, run]
        text = text + jnp.where(slot >= end, runs[0, run], 0)
    image = slot + gaps[0, 0]
    end = jnp.int32(0)
    for run in range(3):
        end = end + runs[0, run]
        image = image + jnp.where(slot >= end, gaps[0, run + 1], 0)
    image = jnp.where(slot < LI, image, FAR)
    return jnp.where(is_text, text, image)


def admitted(gaps, runs):
    group = lax.axis_index("grp")
    rows = lax.broadcasted_iota(jnp.int32, (SLOTS, 1), 0)
    query = places(gaps, runs, rows, group == 0)
    key_row = lax.broadcasted_iota(jnp.int32, (1, SLOTS), 1)
    own = places(gaps, runs, key_row, group == 0)
    other = places(gaps, runs, key_row, group != 0)
    return own <= query, other <= query


def head_attn(query, own_key, other_key, own_ok, other_ok):
    scale = HS ** (-0.5)
    own = jnp.where(own_ok, dot_rows(query, own_key) * scale, -1e30)
    other = jnp.where(other_ok, dot_rows(query, other_key) * scale, -1e30)
    row_max = jnp.maximum(
        jnp.max(own, axis=1, keepdims=True), jnp.max(other, axis=1, keepdims=True)
    )
    own = jnp.exp(own - row_max)
    other = jnp.exp(other - row_max)
    row_sum = jnp.sum(own, axis=1, keepdims=True) + jnp.sum(other, axis=1, keepdims=True)
    share = 1.0 / row_sum
    return own * share, other * share


def forward_kernel(gaps, runs, query, own_kv, other_kv, *refs):
    mixed = refs[-1]
    own_ok, other_ok = admitted(gaps, runs)
    for head in range(HEADS):
        cols = slice(head * HS, (head + 1) * HS)
        own, other = head_attn(
            query[:, cols], own_kv[0, :, cols], other_kv[0, :, cols], own_ok, other_ok
        )
        total = dot(own.astype(bf16), own_kv[1, :, cols])
        total = total + dot(other.astype(bf16), other_kv[1, :, cols])
        mixed[:, cols] = total.astype(bf16)


def backward_kernel(gaps, runs, query, own_kv, other_kv, mixed, grad, *refs):
    q_grad, own_grad, other_grad = refs[-3:]
    scale = HS ** (-0.5)
    own_ok, other_ok = admitted(gaps, runs)
    for head in range(HEADS):
        cols = slice(head * HS, (head + 1) * HS)
        q, g = query[:, cols], grad[:, cols]
        row_dot = jnp.sum(g.astype(f32) * mixed[:, cols].astype(f32), axis=1, keepdims=True)
        attns = head_attn(q, own_kv[0, :, cols], other_kv[0, :, cols], own_ok, other_ok)
        dq = None
        for attn, kv, kv_grad in zip(attns, (own_kv, other_kv), (own_grad, other_grad)):
            value_grad = dot_tokens(attn.astype(bf16), g)
            weight_grad = dot_rows(g, kv[1, :, cols])
            score_grad = (attn * (weight_grad - row_dot)).astype(bf16)
            part = dot(score_grad, kv[0, :, cols])
            dq = part if dq is None else dq + part
            key_grad = dot_tokens(score_grad, q) * scale
            kv_grad[0, :, cols] = key_grad.astype(kv_grad.dtype)
            kv_grad[1, :, cols] = value_grad.astype(kv_grad.dtype)
        q_grad[:, cols] = (dq * scale).astype(bf16)


ATTN_FLOPS = 2 * HEADS * SLOTS * 2 * SLOTS * HS


def attend_forward(spans, query, own_kv, other_kv, after):
    return call(
        forward_kernel,
        sds((SLOTS, COLS), bf16),
        vmem=10,
        flops=4 * ATTN_FLOPS,
        nbytes=6 * SLOTS * COLS * 2,
        in_specs=[SMEM] * 2 + [VMEM] * 3 + [ANY] * len(after),
        out_specs=VMEM,
        name="attend_forward",
    )(*spans, query, own_kv, other_kv, *after)


def attend_backward(spans, query, own_kv, other_kv, mixed, grad, after):
    kv = (2, SLOTS, COLS)
    return call(
        backward_kernel,
        [sds((SLOTS, COLS), bf16), sds(kv, f32), sds(kv, bf16)],
        vmem=14,
        flops=8 * ATTN_FLOPS,
        nbytes=12 * SLOTS * COLS * 2,
        in_specs=[SMEM] * 2 + [VMEM] * 5 + [ANY] * len(after),
        out_specs=[VMEM] * 3,
        name="attend_backward",
    )(*spans, query, own_kv, other_kv, mixed, grad, *after)


def out_kernel(grad, mixed, *refs):
    own, sent = refs[-2:]
    y_index, core = where_am_i()[2:4]
    for i in range(8):
        column = ((y_index - STEPS[i % 4]) & 3) * 2 + (1 - core if i < 4 else core)
        start = pl.multiple_of(column * COLS, COLS)
        share = dot_tokens(grad[:, pl.ds(start, COLS)], mixed[...]).astype(bf16)
        if i < 4:
            sent[i] = share
        else:
            own[i - 4] = share


def out_weight_parts(grad_full, mixed, after):
    return call(
        out_kernel,
        [sds((4, COLS, COLS), bf16)] * 2,
        vmem=12,
        flops=2 * SLOTS * WIDTH * COLS,
        nbytes=SLOTS * WIDTH * 2 + WIDTH * COLS * 2,
        in_specs=[VMEM] * 2 + [ANY] * len(after),
        out_specs=[VMEM] * 2,
        name="out_weight_parts",
    )(grad_full, mixed, *after)


def share_kernel(which, full, c1, c2, c3, g0, g1, g2, g3, g4, *refs):
    out, lefts = refs[-2:]
    y_index, core = where_am_i()[2:4]
    column = core if which else 1 - core
    start = pl.multiple_of((y_index * 2 + column) * COLS, COLS)
    lefts[0] = full[:, pl.ds(start, COLS)].T
    start = pl.multiple_of(column * COLS, COLS)
    for k, came in enumerate((c1, c2, c3), 1):
        lefts[k] = came[:, pl.ds(start, COLS)].T
    for part in range(3):
        total = dot(lefts[0], g0[part])
        for k, grad in enumerate((g1, g2), 1):
            total = total + dot(lefts[k], grad[part])
        total = total + dot(lefts[3, :, :SLOTS // 2], g3[part])
        total = total + dot(lefts[3, :, SLOTS // 2:], g4[part])
        out[part] = total.astype(out.dtype)


def weight_shares(which, full, came, grads, dtype, after=()):
    return call(
        functools.partial(share_kernel, which),
        sds((3, COLS, COLS), dtype),
        vmem=20,
        flops=3 * 4 * 2 * SLOTS * COLS * COLS,
        nbytes=16 * SLOTS * COLS * 2 + 3 * COLS * COLS * 4,
        in_specs=[VMEM] * 9 + [ANY] * len(after),
        out_specs=VMEM,
        scratch_shapes=[pltpu.VMEM((4, COLS, SLOTS), bf16)],
        name="weight_shares",
    )(full, *came, *grads, *after)


def chunk_kernel(full, *outs):
    y_index = where_am_i()[2]
    for k, out in zip(STEPS[1:], outs):
        start = pl.multiple_of(((y_index + k) & 3) * 1024, 1024)
        out[...] = full[:, pl.ds(start, 1024)]


def chunks_over_y(full):
    sends = call(
        chunk_kernel,
        [sds((SLOTS, 1024), bf16)] * 3,
        vmem=6,
        nbytes=6 * SLOTS * 1024 * 2,
        in_specs=[VMEM],
        out_specs=[VMEM] * 3,
        name="chunks",
    )(full)
    return [lax.ppermute(sent, "seq", y_shift(k)) for sent, k in zip(sends, STEPS[1:])]


def layer_kernel(x, kept, came, *refs):
    total = x[...].astype(f32) + (kept[...] + came[...].astype(f32))
    refs[-1][...] = (total * valid_rows()).astype(bf16)


def layer_rows(x, kept, came, after=()):
    return call(
        layer_kernel,
        sds((ROWS, WIDTH), bf16),
        vmem=4,
        nbytes=5 * ROWS * WIDTH * 2,
        in_specs=[VMEM] * 3 + [ANY] * len(after),
        out_specs=VMEM,
        name="layer_rows",
    )(x, kept, came, *after)


def per_device(tokens, text_gaps, image_runs, gains, w_qkv, w_out, cotangent):
    x_rows = tokens[0, 0]
    w_parts = jnp.transpose(w_qkv[0], (1, 0, 2))
    spans = (text_gaps, image_runs)

    n_left, n_right, grad_rows, inv = norm_rows(x_rows, gains, cotangent[0, 0])
    pieces = gather_blocks(n_left, n_right)
    grad_other = lax.ppermute(grad_rows, "tp", X_SWAP)
    grad_pair = touch(jnp.stack([grad_rows, grad_other]), w_parts)
    grad_pairs = [grad_pair] + [lax.ppermute(grad_pair, "tp", z_shift(k)) for k in STEPS[1:]]
    normed_full, own_kv = key_value(pieces, w_parts, [grad_pair])
    other_kv = lax.ppermute(own_kv, "grp", GRP_SWAP)
    query = query_of(normed_full, w_parts, grad_pairs[1:3])
    chunks = chunks_over_y(normed_full)

    mixed = attend_forward(spans, query, own_kv, other_kv, [])
    proj = proj_parts(mixed, w_out, [])
    grad_full, grad_mixed = grad_mixed_of(grad_pairs, w_out, [proj[0]] + chunks[:2])
    q_grad, own_part, other_part = attend_backward(
        spans, query, own_kv, other_kv, mixed, grad_mixed, []
    )
    back = lax.ppermute(other_part, "grp", GRP_SWAP)
    sends = late(proj[1:], [q_grad])
    proj_came = [lax.ppermute(v, "tp", z_shift(-k)) for v, k in zip(sends, STEPS[1:])]
    out_own, out_sent = out_weight_parts(grad_full, mixed, [q_grad])
    out_came = lax.ppermute(out_sent, "seq", CORE_SWAP)
    own_grads = sum_keys(q_grad, own_part, back, sends[:1])
    back_grads = lax.ppermute(own_grads, "seq", y_shift(1))
    next_grads = lax.ppermute(own_grads, "seq", y_shift(3))

    right = back_right(own_grads, w_parts, normed_full, [out_came] + chunks[2:])
    right_x = lax.ppermute(right[1], "tp", X_SWAP)
    left = back_left(own_grads, w_parts, normed_full, right[2], proj_came[:2])
    left_far_a = lax.ppermute(left[3], "tp", z_shift(1))
    left_far_b = lax.ppermute(left[4], "tp", z_shift(3))
    left_back, left_forth = pass_left(left[1], left[2], left_far_a, left_far_b, proj_came[2:])
    left_came = [
        lax.ppermute(left_forth, "tp", z_shift(1)), lax.ppermute(left_back, "tp", z_shift(3))
    ]
    out_kept, *out_sends = sum_out(
        out_own, out_came, [left_back, back_grads, next_grads, right_x]
    )
    out_far_a = lax.ppermute(out_sends[2], "seq", y_shift(1))
    out_far_b = lax.ppermute(out_sends[3], "seq", y_shift(3))
    out_back, out_forth = pass_out(
        out_sends[0], out_sends[1], out_far_a, out_far_b
    )
    out_terms = [
        lax.ppermute(out_forth, "seq", y_shift(1)), lax.ppermute(out_back, "seq", y_shift(3))
    ]
    left_kept, left_sent, gain_kept = sum_left(left[0], left_came, [out_back])
    left_x = lax.ppermute(left_sent, "tp", X_SWAP)
    gain_tp = sum_gain(gain_kept, left_x, gains)
    gain_sum = gain_tp + lax.ppermute(gain_tp, "seq", CORE_SWAP)
    gain_grad = gain_sum
    for k in STEPS[1:]:
        gain_grad = gain_grad + lax.ppermute(gain_sum, "seq", y_shift(k))
    right_kept, *right_sends = sum_x(
        right[0], right_x, [left_sent]
    )
    right_came = [lax.ppermute(v, "tp", z_shift(-k)) for v, k in zip(right_sends, STEPS[1:])]
    relayed = halves(
        back_grads, next_grads, [gain_tp] + right_came + out_terms
    )
    grads = [own_grads, back_grads, next_grads]
    grads += [lax.ppermute(v, "seq", y_shift(k)) for v, k in zip(relayed, (1, 3))]
    shares = (normed_full, chunks, grads)
    qkv_sent = weight_shares(0, *shares, bf16, [gain_sum])
    qkv_mine = weight_shares(1, *shares, f32, [qkv_sent])
    out_share = sum_rest(out_kept, out_terms, [qkv_sent])
    tokens_grad = token_rows(
        x_rows, grad_rows, gains, inv, (left_kept, left_x), (right_kept, *right_came), [qkv_mine, out_share]
    )

    qkv_share = qkv_mine + lax.ppermute(qkv_sent, "seq", CORE_SWAP).astype(f32)
    proj_kept, proj_sent = sum_z(proj[0], proj_came)
    proj_x = lax.ppermute(proj_sent, "tp", X_SWAP)
    layer_out = layer_rows(x_rows, proj_kept, proj_x, [tokens_grad])
    return (
        layer_out[None, None],
        tokens_grad[None, None],
        gain_grad,
        jnp.transpose(qkv_share, (1, 0, 2))[None],
        out_share[None],
    )


def solution(mesh):
    in_specs = (
        P("grp", "seq", "tp", None),
        P("seq", None),
        P("seq", None),
        P("grp", None),
        P("grp", None, None, "tp"),
        P("grp", None, "tp"),
        P("grp", "seq", "tp", None),
    )
    out_specs = (
        P("grp", "seq", "tp", None),
        P("grp", "seq", "tp", None),
        P("grp", None),
        P("grp", "seq", None, "tp"),
        P("grp", "seq", "tp"),
    )
    return jax.shard_map(
        per_device, mesh=mesh, in_specs=in_specs, out_specs=out_specs, check_vma=False
    )
```
